32 devices in a mesh: ex: 4 (over z), feat: 8 (over y, x, core).
Axes of the slice: x: 2, y: 2, z: 4, core: 2. Of those that a mesh axis runs over, the one named last changes fastest.
Arguments:
- dosages: bfloat16 [16384, 4096], P('ex', 'feat'), may hold values from -6 to 6
- coefficients: bfloat16 [4096], P('feat'), may hold values from -0.046875 to 0.046875
- directions: bfloat16 [4096, 128], P('feat'), may hold values from -6 to 6
- event_rank: int32 [16384], P('ex'), may hold values from 0 to 16383, as said below
- events: int32 [16384], P('ex'), may hold values from 0 to 1, as said below
Outputs:
- hessian_product: float32 [4096, 128], P('feat')
The draws below stay inside these ranges and needn't reach their ends.
Inputs may be any that keep to these rules, and one draw needn't show every extreme that they name: `event_rank`: the 4096 persons of each aligned block b (one index of ex) hold the ranks b * 4096 to (b + 1) * 4096 - 1, each once, in any order. `events`: the first person of every aligned block of 4096 persons has an event.
All inputs are finite; a program needn't handle non-finite values.
Results may differ from the reference program's by a relative error of at most 0.00084.
Values may be sent and summed in bfloat16 or wider, within the bound.
No kernel may reach another device: no remote copies, remote signals or barrier semaphores. Data moves between devices by JAX's collectives and lax.ppermute only.
A program may use at most 64 MiB of HBM per device.

```python
import jax
import jax.numpy as jnp

P_SIZE = 4096
K = 128
ROWS = 4096
PERSONS = 16384


def draw_dosages(key, part):
    blocks = PERSONS // ROWS
    spread = jax.random.normal(jax.random.fold_in(key, 3), (P_SIZE,), jnp.float32)
    block_of = (jnp.arange(PERSONS, dtype=jnp.int32) // ROWS).astype(jnp.float32)
    level = 2.0 * block_of / max(blocks - 1, 1) - 1.0
    noise = jax.random.normal(jax.random.fold_in(key, 5), (PERSONS, P_SIZE), jnp.float32)
    amplitude = 0.5
    values = noise + amplitude * level[:, None] * spread[None, :]
    return jnp.clip(values, -6.0, 6.0).astype(jnp.bfloat16)


def draw_event_rank(key, part):
    blocks = PERSONS // ROWS
    orders = jax.vmap(lambda number: jax.random.permutation(jax.random.fold_in(key, number), ROWS))(jnp.arange(blocks))
    return (orders + jnp.arange(blocks)[:, None] * ROWS).reshape(-1).astype(jnp.int32)


def draw_events(key, part):
    position = jnp.arange(PERSONS, dtype=jnp.int32)
    limit = 100 + 400 * position // PERSONS
    drawn = jax.random.randint(jax.random.fold_in(key, 7), (PERSONS,), 0, 1000)
    return ((drawn < limit) | (position % ROWS == 0)).astype(jnp.int32)


def block_levels(rng, shape, shards, low, high):
    level, own = 1.0, jax.random.fold_in(rng, 6)
    for dim, parts in shards:
        steps = jnp.exp(jax.random.uniform(jax.random.fold_in(own, dim), (parts,), jnp.float32, low / len(shards), high / len(shards)))
        level = level * jnp.repeat(steps, shape[dim] // parts).reshape([-1 if axis == dim else 1 for axis in range(len(shape))])
    return level


def centred(rng, shape, width, most, cuts=(), kind=jnp.bfloat16):
    array = jax.random.normal(rng, shape, jnp.float32) * width
    if len(cuts) > 0:
        array = block_levels(rng, shape, cuts, -0.22, 0.18) * array
    return jnp.clip(array, min=-most, max=most).astype(kind)


def setup_inputs(seed: int = 0) -> dict:
    keys = jax.random.split(jax.random.key(seed), 6)
    return {
        "dosages": draw_dosages(jax.random.fold_in(keys[5], 71), 0),
        "coefficients": centred(keys[1], (P_SIZE,), (4 * P_SIZE) ** -0.5, 0.046875, ((0, 8),)),
        "directions": centred(keys[2], (P_SIZE, K), 1.0, 6.0, ((0, 8),)),
        "event_rank": draw_event_rank(jax.random.fold_in(keys[5], 71), 0),
        "events": draw_events(jax.random.fold_in(keys[5], 71), 0),
    }


def reference(dosages, coefficients, directions, event_rank, events):
    linear = jnp.dot(dosages, coefficients, preferred_element_type=jnp.float32)
    risk = jnp.exp(linear)
    tangent = jnp.dot(dosages, directions, preferred_element_type=jnp.float32)
    weighted_t = tangent * risk[:, None]
    order = jnp.argsort(event_rank)
    risk_sorted = risk[order]
    tangent_sorted = weighted_t[order]
    event_sorted = events[order].astype(jnp.float32)
    risk_sum = jnp.cumsum(risk_sorted[::-1])[::-1]
    tangent_sum = jnp.cumsum(tangent_sorted[::-1], axis=0)[::-1]
    hazard = event_sorted / risk_sum
    hazard_tangent = tangent_sum * (event_sorted / (risk_sum * risk_sum))[:, None]
    cumulative = jnp.cumsum(hazard)[event_rank]
    cumulative_tangent = jnp.cumsum(hazard_tangent, axis=0)[event_rank]
    weighted = (risk[:, None] * (tangent * cumulative[:, None] - cumulative_tangent)).astype(jnp.bfloat16)
    total = jnp.dot(dosages.T, weighted, preferred_element_type=jnp.float32)
    return total / jnp.sum(events.astype(jnp.float32))
```

```python
import functools

import jax
import jax.numpy as jnp
from jax import lax
from jax.experimental import pallas as pl
from jax.experimental.pallas import tpu as pltpu
from jax.sharding import PartitionSpec as P

F32 = jnp.float32
BF16 = jnp.bfloat16
LO = 256
NT = (((1,), (1,)), ((), ()))
VMEM = pl.BlockSpec(memory_space=pltpu.VMEM)
HIGHEST = lax.Precision.HIGHEST
PARAMS = dict(vmem_limit_bytes=48 * 1024 * 1024)


def swap(x, axis, i):
    count = lax.axis_size(axis)
    return lax.ppermute(x, axis, [(s, s ^ i) for s in range(count)])


def split_two(x):
    high = x.astype(BF16).astype(F32)
    return high, x - high


def split_three(x):
    first, rest = split_two(x)
    second, third = split_two(rest)
    return first, second, third


def one_hot(values, count, kind=BF16):
    shape = (count, values.shape[1])
    return jnp.where(lax.broadcasted_iota(jnp.int32, shape, 0) == values, 1.0, 0.0).astype(kind)


def triangle(n, keep):
    first = lax.broadcasted_iota(jnp.int32, (n, n), 0)
    second = lax.broadcasted_iota(jnp.int32, (n, n), 1)
    return jnp.where(keep(first, second), 1.0, 0.0)


def exact_dot(a, b):
    return jnp.dot(a, b, precision=HIGHEST, preferred_element_type=F32)


def product_kernel(feat, kf, directions, coefficients, dosages, *refs):
    linear, keep, send = refs[0], refs[1 : 1 + feat // 2], refs[1 + feat // 2 : 1 + feat]
    lhs, turned = refs[1 + feat :]
    me = lax.axis_index("feat")
    width = feat * kf

    @pl.when(pl.program_id(0) == 0)
    def _():
        turned[...] = directions[...].astype(F32).T.reshape(turned.shape)
        for i in range(feat):
            lhs[i * kf : (i + 1) * kf] = turned[me ^ i].astype(BF16)
        lhs[width:] = jnp.broadcast_to(coefficients[...].astype(F32), (16, lhs.shape[1])).astype(BF16)

    result = lax.dot_general(lhs[...], dosages[...], NT, preferred_element_type=F32)
    linear[...] = result[width : width + 1]
    for i in range(feat):
        (send if i % 2 else keep)[i // 2][...] = result[i * kf : (i + 1) * kf]


def products(dosages, coefficients, directions, feat):
    persons, variants = dosages.shape
    k = directions.shape[1]
    kf = k // feat
    chunk = min(512, persons)
    piece = jax.ShapeDtypeStruct((kf, persons), F32)
    out = pl.pallas_call(
        functools.partial(product_kernel, feat, kf),
        grid=(persons // chunk,),
        in_specs=[
            pl.BlockSpec((variants, k), lambda s: (0, 0)),
            pl.BlockSpec((1, variants), lambda s: (0, 0)),
            pl.BlockSpec((chunk, variants), lambda s: (s, 0)),
        ],
        out_shape=[jax.ShapeDtypeStruct((1, persons), F32)] + [piece] * feat,
        out_specs=[pl.BlockSpec((1, chunk), lambda s: (0, s))]
        + [pl.BlockSpec((kf, chunk), lambda s: (0, s))] * feat,
        scratch_shapes=[
            pltpu.VMEM((k + 16, variants), BF16),
            pltpu.VMEM((feat, kf, variants), F32),
        ],
        compiler_params=pltpu.CompilerParams(**PARAMS),
        cost_estimate=pl.CostEstimate(
            flops=2 * persons * variants * k, bytes_accessed=persons * (variants * 2 + k * 4), transcendentals=0
        ),
        name="products",
    )(directions, coefficients[None], dosages)
    return out[0], out[1 : 1 + feat // 2], out[1 + feat // 2 :]


def risk_kernel(rows, parts, *refs):
    linear, (rank, events) = refs[:parts], refs[parts : parts + 2]
    risk_out, sums_out, events_out, message = refs[parts + 2 :]
    groups = rows // LO
    total = linear[0][...]
    for part in linear[1:]:
        total = total + part[...]
    risk = jnp.exp(total)
    risk_out[...] = risk
    place = lax.rem(rank[...], rows)
    mask = one_hot(place // LO, groups, F32)
    pieces = [mask * part for part in split_three(risk)] + [mask * events[...].astype(F32)]
    lhs = jnp.concatenate(pieces, axis=0).astype(BF16)
    sorted_all = lax.dot_general(lhs, one_hot(lax.rem(place, LO), LO), NT, preferred_element_type=F32)
    ordered = sorted_all[:groups] + sorted_all[groups : 2 * groups] + sorted_all[2 * groups : 3 * groups]
    happened = sorted_all[3 * groups :]
    inside = exact_dot(ordered, triangle(LO, lambda a, b: a >= b))
    totals = exact_dot(ordered, jnp.ones((LO, LO), F32))
    carried = exact_dot(triangle(groups, lambda a, b: a < b), totals)
    sums_out[...] = inside + carried
    events_out[...] = happened
    everything = jnp.sum(totals, axis=0, keepdims=True)[:, :128]
    count = jnp.sum(exact_dot(happened, jnp.ones((LO, 128), F32)), axis=0, keepdims=True)
    message[...] = jnp.concatenate([everything, count, jnp.zeros((6, 128), F32)], axis=0)


def risks(linear, rank, events, rows):
    groups = rows // LO
    return pl.pallas_call(
        functools.partial(risk_kernel, rows, len(linear)),
        in_specs=[VMEM] * (len(linear) + 2),
        out_shape=[
            jax.ShapeDtypeStruct((1, rows), F32),
            jax.ShapeDtypeStruct((groups, LO), F32),
            jax.ShapeDtypeStruct((groups, LO), F32),
            jax.ShapeDtypeStruct((8, 128), F32),
        ],
        out_specs=[VMEM] * 4,
        compiler_params=pltpu.CompilerParams(**PARAMS),
        cost_estimate=pl.CostEstimate(flops=rows * LO * 128, bytes_accessed=rows * 64, transcendentals=rows),
        name="risks",
    )(*linear, rank, events)


def hazard_kernel(rows, ex, *refs):
    messages, (sums, events, rank) = refs[:ex], refs[ex : ex + 3]
    cumulative, squares, ordered_squares, message, count_out = refs[ex + 3 :]
    groups = rows // LO
    me = lax.axis_index("ex")
    later = jnp.zeros((1, 1), F32)
    count = messages[0][1:2, :]
    for i in range(1, ex):
        later = later + jnp.where((me ^ i) > me, messages[i][0:1, 0:1], 0.0)
        count = count + messages[i][1:2, :]
    count_out[...] = jnp.broadcast_to(count, count_out.shape)
    risk_sum = sums[...] + later
    hazard = events[...] / risk_sum
    square = events[...] / (risk_sum * risk_sum)
    ordered_squares[...] = square
    both = jnp.concatenate([hazard, square], axis=0)
    inside = exact_dot(both, triangle(LO, lambda a, b: a <= b))
    totals = exact_dot(both, jnp.ones((LO, LO), F32))
    before = triangle(groups, lambda a, b: a > b)
    carried = jnp.concatenate(
        [exact_dot(before, totals[:groups]), exact_dot(before, totals[groups:])], axis=0
    )
    message[...] = jnp.concatenate(
        [
            jnp.sum(totals[:groups], axis=0, keepdims=True)[:, :128],
            jnp.sum(totals[groups:], axis=0, keepdims=True)[:, :128],
            jnp.zeros((6, 128), F32),
        ],
        axis=0,
    )
    place = lax.rem(rank[...], rows)
    mask = one_hot(place // LO, groups, F32)
    spread = one_hot(lax.rem(place, LO), LO)
    placed = jnp.zeros((2 * groups, rows), F32)
    for part in split_three(inside + carried):
        placed = placed + jnp.dot(part.astype(BF16), spread, preferred_element_type=F32)
    cumulative[...] = jnp.sum(mask * placed[:groups], axis=0, keepdims=True)
    squares[...] = jnp.sum(mask * placed[groups:], axis=0, keepdims=True)


def hazards(messages, sums, events, rank, rows):
    groups = rows // LO
    row = jax.ShapeDtypeStruct((1, rows), F32)
    small = jax.ShapeDtypeStruct((8, 128), F32)
    return pl.pallas_call(
        functools.partial(hazard_kernel, rows, len(messages)),
        in_specs=[VMEM] * (len(messages) + 3),
        out_shape=[row, row, jax.ShapeDtypeStruct((groups, LO), F32), small, small],
        out_specs=[VMEM] * 5,
        compiler_params=pltpu.CompilerParams(**PARAMS),
        cost_estimate=pl.CostEstimate(flops=rows * LO * 200, bytes_accessed=rows * 64, transcendentals=0),
        name="hazards",
    )(*messages, sums, events, rank)


def scan_kernel(rows, kf, parts, *refs):
    tangents = refs[:parts]
    risk, rank, squares, hazard_message = refs[parts : parts + 4]
    tangent_out, cumulative_out, message = refs[parts + 4 : parts + 7]
    lhs, spread = refs[parts + 7 :]
    groups = rows // LO
    chunk = min(1024, rows)
    ordered = jnp.zeros((groups * 2 * kf, LO), F32)
    for start in range(0, rows, chunk):
        at = slice(start, start + chunk)
        tangent = tangents[0][:, at]
        for part in tangents[1:]:
            tangent = tangent + part[:, at]
        tangent_out[:, at] = tangent
        place = lax.rem(rank[:, at], rows)
        group = place // LO
        spread[:, at] = one_hot(lax.rem(place, LO), LO)
        both = jnp.concatenate(split_two(tangent * risk[:, at]), axis=0)
        for g in range(groups):
            lhs[g * 2 * kf : (g + 1) * 2 * kf, at] = jnp.where(group == g, both, 0.0).astype(BF16)
        ordered = ordered + lax.dot_general(lhs[:, at], spread[:, at], NT, preferred_element_type=F32)
    ordered = jnp.concatenate(
        [
            ordered[g * 2 * kf : g * 2 * kf + kf] + ordered[g * 2 * kf + kf : (g + 1) * 2 * kf]
            for g in range(groups)
        ],
        axis=0,
    )
    everything = jnp.ones((LO, LO), F32)
    inside = exact_dot(ordered, triangle(LO, lambda a, b: a >= b))
    totals = exact_dot(ordered, everything)
    carried = jnp.zeros((kf, LO), F32)
    hazard = [None] * groups
    for g in reversed(range(groups)):
        rows_of = slice(g * kf, (g + 1) * kf)
        hazard[g] = (inside[rows_of] + carried) * squares[g : g + 1, :]
        carried = carried + totals[rows_of]
    message[0] = carried[:, :128]
    hazard = jnp.concatenate(hazard, axis=0)
    inside = exact_dot(hazard, triangle(LO, lambda a, b: a <= b))
    totals = exact_dot(hazard, everything)
    carried = jnp.zeros((kf, LO), F32)
    summed = [None] * groups
    for g in range(groups):
        rows_of = slice(g * kf, (g + 1) * kf)
        summed[g] = inside[rows_of] + carried
        carried = carried + totals[rows_of]
    message[1] = carried[:, :128]
    message[2] = jnp.broadcast_to(hazard_message[0:1, :], (kf, 128))
    message[3] = jnp.broadcast_to(hazard_message[1:2, :], (kf, 128))
    high, low = split_two(jnp.concatenate(summed, axis=0))
    high, low = high.astype(BF16), low.astype(BF16)
    for start in range(0, rows, chunk):
        at = slice(start, start + chunk)
        group = lax.rem(rank[:, at], rows) // LO
        placed = jnp.dot(high, spread[:, at], preferred_element_type=F32) + jnp.dot(
            low, spread[:, at], preferred_element_type=F32
        )
        picked = jnp.zeros((kf, chunk), F32)
        for g in range(groups):
            picked = picked + jnp.where(group == g, placed[g * kf : (g + 1) * kf], 0.0)
        cumulative_out[:, at] = picked


def scans(tangents, risk, rank, squares, hazard_message, rows):
    kf = tangents[0].shape[0]
    groups = rows // LO
    block = jax.ShapeDtypeStruct((kf, rows), F32)
    return pl.pallas_call(
        functools.partial(scan_kernel, rows, kf, len(tangents)),
        in_specs=[VMEM] * (len(tangents) + 4),
        out_shape=[block, block, jax.ShapeDtypeStruct((4, kf, 128), F32)],
        out_specs=[VMEM] * 3,
        scratch_shapes=[pltpu.VMEM((groups * 2 * kf, rows), BF16), pltpu.VMEM((LO, rows), BF16)],
        compiler_params=pltpu.CompilerParams(**PARAMS),
        cost_estimate=pl.CostEstimate(
            flops=4 * rows * LO * groups * 2 * kf, bytes_accessed=rows * kf * 24, transcendentals=0
        ),
        name="scans",
    )(*tangents, risk, rank, squares, hazard_message)


def weight_kernel(ex, *refs):
    messages, (tangent, local, risk, cumulative, squares) = refs[:ex], refs[ex : ex + 5]
    weighted, placed = refs[ex + 5 :]
    me = lax.axis_index("ex")
    for i in range(ex):
        placed[me ^ i] = messages[i][...]
    later = jnp.zeros(placed.shape[2:], F32)
    own_later = later
    before = later
    hazard_before = later
    for b in reversed(range(ex)):
        own_later = own_later + jnp.where(b > me, placed[b, 0], 0.0)
        before = before + jnp.where(b < me, placed[b, 1] + placed[b, 3] * later, 0.0)
        hazard_before = hazard_before + jnp.where(b < me, placed[b, 2], 0.0)
        later = later + placed[b, 0]
    own_later, before = own_later[:, :1], before[:, :1]
    hazard_before = hazard_before[:1, :1]
    value = tangent[...] * (cumulative[...] + hazard_before) - (local[...] + squares[...] * own_later + before)
    weighted[...] = (risk[...] * value).astype(BF16)


def weights(messages, tangent, local, risk, cumulative, squares):
    ex = len(messages)
    return pl.pallas_call(
        functools.partial(weight_kernel, ex),
        in_specs=[VMEM] * (ex + 5),
        out_shape=jax.ShapeDtypeStruct(tangent.shape, BF16),
        out_specs=VMEM,
        scratch_shapes=[pltpu.VMEM((ex,) + messages[0].shape, F32)],
        compiler_params=pltpu.CompilerParams(**PARAMS),
        name="weights",
    )(*messages, tangent, local, risk, cumulative, squares)


def gradient_kernel(feat, ex, kf, *refs):
    parts, dosages, outs = refs[:feat], refs[feat], refs[feat + 1 : feat + 1 + ex]
    weighted, total, turned = refs[feat + 1 + ex :]
    step, steps = pl.program_id(0), pl.num_programs(0)
    me = lax.axis_index("feat")
    place = lax.axis_index("ex")
    chunk = dosages.shape[0]

    @pl.when(step == 0)
    def _():
        total[...] = jnp.zeros_like(total)
        for i in range(feat):
            weighted[pl.ds(pl.multiple_of((me ^ i) * kf, kf), kf), :] = parts[i][...]

    at = pl.ds(pl.multiple_of(step * chunk, chunk), chunk)
    total[...] += jnp.dot(weighted[:, at], dosages[...], preferred_element_type=F32)

    @pl.when(step == steps - 1)
    def _():
        turned[...] = total[...].T.reshape(turned.shape)
        for i in range(ex):
            outs[i][...] = turned[place ^ i]


def gradients(parts, dosages, ex):
    feat = len(parts)
    kf, persons = parts[0].shape
    k, variants = kf * feat, dosages.shape[1]
    chunk = min(512, persons)
    piece = (variants // ex, k)
    return pl.pallas_call(
        functools.partial(gradient_kernel, feat, ex, kf),
        grid=(persons // chunk,),
        in_specs=[pl.BlockSpec((kf, persons), lambda s: (0, 0))] * feat
        + [pl.BlockSpec((chunk, variants), lambda s: (s, 0))],
        out_shape=[jax.ShapeDtypeStruct(piece, F32)] * ex,
        out_specs=[pl.BlockSpec(piece, lambda s: (0, 0))] * ex,
        scratch_shapes=[
            pltpu.VMEM((k, persons), BF16),
            pltpu.VMEM((k, variants), F32),
            pltpu.VMEM((ex,) + piece, F32),
        ],
        compiler_params=pltpu.CompilerParams(**PARAMS),
        cost_estimate=pl.CostEstimate(
            flops=2 * persons * variants * k, bytes_accessed=persons * (variants * 2 + k * 2), transcendentals=0
        ),
        name="gradients",
    )(*parts, dosages)


def place_kernel(ex, *refs):
    parts, out = refs[:ex], refs[ex]
    me = lax.axis_index("ex")
    for i in range(ex):
        out[me ^ i] = parts[i][...]


def place_all(parts):
    ex = len(parts)
    out = pl.pallas_call(
        functools.partial(place_kernel, ex),
        in_specs=[VMEM] * ex,
        out_shape=jax.ShapeDtypeStruct((ex,) + parts[0].shape, F32),
        out_specs=VMEM,
        compiler_params=pltpu.CompilerParams(**PARAMS),
        name="place",
    )(*parts)
    return out.reshape(-1, parts[0].shape[1])


def local(dosages, coefficients, directions, event_rank, events):
    feat, ex = lax.axis_size("feat"), lax.axis_size("ex")
    rows = dosages.shape[0]
    variants, k = directions.shape
    each = k // feat
    padded = -(-each // 16) * 16
    if padded != each:
        directions = jnp.pad(directions.reshape(variants, feat, each), ((0, 0), (0, 0), (0, padded - each)))
        directions = directions.reshape(variants, feat * padded)
    rank, event_row = event_rank[None], events[None]

    linear, keep, send = products(dosages, coefficients, directions, feat)
    linear_parts = [linear] + [swap(linear, "feat", i) for i in range(1, feat)]
    order = list(range(1, feat // 2)) + [0]
    joined = {q: (keep[q], swap(send[q], "feat", 1)) for q in order}
    others = [swap(joined[q][0] + joined[q][1], "feat", 2 * q) for q in order[:-1]]

    risk, sums, ordered_events, message = risks(linear_parts, rank, event_row, rows)
    messages = [message] + [swap(message, "ex", i) for i in range(1, ex)]
    cumulative, squares, ordered_squares, hazard_message, count = hazards(
        messages, sums, ordered_events, rank, rows
    )

    tangent, summed, message = scans(
        list(joined[0]) + others, risk, rank, ordered_squares, hazard_message, rows
    )
    messages = [message] + [swap(message, "ex", i) for i in range(1, ex)]
    own = weights(messages, tangent, summed, risk, cumulative, squares)

    chips = {0: own}
    for q in order[:-1]:
        chips[q] = swap(own, "feat", 2 * q)
    parts = []
    for q in range(feat // 2):
        parts += [chips[q], swap(chips[q], "feat", 1)]

    pieces = gradients(parts, dosages, ex)
    total = pieces[0]
    for i in range(1, ex):
        total = total + swap(pieces[i], "ex", i)
    total = total / count[0, 0]
    result = place_all([total] + [swap(total, "ex", i) for i in range(1, ex)])
    if padded != each:
        result = result.reshape(variants, feat, padded)[:, :, :each].reshape(variants, k)
    return result


def solution(mesh):
    placed = (P("ex", "feat"), P("feat"), P("feat", None), P("ex"), P("ex"))
    return jax.shard_map(
        local, mesh=mesh, in_specs=placed, out_specs=P("feat", None), check_vma=False
    )
```

```python
import functools

import jax
import jax.numpy as jnp
from jax import lax
from jax.experimental import pallas as pl
from jax.experimental.pallas import tpu as pltpu
from jax.sharding import PartitionSpec as P

F32 = jnp.float32
BF16 = jnp.bfloat16
LO = 256
NT = (((1,), (1,)), ((), ()))
VMEM = pl.BlockSpec(memory_space=pltpu.VMEM)
HIGHEST = lax.Precision.HIGHEST
PARAMS = dict(vmem_limit_bytes=48 * 1024 * 1024)


def swap(x, axis, i):
    count = lax.axis_size(axis)
    return lax.ppermute(x, axis, [(s, s ^ i) for s in range(count)])


def exchange(x, axis):
    return lax.all_to_all(x, axis, 0, 0)


def split_two(x):
    high = x.astype(BF16).astype(F32)
    return high, x - high


def split_three(x):
    first, rest = split_two(x)
    second, third = split_two(rest)
    return first, second, third


def one_hot(values, count, kind=BF16):
    shape = (count, values.shape[1])
    return jnp.where(lax.broadcasted_iota(jnp.int32, shape, 0) == values, 1.0, 0.0).astype(kind)


def triangle(n, keep):
    first = lax.broadcasted_iota(jnp.int32, (n, n), 0)
    second = lax.broadcasted_iota(jnp.int32, (n, n), 1)
    return jnp.where(keep(first, second), 1.0, 0.0)


def exact_dot(a, b):
    return jnp.dot(a, b, precision=HIGHEST, preferred_element_type=F32)


def dot_binary(a, b):
    b = b.astype(BF16)
    total = None
    for part in split_three(a):
        term = jnp.dot(part.astype(BF16), b, preferred_element_type=F32)
        total = term if total is None else total + term
    return total


def product_kernel(feat, kf, directions, coefficients, dosages, *refs):
    linear, keep, send = refs[0], refs[1 : 1 + feat // 2], refs[1 + feat // 2 : 1 + feat]
    rhs, turned = refs[1 + feat :]
    me = lax.axis_index("feat")
    width = feat * kf
    variants = rhs.shape[0]

    @pl.when(pl.program_id(0) == 0)
    def _():
        rhs[:, :width] = directions[...]
        spread = jnp.broadcast_to(coefficients[...].astype(F32), (128, variants)).T
        rhs[:, width:] = spread.astype(BF16)

    result = jnp.dot(dosages[...], rhs[...], preferred_element_type=F32)
    turned[...] = result[:, :width].T.reshape(turned.shape)
    for i in range(feat):
        (send if i % 2 else keep)[i // 2][...] = turned[me ^ i]
    diagonal = triangle(128, lambda a, b: a == b)
    for start in range(0, dosages.shape[0], 128):
        block = result[start : start + 128, width:]
        row = jnp.sum(block * diagonal, axis=0, keepdims=True)
        linear[:, :, start : start + 128] = jnp.broadcast_to(row[None], (feat, 1, 128))


def products(dosages, coefficients, directions, feat):
    persons, variants = dosages.shape
    k = directions.shape[1]
    kf = k // feat
    chunk = min(512, persons)
    piece = jax.ShapeDtypeStruct((kf, persons), F32)
    out = pl.pallas_call(
        functools.partial(product_kernel, feat, kf),
        grid=(persons // chunk,),
        in_specs=[
            pl.BlockSpec((variants, k), lambda s: (0, 0)),
            pl.BlockSpec((1, variants), lambda s: (0, 0)),
            pl.BlockSpec((chunk, variants), lambda s: (s, 0)),
        ],
        out_shape=[jax.ShapeDtypeStruct((feat, 1, persons), F32)] + [piece] * feat,
        out_specs=[pl.BlockSpec((feat, 1, chunk), lambda s: (0, 0, s))]
        + [pl.BlockSpec((kf, chunk), lambda s: (0, s))] * feat,
        scratch_shapes=[
            pltpu.VMEM((variants, k + 128), BF16),
            pltpu.VMEM((feat, kf, chunk), F32),
        ],
        compiler_params=pltpu.CompilerParams(**PARAMS),
        cost_estimate=pl.CostEstimate(
            flops=2 * persons * variants * k, bytes_accessed=persons * (variants * 2 + k * 4), transcendentals=0
        ),
        name="products",
    )(directions, coefficients[None], dosages)
    return out[0], out[1 : 1 + feat // 2], out[1 + feat // 2 :]


def risk_kernel(rows, linear, rank, events, risk_out, sums_out, events_out, message):
    groups = rows // LO
    total = linear[0]
    for i in range(1, linear.shape[0]):
        total = total + linear[i]
    risk = jnp.exp(total)
    risk_out[...] = risk
    place = lax.rem(rank[...], rows)
    mask = one_hot(place // LO, groups, F32)
    pieces = [mask * part for part in split_three(risk)] + [mask * events[...].astype(F32)]
    lhs = jnp.concatenate(pieces, axis=0).astype(BF16)
    sorted_all = lax.dot_general(lhs, one_hot(lax.rem(place, LO), LO), NT, preferred_element_type=F32)
    ordered = sorted_all[:groups] + sorted_all[groups : 2 * groups] + sorted_all[2 * groups : 3 * groups]
    happened = sorted_all[3 * groups :]
    inside = dot_binary(ordered, triangle(LO, lambda a, b: a >= b))
    totals = jnp.broadcast_to(inside[:, :1], inside.shape)
    carried = exact_dot(triangle(groups, lambda a, b: a < b), totals)
    sums_out[...] = inside + carried
    events_out[...] = happened
    everything = jnp.sum(totals, axis=0, keepdims=True)[:, :128]
    count = jnp.sum(dot_binary(happened, jnp.ones((LO, 128), F32)), axis=0, keepdims=True)
    packed = jnp.concatenate([everything, count, jnp.zeros((6, 128), F32)], axis=0)
    message[...] = jnp.broadcast_to(packed[None], message.shape)


def risks(linear, rank, events, rows, ex):
    groups = rows // LO
    return pl.pallas_call(
        functools.partial(risk_kernel, rows),
        in_specs=[VMEM] * 3,
        out_shape=[
            jax.ShapeDtypeStruct((1, rows), F32),
            jax.ShapeDtypeStruct((groups, LO), F32),
            jax.ShapeDtypeStruct((groups, LO), F32),
            jax.ShapeDtypeStruct((ex, 8, 128), F32),
        ],
        out_specs=[VMEM] * 4,
        compiler_params=pltpu.CompilerParams(**PARAMS),
        cost_estimate=pl.CostEstimate(flops=rows * LO * 128, bytes_accessed=rows * 64, transcendentals=rows),
        name="risks",
    )(linear, rank, events)


def hazard_kernel(rows, messages, sums, events, rank, *outs):
    cumulative, squares, ordered_squares, message, count_out = outs
    groups = rows // LO
    me = lax.axis_index("ex")
    later = jnp.zeros((1, 1), F32)
    count = jnp.zeros((1, 128), F32)
    for b in range(messages.shape[0]):
        later = later + jnp.where(b > me, messages[b, 0:1, 0:1], 0.0)
        count = count + messages[b, 1:2, :]
    count_out[...] = jnp.broadcast_to(count, count_out.shape)
    risk_sum = sums[...] + later
    hazard = events[...] / risk_sum
    square = events[...] / (risk_sum * risk_sum)
    ordered_squares[...] = square
    both = jnp.concatenate([hazard, square], axis=0)
    inside = dot_binary(both, triangle(LO, lambda a, b: a <= b))
    totals = jnp.broadcast_to(inside[:, LO - 1 :], inside.shape)
    before = triangle(groups, lambda a, b: a > b)
    carried = jnp.concatenate(
        [exact_dot(before, totals[:groups]), exact_dot(before, totals[groups:])], axis=0
    )
    message[...] = jnp.concatenate(
        [
            jnp.sum(totals[:groups], axis=0, keepdims=True)[:, :128],
            jnp.sum(totals[groups:], axis=0, keepdims=True)[:, :128],
            jnp.zeros((6, 128), F32),
        ],
        axis=0,
    )
    place = lax.rem(rank[...], rows)
    mask = one_hot(place // LO, groups, F32)
    placed = dot_binary(inside + carried, one_hot(lax.rem(place, LO), LO))
    cumulative[...] = jnp.sum(mask * placed[:groups], axis=0, keepdims=True)
    squares[...] = jnp.sum(mask * placed[groups:], axis=0, keepdims=True)


def hazards(messages, sums, events, rank, rows):
    groups = rows // LO
    row = jax.ShapeDtypeStruct((1, rows), F32)
    small = jax.ShapeDtypeStruct((8, 128), F32)
    return pl.pallas_call(
        functools.partial(hazard_kernel, rows),
        in_specs=[VMEM] * 4,
        out_shape=[row, row, jax.ShapeDtypeStruct((groups, LO), F32), small, small],
        out_specs=[VMEM] * 5,
        compiler_params=pltpu.CompilerParams(**PARAMS),
        cost_estimate=pl.CostEstimate(flops=rows * LO * 200, bytes_accessed=rows * 64, transcendentals=0),
        name="hazards",
    )(messages, sums, events, rank)


def total_kernel(parts, *refs):
    tangents = refs[:parts]
    risk, squares, hazard_message, tangent_out, message = refs[parts:]
    kf, rows = tangent_out.shape
    plain = jnp.zeros((kf, 128), F32)
    scaled = jnp.zeros((kf, 128), F32)
    for start in range(0, rows, 128):
        at = slice(start, start + 128)
        tangent = tangents[0][:, at]
        for part in tangents[1:]:
            tangent = tangent + part[:, at]
        tangent_out[:, at] = tangent
        weighted = tangent * risk[:, at]
        plain = plain + weighted
        scaled = scaled + weighted * squares[:, at]
    packed = jnp.concatenate([plain, scaled, hazard_message[...]], axis=0)
    message[...] = jnp.broadcast_to(packed[None], message.shape)


def block_totals(tangents, risk, squares, hazard_message, ex):
    kf, rows = tangents[0].shape
    return pl.pallas_call(
        functools.partial(total_kernel, len(tangents)),
        in_specs=[VMEM] * (len(tangents) + 3),
        out_shape=[
            jax.ShapeDtypeStruct((kf, rows), F32),
            jax.ShapeDtypeStruct((ex, 2 * kf + 8, 128), F32),
        ],
        out_specs=[VMEM] * 2,
        compiler_params=pltpu.CompilerParams(**PARAMS),
        name="block_totals",
    )(*tangents, risk, squares, hazard_message)


def scan_kernel(rows, kf, tangent, risk, rank, squares, cumulative_out, lhs, spread):
    groups = rows // LO
    chunk = min(1024, rows)
    ordered = jnp.zeros((groups * 2 * kf, LO), F32)
    for start in range(0, rows, chunk):
        at = slice(start, start + chunk)
        place = lax.rem(rank[:, at], rows)
        group = place // LO
        spread[:, at] = one_hot(lax.rem(place, LO), LO)
        both = jnp.concatenate(split_two(tangent[:, at] * risk[:, at]), axis=0)
        for g in range(groups):
            lhs[g * 2 * kf : (g + 1) * 2 * kf, at] = jnp.where(group == g, both, 0.0).astype(BF16)
        ordered = ordered + lax.dot_general(lhs[:, at], spread[:, at], NT, preferred_element_type=F32)
    ordered = jnp.concatenate(
        [
            ordered[g * 2 * kf : g * 2 * kf + kf] + ordered[g * 2 * kf + kf : (g + 1) * 2 * kf]
            for g in range(groups)
        ],
        axis=0,
    )
    inside = dot_binary(ordered, triangle(LO, lambda a, b: a >= b))
    carried = jnp.zeros((kf, 1), F32)
    hazard = [None] * groups
    for g in reversed(range(groups)):
        rows_of = slice(g * kf, (g + 1) * kf)
        hazard[g] = (inside[rows_of] + carried) * squares[g : g + 1, :]
        carried = carried + inside[rows_of, :1]
    inside = dot_binary(jnp.concatenate(hazard, axis=0), triangle(LO, lambda a, b: a <= b))
    carried = jnp.zeros((kf, 1), F32)
    summed = [None] * groups
    for g in range(groups):
        rows_of = slice(g * kf, (g + 1) * kf)
        summed[g] = inside[rows_of] + carried
        carried = carried + inside[rows_of, LO - 1 :]
    high, low = split_two(jnp.concatenate(summed, axis=0))
    high, low = high.astype(BF16), low.astype(BF16)
    for start in range(0, rows, chunk):
        at = slice(start, start + chunk)
        group = lax.rem(rank[:, at], rows) // LO
        placed = jnp.dot(high, spread[:, at], preferred_element_type=F32) + jnp.dot(
            low, spread[:, at], preferred_element_type=F32
        )
        picked = jnp.zeros((kf, chunk), F32)
        for g in range(groups):
            picked = picked + jnp.where(group == g, placed[g * kf : (g + 1) * kf], 0.0)
        cumulative_out[:, at] = picked


def scans(tangent, risk, rank, squares):
    kf, rows = tangent.shape
    groups = rows // LO
    return pl.pallas_call(
        functools.partial(scan_kernel, rows, kf),
        in_specs=[VMEM] * 4,
        out_shape=jax.ShapeDtypeStruct((kf, rows), F32),
        out_specs=VMEM,
        scratch_shapes=[pltpu.VMEM((groups * 2 * kf, rows), BF16), pltpu.VMEM((LO, rows), BF16)],
        compiler_params=pltpu.CompilerParams(**PARAMS),
        cost_estimate=pl.CostEstimate(
            flops=4 * rows * LO * groups * 2 * kf, bytes_accessed=rows * kf * 24, transcendentals=0
        ),
        name="scans",
    )(tangent, risk, rank, squares)


def weight_kernel(kf, messages, tangent, local, risk, cumulative, squares, weighted):
    me = lax.axis_index("ex")
    ex = messages.shape[0]
    later = jnp.zeros((kf, 1), F32)
    own_later = later
    before = later
    hazard_before = jnp.zeros((1, 1), F32)
    for b in reversed(range(ex)):
        plain = jnp.sum(messages[b, :kf], axis=1, keepdims=True)
        scaled = jnp.sum(messages[b, kf : 2 * kf], axis=1, keepdims=True)
        hazard_total = messages[b, 2 * kf : 2 * kf + 1, :1]
        square_total = messages[b, 2 * kf + 1 : 2 * kf + 2, :1]
        own_later = own_later + jnp.where(b > me, plain, 0.0)
        before = before + jnp.where(b < me, scaled + square_total * later, 0.0)
        hazard_before = hazard_before + jnp.where(b < me, hazard_total, 0.0)
        later = later + plain
    value = tangent[...] * (cumulative[...] + hazard_before) - (local[...] + squares[...] * own_later + before)
    weighted[...] = (risk[...] * value).astype(BF16)


def weights(messages, tangent, local, risk, cumulative, squares):
    return pl.pallas_call(
        functools.partial(weight_kernel, tangent.shape[0]),
        in_specs=[VMEM] * 6,
        out_shape=jax.ShapeDtypeStruct(tangent.shape, BF16),
        out_specs=VMEM,
        compiler_params=pltpu.CompilerParams(**PARAMS),
        name="weights",
    )(messages, tangent, local, risk, cumulative, squares)


def gradient_kernel(feat, kf, *refs):
    parts, dosages, out, weighted = refs[:feat], refs[feat], refs[feat + 1], refs[feat + 2]
    me = lax.axis_index("feat")
    for i in range(feat):
        weighted[pl.ds(pl.multiple_of((me ^ i) * kf, kf), kf), :] = parts[i][...]
    total = jnp.dot(weighted[...], dosages[...], preferred_element_type=F32)
    out[...] = total.T.reshape(out.shape)


def gradients(parts, dosages, ex):
    feat = len(parts)
    kf, persons = parts[0].shape
    k, variants = kf * feat, dosages.shape[1]
    return pl.pallas_call(
        functools.partial(gradient_kernel, feat, kf),
        in_specs=[VMEM] * (feat + 1),
        out_shape=jax.ShapeDtypeStruct((ex, variants // ex, k), F32),
        out_specs=VMEM,
        scratch_shapes=[pltpu.VMEM((k, persons), BF16)],
        compiler_params=pltpu.CompilerParams(**PARAMS),
        cost_estimate=pl.CostEstimate(
            flops=2 * persons * variants * k, bytes_accessed=persons * (variants * 2 + k * 2), transcendentals=0
        ),
        name="gradients",
    )(*parts, dosages)


def finish_kernel(pieces, count, out):
    total = pieces[0]
    for b in range(1, pieces.shape[0]):
        total = total + pieces[b]
    total = total / count[0:1, 0:1]
    out[...] = jnp.broadcast_to(total[None], out.shape)


def finish(pieces, count):
    return pl.pallas_call(
        finish_kernel,
        in_specs=[VMEM] * 2,
        out_shape=jax.ShapeDtypeStruct(pieces.shape, F32),
        out_specs=VMEM,
        compiler_params=pltpu.CompilerParams(**PARAMS),
        name="finish",
    )(pieces, count)


def local(dosages, coefficients, directions, event_rank, events):
    feat, ex = lax.axis_size("feat"), lax.axis_size("ex")
    rows = dosages.shape[0]
    variants, k = directions.shape
    each = k // feat
    padded = -(-each // 16) * 16
    if padded != each:
        directions = jnp.pad(directions.reshape(variants, feat, each), ((0, 0), (0, 0), (0, padded - each)))
        directions = directions.reshape(variants, feat * padded)
    rank, event_row = event_rank[None], events[None]

    linear, keep, send = products(dosages, coefficients, directions, feat)
    order = list(range(1, feat // 2)) + [0]
    joined = {q: (keep[q], swap(send[q], "feat", 1)) for q in order}
    others = [swap(joined[q][0] + joined[q][1], "feat", 2 * q) for q in order[:-1]]

    risk, sums, ordered_events, message = risks(exchange(linear, "feat"), rank, event_row, rows, ex)
    cumulative, squares, ordered_squares, hazard_message, count = hazards(
        exchange(message, "ex"), sums, ordered_events, rank, rows
    )

    tangent, message = block_totals(list(joined[0]) + others, risk, squares, hazard_message, ex)
    messages = exchange(message, "ex")
    summed = scans(tangent, risk, rank, ordered_squares)
    own = weights(messages, tangent, summed, risk, cumulative, squares)

    chips = {0: own}
    for q in order[:-1]:
        chips[q] = swap(own, "feat", 2 * q)
    parts = []
    for q in range(feat // 2):
        parts += [chips[q], swap(chips[q], "feat", 1)]

    pieces = exchange(gradients(parts, dosages, ex), "ex")
    result = exchange(finish(pieces, count), "ex").reshape(variants, -1)
    if padded != each:
        result = result.reshape(variants, feat, padded)[:, :, :each].reshape(variants, k)
    return result


def solution(mesh):
    placed = (P("ex", "feat"), P("feat"), P("feat", None), P("ex"), P("ex"))
    return jax.shard_map(
        local, mesh=mesh, in_specs=placed, out_specs=P("feat", None), check_vma=False
    )
```

```python
import functools

import jax
import jax.numpy as jnp
from jax import lax
from jax.experimental import pallas as pl
from jax.experimental.pallas import tpu as pltpu
from jax.sharding import PartitionSpec as P

F32 = jnp.float32
BF16 = jnp.bfloat16
LO = 256
NT = (((1,), (1,)), ((), ()))
VMEM = pl.BlockSpec(memory_space=pltpu.VMEM)
HIGHEST = lax.Precision.HIGHEST
HBM = pl.BlockSpec(memory_space=pltpu.HBM)
PARAMS = dict(vmem_limit_bytes=24 * 1024 * 1024)


def swap(x, axis, i):
    count = lax.axis_size(axis)
    return lax.ppermute(x, axis, [(s, s ^ i) for s in range(count)])


def split_two(x):
    high = x.astype(BF16).astype(F32)
    return high, x - high


def split_three(x):
    first, rest = split_two(x)
    second, third = split_two(rest)
    return first, second, third


def one_hot(values, count, kind=BF16):
    shape = (count, values.shape[1])
    return jnp.where(lax.broadcasted_iota(jnp.int32, shape, 0) == values, 1.0, 0.0).astype(kind)


def triangle(n, keep):
    first = lax.broadcasted_iota(jnp.int32, (n, n), 0)
    second = lax.broadcasted_iota(jnp.int32, (n, n), 1)
    return jnp.where(keep(first, second), 1.0, 0.0)


def exact_dot(a, b):
    return jnp.dot(a, b, precision=HIGHEST, preferred_element_type=F32)


def dot_binary(a, b):
    b = b.astype(BF16)
    total = None
    for part in split_three(a):
        term = jnp.dot(part.astype(BF16), b, preferred_element_type=F32)
        total = term if total is None else total + term
    return total


def product_kernel(feat, kf, chunk, directions, coefficients, dosages, *refs):
    linear, keep, send = refs[0], refs[1 : 1 + feat // 2], refs[1 + feat // 2 : 1 + feat]
    table, own_directions, own_coefficients, rhs, turned, sems = refs[1 + feat :]
    me = lax.axis_index("feat")
    width = feat * kf
    persons, variants = table.shape
    steps = persons // chunk
    small = [
        pltpu.make_async_copy(directions, own_directions, sems.at[steps]),
        pltpu.make_async_copy(coefficients, own_coefficients, sems.at[steps + 1]),
    ]
    large = [
        pltpu.make_async_copy(
            dosages.at[pl.ds(i * chunk, chunk)], table.at[pl.ds(i * chunk, chunk)], sems.at[i]
        )
        for i in range(steps)
    ]
    for copy in small + large:
        copy.start()
    for copy in small:
        copy.wait()
    turned[...] = own_directions[...].astype(F32).T.reshape(turned.shape)
    placed = jnp.concatenate([turned[me ^ i] for i in range(feat)], axis=0)
    rhs[:, :width] = placed.T.astype(BF16)
    spread = jnp.broadcast_to(own_coefficients[...].astype(F32), (128, variants))
    rhs[:, width:] = spread.T.astype(BF16)
    diagonal = triangle(128, lambda a, b: a == b)
    for i in range(steps):
        large[i].wait()
        at = slice(i * chunk, (i + 1) * chunk)
        result = jnp.dot(table[at], rhs[...], preferred_element_type=F32)
        tangent = result[:, :width].T
        for j in range(feat):
            (send if j % 2 else keep)[j // 2][:kf, at] = tangent[j * kf : (j + 1) * kf]
        for start in range(0, chunk, 128):
            block = result[start : start + 128, width:]
            row = jnp.sum(block * diagonal, axis=0, keepdims=True)
            here = slice(i * chunk + start, i * chunk + start + 128)
            linear[:, here] = row
            send[1][kf:, here] = jnp.broadcast_to(row, (8, 128))


def products(dosages, coefficients, directions, feat):
    persons, variants = dosages.shape
    k = directions.shape[1]
    kf = k // feat
    chunk = min(512, persons)
    piece = jax.ShapeDtypeStruct((kf, persons), F32)
    first = jax.ShapeDtypeStruct((kf + 8, persons), F32)
    out = pl.pallas_call(
        functools.partial(product_kernel, feat, kf, chunk),
        in_specs=[HBM, HBM, HBM],
        out_shape=[jax.ShapeDtypeStruct((1, persons), F32)]
        + [piece] * (feat // 2 + 1)
        + [first]
        + [piece] * (feat // 2 - 2),
        out_specs=[VMEM] * (feat + 1),
        scratch_shapes=[
            pltpu.VMEM((persons, variants), BF16),
            pltpu.VMEM((variants, k), BF16),
            pltpu.VMEM((1, variants), BF16),
            pltpu.VMEM((variants, k + 128), BF16),
            pltpu.VMEM((feat, kf, variants), F32),
            pltpu.SemaphoreType.DMA((persons // chunk + 2,)),
        ],
        compiler_params=pltpu.CompilerParams(**PARAMS),
        cost_estimate=pl.CostEstimate(
            flops=2 * persons * variants * k, bytes_accessed=persons * (variants * 2 + k * 4), transcendentals=0
        ),
        name="products",
    )(directions, coefficients[None], dosages)
    return out[0], out[1 : 1 + feat // 2], out[1 + feat // 2 :]


def pair_kernel(linear, received, out):
    kf = received.shape[0] - 8
    out[...] = linear[...] + received[kf : kf + 1, :]


def pair(linear, received):
    return pl.pallas_call(
        pair_kernel,
        in_specs=[VMEM] * 2,
        out_shape=jax.ShapeDtypeStruct(linear.shape, F32),
        out_specs=VMEM,
        compiler_params=pltpu.CompilerParams(**PARAMS),
        name="pair",
    )(linear, received)


def join_kernel(count, *refs):
    keep, received, outs = refs[:count], refs[count : 2 * count], refs[-count:]
    for mine, other, out in zip(keep, received, outs):
        kf = mine.shape[0]
        out[...] = mine[...] + other[:kf, :]


def join(keep, received, waited):
    count = len(keep)
    return pl.pallas_call(
        functools.partial(join_kernel, count),
        in_specs=[VMEM] * (2 * count) + [pl.BlockSpec(memory_space=pl.ANY)] * len(waited),
        out_shape=[jax.ShapeDtypeStruct(k.shape, F32) for k in keep],
        out_specs=[VMEM] * count,
        compiler_params=pltpu.CompilerParams(**PARAMS),
        name="join",
    )(*keep, *received, *waited)


def risk_kernel(rows, parts, *refs):
    linear, (rank, events) = refs[:parts], refs[parts : parts + 2]
    risk_out, sums_out, events_out, message = refs[parts + 2 :]
    groups = rows // LO
    total = linear[0][...]
    for part in linear[1:]:
        total = total + part[...]
    risk = jnp.exp(total)
    risk_out[...] = risk
    place = lax.rem(rank[...], rows)
    mask = one_hot(place // LO, groups, F32)
    pieces = [mask * part for part in split_three(risk)] + [mask * events[...].astype(F32)]
    lhs = jnp.concatenate(pieces, axis=0).astype(BF16)
    sorted_all = lax.dot_general(lhs, one_hot(lax.rem(place, LO), LO), NT, preferred_element_type=F32)
    ordered = sorted_all[:groups] + sorted_all[groups : 2 * groups] + sorted_all[2 * groups : 3 * groups]
    happened = sorted_all[3 * groups :]
    inside = dot_binary(ordered, triangle(LO, lambda a, b: a >= b))
    totals = jnp.broadcast_to(inside[:, :1], inside.shape)
    carried = exact_dot(triangle(groups, lambda a, b: a < b), totals)
    sums_out[...] = inside + carried
    events_out[...] = happened
    everything = jnp.sum(totals, axis=0, keepdims=True)[:, :128]
    count = jnp.sum(dot_binary(happened, jnp.ones((LO, 128), F32)), axis=0, keepdims=True)
    message[...] = jnp.concatenate([everything, count, jnp.zeros((6, 128), F32)], axis=0)


def risks(linear, rank, events, rows):
    groups = rows // LO
    return pl.pallas_call(
        functools.partial(risk_kernel, rows, len(linear)),
        in_specs=[VMEM] * (len(linear) + 2),
        out_shape=[
            jax.ShapeDtypeStruct((1, rows), F32),
            jax.ShapeDtypeStruct((groups, LO), F32),
            jax.ShapeDtypeStruct((groups, LO), F32),
            jax.ShapeDtypeStruct((8, 128), F32),
        ],
        out_specs=[VMEM] * 4,
        compiler_params=pltpu.CompilerParams(**PARAMS),
        cost_estimate=pl.CostEstimate(flops=rows * LO * 128, bytes_accessed=rows * 64, transcendentals=rows),
        name="risks",
    )(*linear, rank, events)


def hazard_kernel(rows, later, sums, events, rank, *outs):
    cumulative, squares, ordered_squares, message = outs
    groups = rows // LO
    risk_sum = sums[...] + later[0:1, 0:1]
    hazard = events[...] / risk_sum
    square = events[...] / (risk_sum * risk_sum)
    ordered_squares[...] = square
    both = jnp.concatenate([hazard, square], axis=0)
    inside = dot_binary(both, triangle(LO, lambda a, b: a <= b))
    totals = jnp.broadcast_to(inside[:, LO - 1 :], inside.shape)
    before = triangle(groups, lambda a, b: a > b)
    carried = jnp.concatenate(
        [exact_dot(before, totals[:groups]), exact_dot(before, totals[groups:])], axis=0
    )
    message[...] = jnp.concatenate(
        [
            jnp.sum(totals[:groups], axis=0, keepdims=True)[:, :128],
            jnp.sum(totals[groups:], axis=0, keepdims=True)[:, :128],
            jnp.zeros((6, 128), F32),
        ],
        axis=0,
    )
    place = lax.rem(rank[...], rows)
    mask = one_hot(place // LO, groups, F32)
    placed = dot_binary(inside + carried, one_hot(lax.rem(place, LO), LO))
    cumulative[...] = jnp.sum(mask * placed[:groups], axis=0, keepdims=True)
    squares[...] = jnp.sum(mask * placed[groups:], axis=0, keepdims=True)


def hazards(later, sums, events, rank, rows):
    groups = rows // LO
    row = jax.ShapeDtypeStruct((1, rows), F32)
    small = jax.ShapeDtypeStruct((8, 128), F32)
    return pl.pallas_call(
        functools.partial(hazard_kernel, rows),
        in_specs=[VMEM] * 4,
        out_shape=[row, row, jax.ShapeDtypeStruct((groups, LO), F32), small],
        out_specs=[VMEM] * 4,
        compiler_params=pltpu.CompilerParams(**PARAMS),
        cost_estimate=pl.CostEstimate(flops=rows * LO * 200, bytes_accessed=rows * 64, transcendentals=0),
        name="hazards",
    )(later, sums, events, rank)


def total_kernel(parts, *refs):
    tangents = refs[:parts]
    risk, squares, hazard_message, tangent_out, message = refs[parts:]
    kf, rows = tangent_out.shape
    plain = jnp.zeros((kf, 128), F32)
    scaled = jnp.zeros((kf, 128), F32)
    for start in range(0, rows, 128):
        at = slice(start, start + 128)
        tangent = tangents[0][:, at]
        for part in tangents[1:]:
            tangent = tangent + part[:kf, at]
        tangent_out[:, at] = tangent
        weighted = tangent * risk[:, at]
        plain = plain + weighted
        scaled = scaled + weighted * squares[:, at]
    message[...] = jnp.concatenate([plain, scaled, hazard_message[...]], axis=0)


def block_totals(tangents, risk, squares, hazard_message):
    kf, rows = tangents[0].shape
    return pl.pallas_call(
        functools.partial(total_kernel, len(tangents)),
        in_specs=[VMEM] * (len(tangents) + 3),
        out_shape=[
            jax.ShapeDtypeStruct((kf, rows), F32),
            jax.ShapeDtypeStruct((2 * kf + 8, 128), F32),
        ],
        out_specs=[VMEM] * 2,
        compiler_params=pltpu.CompilerParams(**PARAMS),
        name="block_totals",
    )(*tangents, risk, squares, hazard_message)


def scan_kernel(rows, kf, tangent, risk, rank, squares, cumulative_out, lhs, spread):
    groups = rows // LO
    chunk = min(1024, rows)
    ordered = jnp.zeros((groups * 2 * kf, LO), F32)
    for start in range(0, rows, chunk):
        at = slice(start, start + chunk)
        place = lax.rem(rank[:, at], rows)
        group = place // LO
        spread[:, at] = one_hot(lax.rem(place, LO), LO)
        both = jnp.concatenate(split_two(tangent[:, at] * risk[:, at]), axis=0)
        for g in range(groups):
            lhs[g * 2 * kf : (g + 1) * 2 * kf, at] = jnp.where(group == g, both, 0.0).astype(BF16)
        ordered = ordered + lax.dot_general(lhs[:, at], spread[:, at], NT, preferred_element_type=F32)
    ordered = jnp.concatenate(
        [
            ordered[g * 2 * kf : g * 2 * kf + kf] + ordered[g * 2 * kf + kf : (g + 1) * 2 * kf]
            for g in range(groups)
        ],
        axis=0,
    )
    inside = dot_binary(ordered, triangle(LO, lambda a, b: a >= b))
    carried = jnp.zeros((kf, 1), F32)
    hazard = [None] * groups
    for g in reversed(range(groups)):
        rows_of = slice(g * kf, (g + 1) * kf)
        hazard[g] = (inside[rows_of] + carried) * squares[g : g + 1, :]
        carried = carried + inside[rows_of, :1]
    inside = dot_binary(jnp.concatenate(hazard, axis=0), triangle(LO, lambda a, b: a <= b))
    carried = jnp.zeros((kf, 1), F32)
    summed = [None] * groups
    for g in range(groups):
        rows_of = slice(g * kf, (g + 1) * kf)
        summed[g] = inside[rows_of] + carried
        carried = carried + inside[rows_of, LO - 1 :]
    high, low = split_two(jnp.concatenate(summed, axis=0))
    high, low = high.astype(BF16), low.astype(BF16)
    for start in range(0, rows, chunk):
        at = slice(start, start + chunk)
        group = lax.rem(rank[:, at], rows) // LO
        placed = jnp.dot(high, spread[:, at], preferred_element_type=F32) + jnp.dot(
            low, spread[:, at], preferred_element_type=F32
        )
        picked = jnp.zeros((kf, chunk), F32)
        for g in range(groups):
            picked = picked + jnp.where(group == g, placed[g * kf : (g + 1) * kf], 0.0)
        cumulative_out[:, at] = picked


def scans(tangent, risk, rank, squares):
    kf, rows = tangent.shape
    groups = rows // LO
    return pl.pallas_call(
        functools.partial(scan_kernel, rows, kf),
        in_specs=[VMEM] * 4,
        out_shape=jax.ShapeDtypeStruct((kf, rows), F32),
        out_specs=VMEM,
        scratch_shapes=[pltpu.VMEM((groups * 2 * kf, rows), BF16), pltpu.VMEM((LO, rows), BF16)],
        compiler_params=pltpu.CompilerParams(**PARAMS),
        cost_estimate=pl.CostEstimate(
            flops=4 * rows * LO * groups * 2 * kf, bytes_accessed=rows * kf * 24, transcendentals=0
        ),
        name="scans",
    )(tangent, risk, rank, squares)


def weight_kernel(kf, ex, *refs):
    messages, (tangent, local, risk, cumulative, squares) = refs[:ex], refs[ex : ex + 5]
    weighted, placed = refs[ex + 5 :]
    me = lax.axis_index("ex")
    for i in range(ex):
        placed[me ^ i] = messages[i][...]
    later = jnp.zeros((kf, 1), F32)
    own_later = later
    before = later
    hazard_before = jnp.zeros((1, 1), F32)
    for b in reversed(range(ex)):
        plain = jnp.sum(placed[b, :kf], axis=1, keepdims=True)
        scaled = jnp.sum(placed[b, kf : 2 * kf], axis=1, keepdims=True)
        hazard_total = placed[b, 2 * kf : 2 * kf + 1, :1]
        square_total = placed[b, 2 * kf + 1 : 2 * kf + 2, :1]
        own_later = own_later + jnp.where(b > me, plain, 0.0)
        before = before + jnp.where(b < me, scaled + square_total * later, 0.0)
        hazard_before = hazard_before + jnp.where(b < me, hazard_total, 0.0)
        later = later + plain
    value = tangent[...] * (cumulative[...] + hazard_before) - (local[...] + squares[...] * own_later + before)
    weighted[...] = (risk[...] * value).astype(BF16)


def weights(messages, tangent, local, risk, cumulative, squares):
    return pl.pallas_call(
        functools.partial(weight_kernel, tangent.shape[0], len(messages)),
        in_specs=[VMEM] * (len(messages) + 5),
        out_shape=jax.ShapeDtypeStruct(tangent.shape, BF16),
        out_specs=VMEM,
        scratch_shapes=[pltpu.VMEM((len(messages),) + messages[0].shape, F32)],
        compiler_params=pltpu.CompilerParams(**PARAMS),
        name="weights",
    )(*messages, tangent, local, risk, cumulative, squares)


def gradient_kernel(feat, ex, kf, *refs):
    parts, dosages, outs = refs[:feat], refs[feat], refs[feat + 1 : feat + 1 + ex]
    weighted, turned = refs[feat + 1 + ex :]
    me = lax.axis_index("feat")
    place = lax.axis_index("ex")
    for i in range(feat):
        weighted[pl.ds(pl.multiple_of((me ^ i) * kf, kf), kf), :] = parts[i][...]
    total = jnp.dot(weighted[...], dosages[...], preferred_element_type=F32)
    turned[...] = total.T.reshape(turned.shape)
    for i in range(ex):
        outs[i][...] = turned[place ^ i]


def gradients(parts, dosages, ex):
    feat = len(parts)
    kf, persons = parts[0].shape
    k, variants = kf * feat, dosages.shape[1]
    piece = (variants // ex, k)
    return pl.pallas_call(
        functools.partial(gradient_kernel, feat, ex, kf),
        in_specs=[VMEM] * (feat + 1),
        out_shape=[jax.ShapeDtypeStruct(piece, F32)] * ex,
        out_specs=[VMEM] * ex,
        scratch_shapes=[pltpu.VMEM((k, persons), BF16), pltpu.VMEM((ex,) + piece, F32)],
        compiler_params=pltpu.CompilerParams(**PARAMS),
        cost_estimate=pl.CostEstimate(
            flops=2 * persons * variants * k, bytes_accessed=persons * (variants * 2 + k * 2), transcendentals=0
        ),
        name="gradients",
    )(*parts, dosages)


def finish_kernel(ex, *refs):
    pieces, count, out = refs[:ex], refs[ex], refs[ex + 1]
    total = pieces[0][...]
    for piece in pieces[1:]:
        total = total + piece[...]
    out[...] = total / count[1:2, 0:1]


def finish(pieces, count):
    return pl.pallas_call(
        functools.partial(finish_kernel, len(pieces)),
        in_specs=[VMEM] * (len(pieces) + 1),
        out_shape=jax.ShapeDtypeStruct(pieces[0].shape, F32),
        out_specs=VMEM,
        compiler_params=pltpu.CompilerParams(**PARAMS),
        name="finish",
    )(*pieces, count)


def place_kernel(ex, *refs):
    parts, out, sems = refs[:ex], refs[ex], refs[ex + 1]
    me = lax.axis_index("ex")
    copies = [pltpu.make_async_copy(parts[i], out.at[me ^ i], sems.at[i]) for i in range(ex)]
    for copy in copies:
        copy.start()
    for copy in copies:
        copy.wait()


def place_all(parts):
    ex = len(parts)
    out = pl.pallas_call(
        functools.partial(place_kernel, ex),
        in_specs=[VMEM] * ex,
        out_shape=jax.ShapeDtypeStruct((ex,) + parts[0].shape, F32),
        out_specs=HBM,
        scratch_shapes=[pltpu.SemaphoreType.DMA((ex,))],
        compiler_params=pltpu.CompilerParams(**PARAMS),
        name="place",
    )(*parts)
    return out.reshape(-1, parts[0].shape[1])


def local(dosages, coefficients, directions, event_rank, events):
    feat, ex = lax.axis_size("feat"), lax.axis_size("ex")
    rows = dosages.shape[0]
    variants, k = directions.shape
    each = k // feat
    padded = -(-each // 16) * 16
    if padded != each:
        directions = jnp.pad(directions.reshape(variants, feat, each), ((0, 0), (0, 0), (0, padded - each)))
        directions = directions.reshape(variants, feat * padded)
    rank, event_row = event_rank[None], events[None]

    linear, keep, send = products(dosages, coefficients, directions, feat)
    received = [swap(piece, "feat", 1) for piece in send]
    linear = pair(linear, received[1])
    linears = [linear] + [swap(linear, "feat", 2 * q) for q in range(1, feat // 2)]
    joined = join(keep[1:], received[1:], linears[1:])
    others = [swap(joined[q - 1], "feat", 2 * q) for q in reversed(range(1, feat // 2))]

    risk, sums, ordered_events, total = risks(linears, rank, event_row, rows)
    later = jnp.zeros_like(total)
    bit = 1
    while bit < ex:
        other = swap(total, "ex", bit)
        later = later + jnp.where((lax.axis_index("ex") & bit) == 0, other, 0.0)
        total = total + other
        bit *= 2
    cumulative, squares, ordered_squares, hazard_message = hazards(
        later, sums, ordered_events, rank, rows
    )

    tangent, message = block_totals([keep[0], received[0]] + others, risk, squares, hazard_message)
    messages = [message] + [swap(message, "ex", i) for i in range(1, ex)]
    summed = scans(tangent, risk, rank, ordered_squares)
    own = weights(messages, tangent, summed, risk, cumulative, squares)

    chips = {0: own}
    for q in reversed(range(1, feat // 2)):
        chips[q] = swap(own, "feat", 2 * q)
    parts = []
    for q in range(feat // 2):
        parts += [chips[q], swap(chips[q], "feat", 1)]

    pieces = gradients(parts, dosages, ex)
    mine = finish([pieces[0]] + [swap(pieces[i], "ex", i) for i in range(1, ex)], total)
    result = place_all([mine] + [swap(mine, "ex", i) for i in range(1, ex)])
    if padded != each:
        result = result.reshape(variants, feat, padded)[:, :, :each].reshape(variants, k)
    return result


def solution(mesh):
    placed = (P("ex", "feat"), P("feat"), P("feat", None), P("ex"), P("ex"))
    return jax.shard_map(
        local, mesh=mesh, in_specs=placed, out_specs=P("feat", None), check_vma=False
    )
```

```python
import functools

import jax
import jax.numpy as jnp
from jax import lax
from jax.experimental import pallas as pl
from jax.experimental.pallas import tpu as pltpu
from jax.sharding import PartitionSpec as P

F32 = jnp.float32
BF16 = jnp.bfloat16
LO = 256
BLOCK = 64
NT = (((1,), (1,)), ((), ()))
VMEM = pl.BlockSpec(memory_space=pltpu.VMEM)
HIGHEST = lax.Precision.HIGHEST
HBM = pl.BlockSpec(memory_space=pltpu.HBM)
PRODUCT_BYTES = 48 * 1024 * 1024
PARAMS = dict(vmem_limit_bytes=24 * 1024 * 1024)


def swap(x, axis, i):
    count = lax.axis_size(axis)
    return lax.ppermute(x, axis, [(s, s ^ i) for s in range(count)])


def split_two(x):
    high = x.astype(BF16).astype(F32)
    return high, x - high


def split_three(x):
    first, rest = split_two(x)
    second, third = split_two(rest)
    return first, second, third


def one_hot(values, count, kind=BF16):
    shape = (count, values.shape[1])
    return jnp.where(lax.broadcasted_iota(jnp.int32, shape, 0) == values, 1.0, 0.0).astype(kind)


def triangle(n, keep):
    first = lax.broadcasted_iota(jnp.int32, (n, n), 0)
    second = lax.broadcasted_iota(jnp.int32, (n, n), 1)
    return jnp.where(keep(first, second), 1.0, 0.0)


def exact_dot(a, b):
    return jnp.dot(a, b, precision=HIGHEST, preferred_element_type=F32)


def dot_binary(a, b):
    b = b.astype(BF16)
    total = None
    for part in split_three(a):
        term = jnp.dot(part.astype(BF16), b, preferred_element_type=F32)
        total = term if total is None else total + term
    return total


def product_kernel(feat, kf, chunk, directions, coefficients, dosages, *refs):
    linear, keep, send = refs[0], refs[1 : 1 + feat // 2], refs[1 + feat // 2 : 1 + feat]
    table, own_directions, own_coefficients, rhs, turned, sems = refs[1 + feat :]
    me = lax.axis_index("feat")
    width = feat * kf
    persons, variants = table.shape
    steps = persons // chunk
    small = [
        pltpu.make_async_copy(directions, own_directions, sems.at[steps]),
        pltpu.make_async_copy(coefficients, own_coefficients, sems.at[steps + 1]),
    ]
    large = [
        pltpu.make_async_copy(
            dosages.at[pl.ds(i * chunk, chunk)], table.at[pl.ds(i * chunk, chunk)], sems.at[i]
        )
        for i in range(steps)
    ]
    for copy in small + large:
        copy.start()
    for copy in small:
        copy.wait()
    rhs[:, :width] = own_directions[...]
    spread = jnp.broadcast_to(own_coefficients[...].astype(F32)[None, :], (128, variants))
    rhs[:, width:] = spread.T.astype(BF16)
    diagonal = triangle(128, lambda a, b: a == b)
    for i in range(steps):
        large[i].wait()
        at = slice(i * chunk, (i + 1) * chunk)
        result = jnp.dot(table[at], rhs[...], preferred_element_type=F32)
        turned[i] = result[:, :width].T.reshape(feat, kf, chunk)
        for j in range(feat):
            (send if j % 2 else keep)[j // 2][:kf, at] = turned[i, me ^ j]
        for start in range(0, chunk, 128):
            block = result[start : start + 128, width:]
            row = jnp.sum(block * diagonal, axis=0, keepdims=True)
            here = slice(i * chunk + start, i * chunk + start + 128)
            linear[:, here] = row
            send[1][kf:, here] = jnp.broadcast_to(row, (8, 128))


def products(dosages, coefficients, directions, feat):
    persons, variants = dosages.shape
    k = directions.shape[1]
    kf = k // feat
    chunk = min(512, persons)
    piece = jax.ShapeDtypeStruct((kf, persons), F32)
    first = jax.ShapeDtypeStruct((kf + 8, persons), F32)
    out = pl.pallas_call(
        functools.partial(product_kernel, feat, kf, chunk),
        in_specs=[HBM, HBM, HBM],
        out_shape=[jax.ShapeDtypeStruct((1, persons), F32)]
        + [piece] * (feat // 2 + 1)
        + [first]
        + [piece] * (feat // 2 - 2),
        out_specs=[VMEM] * (feat + 1),
        scratch_shapes=[
            pltpu.VMEM((persons, variants), BF16),
            pltpu.VMEM((variants, k), BF16),
            pltpu.VMEM((variants,), BF16),
            pltpu.VMEM((variants, k + 128), BF16),
            pltpu.VMEM((persons // chunk, feat, kf, chunk), F32),
            pltpu.SemaphoreType.DMA((persons // chunk + 2,)),
        ],
        compiler_params=pltpu.CompilerParams(vmem_limit_bytes=PRODUCT_BYTES),
        cost_estimate=pl.CostEstimate(
            flops=2 * persons * variants * k, bytes_accessed=persons * (variants * 2 + k * 4), transcendentals=0
        ),
        name="products",
    )(directions, coefficients, dosages)
    return out[0], out[1 : 1 + feat // 2], out[1 + feat // 2 :]


def pair_kernel(linear, received, out):
    kf = received.shape[0] - 8
    out[...] = linear[...] + received[kf : kf + 1, :]


def pair(linear, received):
    return pl.pallas_call(
        pair_kernel,
        in_specs=[VMEM] * 2,
        out_shape=jax.ShapeDtypeStruct(linear.shape, F32),
        out_specs=VMEM,
        compiler_params=pltpu.CompilerParams(**PARAMS),
        name="pair",
    )(linear, received)


def join_kernel(count, *refs):
    keep, received, outs = refs[:count], refs[count : 2 * count], refs[-count:]
    for mine, other, out in zip(keep, received, outs):
        kf = mine.shape[0]
        out[...] = mine[...] + other[:kf, :]


def join(keep, received, waited):
    count = len(keep)
    return pl.pallas_call(
        functools.partial(join_kernel, count),
        in_specs=[VMEM] * (2 * count) + [pl.BlockSpec(memory_space=pl.ANY)] * len(waited),
        out_shape=[jax.ShapeDtypeStruct(k.shape, F32) for k in keep],
        out_specs=[VMEM] * count,
        compiler_params=pltpu.CompilerParams(**PARAMS),
        name="join",
    )(*keep, *received, *waited)


def risk_kernel(rows, parts, *refs):
    linear, (rank, events) = refs[:parts], refs[parts : parts + 2]
    risk_out, sums_out, events_out, message = refs[parts + 2 :]
    groups = rows // LO
    total = linear[0][...]
    for part in linear[1:]:
        total = total + part[...]
    risk = jnp.exp(total)
    risk_out[...] = risk
    place = lax.rem(rank[...], rows)
    mask = one_hot(place // LO, groups, F32)
    pieces = [mask * part for part in split_three(risk)] + [mask * events[...].astype(F32)]
    lhs = jnp.concatenate(pieces, axis=0).astype(BF16)
    sorted_all = lax.dot_general(lhs, one_hot(lax.rem(place, LO), LO), NT, preferred_element_type=F32)
    ordered = sorted_all[:groups] + sorted_all[groups : 2 * groups] + sorted_all[2 * groups : 3 * groups]
    happened = sorted_all[3 * groups :]
    inside = dot_binary(ordered, triangle(LO, lambda a, b: a >= b))
    totals = jnp.broadcast_to(inside[:, :1], inside.shape)
    carried = exact_dot(triangle(groups, lambda a, b: a < b), totals)
    sums_out[...] = inside + carried
    events_out[...] = happened
    everything = jnp.sum(totals, axis=0, keepdims=True)[:, :128]
    count = jnp.sum(dot_binary(happened, jnp.ones((LO, 128), F32)), axis=0, keepdims=True)
    message[...] = jnp.concatenate([everything, count, jnp.zeros((6, 128), F32)], axis=0)


def risks(linear, rank, events, rows):
    groups = rows // LO
    return pl.pallas_call(
        functools.partial(risk_kernel, rows, len(linear)),
        in_specs=[VMEM] * (len(linear) + 2),
        out_shape=[
            jax.ShapeDtypeStruct((1, rows), F32),
            jax.ShapeDtypeStruct((groups, LO), F32),
            jax.ShapeDtypeStruct((groups, LO), F32),
            jax.ShapeDtypeStruct((8, 128), F32),
        ],
        out_specs=[VMEM] * 4,
        compiler_params=pltpu.CompilerParams(**PARAMS),
        cost_estimate=pl.CostEstimate(flops=rows * LO * 128, bytes_accessed=rows * 64, transcendentals=rows),
        name="risks",
    )(*linear, rank, events)


def hazard_kernel(rows, later, sums, events, rank, *outs):
    cumulative, squares, ordered_squares, message = outs
    groups = rows // LO
    risk_sum = sums[...] + later[0:1, 0:1]
    hazard = events[...] / risk_sum
    square = events[...] / (risk_sum * risk_sum)
    ordered_squares[...] = square
    both = jnp.concatenate([hazard, square], axis=0)
    inside = dot_binary(both, triangle(LO, lambda a, b: a <= b))
    totals = jnp.broadcast_to(inside[:, LO - 1 :], inside.shape)
    before = triangle(groups, lambda a, b: a > b)
    carried = jnp.concatenate(
        [exact_dot(before, totals[:groups]), exact_dot(before, totals[groups:])], axis=0
    )
    message[...] = jnp.concatenate(
        [
            jnp.sum(totals[:groups], axis=0, keepdims=True)[:, :128],
            jnp.sum(totals[groups:], axis=0, keepdims=True)[:, :128],
            jnp.zeros((6, 128), F32),
        ],
        axis=0,
    )
    place = lax.rem(rank[...], rows)
    mask = one_hot(place // LO, groups, F32)
    placed = dot_binary(inside + carried, one_hot(lax.rem(place, LO), LO))
    cumulative[...] = jnp.sum(mask * placed[:groups], axis=0, keepdims=True)
    squares[...] = jnp.sum(mask * placed[groups:], axis=0, keepdims=True)


def hazards(later, sums, events, rank, rows):
    groups = rows // LO
    row = jax.ShapeDtypeStruct((1, rows), F32)
    small = jax.ShapeDtypeStruct((8, 128), F32)
    return pl.pallas_call(
        functools.partial(hazard_kernel, rows),
        in_specs=[VMEM] * 4,
        out_shape=[row, row, jax.ShapeDtypeStruct((groups, LO), F32), small],
        out_specs=[VMEM] * 4,
        compiler_params=pltpu.CompilerParams(**PARAMS),
        cost_estimate=pl.CostEstimate(flops=rows * LO * 200, bytes_accessed=rows * 64, transcendentals=0),
        name="hazards",
    )(later, sums, events, rank)


def total_kernel(parts, *refs):
    tangents = refs[:parts]
    risk, squares, hazard_message, tangent_out, message = refs[parts:]
    kf, rows = tangent_out.shape
    plain = jnp.zeros((kf, 128), F32)
    scaled = jnp.zeros((kf, 128), F32)
    for start in range(0, rows, 128):
        at = slice(start, start + 128)
        tangent = tangents[0][:, at]
        for part in tangents[1:]:
            tangent = tangent + part[:kf, at]
        tangent_out[:, at] = tangent
        weighted = tangent * risk[:, at]
        plain = plain + weighted
        scaled = scaled + weighted * squares[:, at]
    message[...] = jnp.concatenate([plain, scaled, hazard_message[...]], axis=0)


def block_totals(tangents, risk, squares, hazard_message):
    kf, rows = tangents[0].shape
    return pl.pallas_call(
        functools.partial(total_kernel, len(tangents)),
        in_specs=[VMEM] * (len(tangents) + 3),
        out_shape=[
            jax.ShapeDtypeStruct((kf, rows), F32),
            jax.ShapeDtypeStruct((2 * kf + 8, 128), F32),
        ],
        out_specs=[VMEM] * 2,
        compiler_params=pltpu.CompilerParams(**PARAMS),
        name="block_totals",
    )(*tangents, risk, squares, hazard_message)


def scan_kernel(rows, kf, tangent, risk, rank, squares, cumulative_out, lhs, spread):
    groups = rows // LO
    chunk = min(1024, rows)
    ordered = jnp.zeros((groups * 2 * kf, LO), F32)
    for start in range(0, rows, chunk):
        at = slice(start, start + chunk)
        place = lax.rem(rank[:, at], rows)
        group = place // LO
        spread[:, at] = one_hot(lax.rem(place, LO), LO)
        both = jnp.concatenate(split_two(tangent[:, at] * risk[:, at]), axis=0)
        for g in range(groups):
            lhs[g * 2 * kf : (g + 1) * 2 * kf, at] = jnp.where(group == g, both, 0.0).astype(BF16)
        ordered = ordered + lax.dot_general(lhs[:, at], spread[:, at], NT, preferred_element_type=F32)
    ordered = jnp.concatenate(
        [
            ordered[g * 2 * kf : g * 2 * kf + kf] + ordered[g * 2 * kf + kf : (g + 1) * 2 * kf]
            for g in range(groups)
        ],
        axis=0,
    )
    inside = dot_binary(ordered, triangle(LO, lambda a, b: a >= b))
    carried = jnp.zeros((kf, 1), F32)
    hazard = [None] * groups
    for g in reversed(range(groups)):
        rows_of = slice(g * kf, (g + 1) * kf)
        hazard[g] = (inside[rows_of] + carried) * squares[g : g + 1, :]
        carried = carried + inside[rows_of, :1]
    inside = dot_binary(jnp.concatenate(hazard, axis=0), triangle(LO, lambda a, b: a <= b))
    carried = jnp.zeros((kf, 1), F32)
    summed = [None] * groups
    for g in range(groups):
        rows_of = slice(g * kf, (g + 1) * kf)
        summed[g] = inside[rows_of] + carried
        carried = carried + inside[rows_of, LO - 1 :]
    high, low = split_two(jnp.concatenate(summed, axis=0))
    high, low = high.astype(BF16), low.astype(BF16)
    for start in range(0, rows, chunk):
        at = slice(start, start + chunk)
        group = lax.rem(rank[:, at], rows) // LO
        placed = jnp.dot(high, spread[:, at], preferred_element_type=F32) + jnp.dot(
            low, spread[:, at], preferred_element_type=F32
        )
        picked = jnp.zeros((kf, chunk), F32)
        for g in range(groups):
            picked = picked + jnp.where(group == g, placed[g * kf : (g + 1) * kf], 0.0)
        cumulative_out[:, at] = picked


def scans(tangent, risk, rank, squares):
    kf, rows = tangent.shape
    groups = rows // LO
    return pl.pallas_call(
        functools.partial(scan_kernel, rows, kf),
        in_specs=[VMEM] * 4,
        out_shape=jax.ShapeDtypeStruct((kf, rows), F32),
        out_specs=VMEM,
        scratch_shapes=[pltpu.VMEM((groups * 2 * kf, rows), BF16), pltpu.VMEM((LO, rows), BF16)],
        compiler_params=pltpu.CompilerParams(**PARAMS),
        cost_estimate=pl.CostEstimate(
            flops=4 * rows * LO * groups * 2 * kf, bytes_accessed=rows * kf * 24, transcendentals=0
        ),
        name="scans",
    )(tangent, risk, rank, squares)


def weight_kernel(kf, ex, *refs):
    messages, (tangent, local, risk, cumulative, squares) = refs[:ex], refs[ex : ex + 5]
    weighted, placed = refs[ex + 5 :]
    me = lax.axis_index("ex")
    for i in range(ex):
        placed[me ^ i] = messages[i][...]
    later = jnp.zeros((kf, 1), F32)
    own_later = later
    before = later
    hazard_before = jnp.zeros((1, 1), F32)
    for b in reversed(range(ex)):
        plain = jnp.sum(placed[b, :kf], axis=1, keepdims=True)
        scaled = jnp.sum(placed[b, kf : 2 * kf], axis=1, keepdims=True)
        hazard_total = placed[b, 2 * kf : 2 * kf + 1, :1]
        square_total = placed[b, 2 * kf + 1 : 2 * kf + 2, :1]
        own_later = own_later + jnp.where(b > me, plain, 0.0)
        before = before + jnp.where(b < me, scaled + square_total * later, 0.0)
        hazard_before = hazard_before + jnp.where(b < me, hazard_total, 0.0)
        later = later + plain
    value = tangent[...] * (cumulative[...] + hazard_before) - (local[...] + squares[...] * own_later + before)
    weighted[...] = (risk[...] * value).astype(BF16)


def weights(messages, tangent, local, risk, cumulative, squares):
    return pl.pallas_call(
        functools.partial(weight_kernel, tangent.shape[0], len(messages)),
        in_specs=[VMEM] * (len(messages) + 5),
        out_shape=jax.ShapeDtypeStruct(tangent.shape, BF16),
        out_specs=VMEM,
        scratch_shapes=[pltpu.VMEM((len(messages),) + messages[0].shape, F32)],
        compiler_params=pltpu.CompilerParams(**PARAMS),
        name="weights",
    )(*messages, tangent, local, risk, cumulative, squares)


def encode(values, message):
    height = values.shape[0]
    block = min(BLOCK, height)
    powers = []
    for start in range(0, height, block):
        part = values[start : start + block]
        largest = jnp.max(jnp.abs(part), axis=0, keepdims=True)
        power = jnp.ceil(jnp.log2(jnp.maximum(largest, 1e-30))) - 14.0
        message[start : start + block] = jnp.round(part * jnp.exp2(-power)).astype(jnp.int32).astype(jnp.int16)
        powers.append(power)
    powers.append(jnp.zeros((message.shape[0] - height - len(powers), values.shape[1]), F32))
    message[height:] = jnp.concatenate(powers, axis=0).astype(jnp.int32).astype(jnp.int16)


def decode(message, height):
    block = min(BLOCK, height)
    powers = message[height:].astype(jnp.int32).astype(F32)
    parts = []
    for i in range(height // block):
        part = message[i * block : (i + 1) * block].astype(jnp.int32).astype(F32)
        parts.append(part * jnp.exp2(powers[i : i + 1]))
    return jnp.concatenate(parts, axis=0)


def gradient_kernel(feat, kf, *refs):
    parts, dosages, out, weighted = refs[:feat], refs[feat], refs[feat + 1], refs[feat + 2]
    me = lax.axis_index("feat")
    for i in range(feat):
        weighted[pl.ds(pl.multiple_of((me ^ i) * kf, kf), kf), :] = parts[i][...]
    total = jnp.dot(weighted[...], dosages[...], preferred_element_type=F32)
    encode(total.T, out)


def gradients(parts, dosages):
    feat = len(parts)
    kf, persons = parts[0].shape
    k, variants = kf * feat, dosages.shape[1]
    return pl.pallas_call(
        functools.partial(gradient_kernel, feat, kf),
        in_specs=[VMEM] * (feat + 1),
        out_shape=jax.ShapeDtypeStruct((variants + 16, k), jnp.int16),
        out_specs=VMEM,
        scratch_shapes=[pltpu.VMEM((k, persons), BF16)],
        compiler_params=pltpu.CompilerParams(**PARAMS),
        cost_estimate=pl.CostEstimate(
            flops=2 * persons * variants * k, bytes_accessed=persons * (variants * 2 + k * 2), transcendentals=0
        ),
        name="gradients",
    )(*parts, dosages)


def merge_kernel(mine, other, out):
    height = mine.shape[0] - 16
    encode(decode(mine, height) + decode(other, height), out)


def merge(mine, other):
    return pl.pallas_call(
        merge_kernel,
        in_specs=[VMEM] * 2,
        out_shape=jax.ShapeDtypeStruct(mine.shape, jnp.int16),
        out_specs=VMEM,
        compiler_params=pltpu.CompilerParams(**PARAMS),
        name="merge",
    )(mine, other)


def finish_kernel(mine, other, count, out):
    height = mine.shape[0] - 16
    out[...] = (decode(mine, height) + decode(other, height)) / count[1:2, 0:1]


def finish(mine, other, count):
    return pl.pallas_call(
        finish_kernel,
        in_specs=[VMEM] * 3,
        out_shape=jax.ShapeDtypeStruct((mine.shape[0] - 16, mine.shape[1]), F32),
        out_specs=VMEM,
        compiler_params=pltpu.CompilerParams(**PARAMS),
        name="finish",
    )(mine, other, count)


def local(dosages, coefficients, directions, event_rank, events):
    feat, ex = lax.axis_size("feat"), lax.axis_size("ex")
    rows = dosages.shape[0]
    variants, k = directions.shape
    each = k // feat
    padded = -(-each // 16) * 16
    if padded != each:
        directions = jnp.pad(directions.reshape(variants, feat, each), ((0, 0), (0, 0), (0, padded - each)))
        directions = directions.reshape(variants, feat * padded)
    rank, event_row = event_rank[None], events[None]

    linear, keep, send = products(dosages, coefficients, directions, feat)
    received = [swap(piece, "feat", 1) for piece in send]
    linear = pair(linear, received[1])
    linears = [linear] + [swap(linear, "feat", 2 * q) for q in range(1, feat // 2)]
    joined = join(keep[1:], received[1:], linears[1:])
    others = [swap(joined[q - 1], "feat", 2 * q) for q in reversed(range(1, feat // 2))]

    risk, sums, ordered_events, total = risks(linears, rank, event_row, rows)
    later = jnp.zeros_like(total)
    bit = 1
    while bit < ex:
        other = swap(total, "ex", bit)
        later = later + jnp.where((lax.axis_index("ex") & bit) == 0, other, 0.0)
        total = total + other
        bit *= 2
    cumulative, squares, ordered_squares, hazard_message = hazards(
        later, sums, ordered_events, rank, rows
    )

    tangent, message = block_totals([keep[0], received[0]] + others, risk, squares, hazard_message)
    messages = [message] + [swap(message, "ex", i) for i in range(1, ex)]
    summed = scans(tangent, risk, rank, ordered_squares)
    own = weights(messages, tangent, summed, risk, cumulative, squares)

    chips = {0: own}
    for q in reversed(range(1, feat // 2)):
        chips[q] = swap(own, "feat", 2 * q)
    parts = []
    for q in range(feat // 2):
        parts += [chips[q], swap(chips[q], "feat", 1)]

    partial_sum = gradients(parts, dosages)
    bit = 1
    while 2 * bit < ex:
        partial_sum = merge(partial_sum, swap(partial_sum, "ex", bit))
        bit *= 2
    result = finish(partial_sum, swap(partial_sum, "ex", bit), total)
    if padded != each:
        result = result.reshape(variants, feat, padded)[:, :, :each].reshape(variants, k)
    return result


def solution(mesh):
    placed = (P("ex", "feat"), P("feat"), P("feat", None), P("ex"), P("ex"))
    return jax.shard_map(
        local, mesh=mesh, in_specs=placed, out_specs=P("feat", None), check_vma=False
    )
```

```python
import functools

import jax
import jax.numpy as jnp
from jax import lax
from jax.experimental import pallas as pl
from jax.experimental.pallas import tpu as pltpu
from jax.sharding import PartitionSpec as P

F32 = jnp.float32
BF16 = jnp.bfloat16
LO = 256
BLOCK = 64
SPAN = 512
VMEM = pl.BlockSpec(memory_space=pltpu.VMEM)
HIGHEST = lax.Precision.HIGHEST
HBM = pl.BlockSpec(memory_space=pltpu.HBM)
PRODUCT_BYTES = 48 * 1024 * 1024
PARAMS = dict(vmem_limit_bytes=24 * 1024 * 1024)


def swap(x, axis, i):
    count = lax.axis_size(axis)
    return lax.ppermute(x, axis, [(s, s ^ i) for s in range(count)])


def split_two(x):
    high = x.astype(BF16).astype(F32)
    return high, x - high


def split_three(x):
    first, rest = split_two(x)
    second, third = split_two(rest)
    return first, second, third


def one_hot(values, count, kind=BF16):
    shape = (count, values.shape[1])
    return jnp.where(lax.broadcasted_iota(jnp.int32, shape, 0) == values, 1.0, 0.0).astype(kind)


def triangle(n, keep):
    first = lax.broadcasted_iota(jnp.int32, (n, n), 0)
    second = lax.broadcasted_iota(jnp.int32, (n, n), 1)
    return jnp.where(keep(first, second), 1.0, 0.0)


def exact_dot(a, b):
    return jnp.dot(a, b, precision=HIGHEST, preferred_element_type=F32)


def dot_binary(a, b):
    b = b.astype(BF16)
    total = None
    for part in split_three(a):
        term = jnp.dot(part.astype(BF16), b, preferred_element_type=F32)
        total = term if total is None else total + term
    return total


def product_kernel(feat, kf, chunk, directions, coefficients, dosages, *refs):
    linear, keep, send = refs[0], refs[1 : 1 + feat // 2], refs[1 + feat // 2 : 1 + feat]
    table, own_directions, own_coefficients, rhs, results, turned, sems = refs[1 + feat :]
    me = lax.axis_index("feat")
    width = feat * kf
    persons, variants = table.shape
    steps = persons // chunk
    small = [
        pltpu.make_async_copy(directions, own_directions, sems.at[steps]),
        pltpu.make_async_copy(coefficients, own_coefficients, sems.at[steps + 1]),
    ]
    large = [
        pltpu.make_async_copy(
            dosages.at[pl.ds(i * chunk, chunk)], table.at[pl.ds(i * chunk, chunk)], sems.at[i]
        )
        for i in range(steps)
    ]
    for copy in small + large:
        copy.start()
    for copy in small:
        copy.wait()
    rhs[:, :width] = own_directions[...]
    spread = jnp.broadcast_to(own_coefficients[...].astype(F32)[None, :], (128, variants))
    rhs[:, width:] = spread.T.astype(BF16)
    diagonal = triangle(128, lambda a, b: a == b)
    for i in range(steps + 1):
        if i < steps:
            large[i].wait()
            results[i % 2] = jnp.dot(
                table[i * chunk : (i + 1) * chunk], rhs[...], preferred_element_type=F32
            )
        if i > 0:
            result = results.at[(i - 1) % 2]
            first = (i - 1) * chunk
            turned[i % 2] = result[:, :width].T.reshape(feat, kf, chunk)
            for j in range(feat):
                (send if j % 2 else keep)[j // 2][:, first : first + chunk] = turned[i % 2, me ^ j]
            for start in range(0, chunk, 128):
                block = result[start : start + 128, width:]
                row = jnp.sum(block * diagonal, axis=0, keepdims=True)
                group, lane = divmod(first + start, LO)
                linear[group : group + 1, lane : lane + 128] = row
                send[1][group : group + 1, persons + lane : persons + lane + 128] = row


def products(dosages, coefficients, directions, feat):
    persons, variants = dosages.shape
    k = directions.shape[1]
    kf = k // feat
    chunk = min(512, persons)
    piece = jax.ShapeDtypeStruct((kf, persons), F32)
    first = jax.ShapeDtypeStruct((kf, persons + LO), F32)
    out = pl.pallas_call(
        functools.partial(product_kernel, feat, kf, chunk),
        in_specs=[HBM, HBM, HBM],
        out_shape=[jax.ShapeDtypeStruct((kf, LO), F32)]
        + [piece] * (feat // 2 + 1)
        + [first]
        + [piece] * (feat // 2 - 2),
        out_specs=[VMEM] * (feat + 1),
        scratch_shapes=[
            pltpu.VMEM((persons, variants), BF16),
            pltpu.VMEM((variants, k), BF16),
            pltpu.VMEM((variants,), BF16),
            pltpu.VMEM((variants, k + 128), BF16),
            pltpu.VMEM((2, chunk, k + 128), F32),
            pltpu.VMEM((2, feat, kf, chunk), F32),
            pltpu.SemaphoreType.DMA((persons // chunk + 2,)),
        ],
        compiler_params=pltpu.CompilerParams(vmem_limit_bytes=PRODUCT_BYTES),
        cost_estimate=pl.CostEstimate(
            flops=2 * persons * variants * k, bytes_accessed=persons * (variants * 2 + k * 4), transcendentals=0
        ),
        name="products",
    )(directions, coefficients, dosages)
    return out[0], out[1 : 1 + feat // 2], out[1 + feat // 2 :]


def power_of(largest):
    return jnp.ceil(jnp.log2(jnp.maximum(largest, 1e-30))) - 14.0


def to_short(values):
    return jnp.round(values).astype(jnp.int32).astype(jnp.int16)


def from_short(values):
    return values.astype(jnp.int32).astype(F32)


def join_kernel(count, *refs):
    linear, keep, received = refs[0], refs[1 : 1 + count], refs[1 + count : 1 + 2 * count]
    linear_out, outs = refs[1 + 2 * count], refs[2 + 2 * count :]
    kf, rows = keep[0].shape
    span = min(SPAN, rows)
    lane = lax.broadcasted_iota(jnp.int32, (kf, 128), 1)
    paired = linear[...] + received[0][:, rows:]
    linear_out[...] = paired
    linear_power = power_of(jnp.max(jnp.abs(paired), axis=1, keepdims=True))
    scaled = paired * jnp.exp2(-linear_power)
    whole = jnp.round(scaled)
    high, low = to_short(whole), to_short((scaled - whole) * 32768.0)
    for mine, other, out in zip(keep, received, outs):
        powers = jnp.where(lane == rows // span, linear_power, 0.0)
        for i in range(rows // span):
            at = slice(i * span, (i + 1) * span)
            total = mine[:, at] + other[:, at]
            power = power_of(jnp.max(jnp.abs(total), axis=1, keepdims=True))
            out[:, at] = to_short(total * jnp.exp2(-power))
            powers = jnp.where(lane == i, power, powers)
        out[:, rows : rows + LO] = high
        out[:, rows + LO : rows + 2 * LO] = low
        out[:, rows + 2 * LO :] = to_short(powers)


def join(linear, keep, received):
    count = len(keep)
    kf, rows = keep[0].shape
    message = jax.ShapeDtypeStruct((kf, rows + 2 * LO + 128), jnp.int16)
    out = pl.pallas_call(
        functools.partial(join_kernel, count),
        in_specs=[VMEM] * (2 * count + 1),
        out_shape=[jax.ShapeDtypeStruct(linear.shape, F32)] + [message] * count,
        out_specs=[VMEM] * (count + 1),
        compiler_params=pltpu.CompilerParams(**PARAMS),
        name="join",
    )(linear, *keep, *received)
    return out[0], out[1:]


def table_kernel(rows, rank, waited, spread, table, masks):
    groups, height, _ = masks.shape
    chunk = min(512, rows)
    lane = lax.broadcasted_iota(jnp.int32, (chunk, 128), 1)
    for start in range(0, rows, chunk):
        at = slice(start, start + chunk)
        place = lax.rem(rank[:, at], rows)
        group, inner = place // LO, lax.rem(place, LO)
        spread[:, at] = one_hot(inner, LO)
        column = jnp.broadcast_to(inner.astype(F32), (128, chunk)).T.astype(jnp.int32)
        for first in range(0, LO, 128):
            table[at, first : first + 128] = jnp.where(column == lane + first, 1.0, 0.0).astype(BF16)
        for g in range(groups):
            mask = jnp.where(group == g, 1.0, 0.0)
            masks[g, :, at] = jnp.broadcast_to(mask, (height, chunk)).astype(BF16)


def tables(rank, waited, rows, height):
    return pl.pallas_call(
        functools.partial(table_kernel, rows),
        in_specs=[VMEM, pl.BlockSpec(memory_space=pl.ANY)],
        out_shape=[
            jax.ShapeDtypeStruct((LO, rows), BF16),
            jax.ShapeDtypeStruct((rows, LO), BF16),
            jax.ShapeDtypeStruct((rows // LO, height, rows), BF16),
        ],
        out_specs=[VMEM] * 3,
        compiler_params=pltpu.CompilerParams(**PARAMS),
        cost_estimate=pl.CostEstimate(flops=rows * LO * 8, bytes_accessed=rows * LO * 6, transcendentals=0),
        name="tables",
    )(rank, waited)


def risk_kernel(rows, parts, linear, *refs):
    messages, (rank, events, table) = refs[:parts], refs[parts : parts + 3]
    risk_out, sums_out, events_out, message = refs[parts + 3 :]
    groups = rows // LO
    span = min(SPAN, rows)
    total = linear[...]
    for part in messages:
        power = from_short(part[:, rows + 2 * LO :])[:, rows // span : rows // span + 1]
        high, low = from_short(part[:, rows : rows + LO]), from_short(part[:, rows + LO : rows + 2 * LO])
        total = total + (high + low * (1.0 / 32768.0)) * jnp.exp2(power)
    risk = jnp.exp(total)
    for g in range(groups):
        risk_out[:, g * LO : (g + 1) * LO] = risk[g : g + 1]
    mask = one_hot(lax.rem(rank[...], rows) // LO, groups, F32)
    pieces = [mask * part for part in split_three(risk_out[...])] + [mask * events[...].astype(F32)]
    lhs = jnp.concatenate(pieces, axis=0).astype(BF16)
    sorted_all = jnp.dot(lhs, table[...], preferred_element_type=F32)
    ordered = sorted_all[:groups] + sorted_all[groups : 2 * groups] + sorted_all[2 * groups : 3 * groups]
    happened = sorted_all[3 * groups :]
    inside = dot_binary(ordered, triangle(LO, lambda a, b: a >= b))
    totals = jnp.broadcast_to(inside[:, :1], inside.shape)
    carried = exact_dot(triangle(groups, lambda a, b: a < b), totals)
    sums_out[...] = inside + carried
    events_out[...] = happened
    everything = jnp.sum(totals, axis=0, keepdims=True)[:, :128]
    count = jnp.sum(dot_binary(happened, jnp.ones((LO, 128), F32)), axis=0, keepdims=True)
    message[...] = jnp.concatenate([everything, count, jnp.zeros((6, 128), F32)], axis=0)


def risks(linear, messages, rank, events, table, rows):
    groups = rows // LO
    return pl.pallas_call(
        functools.partial(risk_kernel, rows, len(messages)),
        in_specs=[VMEM] * (len(messages) + 4),
        out_shape=[
            jax.ShapeDtypeStruct((1, rows), F32),
            jax.ShapeDtypeStruct((groups, LO), F32),
            jax.ShapeDtypeStruct((groups, LO), F32),
            jax.ShapeDtypeStruct((8, 128), F32),
        ],
        out_specs=[VMEM] * 4,
        compiler_params=pltpu.CompilerParams(**PARAMS),
        cost_estimate=pl.CostEstimate(flops=rows * LO * 128, bytes_accessed=rows * 64, transcendentals=rows),
        name="risks",
    )(linear, *messages, rank, events, table)


def hazard_kernel(rows, later, sums, events, rank, spread, *outs):
    cumulative, squares, ordered_squares, message = outs
    groups = rows // LO
    risk_sum = sums[...] + later[0:1, 0:1]
    hazard = events[...] / risk_sum
    square = events[...] / (risk_sum * risk_sum)
    ordered_squares[...] = square
    both = jnp.concatenate([hazard, square], axis=0)
    inside = dot_binary(both, triangle(LO, lambda a, b: a <= b))
    totals = jnp.broadcast_to(inside[:, LO - 1 :], inside.shape)
    before = triangle(groups, lambda a, b: a > b)
    carried = jnp.concatenate(
        [exact_dot(before, totals[:groups]), exact_dot(before, totals[groups:])], axis=0
    )
    message[...] = jnp.concatenate(
        [
            jnp.sum(totals[:groups], axis=0, keepdims=True)[:, :128],
            jnp.sum(totals[groups:], axis=0, keepdims=True)[:, :128],
            jnp.zeros((6, 128), F32),
        ],
        axis=0,
    )
    mask = one_hot(lax.rem(rank[...], rows) // LO, groups, F32)
    placed = dot_binary(inside + carried, spread[...])
    cumulative[...] = jnp.sum(mask * placed[:groups], axis=0, keepdims=True)
    squares[...] = jnp.sum(mask * placed[groups:], axis=0, keepdims=True)


def hazards(later, sums, events, rank, spread, rows):
    groups = rows // LO
    row = jax.ShapeDtypeStruct((1, rows), F32)
    small = jax.ShapeDtypeStruct((8, 128), F32)
    return pl.pallas_call(
        functools.partial(hazard_kernel, rows),
        in_specs=[VMEM] * 5,
        out_shape=[row, row, jax.ShapeDtypeStruct((groups, LO), F32), small],
        out_specs=[VMEM] * 4,
        compiler_params=pltpu.CompilerParams(**PARAMS),
        cost_estimate=pl.CostEstimate(flops=rows * LO * 200, bytes_accessed=rows * 64, transcendentals=0),
        name="hazards",
    )(later, sums, events, rank, spread)


def total_kernel(tangent, risk, squares, hazard_message, message):
    kf, rows = tangent.shape
    plain = jnp.zeros((kf, 128), F32)
    scaled = jnp.zeros((kf, 128), F32)
    for start in range(0, rows, 128):
        at = slice(start, start + 128)
        weighted = tangent[:, at] * risk[:, at]
        plain = plain + weighted
        scaled = scaled + weighted * squares[:, at]
    message[...] = jnp.concatenate([plain, scaled, hazard_message[...]], axis=0)


def block_totals(tangent, risk, squares, hazard_message):
    kf, rows = tangent.shape
    return pl.pallas_call(
        total_kernel,
        in_specs=[VMEM] * 4,
        out_shape=jax.ShapeDtypeStruct((2 * kf + 8, 128), F32),
        out_specs=VMEM,
        compiler_params=pltpu.CompilerParams(**PARAMS),
        name="block_totals",
    )(tangent, risk, squares, hazard_message)


def suffix_kernel(parts, own, other, *refs):
    messages, (risk, masks, table) = refs[:parts], refs[parts : parts + 3]
    tangent_out, sums, lhs = refs[parts + 3 :]
    kf, rows = own.shape
    groups = masks.shape[0]
    span = min(SPAN, rows)
    powers = [jnp.exp2(from_short(part[:, rows + 2 * LO :])) for part in messages]
    for i in range(rows // span):
        at = slice(i * span, (i + 1) * span)
        tangent = own[:, at] + other[:, at]
        for part, power in zip(messages, powers):
            tangent = tangent + from_short(part[:, at]) * power[:, i : i + 1]
        tangent_out[:, at] = tangent
        high, low = split_two(tangent * risk[:, at])
        high, low = high.astype(BF16), low.astype(BF16)
        for g in range(groups):
            lhs[2 * g * kf : (2 * g + 1) * kf, at] = high * masks[g, :, at]
            lhs[(2 * g + 1) * kf : (2 * g + 2) * kf, at] = low * masks[g, :, at]
    ordered = jnp.dot(lhs[...], table[...], preferred_element_type=F32)
    ordered = jnp.concatenate(
        [
            ordered[2 * g * kf : (2 * g + 1) * kf] + ordered[(2 * g + 1) * kf : (2 * g + 2) * kf]
            for g in range(groups)
        ],
        axis=0,
    )
    inside = dot_binary(ordered, triangle(LO, lambda a, b: a >= b))
    carried = jnp.zeros((kf, 1), F32)
    for g in reversed(range(groups)):
        rows_of = slice(g * kf, (g + 1) * kf)
        sums[rows_of] = inside[rows_of] + carried
        carried = carried + inside[rows_of, :1]


def suffix_sums(own, other, messages, risk, masks, table):
    kf, rows = own.shape
    groups = rows // LO
    return pl.pallas_call(
        functools.partial(suffix_kernel, len(messages)),
        in_specs=[VMEM] * (len(messages) + 5),
        out_shape=[
            jax.ShapeDtypeStruct((kf, rows), F32),
            jax.ShapeDtypeStruct((groups * kf, LO), F32),
        ],
        out_specs=[VMEM] * 2,
        scratch_shapes=[pltpu.VMEM((groups * 2 * kf, rows), BF16)],
        compiler_params=pltpu.CompilerParams(**PARAMS),
        cost_estimate=pl.CostEstimate(
            flops=2 * rows * LO * groups * 2 * kf, bytes_accessed=rows * kf * 24, transcendentals=0
        ),
        name="suffix_sums",
    )(own, other, *messages, risk, masks, table)


def prefix_kernel(sums, squares, rank, spread, out):
    kf, rows = out.shape
    groups = squares.shape[0]
    chunk = min(512, rows)
    hazard = [sums[g * kf : (g + 1) * kf] * squares[g : g + 1, :] for g in range(groups)]
    inside = dot_binary(jnp.concatenate(hazard, axis=0), triangle(LO, lambda a, b: a <= b))
    carried = jnp.zeros((kf, 1), F32)
    summed = [None] * groups
    for g in range(groups):
        rows_of = slice(g * kf, (g + 1) * kf)
        summed[g] = inside[rows_of] + carried
        carried = carried + inside[rows_of, LO - 1 :]
    high, low = split_two(jnp.concatenate(summed, axis=0))
    high, low = high.astype(BF16), low.astype(BF16)
    for start in range(0, rows, chunk):
        at = slice(start, start + chunk)
        group = lax.rem(rank[:, at], rows) // LO
        placed = jnp.dot(high, spread[:, at], preferred_element_type=F32) + jnp.dot(
            low, spread[:, at], preferred_element_type=F32
        )
        picked = jnp.zeros((kf, chunk), F32)
        for g in range(groups):
            picked = picked + jnp.where(group == g, placed[g * kf : (g + 1) * kf], 0.0)
        out[:, at] = picked


def prefix_sums(sums, squares, rank, spread, kf):
    rows = rank.shape[1]
    return pl.pallas_call(
        prefix_kernel,
        in_specs=[VMEM] * 4,
        out_shape=jax.ShapeDtypeStruct((kf, rows), F32),
        out_specs=VMEM,
        compiler_params=pltpu.CompilerParams(**PARAMS),
        cost_estimate=pl.CostEstimate(
            flops=4 * rows * LO * (rows // LO) * kf, bytes_accessed=rows * kf * 24, transcendentals=0
        ),
        name="prefix_sums",
    )(sums, squares, rank, spread)


def weight_kernel(kf, ex, *refs):
    messages, (tangent, local, risk, cumulative, squares) = refs[:ex], refs[ex : ex + 5]
    weighted, placed = refs[ex + 5 :]
    me = lax.axis_index("ex")
    for i in range(ex):
        placed[me ^ i] = messages[i][...]
    later = jnp.zeros((kf, 1), F32)
    own_later = later
    before = later
    hazard_before = jnp.zeros((1, 1), F32)
    for b in reversed(range(ex)):
        plain = jnp.sum(placed[b, :kf], axis=1, keepdims=True)
        scaled = jnp.sum(placed[b, kf : 2 * kf], axis=1, keepdims=True)
        hazard_total = placed[b, 2 * kf : 2 * kf + 1, :1]
        square_total = placed[b, 2 * kf + 1 : 2 * kf + 2, :1]
        own_later = own_later + jnp.where(b > me, plain, 0.0)
        before = before + jnp.where(b < me, scaled + square_total * later, 0.0)
        hazard_before = hazard_before + jnp.where(b < me, hazard_total, 0.0)
        later = later + plain
    value = tangent[...] * (cumulative[...] + hazard_before) - (local[...] + squares[...] * own_later + before)
    weighted[...] = (risk[...] * value).astype(BF16)


def weights(messages, tangent, local, risk, cumulative, squares):
    return pl.pallas_call(
        functools.partial(weight_kernel, tangent.shape[0], len(messages)),
        in_specs=[VMEM] * (len(messages) + 5),
        out_shape=jax.ShapeDtypeStruct(tangent.shape, BF16),
        out_specs=VMEM,
        scratch_shapes=[pltpu.VMEM((len(messages),) + messages[0].shape, F32)],
        compiler_params=pltpu.CompilerParams(**PARAMS),
        name="weights",
    )(*messages, tangent, local, risk, cumulative, squares)


def encode(values, message):
    height = values.shape[0]
    block = min(BLOCK, height)
    powers = []
    for start in range(0, height, block):
        part = values[start : start + block]
        largest = jnp.max(jnp.abs(part), axis=0, keepdims=True)
        power = power_of(largest)
        message[start : start + block] = to_short(part * jnp.exp2(-power))
        powers.append(power)
    powers.append(jnp.zeros((message.shape[0] - height - len(powers), values.shape[1]), F32))
    message[height:] = to_short(jnp.concatenate(powers, axis=0))


def decode(message, height):
    block = min(BLOCK, height)
    powers = from_short(message[height:])
    parts = []
    for i in range(height // block):
        part = from_short(message[i * block : (i + 1) * block])
        parts.append(part * jnp.exp2(powers[i : i + 1]))
    return jnp.concatenate(parts, axis=0)


def gradient_kernel(feat, kf, *refs):
    parts, dosages, out, weighted = refs[:feat], refs[feat], refs[feat + 1], refs[feat + 2]
    me = lax.axis_index("feat")
    for i in range(feat):
        weighted[pl.ds(pl.multiple_of((me ^ i) * kf, kf), kf), :] = parts[i][...]
    total = jnp.dot(weighted[...], dosages[...], preferred_element_type=F32)
    encode(total.T, out)


def gradients(parts, dosages):
    feat = len(parts)
    kf, persons = parts[0].shape
    k, variants = kf * feat, dosages.shape[1]
    return pl.pallas_call(
        functools.partial(gradient_kernel, feat, kf),
        in_specs=[VMEM] * (feat + 1),
        out_shape=jax.ShapeDtypeStruct((variants + 16, k), jnp.int16),
        out_specs=VMEM,
        scratch_shapes=[pltpu.VMEM((k, persons), BF16)],
        compiler_params=pltpu.CompilerParams(**PARAMS),
        cost_estimate=pl.CostEstimate(
            flops=2 * persons * variants * k, bytes_accessed=persons * (variants * 2 + k * 2), transcendentals=0
        ),
        name="gradients",
    )(*parts, dosages)


def merge_kernel(mine, other, out):
    height = mine.shape[0] - 16
    encode(decode(mine, height) + decode(other, height), out)


def merge(mine, other):
    return pl.pallas_call(
        merge_kernel,
        in_specs=[VMEM] * 2,
        out_shape=jax.ShapeDtypeStruct(mine.shape, jnp.int16),
        out_specs=VMEM,
        compiler_params=pltpu.CompilerParams(**PARAMS),
        name="merge",
    )(mine, other)


def finish_kernel(mine, other, count, out):
    height = mine.shape[0] - 16
    out[...] = (decode(mine, height) + decode(other, height)) / count[1:2, 0:1]


def finish(mine, other, count):
    return pl.pallas_call(
        finish_kernel,
        in_specs=[VMEM] * 3,
        out_shape=jax.ShapeDtypeStruct((mine.shape[0] - 16, mine.shape[1]), F32),
        out_specs=VMEM,
        compiler_params=pltpu.CompilerParams(**PARAMS),
        name="finish",
    )(mine, other, count)


def local(dosages, coefficients, directions, event_rank, events):
    feat, ex = lax.axis_size("feat"), lax.axis_size("ex")
    rows = dosages.shape[0]
    variants, k = directions.shape
    each = k // feat
    padded = -(-each // 16) * 16
    if padded != each:
        directions = jnp.pad(directions.reshape(variants, feat, each), ((0, 0), (0, 0), (0, padded - each)))
        directions = directions.reshape(variants, feat * padded)
    rank, event_row = event_rank[None], events[None]

    linear, keep, send = products(dosages, coefficients, directions, feat)
    received = [swap(piece, "feat", 1) for piece in send]
    paired, joined = join(linear, keep[1:], received[1:])
    others = [swap(joined[q - 1], "feat", 2 * q) for q in range(1, feat // 2)]
    spread, table, masks = tables(rank, paired, rows, padded)

    risk, sums, ordered_events, total = risks(paired, others, rank, event_row, table, rows)
    later = jnp.zeros_like(total)
    bit = 1
    while bit < ex:
        other = swap(total, "ex", bit)
        later = later + jnp.where((lax.axis_index("ex") & bit) == 0, other, 0.0)
        total = total + other
        bit *= 2
    tangent, later_sums = suffix_sums(keep[0], received[0], others, risk, masks, table)
    cumulative, squares, ordered_squares, hazard_message = hazards(
        later, sums, ordered_events, rank, spread, rows
    )
    message = block_totals(tangent, risk, squares, hazard_message)
    messages = [message] + [swap(message, "ex", i) for i in range(1, ex)]
    summed = prefix_sums(later_sums, ordered_squares, rank, spread, padded)
    own = weights(messages, tangent, summed, risk, cumulative, squares)

    chips = {0: own}
    for q in reversed(range(1, feat // 2)):
        chips[q] = swap(own, "feat", 2 * q)
    parts = []
    for q in range(feat // 2):
        parts += [chips[q], swap(chips[q], "feat", 1)]

    partial_sum = gradients(parts, dosages)
    bit = 1
    while 2 * bit < ex:
        partial_sum = merge(partial_sum, swap(partial_sum, "ex", bit))
        bit *= 2
    result = finish(partial_sum, swap(partial_sum, "ex", bit), total)
    if padded != each:
        result = result.reshape(variants, feat, padded)[:, :, :each].reshape(variants, k)
    return result


def solution(mesh):
    placed = (P("ex", "feat"), P("feat"), P("feat", None), P("ex"), P("ex"))
    return jax.shard_map(
        local, mesh=mesh, in_specs=placed, out_specs=P("feat", None), check_vma=False
    )
```

```python
import functools

import jax
import jax.numpy as jnp
from jax import lax
from jax.experimental import pallas as pl
from jax.experimental.pallas import tpu as pltpu
from jax.sharding import PartitionSpec as P

F32 = jnp.float32
BF16 = jnp.bfloat16
LO = 256
BLOCK = 64
SPAN = 512
VMEM = pl.BlockSpec(memory_space=pltpu.VMEM)
HBM = pl.BlockSpec(memory_space=pltpu.HBM)
PRODUCT_BYTES = 24 * 1024 * 1024
PARAMS = dict(vmem_limit_bytes=24 * 1024 * 1024)


def swap(x, axis, i):
    count = lax.axis_size(axis)
    return lax.ppermute(x, axis, [(s, s ^ i) for s in range(count)])


def split_two(x):
    high = x.astype(BF16).astype(F32)
    return high, x - high


def split_three(x):
    first, rest = split_two(x)
    second, third = split_two(rest)
    return first, second, third


def one_hot(values, count, kind=BF16):
    shape = (count, values.shape[1])
    return jnp.where(lax.broadcasted_iota(jnp.int32, shape, 0) == values, 1.0, 0.0).astype(kind)


def triangle(n, keep):
    first = lax.broadcasted_iota(jnp.int32, (n, n), 0)
    second = lax.broadcasted_iota(jnp.int32, (n, n), 1)
    return jnp.where(keep(first, second), 1.0, 0.0)


def dot_binary(a, b):
    b = b.astype(BF16)
    total = None
    for part in split_three(a):
        term = jnp.dot(part.astype(BF16), b, preferred_element_type=F32)
        total = term if total is None else total + term
    return total


def binary_dot(a, b):
    a = a.astype(BF16)
    total = None
    for part in split_three(b):
        term = jnp.dot(a, part.astype(BF16), preferred_element_type=F32)
        total = term if total is None else total + term
    return total


def product_kernel(feat, kf, chunk, directions, coefficients, dosages, *refs):
    linear, keep, send = refs[0], refs[1 : 1 + feat // 2], refs[1 + feat // 2 : 1 + feat]
    table, own_directions, own_coefficients, rhs, results, turned, sems = refs[1 + feat :]
    me = lax.axis_index("feat")
    width = feat * kf
    persons, variants = table.shape
    steps = persons // chunk
    small = [
        pltpu.make_async_copy(directions, own_directions, sems.at[steps]),
        pltpu.make_async_copy(coefficients, own_coefficients, sems.at[steps + 1]),
    ]
    large = [
        pltpu.make_async_copy(
            dosages.at[pl.ds(i * chunk, chunk)], table.at[pl.ds(i * chunk, chunk)], sems.at[i]
        )
        for i in range(steps)
    ]
    for copy in small + large:
        copy.start()
    for copy in small:
        copy.wait()
    rhs[:, :width] = own_directions[...]
    spread = jnp.broadcast_to(own_coefficients[...].astype(F32)[None, :], (128, variants))
    rhs[:, width:] = spread.T.astype(BF16)
    diagonal = triangle(128, lambda a, b: a == b)
    for i in range(steps + 1):
        if i < steps:
            large[i].wait()
            results[i % 2] = jnp.dot(
                table[i * chunk : (i + 1) * chunk], rhs[...], preferred_element_type=F32
            )
        if i > 0:
            result = results.at[(i - 1) % 2]
            first = (i - 1) * chunk
            turned[i % 2] = result[:, :width].T.reshape(feat, kf, chunk)
            for j in range(feat):
                (send if j % 2 else keep)[j // 2][:, first : first + chunk] = turned[i % 2, me ^ j]
            for start in range(0, chunk, 128):
                block = result[start : start + 128, width:]
                row = jnp.sum(block * diagonal, axis=0, keepdims=True)
                group, lane = divmod(first + start, LO)
                linear[group : group + 1, lane : lane + 128] = row
                send[1][group : group + 1, persons + lane : persons + lane + 128] = row


def products(dosages, coefficients, directions, feat):
    persons, variants = dosages.shape
    k = directions.shape[1]
    kf = k // feat
    chunk = min(512, persons)
    piece = jax.ShapeDtypeStruct((kf, persons), F32)
    first = jax.ShapeDtypeStruct((kf, persons + LO), F32)
    out = pl.pallas_call(
        functools.partial(product_kernel, feat, kf, chunk),
        in_specs=[HBM, HBM, HBM],
        out_shape=[jax.ShapeDtypeStruct((kf, LO), F32)]
        + [piece] * (feat // 2 + 1)
        + [first]
        + [piece] * (feat // 2 - 2),
        out_specs=[VMEM] * (feat + 1),
        scratch_shapes=[
            pltpu.VMEM((persons, variants), BF16),
            pltpu.VMEM((variants, k), BF16),
            pltpu.VMEM((variants,), BF16),
            pltpu.VMEM((variants, k + 128), BF16),
            pltpu.VMEM((2, chunk, k + 128), F32),
            pltpu.VMEM((2, feat, kf, chunk), F32),
            pltpu.SemaphoreType.DMA((persons // chunk + 2,)),
        ],
        compiler_params=pltpu.CompilerParams(vmem_limit_bytes=PRODUCT_BYTES),
        cost_estimate=pl.CostEstimate(
            flops=2 * persons * variants * k, bytes_accessed=persons * (variants * 2 + k * 4), transcendentals=0
        ),
        name="products",
    )(*[pltpu.with_memory_space_constraint(x, pltpu.HBM) for x in (directions, coefficients, dosages)])
    return out[0], out[1 : 1 + feat // 2], out[1 + feat // 2 :]


def power_of(largest):
    return jnp.ceil(jnp.log2(jnp.maximum(largest, 1e-30))) - 14.0


def to_short(values):
    return jnp.round(values).astype(jnp.int32).astype(jnp.int16)


def from_short(values):
    return values.astype(jnp.int32).astype(F32)


def join_kernel(count, *refs):
    linear, keep, received = refs[0], refs[1 : 1 + count], refs[1 + count : 1 + 2 * count]
    linear_out, outs = refs[1 + 2 * count], refs[2 + 2 * count :]
    kf, rows = keep[0].shape
    span = min(SPAN, rows)
    lane = lax.broadcasted_iota(jnp.int32, (kf, 128), 1)
    paired = linear[...] + received[0][:, rows:]
    linear_out[...] = paired
    linear_power = power_of(jnp.max(jnp.abs(paired), axis=1, keepdims=True))
    scaled = paired * jnp.exp2(-linear_power)
    whole = jnp.round(scaled)
    high, low = to_short(whole), to_short((scaled - whole) * 32768.0)
    for mine, other, out in zip(keep, received, outs):
        powers = jnp.where(lane == rows // span, linear_power, 0.0)
        for i in range(rows // span):
            at = slice(i * span, (i + 1) * span)
            total = mine[:, at] + other[:, at]
            power = power_of(jnp.max(jnp.abs(total), axis=1, keepdims=True))
            out[:, at] = to_short(total * jnp.exp2(-power))
            powers = jnp.where(lane == i, power, powers)
        out[:, rows : rows + LO] = high
        out[:, rows + LO : rows + 2 * LO] = low
        out[:, rows + 2 * LO :] = to_short(powers)


def join(linear, keep, received):
    count = len(keep)
    kf, rows = keep[0].shape
    message = jax.ShapeDtypeStruct((kf, rows + 2 * LO + 128), jnp.int16)
    out = pl.pallas_call(
        functools.partial(join_kernel, count),
        in_specs=[VMEM] * (2 * count + 1),
        out_shape=[jax.ShapeDtypeStruct(linear.shape, F32)] + [message] * count,
        out_specs=[VMEM] * (count + 1),
        compiler_params=pltpu.CompilerParams(**PARAMS),
        name="join",
    )(linear, *keep, *received)
    return out[0], out[1:]


def table_kernel(rows, rank, waited, table):
    chunk = min(512, rows)
    lane = lax.broadcasted_iota(jnp.int32, (chunk, 128), 1)
    for start in range(0, rows, chunk):
        at = slice(start, start + chunk)
        inner = lax.rem(rank[:, at], LO)
        column = jnp.broadcast_to(inner.astype(F32), (128, chunk)).T.astype(jnp.int32)
        for first in range(0, LO, 128):
            table[at, first : first + 128] = jnp.where(column == lane + first, 1.0, 0.0).astype(BF16)


def tables(rank, waited, rows):
    return pl.pallas_call(
        functools.partial(table_kernel, rows),
        in_specs=[VMEM, pl.BlockSpec(memory_space=pl.ANY)],
        out_shape=jax.ShapeDtypeStruct((rows, LO), BF16),
        out_specs=VMEM,
        compiler_params=pltpu.CompilerParams(**PARAMS),
        cost_estimate=pl.CostEstimate(flops=rows * LO * 8, bytes_accessed=rows * LO * 2, transcendentals=0),
        name="tables",
    )(rank, waited)


def risk_kernel(rows, parts, linear, *refs):
    messages, (rank, events, table) = refs[:parts], refs[parts : parts + 3]
    risk_out, sums_out, events_out, message = refs[parts + 3 :]
    groups = rows // LO
    span = min(SPAN, rows)
    total = linear[...]
    for part in messages:
        power = from_short(part[:, rows + 2 * LO :])[:, rows // span : rows // span + 1]
        high, low = from_short(part[:, rows : rows + LO]), from_short(part[:, rows + LO : rows + 2 * LO])
        total = total + (high + low * (1.0 / 32768.0)) * jnp.exp2(power)
    risk = jnp.exp(total)
    for g in range(groups):
        risk_out[:, g * LO : (g + 1) * LO] = risk[g : g + 1]
    mask = one_hot(lax.rem(rank[...], rows) // LO, groups, F32)
    pieces = [mask * part for part in split_three(risk_out[...])] + [mask * events[...].astype(F32)]
    lhs = jnp.concatenate(pieces, axis=0).astype(BF16)
    sorted_all = jnp.dot(lhs, table[...], preferred_element_type=F32)
    ordered = sorted_all[:groups] + sorted_all[groups : 2 * groups] + sorted_all[2 * groups : 3 * groups]
    happened = sorted_all[3 * groups :]
    inside = dot_binary(ordered, triangle(LO, lambda a, b: a >= b))
    totals = jnp.broadcast_to(inside[:, :1], inside.shape)
    carried = binary_dot(triangle(groups, lambda a, b: a < b), totals)
    sums_out[...] = inside + carried
    events_out[...] = happened
    everything = jnp.sum(totals, axis=0, keepdims=True)[:, :128]
    count = jnp.sum(dot_binary(happened, jnp.ones((LO, 128), F32)), axis=0, keepdims=True)
    message[...] = jnp.concatenate([everything, count, jnp.zeros((6, 128), F32)], axis=0)


def risks(linear, messages, rank, events, table, rows):
    groups = rows // LO
    return pl.pallas_call(
        functools.partial(risk_kernel, rows, len(messages)),
        in_specs=[VMEM] * (len(messages) + 4),
        out_shape=[
            jax.ShapeDtypeStruct((1, rows), F32),
            jax.ShapeDtypeStruct((groups, LO), F32),
            jax.ShapeDtypeStruct((groups, LO), F32),
            jax.ShapeDtypeStruct((8, 128), F32),
        ],
        out_specs=[VMEM] * 4,
        compiler_params=pltpu.CompilerParams(**PARAMS),
        cost_estimate=pl.CostEstimate(flops=rows * LO * 128, bytes_accessed=rows * 64, transcendentals=rows),
        name="risks",
    )(linear, *messages, rank, events, table)


def hazard_kernel(rows, later, sums, events, rank, *outs):
    cumulative, squares, ordered_squares, message = outs
    groups = rows // LO
    risk_sum = sums[...] + later[0:1, 0:1]
    hazard = events[...] / risk_sum
    square = events[...] / (risk_sum * risk_sum)
    ordered_squares[...] = square
    inside = dot_binary(jnp.concatenate([hazard, square], axis=0), triangle(LO, lambda a, b: a <= b))
    totals = jnp.broadcast_to(inside[:, LO - 1 :], (2 * groups, 128))
    place = lax.rem(rank[...], rows)
    mask = one_hot(place // LO, groups, F32)
    placed = dot_binary(inside, one_hot(lax.rem(place, LO), LO))
    before = triangle(groups, lambda a, b: a > b)
    for first, out in ((0, cumulative), (groups, squares)):
        carried = binary_dot(before, totals[first : first + groups])[:, :1]
        out[...] = jnp.sum(mask * (placed[first : first + groups] + carried), axis=0, keepdims=True)
    message[...] = jnp.concatenate(
        [
            jnp.sum(totals[:groups], axis=0, keepdims=True),
            jnp.sum(totals[groups:], axis=0, keepdims=True),
            jnp.zeros((6, 128), F32),
        ],
        axis=0,
    )


def hazards(later, sums, events, rank, rows):
    groups = rows // LO
    row = jax.ShapeDtypeStruct((1, rows), F32)
    small = jax.ShapeDtypeStruct((8, 128), F32)
    return pl.pallas_call(
        functools.partial(hazard_kernel, rows),
        in_specs=[VMEM] * 4,
        out_shape=[row, row, jax.ShapeDtypeStruct((groups, LO), F32), small],
        out_specs=[VMEM] * 4,
        compiler_params=pltpu.CompilerParams(**PARAMS),
        cost_estimate=pl.CostEstimate(flops=rows * LO * 200, bytes_accessed=rows * 64, transcendentals=0),
        name="hazards",
    )(later, sums, events, rank)


def total_kernel(tangent, risk, squares, hazard_message, message):
    kf, rows = tangent.shape
    plain = jnp.zeros((kf, 128), F32)
    scaled = jnp.zeros((kf, 128), F32)
    for start in range(0, rows, 128):
        at = slice(start, start + 128)
        weighted = tangent[:, at] * risk[:, at]
        plain = plain + weighted
        scaled = scaled + weighted * squares[:, at]
    message[...] = jnp.concatenate([plain, scaled, hazard_message[...]], axis=0)


def block_totals(tangent, risk, squares, hazard_message):
    kf, rows = tangent.shape
    return pl.pallas_call(
        total_kernel,
        in_specs=[VMEM] * 4,
        out_shape=jax.ShapeDtypeStruct((2 * kf + 8, 128), F32),
        out_specs=VMEM,
        compiler_params=pltpu.CompilerParams(**PARAMS),
        name="block_totals",
    )(tangent, risk, squares, hazard_message)


def suffix_kernel(parts, own, other, *refs):
    messages, (risk, rank, table) = refs[:parts], refs[parts : parts + 3]
    tangent_out, sums, lhs = refs[parts + 3 :]
    kf, rows = own.shape
    groups = rows // LO
    span = min(SPAN, rows)
    powers = [jnp.exp2(from_short(part[:, rows + 2 * LO :])) for part in messages]
    for i in range(rows // span):
        at = slice(i * span, (i + 1) * span)
        tangent = own[:, at] + other[:, at]
        for part, power in zip(messages, powers):
            tangent = tangent + from_short(part[:, at]) * power[:, i : i + 1]
        tangent_out[:, at] = tangent
        high, low = split_two(tangent * risk[:, at])
        high, low = high.astype(BF16), low.astype(BF16)
        group = jnp.broadcast_to(lax.rem(rank[:, at], rows) // LO, (kf, span))
        for g in range(groups):
            mask = jnp.where(group == g, 1.0, 0.0).astype(BF16)
            lhs[2 * g * kf : (2 * g + 1) * kf, at] = high * mask
            lhs[(2 * g + 1) * kf : (2 * g + 2) * kf, at] = low * mask
    ordered = jnp.dot(lhs[...], table[...], preferred_element_type=F32)
    ordered = jnp.concatenate(
        [
            ordered[2 * g * kf : (2 * g + 1) * kf] + ordered[(2 * g + 1) * kf : (2 * g + 2) * kf]
            for g in range(groups)
        ],
        axis=0,
    )
    inside = dot_binary(ordered, triangle(LO, lambda a, b: a >= b))
    carried = jnp.zeros((kf, 1), F32)
    for g in reversed(range(groups)):
        rows_of = slice(g * kf, (g + 1) * kf)
        sums[rows_of] = inside[rows_of] + carried
        carried = carried + inside[rows_of, :1]


def suffix_sums(own, other, messages, risk, rank, table):
    kf, rows = own.shape
    groups = rows // LO
    return pl.pallas_call(
        functools.partial(suffix_kernel, len(messages)),
        in_specs=[VMEM] * (len(messages) + 5),
        out_shape=[
            jax.ShapeDtypeStruct((kf, rows), F32),
            jax.ShapeDtypeStruct((groups * kf, LO), F32),
        ],
        out_specs=[VMEM] * 2,
        scratch_shapes=[pltpu.VMEM((groups * 2 * kf, rows), BF16)],
        compiler_params=pltpu.CompilerParams(**PARAMS),
        cost_estimate=pl.CostEstimate(
            flops=2 * rows * LO * groups * 2 * kf, bytes_accessed=rows * kf * 24, transcendentals=0
        ),
        name="suffix_sums",
    )(own, other, *messages, risk, rank, table)


def prefix_kernel(sums, squares, rank, out):
    kf, rows = out.shape
    groups = squares.shape[0]
    chunk = min(512, rows)
    hazard = [sums[g * kf : (g + 1) * kf] * squares[g : g + 1, :] for g in range(groups)]
    inside = dot_binary(jnp.concatenate(hazard, axis=0), triangle(LO, lambda a, b: a <= b))
    carried = jnp.zeros((kf, 1), F32)
    summed = [None] * groups
    for g in range(groups):
        rows_of = slice(g * kf, (g + 1) * kf)
        summed[g] = inside[rows_of] + carried
        carried = carried + inside[rows_of, LO - 1 :]
    high, low = split_two(jnp.concatenate(summed, axis=0))
    high, low = high.astype(BF16), low.astype(BF16)
    for start in range(0, rows, chunk):
        at = slice(start, start + chunk)
        place = lax.rem(rank[:, at], rows)
        group = place // LO
        spread = one_hot(lax.rem(place, LO), LO)
        placed = jnp.dot(high, spread, preferred_element_type=F32) + jnp.dot(
            low, spread, preferred_element_type=F32
        )
        picked = jnp.zeros((kf, chunk), F32)
        for g in range(groups):
            picked = picked + jnp.where(group == g, placed[g * kf : (g + 1) * kf], 0.0)
        out[:, at] = picked


def prefix_sums(sums, squares, rank, kf):
    rows = rank.shape[1]
    return pl.pallas_call(
        prefix_kernel,
        in_specs=[VMEM] * 3,
        out_shape=jax.ShapeDtypeStruct((kf, rows), F32),
        out_specs=VMEM,
        compiler_params=pltpu.CompilerParams(**PARAMS),
        cost_estimate=pl.CostEstimate(
            flops=4 * rows * LO * (rows // LO) * kf, bytes_accessed=rows * kf * 24, transcendentals=0
        ),
        name="prefix_sums",
    )(sums, squares, rank)


def merged(kf, bit, mine, other, state):
    later_other = (lax.axis_index("ex") & bit) == 0
    plain, scaled, rest = mine[:kf], mine[kf : 2 * kf], mine[2 * kf :]
    other_plain, other_scaled, other_rest = other[:kf], other[kf : 2 * kf], other[2 * kf :]
    square, other_square = rest[1:2], other_rest[1:2]
    crossed = jnp.where(later_other, square * other_plain, other_square * plain)
    total = jnp.concatenate([plain + other_plain, scaled + other_scaled + crossed, rest + other_rest], axis=0)
    if state is None:
        state = jnp.zeros_like(mine)
    later, before, before_rest = state[:kf], state[kf : 2 * kf], state[2 * kf :]
    state = jnp.concatenate(
        [
            later + jnp.where(later_other, other_plain, 0.0),
            before + jnp.where(later_other, before_rest[1:2] * other_plain, other_scaled + other_square * plain),
            before_rest + jnp.where(later_other, 0.0, other_rest),
        ],
        axis=0,
    )
    return total, state


def combine_kernel(kf, bit, count, *refs):
    inputs, (total, state) = [ref[...] for ref in refs[:count]], refs[count:]
    total[...], state[...] = merged(kf, bit, inputs[0], inputs[1], inputs[2] if count > 2 else None)


def combine(kf, bit, inputs):
    shape = jax.ShapeDtypeStruct(inputs[0].shape, F32)
    return pl.pallas_call(
        functools.partial(combine_kernel, kf, bit, len(inputs)),
        in_specs=[VMEM] * len(inputs),
        out_shape=[shape, shape],
        out_specs=[VMEM] * 2,
        compiler_params=pltpu.CompilerParams(**PARAMS),
        name="combine",
    )(*inputs)


def weight_kernel(kf, bit, count, *refs):
    inputs = [ref[...] for ref in refs[:count]]
    tangent, local, risk, cumulative, squares, weighted = refs[count:]
    _, state = merged(kf, bit, inputs[0], inputs[1], inputs[2] if count > 2 else None)
    later = jnp.sum(state[:kf], axis=1, keepdims=True)
    before = jnp.sum(state[kf : 2 * kf], axis=1, keepdims=True)
    hazard_before = state[2 * kf : 2 * kf + 1, :1]
    value = tangent[...] * (cumulative[...] + hazard_before) - (local[...] + squares[...] * later + before)
    weighted[...] = (risk[...] * value).astype(BF16)


def weights(bit, inputs, tangent, local, risk, cumulative, squares):
    return pl.pallas_call(
        functools.partial(weight_kernel, tangent.shape[0], bit, len(inputs)),
        in_specs=[VMEM] * (len(inputs) + 5),
        out_shape=jax.ShapeDtypeStruct(tangent.shape, BF16),
        out_specs=VMEM,
        compiler_params=pltpu.CompilerParams(**PARAMS),
        name="weights",
    )(*inputs, tangent, local, risk, cumulative, squares)


def encode(values, message):
    height = values.shape[0]
    block = min(BLOCK, height)
    powers = []
    for start in range(0, height, block):
        part = values[start : start + block]
        largest = jnp.max(jnp.abs(part), axis=0, keepdims=True)
        power = power_of(largest)
        message[start : start + block] = to_short(part * jnp.exp2(-power))
        powers.append(power)
    powers.append(jnp.zeros((message.shape[0] - height - len(powers), values.shape[1]), F32))
    message[height:] = to_short(jnp.concatenate(powers, axis=0))


def decode(message, height):
    block = min(BLOCK, height)
    powers = from_short(message[height:])
    parts = []
    for i in range(height // block):
        part = from_short(message[i * block : (i + 1) * block])
        parts.append(part * jnp.exp2(powers[i : i + 1]))
    return jnp.concatenate(parts, axis=0)


def gradient_kernel(feat, kf, *refs):
    parts, dosages, out, weighted = refs[:feat], refs[feat], refs[feat + 1], refs[feat + 2]
    me = lax.axis_index("feat")
    for i in range(feat):
        weighted[pl.ds(pl.multiple_of((me ^ i) * kf, kf), kf), :] = parts[i][...]
    total = jnp.dot(weighted[...], dosages[...], preferred_element_type=F32)
    encode(total.T, out)


def gradients(parts, dosages):
    feat = len(parts)
    kf, persons = parts[0].shape
    k, variants = kf * feat, dosages.shape[1]
    return pl.pallas_call(
        functools.partial(gradient_kernel, feat, kf),
        in_specs=[VMEM] * (feat + 1),
        out_shape=jax.ShapeDtypeStruct((variants + 16, k), jnp.int16),
        out_specs=VMEM,
        scratch_shapes=[pltpu.VMEM((k, persons), BF16)],
        compiler_params=pltpu.CompilerParams(**PARAMS),
        cost_estimate=pl.CostEstimate(
            flops=2 * persons * variants * k, bytes_accessed=persons * (variants * 2 + k * 2), transcendentals=0
        ),
        name="gradients",
    )(*parts, dosages)


def merge_kernel(mine, other, out):
    height = mine.shape[0] - 16
    encode(decode(mine, height) + decode(other, height), out)


def merge(mine, other):
    return pl.pallas_call(
        merge_kernel,
        in_specs=[VMEM] * 2,
        out_shape=jax.ShapeDtypeStruct(mine.shape, jnp.int16),
        out_specs=VMEM,
        compiler_params=pltpu.CompilerParams(**PARAMS),
        name="merge",
    )(mine, other)


def finish_kernel(steps, mine, other, count, out, total, sems):
    height = mine.shape[0] - 16
    step = height // steps
    block = min(BLOCK, step)
    scale = count[1:2, 0:1]
    powers = [from_short(message[height:]) for message in (mine, other)]
    copies = []
    for i in range(steps):
        for start in range(i * step, (i + 1) * step, block):
            at, j = slice(start, start + block), start // block
            terms = [from_short(m[at]) * jnp.exp2(p[j : j + 1]) for m, p in zip((mine, other), powers)]
            total[at] = (terms[0] + terms[1]) / scale
        at = pl.ds(i * step, step)
        copies.append(pltpu.make_async_copy(total.at[at], out.at[at], sems.at[i]))
        copies[i].start()
    for copy in copies:
        copy.wait()


def finish(mine, other, count):
    height, k = mine.shape[0] - 16, mine.shape[1]
    steps = max(1, min(4, height // BLOCK))
    return pl.pallas_call(
        functools.partial(finish_kernel, steps),
        in_specs=[VMEM] * 3,
        out_shape=jax.ShapeDtypeStruct((height, k), F32),
        out_specs=HBM,
        scratch_shapes=[pltpu.VMEM((height, k), F32), pltpu.SemaphoreType.DMA((steps,))],
        compiler_params=pltpu.CompilerParams(**PARAMS),
        name="finish",
    )(mine, other, count)


def local(dosages, coefficients, directions, event_rank, events):
    feat, ex = lax.axis_size("feat"), lax.axis_size("ex")
    rows = dosages.shape[0]
    variants, k = directions.shape
    each = k // feat
    padded = -(-each // 16) * 16
    if padded != each:
        directions = jnp.pad(directions.reshape(variants, feat, each), ((0, 0), (0, 0), (0, padded - each)))
        directions = directions.reshape(variants, feat * padded)
    rank, event_row = event_rank[None], events[None]

    linear, keep, send = products(dosages, coefficients, directions, feat)
    received = [swap(piece, "feat", 1) for piece in send]
    paired, joined = join(linear, keep[1:], received[1:])
    others = [swap(joined[q - 1], "feat", 2 * q) for q in range(1, feat // 2)]
    table = tables(rank, paired, rows)

    risk, sums, ordered_events, total = risks(paired, others, rank, event_row, table, rows)
    later = jnp.zeros_like(total)
    bit = 1
    while bit < ex:
        other = swap(total, "ex", bit)
        later = later + jnp.where((lax.axis_index("ex") & bit) == 0, other, 0.0)
        total = total + other
        bit *= 2
    tangent, later_sums = suffix_sums(keep[0], received[0], others, risk, rank, table)
    cumulative, squares, ordered_squares, hazard_message = hazards(
        later, sums, ordered_events, rank, rows
    )
    message = block_totals(tangent, risk, squares, hazard_message)
    state, bit = [], 1
    while 2 * bit < ex:
        message, *state = combine(padded, bit, [message, swap(message, "ex", bit)] + state)
        bit *= 2
    inputs = [message, swap(message, "ex", bit)] + state
    summed = prefix_sums(later_sums, ordered_squares, rank, padded)
    own = weights(bit, inputs, tangent, summed, risk, cumulative, squares)

    chips = {0: own}
    for q in reversed(range(1, feat // 2)):
        chips[q] = swap(own, "feat", 2 * q)
    parts = []
    for q in range(feat // 2):
        parts += [chips[q], swap(chips[q], "feat", 1)]

    partial_sum = gradients(parts, dosages)
    bit = 1
    while 2 * bit < ex:
        partial_sum = merge(partial_sum, swap(partial_sum, "ex", bit))
        bit *= 2
    result = finish(partial_sum, swap(partial_sum, "ex", bit), total)
    if padded != each:
        result = result.reshape(variants, feat, padded)[:, :, :each].reshape(variants, k)
    return result


def solution(mesh):
    placed = (P("ex", "feat"), P("feat"), P("feat", None), P("ex"), P("ex"))
    return jax.shard_map(
        local, mesh=mesh, in_specs=placed, out_specs=P("feat", None), check_vma=False
    )
```

```python
import functools

import jax
import jax.numpy as jnp
from jax import lax
from jax.experimental import pallas as pl
from jax.experimental.pallas import tpu as pltpu
from jax.sharding import PartitionSpec as P

F32 = jnp.float32
BF16 = jnp.bfloat16
LO = 256
NT = (((1,), (1,)), ((), ()))
BLOCK = 64
SPAN = 512
VMEM = pl.BlockSpec(memory_space=pltpu.VMEM)
HBM = pl.BlockSpec(memory_space=pltpu.HBM)
PARAMS = dict(vmem_limit_bytes=24 * 1024 * 1024)


def swap(x, axis, i):
    count = lax.axis_size(axis)
    return lax.ppermute(x, axis, [(s, s ^ i) for s in range(count)])


def split_two(x):
    high = x.astype(BF16).astype(F32)
    return high, x - high


def split_three(x):
    first, rest = split_two(x)
    second, third = split_two(rest)
    return first, second, third


def one_hot(values, count, kind=BF16):
    shape = (count, values.shape[1])
    return jnp.where(lax.broadcasted_iota(jnp.int32, shape, 0) == values, 1.0, 0.0).astype(kind)


def triangle(n, keep):
    first = lax.broadcasted_iota(jnp.int32, (n, n), 0)
    second = lax.broadcasted_iota(jnp.int32, (n, n), 1)
    return jnp.where(keep(first, second), 1.0, 0.0)


def dot_binary(a, b):
    b = b.astype(BF16)
    total = None
    for part in split_three(a):
        term = jnp.dot(part.astype(BF16), b, preferred_element_type=F32)
        total = term if total is None else total + term
    return total


def binary_dot(a, b):
    a = a.astype(BF16)
    total = None
    for part in split_three(b):
        term = jnp.dot(a, part.astype(BF16), preferred_element_type=F32)
        total = term if total is None else total + term
    return total


def product_kernel(feat, kf, chunk, directions, coefficients, dosages, *refs):
    linear, keep, send = refs[0], refs[1 : 1 + feat // 2], refs[1 + feat // 2 : 1 + feat]
    table, own_directions, own_coefficients, lhs, turned, sems = refs[1 + feat :]
    me = lax.axis_index("feat")
    width = feat * kf
    persons, variants = table.shape
    steps = persons // chunk
    small = [
        pltpu.make_async_copy(directions, own_directions, sems.at[steps]),
        pltpu.make_async_copy(coefficients, own_coefficients, sems.at[steps + 1]),
    ]
    large = [
        pltpu.make_async_copy(
            dosages.at[pl.ds(i * chunk, chunk)], table.at[pl.ds(i * chunk, chunk)], sems.at[i]
        )
        for i in range(steps)
    ]
    for copy in small + large:
        copy.start()
    for copy in small:
        copy.wait()
    turned[...] = own_directions[...].astype(F32).T.reshape(turned.shape)
    for j in range(feat):
        lhs[j * kf : (j + 1) * kf] = turned[me ^ j].astype(BF16)
    lhs[width:] = jnp.broadcast_to(own_coefficients[...].astype(F32)[None, :], (16, variants)).astype(BF16)
    for i in range(steps):
        large[i].wait()
        first = i * chunk
        result = lax.dot_general(
            lhs[...], table[first : first + chunk], NT, preferred_element_type=F32
        )
        for j in range(feat):
            (send if j % 2 else keep)[j // 2][:, first : first + chunk] = result[j * kf : (j + 1) * kf]
        for start in range(0, chunk, LO):
            row = result[width : width + 1, start : start + LO]
            group = (first + start) // LO
            linear[group : group + 1, :] = row
            send[1][group : group + 1, persons:] = row


def products(dosages, coefficients, directions, feat):
    persons, variants = dosages.shape
    k = directions.shape[1]
    kf = k // feat
    chunk = min(512, persons)
    piece = jax.ShapeDtypeStruct((kf, persons), F32)
    first = jax.ShapeDtypeStruct((kf, persons + LO), F32)
    out = pl.pallas_call(
        functools.partial(product_kernel, feat, kf, chunk),
        in_specs=[HBM, HBM, HBM],
        out_shape=[jax.ShapeDtypeStruct((kf, LO), F32)]
        + [piece] * (feat // 2 + 1)
        + [first]
        + [piece] * (feat // 2 - 2),
        out_specs=[VMEM] * (feat + 1),
        scratch_shapes=[
            pltpu.VMEM((persons, variants), BF16),
            pltpu.VMEM((variants, k), BF16),
            pltpu.VMEM((variants,), BF16),
            pltpu.VMEM((k + 16, variants), BF16),
            pltpu.VMEM((feat, kf, variants), F32),
            pltpu.SemaphoreType.DMA((persons // chunk + 2,)),
        ],
        compiler_params=pltpu.CompilerParams(**PARAMS),
        cost_estimate=pl.CostEstimate(
            flops=2 * persons * variants * k, bytes_accessed=persons * (variants * 2 + k * 4), transcendentals=0
        ),
        name="products",
    )(*[pltpu.with_memory_space_constraint(x, pltpu.HBM) for x in (directions, coefficients, dosages)])
    return out[0], out[1 : 1 + feat // 2], out[1 + feat // 2 :]


def power_of(largest):
    return jnp.ceil(jnp.log2(jnp.maximum(largest, 1e-30))) - 14.0


def to_short(values):
    return jnp.round(values).astype(jnp.int32).astype(jnp.int16)


def from_short(values):
    return values.astype(jnp.int32).astype(F32)


def join_kernel(count, *refs):
    linear, keep, received = refs[0], refs[1 : 1 + count], refs[1 + count : 1 + 2 * count]
    linear_out, outs = refs[1 + 2 * count], refs[2 + 2 * count :]
    kf, rows = keep[0].shape
    span = min(SPAN, rows)
    lane = lax.broadcasted_iota(jnp.int32, (kf, 128), 1)
    paired = linear[...] + received[0][:, rows:]
    linear_out[...] = paired
    linear_power = power_of(jnp.max(jnp.abs(paired), axis=1, keepdims=True))
    scaled = paired * jnp.exp2(-linear_power)
    whole = jnp.round(scaled)
    high, low = to_short(whole), to_short((scaled - whole) * 32768.0)
    for mine, other, out in zip(keep, received, outs):
        powers = jnp.where(lane == rows // span, linear_power, 0.0)
        for i in range(rows // span):
            at = slice(i * span, (i + 1) * span)
            total = mine[:, at] + other[:, at]
            power = power_of(jnp.max(jnp.abs(total), axis=1, keepdims=True))
            out[:, at] = to_short(total * jnp.exp2(-power))
            powers = jnp.where(lane == i, power, powers)
        out[:, rows : rows + LO] = high
        out[:, rows + LO : rows + 2 * LO] = low
        out[:, rows + 2 * LO :] = to_short(powers)


def join(linear, keep, received):
    count = len(keep)
    kf, rows = keep[0].shape
    message = jax.ShapeDtypeStruct((kf, rows + 2 * LO + 128), jnp.int16)
    out = pl.pallas_call(
        functools.partial(join_kernel, count),
        in_specs=[VMEM] * (2 * count + 1),
        out_shape=[jax.ShapeDtypeStruct(linear.shape, F32)] + [message] * count,
        out_specs=[VMEM] * (count + 1),
        compiler_params=pltpu.CompilerParams(**PARAMS),
        name="join",
    )(linear, *keep, *received)
    return out[0], out[1:]


def table_kernel(rows, rank, waited, table):
    chunk = min(512, rows)
    lane = lax.broadcasted_iota(jnp.int32, (chunk, 128), 1)
    for start in range(0, rows, chunk):
        at = slice(start, start + chunk)
        inner = lax.rem(rank[:, at], LO)
        column = jnp.broadcast_to(inner.astype(F32), (128, chunk)).T.astype(jnp.int32)
        for first in range(0, LO, 128):
            table[at, first : first + 128] = jnp.where(column == lane + first, 1.0, 0.0).astype(BF16)


def tables(rank, waited, rows):
    return pl.pallas_call(
        functools.partial(table_kernel, rows),
        in_specs=[VMEM, pl.BlockSpec(memory_space=pl.ANY)],
        out_shape=jax.ShapeDtypeStruct((rows, LO), BF16),
        out_specs=VMEM,
        compiler_params=pltpu.CompilerParams(**PARAMS),
        cost_estimate=pl.CostEstimate(flops=rows * LO * 8, bytes_accessed=rows * LO * 2, transcendentals=0),
        name="tables",
    )(rank, waited)


def risk_kernel(rows, parts, linear, *refs):
    messages, (rank, events, table) = refs[:parts], refs[parts : parts + 3]
    risk_out, sums_out, events_out, message = refs[parts + 3 :]
    groups = rows // LO
    span = min(SPAN, rows)
    total = linear[...]
    for part in messages:
        power = from_short(part[:, rows + 2 * LO :])[:, rows // span : rows // span + 1]
        high, low = from_short(part[:, rows : rows + LO]), from_short(part[:, rows + LO : rows + 2 * LO])
        total = total + (high + low * (1.0 / 32768.0)) * jnp.exp2(power)
    risk = jnp.exp(total)
    for g in range(groups):
        risk_out[:, g * LO : (g + 1) * LO] = risk[g : g + 1]
    mask = one_hot(lax.rem(rank[...], rows) // LO, groups, F32)
    pieces = [mask * part for part in split_three(risk_out[...])] + [mask * events[...].astype(F32)]
    lhs = jnp.concatenate(pieces, axis=0).astype(BF16)
    sorted_all = jnp.dot(lhs, table[...], preferred_element_type=F32)
    ordered = sorted_all[:groups] + sorted_all[groups : 2 * groups] + sorted_all[2 * groups : 3 * groups]
    happened = sorted_all[3 * groups :]
    inside = dot_binary(ordered, triangle(LO, lambda a, b: a >= b))
    totals = jnp.broadcast_to(inside[:, :1], inside.shape)
    carried = binary_dot(triangle(groups, lambda a, b: a < b), totals)
    sums_out[...] = inside + carried
    events_out[...] = happened
    everything = jnp.sum(totals, axis=0, keepdims=True)[:, :128]
    count = jnp.sum(dot_binary(happened, jnp.ones((LO, 128), F32)), axis=0, keepdims=True)
    message[...] = jnp.concatenate([everything, count, jnp.zeros((6, 128), F32)], axis=0)


def risks(linear, messages, rank, events, table, rows):
    groups = rows // LO
    return pl.pallas_call(
        functools.partial(risk_kernel, rows, len(messages)),
        in_specs=[VMEM] * (len(messages) + 4),
        out_shape=[
            jax.ShapeDtypeStruct((1, rows), F32),
            jax.ShapeDtypeStruct((groups, LO), F32),
            jax.ShapeDtypeStruct((groups, LO), F32),
            jax.ShapeDtypeStruct((8, 128), F32),
        ],
        out_specs=[VMEM] * 4,
        compiler_params=pltpu.CompilerParams(**PARAMS),
        cost_estimate=pl.CostEstimate(flops=rows * LO * 128, bytes_accessed=rows * 64, transcendentals=rows),
        name="risks",
    )(linear, *messages, rank, events, table)


def share_kernel(later, sums, events, plain, ordered, hazard_out, squares, message):
    kf = plain.shape[0]
    groups = sums.shape[0]
    risk_sum = sums[...] + later[0:1, 0:1]
    hazard = events[...] / risk_sum
    square = events[...] / (risk_sum * risk_sum)
    hazard_out[...] = hazard
    squares[...] = square
    scaled = jnp.zeros((kf, LO), F32)
    for g in range(groups):
        scaled = scaled + ordered[g * kf : (g + 1) * kf] * square[g : g + 1]
    message[:kf] = plain[...]
    message[kf : 2 * kf] = sum(scaled[:, start : start + 128] for start in range(0, LO, 128))
    totals = [jnp.sum(jnp.sum(v, axis=0, keepdims=True), axis=1, keepdims=True) for v in (hazard, square)]
    rows = [jnp.broadcast_to(v, (1, 128)) for v in totals]
    message[2 * kf :] = jnp.concatenate(rows + [jnp.zeros((6, 128), F32)], axis=0)


def shares(later, sums, events, plain, ordered):
    flat = jax.ShapeDtypeStruct(sums.shape, F32)
    return pl.pallas_call(
        share_kernel,
        in_specs=[VMEM] * 5,
        out_shape=[flat, flat, jax.ShapeDtypeStruct((2 * plain.shape[0] + 8, 128), F32)],
        out_specs=[VMEM] * 3,
        compiler_params=pltpu.CompilerParams(**PARAMS),
        name="shares",
    )(later, sums, events, plain, ordered)


def hazard_kernel(rows, hazard, square, rank, cumulative, squares):
    groups = rows // LO
    inside = dot_binary(
        jnp.concatenate([hazard[...], square[...]], axis=0), triangle(LO, lambda a, b: a <= b)
    )
    totals = jnp.broadcast_to(inside[:, LO - 1 :], (2 * groups, 128))
    place = lax.rem(rank[...], rows)
    mask = one_hot(place // LO, groups, F32)
    placed = dot_binary(inside, one_hot(lax.rem(place, LO), LO))
    before = triangle(groups, lambda a, b: a > b)
    for first, out in ((0, cumulative), (groups, squares)):
        carried = binary_dot(before, totals[first : first + groups])[:, :1]
        out[...] = jnp.sum(mask * (placed[first : first + groups] + carried), axis=0, keepdims=True)


def hazards(hazard, square, rank, rows):
    row = jax.ShapeDtypeStruct((1, rows), F32)
    return pl.pallas_call(
        functools.partial(hazard_kernel, rows),
        in_specs=[VMEM] * 3,
        out_shape=[row, row],
        out_specs=[VMEM] * 2,
        compiler_params=pltpu.CompilerParams(**PARAMS),
        cost_estimate=pl.CostEstimate(flops=rows * LO * 200, bytes_accessed=rows * 64, transcendentals=0),
        name="hazards",
    )(hazard, square, rank)


def suffix_kernel(parts, own, other, *refs):
    messages, (risk, rank, table) = refs[:parts], refs[parts : parts + 3]
    tangent_out, sums, plain, lhs = refs[parts + 3 :]
    kf, rows = own.shape
    folded = jnp.zeros((kf, 128), F32)
    groups = rows // LO
    span = min(SPAN, rows)
    powers = [jnp.exp2(from_short(part[:, rows + 2 * LO :])) for part in messages]
    for i in range(rows // span):
        at = slice(i * span, (i + 1) * span)
        tangent = own[:, at] + other[:, at]
        for part, power in zip(messages, powers):
            tangent = tangent + from_short(part[:, at]) * power[:, i : i + 1]
        tangent_out[:, at] = tangent
        weighted = tangent * risk[:, at]
        folded = folded + sum(weighted[:, j : j + 128] for j in range(0, span, 128))
        high, low = split_two(weighted)
        high, low = high.astype(BF16), low.astype(BF16)
        group = jnp.broadcast_to(lax.rem(rank[:, at], rows) // LO, (kf, span))
        for g in range(groups):
            mask = jnp.where(group == g, 1.0, 0.0).astype(BF16)
            lhs[2 * g * kf : (2 * g + 1) * kf, at] = high * mask
            lhs[(2 * g + 1) * kf : (2 * g + 2) * kf, at] = low * mask
    plain[...] = folded
    ordered = jnp.dot(lhs[...], table[...], preferred_element_type=F32)
    ordered = jnp.concatenate(
        [
            ordered[2 * g * kf : (2 * g + 1) * kf] + ordered[(2 * g + 1) * kf : (2 * g + 2) * kf]
            for g in range(groups)
        ],
        axis=0,
    )
    inside = dot_binary(ordered, triangle(LO, lambda a, b: a >= b))
    carried = jnp.zeros((kf, 1), F32)
    for g in reversed(range(groups)):
        rows_of = slice(g * kf, (g + 1) * kf)
        sums[rows_of] = inside[rows_of] + carried
        carried = carried + inside[rows_of, :1]


def suffix_sums(own, other, messages, risk, rank, table):
    kf, rows = own.shape
    groups = rows // LO
    return pl.pallas_call(
        functools.partial(suffix_kernel, len(messages)),
        in_specs=[VMEM] * (len(messages) + 5),
        out_shape=[
            jax.ShapeDtypeStruct((kf, rows), F32),
            jax.ShapeDtypeStruct((groups * kf, LO), F32),
            jax.ShapeDtypeStruct((kf, 128), F32),
        ],
        out_specs=[VMEM] * 3,
        scratch_shapes=[pltpu.VMEM((groups * 2 * kf, rows), BF16)],
        compiler_params=pltpu.CompilerParams(**PARAMS),
        cost_estimate=pl.CostEstimate(
            flops=2 * rows * LO * groups * 2 * kf, bytes_accessed=rows * kf * 24, transcendentals=0
        ),
        name="suffix_sums",
    )(own, other, *messages, risk, rank, table)


def prefix_kernel(sums, squares, rank, out):
    kf, rows = out.shape
    groups = squares.shape[0]
    chunk = min(512, rows)
    hazard = [sums[g * kf : (g + 1) * kf] * squares[g : g + 1, :] for g in range(groups)]
    inside = dot_binary(jnp.concatenate(hazard, axis=0), triangle(LO, lambda a, b: a <= b))
    carried = jnp.zeros((kf, 1), F32)
    summed = [None] * groups
    for g in range(groups):
        rows_of = slice(g * kf, (g + 1) * kf)
        summed[g] = inside[rows_of] + carried
        carried = carried + inside[rows_of, LO - 1 :]
    high, low = split_two(jnp.concatenate(summed, axis=0))
    high, low = high.astype(BF16), low.astype(BF16)
    for start in range(0, rows, chunk):
        at = slice(start, start + chunk)
        place = lax.rem(rank[:, at], rows)
        group = place // LO
        spread = one_hot(lax.rem(place, LO), LO)
        placed = jnp.dot(high, spread, preferred_element_type=F32) + jnp.dot(
            low, spread, preferred_element_type=F32
        )
        picked = jnp.zeros((kf, chunk), F32)
        for g in range(groups):
            picked = picked + jnp.where(group == g, placed[g * kf : (g + 1) * kf], 0.0)
        out[:, at] = picked


def prefix_sums(sums, squares, rank, kf):
    rows = rank.shape[1]
    return pl.pallas_call(
        prefix_kernel,
        in_specs=[VMEM] * 3,
        out_shape=jax.ShapeDtypeStruct((kf, rows), F32),
        out_specs=VMEM,
        compiler_params=pltpu.CompilerParams(**PARAMS),
        cost_estimate=pl.CostEstimate(
            flops=4 * rows * LO * (rows // LO) * kf, bytes_accessed=rows * kf * 24, transcendentals=0
        ),
        name="prefix_sums",
    )(sums, squares, rank)


def merged(kf, bit, mine, other, state):
    later_other = (lax.axis_index("ex") & bit) == 0
    plain, scaled, rest = mine[:kf], mine[kf : 2 * kf], mine[2 * kf :]
    other_plain, other_scaled, other_rest = other[:kf], other[kf : 2 * kf], other[2 * kf :]
    square, other_square = rest[1:2], other_rest[1:2]
    crossed = jnp.where(later_other, square * other_plain, other_square * plain)
    total = jnp.concatenate([plain + other_plain, scaled + other_scaled + crossed, rest + other_rest], axis=0)
    if state is None:
        state = jnp.zeros_like(mine)
    later, before, before_rest = state[:kf], state[kf : 2 * kf], state[2 * kf :]
    state = jnp.concatenate(
        [
            later + jnp.where(later_other, other_plain, 0.0),
            before + jnp.where(later_other, before_rest[1:2] * other_plain, other_scaled + other_square * plain),
            before_rest + jnp.where(later_other, 0.0, other_rest),
        ],
        axis=0,
    )
    return total, state


def combine_kernel(kf, bit, count, *refs):
    inputs, (total, state) = [ref[...] for ref in refs[:count]], refs[count + 1 :]
    total[...], state[...] = merged(kf, bit, inputs[0], inputs[1], inputs[2] if count > 2 else None)


def combine(kf, bit, inputs, waited):
    shape = jax.ShapeDtypeStruct(inputs[0].shape, F32)
    return pl.pallas_call(
        functools.partial(combine_kernel, kf, bit, len(inputs)),
        in_specs=[VMEM] * len(inputs) + [pl.BlockSpec(memory_space=pl.ANY)],
        out_shape=[shape, shape],
        out_specs=[VMEM] * 2,
        compiler_params=pltpu.CompilerParams(**PARAMS),
        name="combine",
    )(*inputs, waited)


def weight_kernel(kf, bit, count, *refs):
    inputs = [ref[...] for ref in refs[:count]]
    tangent, local, risk, cumulative, squares, weighted = refs[count:]
    _, state = merged(kf, bit, inputs[0], inputs[1], inputs[2] if count > 2 else None)
    later = jnp.sum(state[:kf], axis=1, keepdims=True)
    before = jnp.sum(state[kf : 2 * kf], axis=1, keepdims=True)
    hazard_before = state[2 * kf : 2 * kf + 1, :1]
    value = tangent[...] * (cumulative[...] + hazard_before) - (local[...] + squares[...] * later + before)
    weighted[...] = (risk[...] * value).astype(BF16)


def weights(bit, inputs, tangent, local, risk, cumulative, squares):
    return pl.pallas_call(
        functools.partial(weight_kernel, tangent.shape[0], bit, len(inputs)),
        in_specs=[VMEM] * (len(inputs) + 5),
        out_shape=jax.ShapeDtypeStruct(tangent.shape, BF16),
        out_specs=VMEM,
        compiler_params=pltpu.CompilerParams(**PARAMS),
        name="weights",
    )(*inputs, tangent, local, risk, cumulative, squares)


def encode(values, message):
    height = values.shape[0]
    block = min(BLOCK, height)
    powers = []
    for start in range(0, height, block):
        part = values[start : start + block]
        largest = jnp.max(jnp.abs(part), axis=0, keepdims=True)
        power = power_of(largest)
        message[start : start + block] = to_short(part * jnp.exp2(-power))
        powers.append(power)
    powers.append(jnp.zeros((message.shape[0] - height - len(powers), values.shape[1]), F32))
    message[height:] = to_short(jnp.concatenate(powers, axis=0))


def decode(message, height):
    block = min(BLOCK, height)
    powers = from_short(message[height:])
    parts = []
    for i in range(height // block):
        part = from_short(message[i * block : (i + 1) * block])
        parts.append(part * jnp.exp2(powers[i : i + 1]))
    return jnp.concatenate(parts, axis=0)


def gradient_kernel(feat, kf, *refs):
    parts, dosages, out, weighted = refs[:feat], refs[feat], refs[feat + 1], refs[feat + 2]
    me = lax.axis_index("feat")
    for i in range(feat):
        weighted[pl.ds(pl.multiple_of((me ^ i) * kf, kf), kf), :] = parts[i][...]
    total = jnp.dot(weighted[...], dosages[...], preferred_element_type=F32)
    encode(total.T, out)


def gradients(parts, dosages):
    feat = len(parts)
    kf, persons = parts[0].shape
    k, variants = kf * feat, dosages.shape[1]
    return pl.pallas_call(
        functools.partial(gradient_kernel, feat, kf),
        in_specs=[VMEM] * (feat + 1),
        out_shape=jax.ShapeDtypeStruct((variants + 16, k), jnp.int16),
        out_specs=VMEM,
        scratch_shapes=[pltpu.VMEM((k, persons), BF16)],
        compiler_params=pltpu.CompilerParams(**PARAMS),
        cost_estimate=pl.CostEstimate(
            flops=2 * persons * variants * k, bytes_accessed=persons * (variants * 2 + k * 2), transcendentals=0
        ),
        name="gradients",
    )(*parts, dosages)


def merge_kernel(mine, other, out):
    height = mine.shape[0] - 16
    encode(decode(mine, height) + decode(other, height), out)


def merge(mine, other):
    return pl.pallas_call(
        merge_kernel,
        in_specs=[VMEM] * 2,
        out_shape=jax.ShapeDtypeStruct(mine.shape, jnp.int16),
        out_specs=VMEM,
        compiler_params=pltpu.CompilerParams(**PARAMS),
        name="merge",
    )(mine, other)


def finish_kernel(steps, mine, other, count, out, total, sems):
    height = mine.shape[0] - 16
    step = height // steps
    block = min(BLOCK, step)
    scale = count[1:2, 0:1]
    powers = [from_short(message[height:]) for message in (mine, other)]
    copies = []
    for i in range(steps):
        for start in range(i * step, (i + 1) * step, block):
            at, j = slice(start, start + block), start // block
            terms = [from_short(m[at]) * jnp.exp2(p[j : j + 1]) for m, p in zip((mine, other), powers)]
            total[at] = (terms[0] + terms[1]) / scale
        at = pl.ds(i * step, step)
        copies.append(pltpu.make_async_copy(total.at[at], out.at[at], sems.at[i]))
        copies[i].start()
    for copy in copies:
        copy.wait()


def finish(mine, other, count):
    height, k = mine.shape[0] - 16, mine.shape[1]
    steps = max(1, min(4, height // BLOCK))
    return pl.pallas_call(
        functools.partial(finish_kernel, steps),
        in_specs=[VMEM] * 3,
        out_shape=jax.ShapeDtypeStruct((height, k), F32),
        out_specs=HBM,
        scratch_shapes=[pltpu.VMEM((height, k), F32), pltpu.SemaphoreType.DMA((steps,))],
        compiler_params=pltpu.CompilerParams(**PARAMS),
        name="finish",
    )(mine, other, count)


def local(dosages, coefficients, directions, event_rank, events):
    feat, ex = lax.axis_size("feat"), lax.axis_size("ex")
    rows = dosages.shape[0]
    variants, k = directions.shape
    each = k // feat
    padded = -(-each // 16) * 16
    if padded != each:
        directions = jnp.pad(directions.reshape(variants, feat, each), ((0, 0), (0, 0), (0, padded - each)))
        directions = directions.reshape(variants, feat * padded)
    rank, event_row = event_rank[None], events[None]

    linear, keep, send = products(dosages, coefficients, directions, feat)
    received = [swap(piece, "feat", 1) for piece in send]
    paired, joined = join(linear, keep[1:], received[1:])
    others = [swap(joined[q - 1], "feat", 2 * q) for q in reversed(range(1, feat // 2))]
    table = tables(rank, paired, rows)

    risk, sums, ordered_events, total = risks(paired, others, rank, event_row, table, rows)
    later = jnp.zeros_like(total)
    bit = 1
    while bit < ex:
        other = swap(total, "ex", bit)
        later = later + jnp.where((lax.axis_index("ex") & bit) == 0, other, 0.0)
        total = total + other
        bit *= 2
    tangent, later_sums, plain = suffix_sums(keep[0], received[0], others, risk, rank, table)
    hazard, ordered_squares, message = shares(later, sums, ordered_events, plain, later_sums)
    cumulative, squares = hazards(hazard, ordered_squares, rank, rows)
    state, bit = [], 1
    while 2 * bit < ex:
        message, *state = combine(padded, bit, [message, swap(message, "ex", bit)] + state, cumulative)
        bit *= 2
    inputs = [message, swap(message, "ex", bit)] + state
    summed = prefix_sums(later_sums, ordered_squares, rank, padded)
    own = weights(bit, inputs, tangent, summed, risk, cumulative, squares)

    chips = {0: own}
    for q in reversed(range(1, feat // 2)):
        chips[q] = swap(own, "feat", 2 * q)
    parts = []
    for q in range(feat // 2):
        parts += [chips[q], swap(chips[q], "feat", 1)]

    partial_sum = gradients(parts, dosages)
    bit = 1
    while 2 * bit < ex:
        partial_sum = merge(partial_sum, swap(partial_sum, "ex", bit))
        bit *= 2
    result = finish(partial_sum, swap(partial_sum, "ex", bit), total)
    if padded != each:
        result = result.reshape(variants, feat, padded)[:, :, :each].reshape(variants, k)
    return result


def solution(mesh):
    placed = (P("ex", "feat"), P("feat"), P("feat", None), P("ex"), P("ex"))
    return jax.shard_map(
        local, mesh=mesh, in_specs=placed, out_specs=P("feat", None), check_vma=False
    )
```

```python
import functools

import jax
import jax.numpy as jnp
from jax import lax
from jax.experimental import pallas as pl
from jax.experimental.pallas import tpu as pltpu
from jax.sharding import PartitionSpec as P

F32 = jnp.float32
BF16 = jnp.bfloat16
LO = 256
NT = (((1,), (1,)), ((), ()))
BLOCK = 64
SPAN = 512
VMEM = pl.BlockSpec(memory_space=pltpu.VMEM)
HBM = pl.BlockSpec(memory_space=pltpu.HBM)
PARAMS = dict(vmem_limit_bytes=24 * 1024 * 1024)


def swap(x, axis, i):
    count = lax.axis_size(axis)
    return lax.ppermute(x, axis, [(s, s ^ i) for s in range(count)])


def split_two(x):
    high = x.astype(BF16).astype(F32)
    return high, x - high


def split_three(x):
    first, rest = split_two(x)
    second, third = split_two(rest)
    return first, second, third


def one_hot(values, count, kind=BF16):
    shape = (count, values.shape[1])
    return jnp.where(lax.broadcasted_iota(jnp.int32, shape, 0) == values, 1.0, 0.0).astype(kind)


def triangle(n, keep):
    first = lax.broadcasted_iota(jnp.int32, (n, n), 0)
    second = lax.broadcasted_iota(jnp.int32, (n, n), 1)
    return jnp.where(keep(first, second), 1.0, 0.0)


def stacked(parts):
    return jnp.concatenate(parts, axis=0).astype(BF16)


def unstacked(values, count):
    height = values.shape[0] // count
    return sum(values[i * height : (i + 1) * height] for i in range(count))


def dot_binary(a, b):
    parts = jnp.dot(stacked(split_three(a)), b.astype(BF16), preferred_element_type=F32)
    return unstacked(parts, 3)


def binary_dot(a, b):
    a = a.astype(BF16)
    total = None
    for part in split_three(b):
        term = jnp.dot(a, part.astype(BF16), preferred_element_type=F32)
        total = term if total is None else total + term
    return total


def product_kernel(feat, kf, chunk, directions, coefficients, dosages, *refs):
    linear, keep, send = refs[0], refs[1 : 1 + feat // 2], refs[1 + feat // 2 : 1 + feat]
    table, own_directions, own_coefficients, lhs, turned, sems = refs[1 + feat :]
    me = lax.axis_index("feat")
    width = feat * kf
    persons, variants = table.shape
    steps = persons // chunk
    small = [
        pltpu.make_async_copy(directions, own_directions, sems.at[steps]),
        pltpu.make_async_copy(coefficients, own_coefficients, sems.at[steps + 1]),
    ]
    large = [
        pltpu.make_async_copy(
            dosages.at[pl.ds(i * chunk, chunk)], table.at[pl.ds(i * chunk, chunk)], sems.at[i]
        )
        for i in range(steps)
    ]
    for copy in small + large:
        copy.start()
    for copy in small:
        copy.wait()
    turned[...] = own_directions[...].astype(F32).T.reshape(turned.shape)
    for j in range(feat):
        lhs[j * kf : (j + 1) * kf] = turned[me ^ j].astype(BF16)
    lhs[width:] = jnp.broadcast_to(own_coefficients[...].astype(F32)[None, :], (16, variants)).astype(BF16)
    for i in range(steps):
        large[i].wait()
        first = i * chunk
        result = lax.dot_general(
            lhs[...], table[first : first + chunk], NT, preferred_element_type=F32
        )
        for j in range(feat):
            (send if j % 2 else keep)[j // 2][:, first : first + chunk] = result[j * kf : (j + 1) * kf]
        for start in range(0, chunk, LO):
            row = result[width : width + 1, start : start + LO]
            group = (first + start) // LO
            linear[group : group + 1, :] = row
            send[-1][group : group + 1, persons:] = row


def products(dosages, coefficients, directions, feat):
    persons, variants = dosages.shape
    k = directions.shape[1]
    kf = k // feat
    chunk = min(512, persons)
    piece = jax.ShapeDtypeStruct((kf, persons), F32)
    first = jax.ShapeDtypeStruct((kf, persons + LO), F32)
    out = pl.pallas_call(
        functools.partial(product_kernel, feat, kf, chunk),
        in_specs=[HBM, HBM, HBM],
        out_shape=[jax.ShapeDtypeStruct((kf, LO), F32)]
        + [piece] * (feat - 1)
        + [first],
        out_specs=[VMEM] * (feat + 1),
        scratch_shapes=[
            pltpu.VMEM((persons, variants), BF16),
            pltpu.VMEM((variants, k), BF16),
            pltpu.VMEM((variants,), BF16),
            pltpu.VMEM((k + 16, variants), BF16),
            pltpu.VMEM((feat, kf, variants), F32),
            pltpu.SemaphoreType.DMA((persons // chunk + 2,)),
        ],
        compiler_params=pltpu.CompilerParams(**PARAMS),
        cost_estimate=pl.CostEstimate(
            flops=2 * persons * variants * k, bytes_accessed=persons * (variants * 2 + k * 4), transcendentals=0
        ),
        name="products",
    )(*[pltpu.with_memory_space_constraint(x, pltpu.HBM) for x in (directions, coefficients, dosages)])
    return out[0], out[1 : 1 + feat // 2], out[1 + feat // 2 :]


def power_of(largest):
    return jnp.ceil(jnp.log2(jnp.maximum(largest, 1e-30))) - 14.0


def to_short(values):
    return jnp.round(values).astype(jnp.int32).astype(jnp.int16)


def from_short(values):
    return values.astype(jnp.int32).astype(F32)


def join_kernel(linear, *refs):
    mine, other = refs[:2]
    out = refs[-1]
    kf, rows = mine.shape
    span = min(SPAN, rows)
    lane = lax.broadcasted_iota(jnp.int32, (kf, 128), 1)
    paired = linear[...]
    if len(refs) > 3:
        paired = paired + other[:, rows:]
        refs[2][...] = paired
    linear_power = power_of(jnp.max(jnp.abs(paired), axis=1, keepdims=True))
    scaled = paired * jnp.exp2(-linear_power)
    whole = jnp.round(scaled)
    powers = jnp.where(lane == rows // span, linear_power, 0.0)
    for i in range(rows // span):
        at = slice(i * span, (i + 1) * span)
        total = mine[:, at] + other[:, at]
        power = power_of(jnp.max(jnp.abs(total), axis=1, keepdims=True))
        out[:, at] = to_short(total * jnp.exp2(-power))
        powers = jnp.where(lane == i, power, powers)
    out[:, rows : rows + LO] = to_short(whole)
    out[:, rows + LO : rows + 2 * LO] = to_short((scaled - whole) * 32768.0)
    out[:, rows + 2 * LO :] = to_short(powers)


def join(linear, keep, received):
    kf, rows = keep.shape
    message = jax.ShapeDtypeStruct((kf, rows + 2 * LO + 128), jnp.int16)
    shapes = [message]
    if received.shape[1] > rows:
        shapes = [jax.ShapeDtypeStruct(linear.shape, F32), message]
    return pl.pallas_call(
        join_kernel,
        in_specs=[VMEM] * 3,
        out_shape=shapes,
        out_specs=[VMEM] * len(shapes),
        compiler_params=pltpu.CompilerParams(**PARAMS),
        name="join",
    )(linear, keep, received)


def table_kernel(rows, rank, waited, table):
    chunk = min(512, rows)
    lane = lax.broadcasted_iota(jnp.int32, (chunk, 128), 1)
    for start in range(0, rows, chunk):
        at = slice(start, start + chunk)
        inner = lax.rem(rank[:, at], LO)
        column = jnp.broadcast_to(inner.astype(F32), (128, chunk)).T.astype(jnp.int32)
        for first in range(0, LO, 128):
            table[at, first : first + 128] = jnp.where(column == lane + first, 1.0, 0.0).astype(BF16)


def tables(rank, waited, rows):
    return pl.pallas_call(
        functools.partial(table_kernel, rows),
        in_specs=[VMEM, pl.BlockSpec(memory_space=pl.ANY)],
        out_shape=jax.ShapeDtypeStruct((rows, LO), BF16),
        out_specs=VMEM,
        compiler_params=pltpu.CompilerParams(**PARAMS),
        cost_estimate=pl.CostEstimate(flops=rows * LO * 8, bytes_accessed=rows * LO * 2, transcendentals=0),
        name="tables",
    )(rank, waited)


def risk_kernel(rows, parts, linear, *refs):
    messages, (rank, events, table) = refs[:parts], refs[parts : parts + 3]
    risk_out, sums_out, events_out, message = refs[parts + 3 :]
    groups = rows // LO
    span = min(SPAN, rows)
    total = linear[...]
    for part in messages:
        power = from_short(part[:, rows + 2 * LO :])[:, rows // span : rows // span + 1]
        high, low = from_short(part[:, rows : rows + LO]), from_short(part[:, rows + LO : rows + 2 * LO])
        total = total + (high + low * (1.0 / 32768.0)) * jnp.exp2(power)
    risk = jnp.exp(total)
    for g in range(groups):
        risk_out[:, g * LO : (g + 1) * LO] = risk[g : g + 1]
    mask = one_hot(lax.rem(rank[...], rows) // LO, groups, F32)
    pieces = [mask * part for part in split_three(risk_out[...])] + [mask * events[...].astype(F32)]
    lhs = jnp.concatenate(pieces, axis=0).astype(BF16)
    sorted_all = jnp.dot(lhs, table[...], preferred_element_type=F32)
    ordered = sorted_all[:groups] + sorted_all[groups : 2 * groups] + sorted_all[2 * groups : 3 * groups]
    happened = sorted_all[3 * groups :]
    inside = dot_binary(ordered, triangle(LO, lambda a, b: a >= b))
    totals = jnp.broadcast_to(inside[:, :1], inside.shape)
    carried = binary_dot(triangle(groups, lambda a, b: a < b), totals)
    sums_out[...] = inside + carried
    events_out[...] = happened
    everything = jnp.sum(totals, axis=0, keepdims=True)[:, :128]
    count = jnp.sum(dot_binary(happened, jnp.ones((LO, 128), F32)), axis=0, keepdims=True)
    message[...] = jnp.concatenate([everything, count, jnp.zeros((6, 128), F32)], axis=0)


def risks(linear, messages, rank, events, table, rows):
    groups = rows // LO
    return pl.pallas_call(
        functools.partial(risk_kernel, rows, len(messages)),
        in_specs=[VMEM] * (len(messages) + 4),
        out_shape=[
            jax.ShapeDtypeStruct((1, rows), F32),
            jax.ShapeDtypeStruct((groups, LO), F32),
            jax.ShapeDtypeStruct((groups, LO), F32),
            jax.ShapeDtypeStruct((8, 128), F32),
        ],
        out_specs=[VMEM] * 4,
        compiler_params=pltpu.CompilerParams(**PARAMS),
        cost_estimate=pl.CostEstimate(flops=rows * LO * 128, bytes_accessed=rows * 64, transcendentals=rows),
        name="risks",
    )(linear, *messages, rank, events, table)


def share_kernel(ex, *refs):
    messages, (sums, events, plain, ordered) = refs[:ex], refs[ex : ex + 4]
    hazard_out, squares, message, count_out = refs[ex + 4 :]
    kf = plain.shape[0]
    groups = sums.shape[0]
    me = lax.axis_index("ex")
    later = jnp.zeros((1, 1), F32)
    count = messages[0][1:2]
    for i in range(1, ex):
        later = later + jnp.where((me ^ i) > me, messages[i][0:1, 0:1], 0.0)
        count = count + messages[i][1:2]
    count_out[...] = jnp.broadcast_to(count, count_out.shape)
    risk_sum = sums[...] + later
    hazard = events[...] / risk_sum
    square = events[...] / (risk_sum * risk_sum)
    hazard_out[...] = hazard
    squares[...] = square
    scaled = jnp.zeros((kf, LO), F32)
    for g in range(groups):
        scaled = scaled + ordered[g * kf : (g + 1) * kf] * square[g : g + 1]
    message[:kf] = plain[...]
    message[kf : 2 * kf] = sum(scaled[:, start : start + 128] for start in range(0, LO, 128))
    totals = [jnp.sum(jnp.sum(v, axis=0, keepdims=True), axis=1, keepdims=True) for v in (hazard, square)]
    rows = [jnp.broadcast_to(v, (1, 128)) for v in totals]
    message[2 * kf :] = jnp.concatenate(rows + [jnp.zeros((6, 128), F32)], axis=0)


def shares(messages, sums, events, plain, ordered):
    flat = jax.ShapeDtypeStruct(sums.shape, F32)
    return pl.pallas_call(
        functools.partial(share_kernel, len(messages)),
        in_specs=[VMEM] * (len(messages) + 4),
        out_shape=[
            flat,
            flat,
            jax.ShapeDtypeStruct((2 * plain.shape[0] + 8, 128), F32),
            jax.ShapeDtypeStruct((8, 128), F32),
        ],
        out_specs=[VMEM] * 4,
        compiler_params=pltpu.CompilerParams(**PARAMS),
        name="shares",
    )(*messages, sums, events, plain, ordered)


def hazard_kernel(rows, hazard, square, rank, cumulative, squares):
    groups = rows // LO
    inside = dot_binary(
        jnp.concatenate([hazard[...], square[...]], axis=0), triangle(LO, lambda a, b: a <= b)
    )
    totals = jnp.broadcast_to(inside[:, LO - 1 :], (2 * groups, 128))
    place = lax.rem(rank[...], rows)
    mask = one_hot(place // LO, groups, F32)
    placed = dot_binary(inside, one_hot(lax.rem(place, LO), LO))
    before = triangle(groups, lambda a, b: a > b)
    for first, out in ((0, cumulative), (groups, squares)):
        carried = binary_dot(before, totals[first : first + groups])[:, :1]
        out[...] = jnp.sum(mask * (placed[first : first + groups] + carried), axis=0, keepdims=True)


def hazards(hazard, square, rank, rows):
    row = jax.ShapeDtypeStruct((1, rows), F32)
    return pl.pallas_call(
        functools.partial(hazard_kernel, rows),
        in_specs=[VMEM] * 3,
        out_shape=[row, row],
        out_specs=[VMEM] * 2,
        compiler_params=pltpu.CompilerParams(**PARAMS),
        cost_estimate=pl.CostEstimate(flops=rows * LO * 200, bytes_accessed=rows * 64, transcendentals=0),
        name="hazards",
    )(hazard, square, rank)


def suffix_kernel(parts, own, other, *refs):
    messages, (risk, rank, table) = refs[:parts], refs[parts : parts + 3]
    tangent_out, sums, plain, lhs = refs[parts + 3 :]
    kf, rows = own.shape
    folded = jnp.zeros((kf, 128), F32)
    groups = rows // LO
    span = min(SPAN, rows)
    powers = [jnp.exp2(from_short(part[:, rows + 2 * LO :])) for part in messages]
    for i in range(rows // span):
        at = slice(i * span, (i + 1) * span)
        tangent = own[:, at] + other[:, at]
        for part, power in zip(messages, powers):
            tangent = tangent + from_short(part[:, at]) * power[:, i : i + 1]
        tangent_out[:, at] = tangent
        weighted = tangent * risk[:, at]
        folded = folded + sum(weighted[:, j : j + 128] for j in range(0, span, 128))
        high, low = split_two(weighted)
        high, low = high.astype(BF16), low.astype(BF16)
        group = jnp.broadcast_to(lax.rem(rank[:, at], rows) // LO, (kf, span))
        for g in range(groups):
            mask = jnp.where(group == g, 1.0, 0.0).astype(BF16)
            lhs[2 * g * kf : (2 * g + 1) * kf, at] = high * mask
            lhs[(2 * g + 1) * kf : (2 * g + 2) * kf, at] = low * mask
    plain[...] = folded
    ordered = jnp.dot(lhs[...], table[...], preferred_element_type=F32)
    ordered = jnp.concatenate(
        [
            ordered[2 * g * kf : (2 * g + 1) * kf] + ordered[(2 * g + 1) * kf : (2 * g + 2) * kf]
            for g in range(groups)
        ],
        axis=0,
    )
    inside = dot_binary(ordered, triangle(LO, lambda a, b: a >= b))
    carried = jnp.zeros((kf, 1), F32)
    for g in reversed(range(groups)):
        rows_of = slice(g * kf, (g + 1) * kf)
        sums[rows_of] = inside[rows_of] + carried
        carried = carried + inside[rows_of, :1]


def suffix_sums(own, other, messages, risk, rank, table):
    kf, rows = own.shape
    groups = rows // LO
    return pl.pallas_call(
        functools.partial(suffix_kernel, len(messages)),
        in_specs=[VMEM] * (len(messages) + 5),
        out_shape=[
            jax.ShapeDtypeStruct((kf, rows), F32),
            jax.ShapeDtypeStruct((groups * kf, LO), F32),
            jax.ShapeDtypeStruct((kf, 128), F32),
        ],
        out_specs=[VMEM] * 3,
        scratch_shapes=[pltpu.VMEM((groups * 2 * kf, rows), BF16)],
        compiler_params=pltpu.CompilerParams(**PARAMS),
        cost_estimate=pl.CostEstimate(
            flops=2 * rows * LO * groups * 2 * kf, bytes_accessed=rows * kf * 24, transcendentals=0
        ),
        name="suffix_sums",
    )(own, other, *messages, risk, rank, table)


def prefix_kernel(sums, squares, rank, out):
    kf, rows = out.shape
    groups = squares.shape[0]
    chunk = min(512, rows)
    hazard = [sums[g * kf : (g + 1) * kf] * squares[g : g + 1, :] for g in range(groups)]
    inside = dot_binary(jnp.concatenate(hazard, axis=0), triangle(LO, lambda a, b: a <= b))
    carried = jnp.zeros((kf, 1), F32)
    summed = [None] * groups
    for g in range(groups):
        rows_of = slice(g * kf, (g + 1) * kf)
        summed[g] = inside[rows_of] + carried
        carried = carried + inside[rows_of, LO - 1 :]
    both = stacked(split_two(jnp.concatenate(summed, axis=0)))
    for start in range(0, rows, chunk):
        at = slice(start, start + chunk)
        place = lax.rem(rank[:, at], rows)
        group = place // LO
        spread = one_hot(lax.rem(place, LO), LO)
        placed = unstacked(jnp.dot(both, spread, preferred_element_type=F32), 2)
        picked = jnp.zeros((kf, chunk), F32)
        for g in range(groups):
            picked = picked + jnp.where(group == g, placed[g * kf : (g + 1) * kf], 0.0)
        out[:, at] = picked


def prefix_sums(sums, squares, rank, kf):
    rows = rank.shape[1]
    return pl.pallas_call(
        prefix_kernel,
        in_specs=[VMEM] * 3,
        out_shape=jax.ShapeDtypeStruct((kf, rows), F32),
        out_specs=VMEM,
        compiler_params=pltpu.CompilerParams(**PARAMS),
        cost_estimate=pl.CostEstimate(
            flops=4 * rows * LO * (rows // LO) * kf, bytes_accessed=rows * kf * 24, transcendentals=0
        ),
        name="prefix_sums",
    )(sums, squares, rank)


def weight_kernel(ex, *refs):
    messages, (tangent, local, risk, cumulative, squares) = refs[:ex], refs[ex : ex + 5]
    weighted, placed = refs[ex + 5 :]
    kf = tangent.shape[0]
    me = lax.axis_index("ex")
    for i in range(ex):
        placed[me ^ i] = messages[i][...]
    later = jnp.zeros((kf, 128), F32)
    own_later, before = later, later
    hazard_before = jnp.zeros((1, 128), F32)
    for b in reversed(range(ex)):
        plain, scaled, square = placed[b, :kf], placed[b, kf : 2 * kf], placed[b, 2 * kf + 1 : 2 * kf + 2]
        own_later = own_later + jnp.where(b > me, plain, 0.0)
        before = before + jnp.where(b < me, scaled + square * later, 0.0)
        hazard_before = hazard_before + jnp.where(b < me, placed[b, 2 * kf : 2 * kf + 1], 0.0)
        later = later + plain
    own_later = jnp.sum(own_later, axis=1, keepdims=True)
    before = jnp.sum(before, axis=1, keepdims=True)
    hazard_before = hazard_before[:, :1]
    value = tangent[...] * (cumulative[...] + hazard_before) - (local[...] + squares[...] * own_later + before)
    weighted[...] = (risk[...] * value).astype(BF16)


def weights(messages, tangent, local, risk, cumulative, squares):
    ex = len(messages)
    return pl.pallas_call(
        functools.partial(weight_kernel, ex),
        in_specs=[VMEM] * (ex + 5),
        out_shape=jax.ShapeDtypeStruct(tangent.shape, BF16),
        out_specs=VMEM,
        scratch_shapes=[pltpu.VMEM((ex,) + messages[0].shape, F32)],
        compiler_params=pltpu.CompilerParams(**PARAMS),
        name="weights",
    )(*messages, tangent, local, risk, cumulative, squares)


def encode(values, message):
    height = values.shape[0]
    block = min(BLOCK, height)
    powers = []
    for start in range(0, height, block):
        part = values[start : start + block]
        largest = jnp.max(jnp.abs(part), axis=0, keepdims=True)
        power = power_of(largest)
        message[start : start + block] = to_short(part * jnp.exp2(-power))
        powers.append(power)
    powers.append(jnp.zeros((message.shape[0] - height - len(powers), values.shape[1]), F32))
    message[height:] = to_short(jnp.concatenate(powers, axis=0))


def decode(message, height):
    block = min(BLOCK, height)
    powers = from_short(message[height:])
    parts = []
    for i in range(height // block):
        part = from_short(message[i * block : (i + 1) * block])
        parts.append(part * jnp.exp2(powers[i : i + 1]))
    return jnp.concatenate(parts, axis=0)


def gradient_kernel(feat, kf, start, *refs):
    parts, dosages, out, weighted = refs[:feat], refs[feat], refs[feat + 1], refs[feat + 2]
    width = out.shape[0] - 16
    me = lax.axis_index("feat")
    for i in range(feat):
        weighted[pl.ds(pl.multiple_of((me ^ i) * kf, kf), kf), :] = parts[i][...]
    total = jnp.dot(weighted[...], dosages[:, start : start + width], preferred_element_type=F32)
    encode(total.T, out)


def gradients(parts, dosages, start, variants):
    feat = len(parts)
    kf, persons = parts[0].shape
    k = kf * feat
    return pl.pallas_call(
        functools.partial(gradient_kernel, feat, kf, start),
        in_specs=[VMEM] * (feat + 1),
        out_shape=jax.ShapeDtypeStruct((variants + 16, k), jnp.int16),
        out_specs=VMEM,
        scratch_shapes=[pltpu.VMEM((k, persons), BF16)],
        compiler_params=pltpu.CompilerParams(**PARAMS),
        cost_estimate=pl.CostEstimate(
            flops=2 * persons * variants * k, bytes_accessed=persons * (variants * 2 + k * 2), transcendentals=0
        ),
        name="gradients",
    )(*parts, dosages)


def merge_kernel(mine, other, out):
    height = mine.shape[0] - 16
    encode(decode(mine, height) + decode(other, height), out)


def merge(mine, other):
    return pl.pallas_call(
        merge_kernel,
        in_specs=[VMEM] * 2,
        out_shape=jax.ShapeDtypeStruct(mine.shape, jnp.int16),
        out_specs=VMEM,
        compiler_params=pltpu.CompilerParams(**PARAMS),
        name="merge",
    )(mine, other)


def finish_kernel(first, steps, mine, other, count, *refs):
    out, total, sems = refs[-3:]
    height = mine.shape[0] - 16
    step = height // steps
    block = min(BLOCK, step)
    scale = count[0:1, 0:1]
    powers = [from_short(message[height:]) for message in (mine, other)]
    copies = []
    for i in range(steps):
        for start in range(i * step, (i + 1) * step, block):
            at, j = slice(start, start + block), start // block
            terms = [from_short(m[at]) * jnp.exp2(p[j : j + 1]) for m, p in zip((mine, other), powers)]
            total[at] = (terms[0] + terms[1]) / scale
        copies.append(
            pltpu.make_async_copy(
                total.at[pl.ds(i * step, step)], out.at[pl.ds(first + i * step, step)], sems.at[i]
            )
        )
        copies[i].start()
    for copy in copies:
        copy.wait()


def finish(mine, other, count, first, variants, done):
    height, k = mine.shape[0] - 16, mine.shape[1]
    steps = max(1, min(2, height // BLOCK))
    return pl.pallas_call(
        functools.partial(finish_kernel, first, steps),
        in_specs=[VMEM] * 3 + [HBM] * len(done),
        out_shape=jax.ShapeDtypeStruct((variants, k), F32),
        out_specs=HBM,
        scratch_shapes=[pltpu.VMEM((height, k), F32), pltpu.SemaphoreType.DMA((steps,))],
        input_output_aliases={3: 0} if done else {},
        compiler_params=pltpu.CompilerParams(**PARAMS),
        name="finish",
    )(mine, other, count, *done)


def local(dosages, coefficients, directions, event_rank, events):
    feat, ex = lax.axis_size("feat"), lax.axis_size("ex")
    rows = dosages.shape[0]
    variants, k = directions.shape
    each = k // feat
    padded = -(-each // 16) * 16
    if padded != each:
        directions = jnp.pad(directions.reshape(variants, feat, each), ((0, 0), (0, 0), (0, padded - each)))
        directions = directions.reshape(variants, feat * padded)
    rank, event_row = event_rank[None], events[None]

    linear, keep, send = products(dosages, coefficients, directions, feat)
    order = list(reversed(range(1, feat // 2)))
    received = {q: swap(send[q], "feat", 1) for q in order + [0]}
    others, paired = [], linear
    for q in order:
        *first, message = join(paired, keep[q], received[q])
        paired = first[0] if first else paired
        others.append(swap(message, "feat", 2 * q))
    table = tables(rank, paired, rows)

    risk, sums, ordered_events, message = risks(paired, others, rank, event_row, table, rows)
    messages = [message] + [swap(message, "ex", i) for i in range(1, ex)]
    tangent, later_sums, plain = suffix_sums(keep[0], received[0], others, risk, rank, table)
    hazard, ordered_squares, message, count = shares(messages, sums, ordered_events, plain, later_sums)
    messages = [message] + [swap(message, "ex", i) for i in range(1, ex)]
    cumulative, squares = hazards(hazard, ordered_squares, rank, rows)
    summed = prefix_sums(later_sums, ordered_squares, rank, padded)
    own = weights(messages, tangent, summed, risk, cumulative, squares)

    chips = {0: own}
    for q in reversed(range(1, feat // 2)):
        chips[q] = swap(own, "feat", 2 * q)
    parts = []
    for q in range(feat // 2):
        parts += [chips[q], swap(chips[q], "feat", 1)]

    half = variants // 2
    partial_sums = [gradients(parts, dosages, start, half) for start in (0, half)]
    bit = 1
    while 2 * bit < ex:
        received = [swap(message, "ex", bit) for message in partial_sums]
        partial_sums = [merge(mine, other) for mine, other in zip(partial_sums, received)]
        bit *= 2
    received = [swap(message, "ex", bit) for message in partial_sums]
    done = []
    for i in range(2):
        done = [finish(partial_sums[i], received[i], count, i * half, variants, done)]
    result = done[0]
    if padded != each:
        result = result.reshape(variants, feat, padded)[:, :, :each].reshape(variants, k)
    return result


def solution(mesh):
    placed = (P("ex", "feat"), P("feat"), P("feat", None), P("ex"), P("ex"))
    return jax.shard_map(
        local, mesh=mesh, in_specs=placed, out_specs=P("feat", None), check_vma=False
    )
```

```python
import functools

import jax
import jax.numpy as jnp
from jax import lax
from jax.experimental import pallas as pl
from jax.experimental.pallas import tpu as pltpu
from jax.sharding import PartitionSpec as P

F32 = jnp.float32
BF16 = jnp.bfloat16
LO = 256
NT = (((1,), (1,)), ((), ()))
SPAN = 512
VMEM = pl.BlockSpec(memory_space=pltpu.VMEM)
HBM = pl.BlockSpec(memory_space=pltpu.HBM)
PARAMS = dict(vmem_limit_bytes=24 * 1024 * 1024)


def swap(x, axis, i):
    count = lax.axis_size(axis)
    return lax.ppermute(x, axis, [(s, s ^ i) for s in range(count)])


def split_two(x):
    high = x.astype(BF16).astype(F32)
    return high, x - high


def split_three(x):
    first, rest = split_two(x)
    second, third = split_two(rest)
    return first, second, third


def one_hot(values, count, kind=BF16):
    shape = (count, values.shape[1])
    return jnp.where(lax.broadcasted_iota(jnp.int32, shape, 0) == values, 1.0, 0.0).astype(kind)


def triangle(n, keep):
    first = lax.broadcasted_iota(jnp.int32, (n, n), 0)
    second = lax.broadcasted_iota(jnp.int32, (n, n), 1)
    return jnp.where(keep(first, second), 1.0, 0.0)


def stacked(parts):
    return jnp.concatenate(parts, axis=0).astype(BF16)


def unstacked(values, count):
    height = values.shape[0] // count
    return sum(values[i * height : (i + 1) * height] for i in range(count))


def dot_binary(a, b):
    parts = jnp.dot(stacked(split_three(a)), b.astype(BF16), preferred_element_type=F32)
    return unstacked(parts, 3)


def binary_dot(a, b):
    a = a.astype(BF16)
    total = None
    for part in split_three(b):
        term = jnp.dot(a, part.astype(BF16), preferred_element_type=F32)
        total = term if total is None else total + term
    return total


def product_kernel(feat, kf, chunk, directions, coefficients, dosages, *refs):
    linear, keep, send = refs[0], refs[1 : 1 + feat // 2], refs[1 + feat // 2 : 1 + feat]
    table, own_directions, own_coefficients, lhs, turned, sems = refs[1 + feat :]
    me = lax.axis_index("feat")
    width = feat * kf
    persons, variants = table.shape
    steps = persons // chunk
    small = [
        pltpu.make_async_copy(directions, own_directions, sems.at[steps]),
        pltpu.make_async_copy(coefficients, own_coefficients, sems.at[steps + 1]),
    ]
    large = [
        pltpu.make_async_copy(
            dosages.at[pl.ds(i * chunk, chunk)], table.at[pl.ds(i * chunk, chunk)], sems.at[i]
        )
        for i in range(steps)
    ]
    for copy in small + large:
        copy.start()
    for copy in small:
        copy.wait()
    turned[...] = own_directions[...].astype(F32).T.reshape(turned.shape)
    for j in range(feat):
        lhs[j * kf : (j + 1) * kf] = turned[me ^ j].astype(BF16)
    lhs[width:] = jnp.broadcast_to(own_coefficients[...].astype(F32)[None, :], (16, variants)).astype(BF16)
    for i in range(steps):
        large[i].wait()
        first = i * chunk
        result = lax.dot_general(
            lhs[...], table[first : first + chunk], NT, preferred_element_type=F32
        )
        for j in range(feat):
            (send if j % 2 else keep)[j // 2][:, first : first + chunk] = result[j * kf : (j + 1) * kf]
        for start in range(0, chunk, LO):
            row = result[width : width + 1, start : start + LO]
            group = (first + start) // LO
            linear[group : group + 1, :] = row
            send[-1][group : group + 1, persons:] = row


def products(dosages, coefficients, directions, feat):
    persons, variants = dosages.shape
    k = directions.shape[1]
    kf = k // feat
    chunk = min(512, persons)
    piece = jax.ShapeDtypeStruct((kf, persons), F32)
    first = jax.ShapeDtypeStruct((kf, persons + LO), F32)
    out = pl.pallas_call(
        functools.partial(product_kernel, feat, kf, chunk),
        in_specs=[HBM, HBM, HBM],
        out_shape=[jax.ShapeDtypeStruct((kf, LO), F32)]
        + [piece] * (feat - 1)
        + [first],
        out_specs=[VMEM] * (feat + 1),
        scratch_shapes=[
            pltpu.VMEM((persons, variants), BF16),
            pltpu.VMEM((variants, k), BF16),
            pltpu.VMEM((variants,), BF16),
            pltpu.VMEM((k + 16, variants), BF16),
            pltpu.VMEM((feat, kf, variants), F32),
            pltpu.SemaphoreType.DMA((persons // chunk + 2,)),
        ],
        compiler_params=pltpu.CompilerParams(**PARAMS),
        cost_estimate=pl.CostEstimate(
            flops=2 * persons * variants * k, bytes_accessed=persons * (variants * 2 + k * 4), transcendentals=0
        ),
        name="products",
    )(*[pltpu.with_memory_space_constraint(x, pltpu.HBM) for x in (directions, coefficients, dosages)])
    return out[0], out[1 : 1 + feat // 2], out[1 + feat // 2 :]


def power_of(largest):
    return jnp.ceil(jnp.log2(jnp.maximum(largest, 1e-30))) - 14.0


def to_short(values):
    return jnp.round(values).astype(jnp.int32).astype(jnp.int16)


def from_short(values):
    return values.astype(jnp.int32).astype(F32)


def pair_kernel(linear, received, out):
    out[...] = linear[...] + received[:, received.shape[1] - LO :]


def pair(linear, received):
    return pl.pallas_call(
        pair_kernel,
        in_specs=[VMEM] * 2,
        out_shape=jax.ShapeDtypeStruct(linear.shape, F32),
        out_specs=VMEM,
        compiler_params=pltpu.CompilerParams(**PARAMS),
        name="pair",
    )(linear, received)


def join_kernel(mine, other, *refs):
    out = refs[-1]
    kf, rows = mine.shape
    span = min(SPAN, rows)
    lane = lax.broadcasted_iota(jnp.int32, (kf, 128), 1)
    powers = jnp.zeros((kf, 128), F32)
    for i in range(rows // span):
        at = slice(i * span, (i + 1) * span)
        total = mine[:, at] + other[:, at]
        power = power_of(jnp.max(jnp.abs(total), axis=1, keepdims=True))
        out[:, at] = to_short(total * jnp.exp2(-power))
        powers = jnp.where(lane == i, power, powers)
    out[:, rows:] = to_short(powers)


def join(keep, received, waited):
    kf, rows = keep.shape
    return pl.pallas_call(
        join_kernel,
        in_specs=[VMEM] * 2 + [pl.BlockSpec(memory_space=pl.ANY)] * len(waited),
        out_shape=jax.ShapeDtypeStruct((kf, rows + 128), jnp.int16),
        out_specs=VMEM,
        compiler_params=pltpu.CompilerParams(**PARAMS),
        name="join",
    )(keep, received, *waited)


def table_kernel(rows, rank, waited, table):
    chunk = min(512, rows)
    lane = lax.broadcasted_iota(jnp.int32, (chunk, 128), 1)
    for start in range(0, rows, chunk):
        at = slice(start, start + chunk)
        inner = lax.rem(rank[:, at], LO)
        column = jnp.broadcast_to(inner.astype(F32), (128, chunk)).T.astype(jnp.int32)
        for first in range(0, LO, 128):
            table[at, first : first + 128] = jnp.where(column == lane + first, 1.0, 0.0).astype(BF16)


def tables(rank, waited, rows):
    return pl.pallas_call(
        functools.partial(table_kernel, rows),
        in_specs=[VMEM, pl.BlockSpec(memory_space=pl.ANY)],
        out_shape=jax.ShapeDtypeStruct((rows, LO), BF16),
        out_specs=VMEM,
        compiler_params=pltpu.CompilerParams(**PARAMS),
        cost_estimate=pl.CostEstimate(flops=rows * LO * 8, bytes_accessed=rows * LO * 2, transcendentals=0),
        name="tables",
    )(rank, waited)


def risk_kernel(rows, parts, *refs):
    linear, (rank, events, table) = refs[:parts], refs[parts : parts + 3]
    risk_out, sums_out, events_out, message = refs[-4:]
    groups = rows // LO
    total = linear[0][...]
    for part in linear[1:]:
        total = total + part[...]
    risk = jnp.exp(total)
    for g in range(groups):
        risk_out[:, g * LO : (g + 1) * LO] = risk[g : g + 1]
    mask = one_hot(lax.rem(rank[...], rows) // LO, groups, F32)
    pieces = [mask * part for part in split_three(risk_out[...])] + [mask * events[...].astype(F32)]
    lhs = jnp.concatenate(pieces, axis=0).astype(BF16)
    sorted_all = jnp.dot(lhs, table[...], preferred_element_type=F32)
    ordered = sorted_all[:groups] + sorted_all[groups : 2 * groups] + sorted_all[2 * groups : 3 * groups]
    happened = sorted_all[3 * groups :]
    inside = dot_binary(ordered, triangle(LO, lambda a, b: a >= b))
    totals = jnp.broadcast_to(inside[:, :1], inside.shape)
    carried = binary_dot(triangle(groups, lambda a, b: a < b), totals)
    sums_out[...] = inside + carried
    events_out[...] = happened
    everything = jnp.sum(totals, axis=0, keepdims=True)[:, :128]
    count = jnp.sum(dot_binary(happened, jnp.ones((LO, 128), F32)), axis=0, keepdims=True)
    message[...] = jnp.concatenate([everything, count, jnp.zeros((6, 128), F32)], axis=0)


def risks(linear, rank, events, table, rows, waited):
    groups = rows // LO
    return pl.pallas_call(
        functools.partial(risk_kernel, rows, len(linear)),
        in_specs=[VMEM] * (len(linear) + 3) + [pl.BlockSpec(memory_space=pl.ANY)] * len(waited),
        out_shape=[
            jax.ShapeDtypeStruct((1, rows), F32),
            jax.ShapeDtypeStruct((groups, LO), F32),
            jax.ShapeDtypeStruct((groups, LO), F32),
            jax.ShapeDtypeStruct((8, 128), F32),
        ],
        out_specs=[VMEM] * 4,
        compiler_params=pltpu.CompilerParams(**PARAMS),
        cost_estimate=pl.CostEstimate(flops=rows * LO * 128, bytes_accessed=rows * 64, transcendentals=rows),
        name="risks",
    )(*linear, rank, events, table, *waited)


def share_kernel(later, sums, events, plain, ordered, hazard_out, squares, message):
    kf = plain.shape[0]
    groups = sums.shape[0]
    risk_sum = sums[...] + later[0:1, 0:1]
    hazard = events[...] / risk_sum
    square = events[...] / (risk_sum * risk_sum)
    hazard_out[...] = hazard
    squares[...] = square
    scaled = jnp.zeros((kf, LO), F32)
    for g in range(groups):
        scaled = scaled + ordered[g * kf : (g + 1) * kf] * square[g : g + 1]
    message[:kf] = plain[...]
    message[kf : 2 * kf] = sum(scaled[:, start : start + 128] for start in range(0, LO, 128))
    totals = [jnp.sum(jnp.sum(v, axis=0, keepdims=True), axis=1, keepdims=True) for v in (hazard, square)]
    rows = [jnp.broadcast_to(v, (1, 128)) for v in totals]
    message[2 * kf :] = jnp.concatenate(rows + [jnp.zeros((6, 128), F32)], axis=0)


def shares(later, sums, events, plain, ordered):
    flat = jax.ShapeDtypeStruct(sums.shape, F32)
    return pl.pallas_call(
        share_kernel,
        in_specs=[VMEM] * 5,
        out_shape=[flat, flat, jax.ShapeDtypeStruct((2 * plain.shape[0] + 8, 128), F32)],
        out_specs=[VMEM] * 3,
        compiler_params=pltpu.CompilerParams(**PARAMS),
        name="shares",
    )(later, sums, events, plain, ordered)


def hazard_kernel(rows, hazard, square, rank, cumulative, squares):
    groups = rows // LO
    inside = dot_binary(
        jnp.concatenate([hazard[...], square[...]], axis=0), triangle(LO, lambda a, b: a <= b)
    )
    totals = jnp.broadcast_to(inside[:, LO - 1 :], (2 * groups, 128))
    place = lax.rem(rank[...], rows)
    mask = one_hot(place // LO, groups, F32)
    placed = dot_binary(inside, one_hot(lax.rem(place, LO), LO))
    before = triangle(groups, lambda a, b: a > b)
    for first, out in ((0, cumulative), (groups, squares)):
        carried = binary_dot(before, totals[first : first + groups])[:, :1]
        out[...] = jnp.sum(mask * (placed[first : first + groups] + carried), axis=0, keepdims=True)


def hazards(hazard, square, rank, rows):
    row = jax.ShapeDtypeStruct((1, rows), F32)
    return pl.pallas_call(
        functools.partial(hazard_kernel, rows),
        in_specs=[VMEM] * 3,
        out_shape=[row, row],
        out_specs=[VMEM] * 2,
        compiler_params=pltpu.CompilerParams(**PARAMS),
        cost_estimate=pl.CostEstimate(flops=rows * LO * 200, bytes_accessed=rows * 64, transcendentals=0),
        name="hazards",
    )(hazard, square, rank)


def range_kernel(bit, count, *refs):
    total, other, later = refs[:3]
    total_out, later_out = refs[3 + count :]
    is_later = (lax.axis_index("ex") & bit) == 0
    later_out[...] = later[...] + jnp.where(is_later, other[...], 0.0)
    total_out[...] = total[...] + other[...]


def ranges(bit, total, other, later, waited):
    return pl.pallas_call(
        functools.partial(range_kernel, bit, len(waited)),
        in_specs=[VMEM] * 3 + [pl.BlockSpec(memory_space=pl.ANY)] * len(waited),
        out_shape=[jax.ShapeDtypeStruct(total.shape, F32)] * 2,
        out_specs=[VMEM] * 2,
        compiler_params=pltpu.CompilerParams(**PARAMS),
        name="ranges",
    )(total, other, later, *waited)


def suffix_kernel(parts, own, other, *refs):
    messages, (risk, rank, table) = refs[:parts], refs[parts : parts + 3]
    tangent_out, sums, plain, lhs = refs[parts + 3 :]
    kf, rows = own.shape
    folded = jnp.zeros((kf, 128), F32)
    groups = rows // LO
    span = min(SPAN, rows)
    powers = [jnp.exp2(from_short(part[:, rows:])) for part in messages]
    for i in range(rows // span):
        at = slice(i * span, (i + 1) * span)
        tangent = own[:, at] + other[:, at]
        for part, power in zip(messages, powers):
            tangent = tangent + from_short(part[:, at]) * power[:, i : i + 1]
        tangent_out[:, at] = tangent
        weighted = tangent * risk[:, at]
        folded = folded + sum(weighted[:, j : j + 128] for j in range(0, span, 128))
        high, low = split_two(weighted)
        high, low = high.astype(BF16), low.astype(BF16)
        group = jnp.broadcast_to(lax.rem(rank[:, at], rows) // LO, (kf, span))
        for g in range(groups):
            mask = jnp.where(group == g, 1.0, 0.0).astype(BF16)
            lhs[2 * g * kf : (2 * g + 1) * kf, at] = high * mask
            lhs[(2 * g + 1) * kf : (2 * g + 2) * kf, at] = low * mask
    plain[...] = folded
    ordered = jnp.dot(lhs[...], table[...], preferred_element_type=F32)
    ordered = jnp.concatenate(
        [
            ordered[2 * g * kf : (2 * g + 1) * kf] + ordered[(2 * g + 1) * kf : (2 * g + 2) * kf]
            for g in range(groups)
        ],
        axis=0,
    )
    inside = dot_binary(ordered, triangle(LO, lambda a, b: a >= b))
    carried = jnp.zeros((kf, 1), F32)
    for g in reversed(range(groups)):
        rows_of = slice(g * kf, (g + 1) * kf)
        sums[rows_of] = inside[rows_of] + carried
        carried = carried + inside[rows_of, :1]


def suffix_sums(own, other, messages, risk, rank, table):
    kf, rows = own.shape
    groups = rows // LO
    return pl.pallas_call(
        functools.partial(suffix_kernel, len(messages)),
        in_specs=[VMEM] * (len(messages) + 5),
        out_shape=[
            jax.ShapeDtypeStruct((kf, rows), F32),
            jax.ShapeDtypeStruct((groups * kf, LO), F32),
            jax.ShapeDtypeStruct((kf, 128), F32),
        ],
        out_specs=[VMEM] * 3,
        scratch_shapes=[pltpu.VMEM((groups * 2 * kf, rows), BF16)],
        compiler_params=pltpu.CompilerParams(**PARAMS),
        cost_estimate=pl.CostEstimate(
            flops=2 * rows * LO * groups * 2 * kf, bytes_accessed=rows * kf * 24, transcendentals=0
        ),
        name="suffix_sums",
    )(own, other, *messages, risk, rank, table)


def prefix_kernel(sums, squares, rank, out):
    kf, rows = out.shape
    groups = squares.shape[0]
    chunk = min(512, rows)
    hazard = [sums[g * kf : (g + 1) * kf] * squares[g : g + 1, :] for g in range(groups)]
    inside = dot_binary(jnp.concatenate(hazard, axis=0), triangle(LO, lambda a, b: a <= b))
    carried = jnp.zeros((kf, 1), F32)
    summed = [None] * groups
    for g in range(groups):
        rows_of = slice(g * kf, (g + 1) * kf)
        summed[g] = inside[rows_of] + carried
        carried = carried + inside[rows_of, LO - 1 :]
    both = stacked(split_two(jnp.concatenate(summed, axis=0)))
    for start in range(0, rows, chunk):
        at = slice(start, start + chunk)
        place = lax.rem(rank[:, at], rows)
        group = place // LO
        spread = one_hot(lax.rem(place, LO), LO)
        placed = unstacked(jnp.dot(both, spread, preferred_element_type=F32), 2)
        picked = jnp.zeros((kf, chunk), F32)
        for g in range(groups):
            picked = picked + jnp.where(group == g, placed[g * kf : (g + 1) * kf], 0.0)
        out[:, at] = picked


def prefix_sums(sums, squares, rank, kf):
    rows = rank.shape[1]
    return pl.pallas_call(
        prefix_kernel,
        in_specs=[VMEM] * 3,
        out_shape=jax.ShapeDtypeStruct((kf, rows), F32),
        out_specs=VMEM,
        compiler_params=pltpu.CompilerParams(**PARAMS),
        cost_estimate=pl.CostEstimate(
            flops=4 * rows * LO * (rows // LO) * kf, bytes_accessed=rows * kf * 24, transcendentals=0
        ),
        name="prefix_sums",
    )(sums, squares, rank)


def weight_kernel(ex, *refs):
    messages, (tangent, local, risk, cumulative, squares) = refs[:ex], refs[ex : ex + 5]
    weighted, placed = refs[ex + 5 :]
    kf = tangent.shape[0]
    me = lax.axis_index("ex")
    for i in range(ex):
        placed[me ^ i] = messages[i][...]
    later = jnp.zeros((kf, 128), F32)
    own_later, before = later, later
    hazard_before = jnp.zeros((1, 128), F32)
    for b in reversed(range(ex)):
        plain, scaled, square = placed[b, :kf], placed[b, kf : 2 * kf], placed[b, 2 * kf + 1 : 2 * kf + 2]
        own_later = own_later + jnp.where(b > me, plain, 0.0)
        before = before + jnp.where(b < me, scaled + square * later, 0.0)
        hazard_before = hazard_before + jnp.where(b < me, placed[b, 2 * kf : 2 * kf + 1], 0.0)
        later = later + plain
    own_later = jnp.sum(own_later, axis=1, keepdims=True)
    before = jnp.sum(before, axis=1, keepdims=True)
    hazard_before = hazard_before[:, :1]
    value = tangent[...] * (cumulative[...] + hazard_before) - (local[...] + squares[...] * own_later + before)
    weighted[...] = (risk[...] * value).astype(BF16)


def weights(messages, tangent, local, risk, cumulative, squares):
    ex = len(messages)
    return pl.pallas_call(
        functools.partial(weight_kernel, ex),
        in_specs=[VMEM] * (ex + 5),
        out_shape=jax.ShapeDtypeStruct(tangent.shape, BF16),
        out_specs=VMEM,
        scratch_shapes=[pltpu.VMEM((ex,) + messages[0].shape, F32)],
        compiler_params=pltpu.CompilerParams(**PARAMS),
        name="weights",
    )(*messages, tangent, local, risk, cumulative, squares)


def tiles_of(height, width):
    return [
        (slice(row, row + 16), slice(column, column + 128))
        for row in range(0, height, 16)
        for column in range(0, width, 128)
    ]


def encode(values, message):
    lane = lax.broadcasted_iota(jnp.int32, (16, 128), 1)
    powers = jnp.zeros((16, 128), F32)
    for i, value in enumerate(values):
        power = power_of(jnp.max(jnp.abs(value), axis=1, keepdims=True))
        message[i] = to_short(value * jnp.exp2(-power))
        powers = jnp.where(lane == i, power, powers)
    message[message.shape[0] - 1] = to_short(powers)


def decode(message):
    last = message.shape[0] - 1
    scales = jnp.exp2(from_short(message[last]))
    return [from_short(message[i]) * scales[:, i : i + 1] for i in range(last)]


def decode_sum(mine, other):
    return [one + two for one, two in zip(decode(mine), decode(other))]


def gradient_kernel(parts, kf, *refs):
    pieces, dosages, out, weighted = refs[:parts], refs[parts], refs[parts + 1], refs[parts + 2]
    for i in range(parts):
        weighted[i * kf : (i + 1) * kf, :] = pieces[i][...]
    total = jnp.dot(weighted[...], dosages[...], preferred_element_type=F32)
    encode([total[at] for at in tiles_of(*total.shape)], out)


def gradients(pieces, dosages):
    parts = len(pieces)
    kf, persons = pieces[0].shape
    k, variants = kf * parts, dosages.shape[1]
    return pl.pallas_call(
        functools.partial(gradient_kernel, parts, kf),
        in_specs=[VMEM] * (parts + 1),
        out_shape=jax.ShapeDtypeStruct((k * variants // 2048 + 1, 16, 128), jnp.int16),
        out_specs=VMEM,
        scratch_shapes=[pltpu.VMEM((k, persons), BF16)],
        compiler_params=pltpu.CompilerParams(**PARAMS),
        cost_estimate=pl.CostEstimate(
            flops=2 * persons * variants * k, bytes_accessed=persons * (variants * 2 + k * 2), transcendentals=0
        ),
        name="gradients",
    )(*pieces, dosages)


def merge_kernel(mine, other, out):
    encode(decode_sum(mine, other), out)


def merge(mine, other):
    return pl.pallas_call(
        merge_kernel,
        in_specs=[VMEM] * 2,
        out_shape=jax.ShapeDtypeStruct(mine.shape, jnp.int16),
        out_specs=VMEM,
        compiler_params=pltpu.CompilerParams(**PARAMS),
        name="merge",
    )(mine, other)


def add_kernel(mine, other, out):
    for at, value in zip(tiles_of(*out.shape), decode_sum(mine, other)):
        out[at] = value


def add(mine, other, variants):
    return pl.pallas_call(
        add_kernel,
        in_specs=[VMEM] * 2,
        out_shape=jax.ShapeDtypeStruct(((mine.shape[0] - 1) * 2048 // variants, variants), F32),
        out_specs=VMEM,
        compiler_params=pltpu.CompilerParams(**PARAMS),
        name="add",
    )(mine, other)


def finish_kernel(feat, kf, first, mine, other, count, out, placed, total, sems):
    me = lax.axis_index("feat")
    variants = out.shape[0]
    scale = count[1:2, 0:1]
    for q in range(feat // 2):
        placed[me ^ (2 * q)] = first[q * kf : (q + 1) * kf]
    for (rows, columns), value in zip(tiles_of(feat // 2 * kf, variants), decode_sum(mine, other)):
        q, row = divmod(rows.start, kf)
        placed[me ^ (2 * q + 1), row : row + 16, columns] = value
    copies = []
    for i in range(variants // 128):
        at = slice(i * 128, (i + 1) * 128)
        total[at] = placed[:, :, at].reshape(feat * kf, 128).T / scale
        copies.append(
            pltpu.make_async_copy(
                total.at[pl.ds(i * 128, 128)], out.at[pl.ds(i * 128, 128)], sems.at[i]
            )
        )
        copies[i].start()
    for copy in copies:
        copy.wait()


def finish(first, mine, other, count, feat):
    k, variants = 2 * first.shape[0], first.shape[1]
    kf = k // feat
    return pl.pallas_call(
        functools.partial(finish_kernel, feat, kf),
        in_specs=[VMEM] * 4,
        out_shape=jax.ShapeDtypeStruct((variants, k), F32),
        out_specs=HBM,
        scratch_shapes=[
            pltpu.VMEM((feat, kf, variants), F32),
            pltpu.VMEM((variants, k), F32),
            pltpu.SemaphoreType.DMA((variants // 128,)),
        ],
        compiler_params=pltpu.CompilerParams(**PARAMS),
        name="finish",
    )(first, mine, other, count)


def local(dosages, coefficients, directions, event_rank, events):
    feat, ex = lax.axis_size("feat"), lax.axis_size("ex")
    rows = dosages.shape[0]
    variants, k = directions.shape
    each = k // feat
    padded = -(-each // 16) * 16
    if padded != each:
        directions = jnp.pad(directions.reshape(variants, feat, each), ((0, 0), (0, 0), (0, padded - each)))
        directions = directions.reshape(variants, feat * padded)
    rank, event_row = event_rank[None], events[None]

    linear, keep, send = products(dosages, coefficients, directions, feat)
    order = list(reversed(range(1, feat // 2)))
    received = {q: swap(send[q], "feat", 1) for q in order + [0]}
    paired = pair(linear, received[order[0]])
    linears = [swap(paired, "feat", 2 * q) for q in order]
    table = tables(rank, paired, rows)
    joined = [join(keep[q], received[q], linears + [table]) for q in order]
    others = [swap(message, "feat", 2 * q) for message, q in zip(joined, order)]

    risk, sums, ordered_events, total = risks([paired] + linears, rank, event_row, table, rows, joined)
    later = jnp.zeros_like(total)
    bit = 1
    while bit < ex:
        total, later = ranges(bit, total, swap(total, "ex", bit), later, others if bit == 1 else [])
        bit *= 2
    tangent, later_sums, plain = suffix_sums(keep[0], received[0], others, risk, rank, table)
    hazard, ordered_squares, message = shares(later, sums, ordered_events, plain, later_sums)
    messages = [message] + [swap(message, "ex", i) for i in range(1, ex)]
    cumulative, squares = hazards(hazard, ordered_squares, rank, rows)
    summed = prefix_sums(later_sums, ordered_squares, rank, padded)
    own = weights(messages, tangent, summed, risk, cumulative, squares)

    chips = {0: own}
    for q in reversed(range(1, feat // 2)):
        chips[q] = swap(own, "feat", 2 * q)
    near = [chips[q] for q in range(feat // 2)]
    far = [swap(chips[q], "feat", 1) for q in range(feat // 2)]
    partial_sums = [gradients(pieces, dosages) for pieces in (near, far)]
    bit = 1
    while 2 * bit < ex:
        received = [swap(message, "ex", bit) for message in partial_sums]
        partial_sums = [merge(mine, other) for mine, other in zip(partial_sums, received)]
        bit *= 2
    received = [swap(message, "ex", bit) for message in partial_sums]
    first = add(partial_sums[0], received[0], variants)
    result = finish(first, partial_sums[1], received[1], total, feat)
    if padded != each:
        result = result.reshape(variants, feat, padded)[:, :, :each].reshape(variants, k)
    return result


def solution(mesh):
    placed = (P("ex", "feat"), P("feat"), P("feat", None), P("ex"), P("ex"))
    return jax.shard_map(
        local, mesh=mesh, in_specs=placed, out_specs=P("feat", None), check_vma=False
    )
```

```python
import functools

import jax
import jax.numpy as jnp
from jax import lax
from jax.experimental import pallas as pl
from jax.experimental.pallas import tpu as pltpu
from jax.sharding import PartitionSpec as P

F32 = jnp.float32
BF16 = jnp.bfloat16
LO = 256
NT = (((1,), (1,)), ((), ()))
BLOCK = 64
SPAN = 512
VMEM = pl.BlockSpec(memory_space=pltpu.VMEM)
HBM = pl.BlockSpec(memory_space=pltpu.HBM)
PARAMS = dict(vmem_limit_bytes=24 * 1024 * 1024)


def swap(x, axis, i):
    count = lax.axis_size(axis)
    return lax.ppermute(x, axis, [(s, s ^ i) for s in range(count)])


def split_two(x):
    high = x.astype(BF16).astype(F32)
    return high, x - high


def split_three(x):
    first, rest = split_two(x)
    second, third = split_two(rest)
    return first, second, third


def one_hot(values, count, kind=BF16):
    shape = (count, values.shape[1])
    return jnp.where(lax.broadcasted_iota(jnp.int32, shape, 0) == values, 1.0, 0.0).astype(kind)


def triangle(n, keep):
    first = lax.broadcasted_iota(jnp.int32, (n, n), 0)
    second = lax.broadcasted_iota(jnp.int32, (n, n), 1)
    return jnp.where(keep(first, second), 1.0, 0.0)


def stacked(parts):
    return jnp.concatenate(parts, axis=0).astype(BF16)


def unstacked(values, count):
    height = values.shape[0] // count
    return sum(values[i * height : (i + 1) * height] for i in range(count))


def dot_binary(a, b):
    parts = jnp.dot(stacked(split_three(a)), b.astype(BF16), preferred_element_type=F32)
    return unstacked(parts, 3)


def binary_dot(a, b):
    a = a.astype(BF16)
    total = None
    for part in split_three(b):
        term = jnp.dot(a, part.astype(BF16), preferred_element_type=F32)
        total = term if total is None else total + term
    return total


def product_kernel(feat, kf, chunk, directions, coefficients, dosages, *refs):
    linear, keep, send = refs[0], refs[1 : 1 + feat // 2], refs[1 + feat // 2 : 1 + feat]
    table, own_directions, own_coefficients, lhs, turned, sems = refs[1 + feat :]
    me = lax.axis_index("feat")
    width = feat * kf
    persons, variants = table.shape
    steps = persons // chunk
    small = [
        pltpu.make_async_copy(directions, own_directions, sems.at[steps]),
        pltpu.make_async_copy(coefficients, own_coefficients, sems.at[steps + 1]),
    ]
    large = [
        pltpu.make_async_copy(
            dosages.at[pl.ds(i * chunk, chunk)], table.at[pl.ds(i * chunk, chunk)], sems.at[i]
        )
        for i in range(steps)
    ]
    for copy in small + large:
        copy.start()
    for copy in small:
        copy.wait()
    turned[...] = own_directions[...].astype(F32).T.reshape(turned.shape)
    for j in range(feat):
        lhs[j * kf : (j + 1) * kf] = turned[me ^ j].astype(BF16)
    lhs[width:] = jnp.broadcast_to(own_coefficients[...].astype(F32)[None, :], (16, variants)).astype(BF16)
    for i in range(steps):
        large[i].wait()
        first = i * chunk
        result = lax.dot_general(
            lhs[...], table[first : first + chunk], NT, preferred_element_type=F32
        )
        for j in range(feat):
            (send if j % 2 else keep)[j // 2][:, first : first + chunk] = result[j * kf : (j + 1) * kf]
        for start in range(0, chunk, LO):
            row = result[width : width + 1, start : start + LO]
            group = (first + start) // LO
            linear[group : group + 1, :] = row
            send[-1][group : group + 1, persons:] = row


def products(dosages, coefficients, directions, feat):
    persons, variants = dosages.shape
    k = directions.shape[1]
    kf = k // feat
    chunk = min(512, persons)
    piece = jax.ShapeDtypeStruct((kf, persons), F32)
    first = jax.ShapeDtypeStruct((kf, persons + LO), F32)
    out = pl.pallas_call(
        functools.partial(product_kernel, feat, kf, chunk),
        in_specs=[HBM, HBM, HBM],
        out_shape=[jax.ShapeDtypeStruct((kf, LO), F32)]
        + [piece] * (feat - 1)
        + [first],
        out_specs=[VMEM] * (feat + 1),
        scratch_shapes=[
            pltpu.VMEM((persons, variants), BF16),
            pltpu.VMEM((variants, k), BF16),
            pltpu.VMEM((variants,), BF16),
            pltpu.VMEM((k + 16, variants), BF16),
            pltpu.VMEM((feat, kf, variants), F32),
            pltpu.SemaphoreType.DMA((persons // chunk + 2,)),
        ],
        compiler_params=pltpu.CompilerParams(**PARAMS),
        cost_estimate=pl.CostEstimate(
            flops=2 * persons * variants * k, bytes_accessed=persons * (variants * 2 + k * 4), transcendentals=0
        ),
        name="products",
    )(*[pltpu.with_memory_space_constraint(x, pltpu.HBM) for x in (directions, coefficients, dosages)])
    return out[0], out[1 : 1 + feat // 2], out[1 + feat // 2 :]


def power_of(largest):
    return jnp.ceil(jnp.log2(jnp.maximum(largest, 1e-30))) - 14.0


def to_short(values):
    return jnp.round(values).astype(jnp.int32).astype(jnp.int16)


def from_short(values):
    return values.astype(jnp.int32).astype(F32)


def pair_kernel(linear, received, out):
    out[...] = linear[...] + received[:, received.shape[1] - LO :]


def pair(linear, received):
    return pl.pallas_call(
        pair_kernel,
        in_specs=[VMEM] * 2,
        out_shape=jax.ShapeDtypeStruct(linear.shape, F32),
        out_specs=VMEM,
        compiler_params=pltpu.CompilerParams(**PARAMS),
        name="pair",
    )(linear, received)


def join_kernel(start, width, mine, other, *refs):
    linear, out = refs[0], refs[-1]
    kf = mine.shape[0]
    span = min(SPAN, width)
    lane = lax.broadcasted_iota(jnp.int32, (kf, 128), 1)
    powers = jnp.zeros((kf, 128), F32)
    for i in range(width // span):
        at = slice(start + i * span, start + (i + 1) * span)
        total = mine[:, at] + other[:, at]
        power = power_of(jnp.max(jnp.abs(total), axis=1, keepdims=True))
        out[:, i * span : (i + 1) * span] = to_short(total * jnp.exp2(-power))
        powers = jnp.where(lane == i, power, powers)
    if start == 0:
        power = power_of(jnp.max(jnp.abs(linear[...]), axis=1, keepdims=True))
        scaled = linear[...] * jnp.exp2(-power)
        whole = jnp.round(scaled)
        out[:, width : width + LO] = to_short(whole)
        out[:, width + LO : width + 2 * LO] = to_short((scaled - whole) * 32768.0)
        powers = jnp.where(lane == 127, power, powers)
    out[:, out.shape[1] - 128 :] = to_short(powers)


def join(keep, received, start, width, linear, waited):
    kf, rows = keep.shape
    extra = 2 * LO if start == 0 else 0
    return pl.pallas_call(
        functools.partial(join_kernel, start, width),
        in_specs=[VMEM] * 3 + [pl.BlockSpec(memory_space=pl.ANY)] * len(waited),
        out_shape=jax.ShapeDtypeStruct((kf, width + extra + 128), jnp.int16),
        out_specs=VMEM,
        compiler_params=pltpu.CompilerParams(**PARAMS),
        name="join",
    )(keep, received, linear, *waited)


def table_kernel(rows, rank, waited, table):
    chunk = min(512, rows)
    lane = lax.broadcasted_iota(jnp.int32, (chunk, 128), 1)
    for start in range(0, rows, chunk):
        at = slice(start, start + chunk)
        inner = lax.rem(rank[:, at], LO)
        column = jnp.broadcast_to(inner.astype(F32), (128, chunk)).T.astype(jnp.int32)
        for first in range(0, LO, 128):
            table[at, first : first + 128] = jnp.where(column == lane + first, 1.0, 0.0).astype(BF16)


def tables(rank, waited, rows):
    return pl.pallas_call(
        functools.partial(table_kernel, rows),
        in_specs=[VMEM, pl.BlockSpec(memory_space=pl.ANY)],
        out_shape=jax.ShapeDtypeStruct((rows, LO), BF16),
        out_specs=VMEM,
        compiler_params=pltpu.CompilerParams(**PARAMS),
        cost_estimate=pl.CostEstimate(flops=rows * LO * 8, bytes_accessed=rows * LO * 2, transcendentals=0),
        name="tables",
    )(rank, waited)


def risk_kernel(rows, parts, linear, *refs):
    messages, (rank, events, table) = refs[:parts], refs[parts : parts + 3]
    risk_out, sums_out, events_out, message = refs[-4:]
    groups = rows // LO
    total = linear[...]
    for part in messages:
        end = part.shape[1] - 128
        power = from_short(part[:, end:])[:, 127:]
        high, low = from_short(part[:, end - 2 * LO : end - LO]), from_short(part[:, end - LO : end])
        total = total + (high + low * (1.0 / 32768.0)) * jnp.exp2(power)
    risk = jnp.exp(total)
    for g in range(groups):
        risk_out[:, g * LO : (g + 1) * LO] = risk[g : g + 1]
    mask = one_hot(lax.rem(rank[...], rows) // LO, groups, F32)
    pieces = [mask * part for part in split_three(risk_out[...])] + [mask * events[...].astype(F32)]
    lhs = jnp.concatenate(pieces, axis=0).astype(BF16)
    sorted_all = jnp.dot(lhs, table[...], preferred_element_type=F32)
    ordered = sorted_all[:groups] + sorted_all[groups : 2 * groups] + sorted_all[2 * groups : 3 * groups]
    happened = sorted_all[3 * groups :]
    inside = dot_binary(ordered, triangle(LO, lambda a, b: a >= b))
    totals = jnp.broadcast_to(inside[:, :1], inside.shape)
    carried = binary_dot(triangle(groups, lambda a, b: a < b), totals)
    sums_out[...] = inside + carried
    events_out[...] = happened
    everything = jnp.sum(totals, axis=0, keepdims=True)[:, :128]
    count = jnp.sum(dot_binary(happened, jnp.ones((LO, 128), F32)), axis=0, keepdims=True)
    message[...] = jnp.concatenate([everything, count, jnp.zeros((6, 128), F32)], axis=0)


def risks(linear, messages, rank, events, table, rows):
    groups = rows // LO
    return pl.pallas_call(
        functools.partial(risk_kernel, rows, len(messages)),
        in_specs=[VMEM] * (len(messages) + 4),
        out_shape=[
            jax.ShapeDtypeStruct((1, rows), F32),
            jax.ShapeDtypeStruct((groups, LO), F32),
            jax.ShapeDtypeStruct((groups, LO), F32),
            jax.ShapeDtypeStruct((8, 128), F32),
        ],
        out_specs=[VMEM] * 4,
        compiler_params=pltpu.CompilerParams(**PARAMS),
        cost_estimate=pl.CostEstimate(flops=rows * LO * 128, bytes_accessed=rows * 64, transcendentals=rows),
        name="risks",
    )(linear, *messages, rank, events, table)


def share_kernel(later, sums, events, plain, ordered, hazard_out, squares, message):
    kf = plain.shape[0]
    groups = sums.shape[0]
    risk_sum = sums[...] + later[0:1, 0:1]
    hazard = events[...] / risk_sum
    square = events[...] / (risk_sum * risk_sum)
    hazard_out[...] = hazard
    squares[...] = square
    scaled = jnp.zeros((kf, LO), F32)
    for g in range(groups):
        scaled = scaled + ordered[g * kf : (g + 1) * kf] * square[g : g + 1]
    message[:kf] = plain[...]
    message[kf : 2 * kf] = sum(scaled[:, start : start + 128] for start in range(0, LO, 128))
    totals = [jnp.sum(jnp.sum(v, axis=0, keepdims=True), axis=1, keepdims=True) for v in (hazard, square)]
    rows = [jnp.broadcast_to(v, (1, 128)) for v in totals]
    message[2 * kf :] = jnp.concatenate(rows + [jnp.zeros((6, 128), F32)], axis=0)


def shares(later, sums, events, plain, ordered):
    flat = jax.ShapeDtypeStruct(sums.shape, F32)
    return pl.pallas_call(
        share_kernel,
        in_specs=[VMEM] * 5,
        out_shape=[flat, flat, jax.ShapeDtypeStruct((2 * plain.shape[0] + 8, 128), F32)],
        out_specs=[VMEM] * 3,
        compiler_params=pltpu.CompilerParams(**PARAMS),
        name="shares",
    )(later, sums, events, plain, ordered)


def hazard_kernel(rows, hazard, square, rank, cumulative, squares):
    groups = rows // LO
    inside = dot_binary(
        jnp.concatenate([hazard[...], square[...]], axis=0), triangle(LO, lambda a, b: a <= b)
    )
    totals = jnp.broadcast_to(inside[:, LO - 1 :], (2 * groups, 128))
    place = lax.rem(rank[...], rows)
    mask = one_hot(place // LO, groups, F32)
    placed = dot_binary(inside, one_hot(lax.rem(place, LO), LO))
    before = triangle(groups, lambda a, b: a > b)
    for first, out in ((0, cumulative), (groups, squares)):
        carried = binary_dot(before, totals[first : first + groups])[:, :1]
        out[...] = jnp.sum(mask * (placed[first : first + groups] + carried), axis=0, keepdims=True)


def hazards(hazard, square, rank, rows):
    row = jax.ShapeDtypeStruct((1, rows), F32)
    return pl.pallas_call(
        functools.partial(hazard_kernel, rows),
        in_specs=[VMEM] * 3,
        out_shape=[row, row],
        out_specs=[VMEM] * 2,
        compiler_params=pltpu.CompilerParams(**PARAMS),
        cost_estimate=pl.CostEstimate(flops=rows * LO * 200, bytes_accessed=rows * 64, transcendentals=0),
        name="hazards",
    )(hazard, square, rank)


def range_kernel(bit, count, *refs):
    total, other, later = refs[:3]
    total_out, later_out = refs[3 + count :]
    is_later = (lax.axis_index("ex") & bit) == 0
    later_out[...] = later[...] + jnp.where(is_later, other[...], 0.0)
    total_out[...] = total[...] + other[...]


def ranges(bit, total, other, later, waited):
    return pl.pallas_call(
        functools.partial(range_kernel, bit, len(waited)),
        in_specs=[VMEM] * 3 + [pl.BlockSpec(memory_space=pl.ANY)] * len(waited),
        out_shape=[jax.ShapeDtypeStruct(total.shape, F32)] * 2,
        out_specs=[VMEM] * 2,
        compiler_params=pltpu.CompilerParams(**PARAMS),
        name="ranges",
    )(total, other, later, *waited)


def suffix_kernel(parts, own, other, *refs):
    messages, (risk, rank, table) = refs[:parts], refs[parts : parts + 3]
    tangent_out, sums, plain, lhs = refs[parts + 3 :]
    kf, rows = own.shape
    folded = jnp.zeros((kf, 128), F32)
    groups = rows // LO
    span = min(SPAN, rows)
    powers = [jnp.exp2(from_short(part[:, part.shape[1] - 128 :])) for part in messages]
    half = rows // 2
    later = len(messages) // 2
    for i in range(rows // span):
        at = slice(i * span, (i + 1) * span)
        tangent = own[:, at] + other[:, at]
        first = 0 if i * span < half else later
        here = i - (first and half // span)
        for part, power in zip(messages[first : first + later], powers[first : first + later]):
            tangent = tangent + from_short(part[:, here * span : (here + 1) * span]) * power[:, here : here + 1]
        tangent_out[:, at] = tangent
        weighted = tangent * risk[:, at]
        folded = folded + sum(weighted[:, j : j + 128] for j in range(0, span, 128))
        high, low = split_two(weighted)
        high, low = high.astype(BF16), low.astype(BF16)
        group = jnp.broadcast_to(lax.rem(rank[:, at], rows) // LO, (kf, span))
        for g in range(groups):
            mask = jnp.where(group == g, 1.0, 0.0).astype(BF16)
            lhs[2 * g * kf : (2 * g + 1) * kf, at] = high * mask
            lhs[(2 * g + 1) * kf : (2 * g + 2) * kf, at] = low * mask
    plain[...] = folded
    ordered = jnp.dot(lhs[...], table[...], preferred_element_type=F32)
    ordered = jnp.concatenate(
        [
            ordered[2 * g * kf : (2 * g + 1) * kf] + ordered[(2 * g + 1) * kf : (2 * g + 2) * kf]
            for g in range(groups)
        ],
        axis=0,
    )
    inside = dot_binary(ordered, triangle(LO, lambda a, b: a >= b))
    carried = jnp.zeros((kf, 1), F32)
    for g in reversed(range(groups)):
        rows_of = slice(g * kf, (g + 1) * kf)
        sums[rows_of] = inside[rows_of] + carried
        carried = carried + inside[rows_of, :1]


def suffix_sums(own, other, messages, risk, rank, table):
    kf, rows = own.shape
    groups = rows // LO
    return pl.pallas_call(
        functools.partial(suffix_kernel, len(messages)),
        in_specs=[VMEM] * (len(messages) + 5),
        out_shape=[
            jax.ShapeDtypeStruct((kf, rows), F32),
            jax.ShapeDtypeStruct((groups * kf, LO), F32),
            jax.ShapeDtypeStruct((kf, 128), F32),
        ],
        out_specs=[VMEM] * 3,
        scratch_shapes=[pltpu.VMEM((groups * 2 * kf, rows), BF16)],
        compiler_params=pltpu.CompilerParams(**PARAMS),
        cost_estimate=pl.CostEstimate(
            flops=2 * rows * LO * groups * 2 * kf, bytes_accessed=rows * kf * 24, transcendentals=0
        ),
        name="suffix_sums",
    )(own, other, *messages, risk, rank, table)


def prefix_kernel(sums, squares, rank, out):
    kf, rows = out.shape
    groups = squares.shape[0]
    chunk = min(512, rows)
    hazard = [sums[g * kf : (g + 1) * kf] * squares[g : g + 1, :] for g in range(groups)]
    inside = dot_binary(jnp.concatenate(hazard, axis=0), triangle(LO, lambda a, b: a <= b))
    carried = jnp.zeros((kf, 1), F32)
    summed = [None] * groups
    for g in range(groups):
        rows_of = slice(g * kf, (g + 1) * kf)
        summed[g] = inside[rows_of] + carried
        carried = carried + inside[rows_of, LO - 1 :]
    both = stacked(split_two(jnp.concatenate(summed, axis=0)))
    for start in range(0, rows, chunk):
        at = slice(start, start + chunk)
        place = lax.rem(rank[:, at], rows)
        group = place // LO
        spread = one_hot(lax.rem(place, LO), LO)
        placed = unstacked(jnp.dot(both, spread, preferred_element_type=F32), 2)
        picked = jnp.zeros((kf, chunk), F32)
        for g in range(groups):
            picked = picked + jnp.where(group == g, placed[g * kf : (g + 1) * kf], 0.0)
        out[:, at] = picked


def prefix_sums(sums, squares, rank, kf):
    rows = rank.shape[1]
    return pl.pallas_call(
        prefix_kernel,
        in_specs=[VMEM] * 3,
        out_shape=jax.ShapeDtypeStruct((kf, rows), F32),
        out_specs=VMEM,
        compiler_params=pltpu.CompilerParams(**PARAMS),
        cost_estimate=pl.CostEstimate(
            flops=4 * rows * LO * (rows // LO) * kf, bytes_accessed=rows * kf * 24, transcendentals=0
        ),
        name="prefix_sums",
    )(sums, squares, rank)


def weight_kernel(ex, *refs):
    messages, (tangent, local, risk, cumulative, squares) = refs[:ex], refs[ex : ex + 5]
    weighted, placed = refs[ex + 5 :]
    kf = tangent.shape[0]
    me = lax.axis_index("ex")
    for i in range(ex):
        placed[me ^ i] = messages[i][...]
    later = jnp.zeros((kf, 128), F32)
    own_later, before = later, later
    hazard_before = jnp.zeros((1, 128), F32)
    for b in reversed(range(ex)):
        plain, scaled, square = placed[b, :kf], placed[b, kf : 2 * kf], placed[b, 2 * kf + 1 : 2 * kf + 2]
        own_later = own_later + jnp.where(b > me, plain, 0.0)
        before = before + jnp.where(b < me, scaled + square * later, 0.0)
        hazard_before = hazard_before + jnp.where(b < me, placed[b, 2 * kf : 2 * kf + 1], 0.0)
        later = later + plain
    own_later = jnp.sum(own_later, axis=1, keepdims=True)
    before = jnp.sum(before, axis=1, keepdims=True)
    hazard_before = hazard_before[:, :1]
    value = tangent[...] * (cumulative[...] + hazard_before) - (local[...] + squares[...] * own_later + before)
    weighted[...] = (risk[...] * value).astype(BF16)


def weights(messages, tangent, local, risk, cumulative, squares):
    ex = len(messages)
    return pl.pallas_call(
        functools.partial(weight_kernel, ex),
        in_specs=[VMEM] * (ex + 5),
        out_shape=jax.ShapeDtypeStruct(tangent.shape, BF16),
        out_specs=VMEM,
        scratch_shapes=[pltpu.VMEM((ex,) + messages[0].shape, F32)],
        compiler_params=pltpu.CompilerParams(**PARAMS),
        name="weights",
    )(*messages, tangent, local, risk, cumulative, squares)


def encode(values, message):
    height = values.shape[0]
    block = min(BLOCK, height)
    powers = []
    for start in range(0, height, block):
        part = values[start : start + block]
        largest = jnp.max(jnp.abs(part), axis=0, keepdims=True)
        power = power_of(largest)
        message[start : start + block] = to_short(part * jnp.exp2(-power))
        powers.append(power)
    powers.append(jnp.zeros((message.shape[0] - height - len(powers), values.shape[1]), F32))
    message[height:] = to_short(jnp.concatenate(powers, axis=0))


def decode(message, height):
    block = min(BLOCK, height)
    powers = from_short(message[height:])
    parts = []
    for i in range(height // block):
        part = from_short(message[i * block : (i + 1) * block])
        parts.append(part * jnp.exp2(powers[i : i + 1]))
    return jnp.concatenate(parts, axis=0)


def gradient_kernel(feat, kf, start, *refs):
    parts, dosages, out, weighted = refs[:feat], refs[feat], refs[feat + 1], refs[feat + 2]
    width = out.shape[0] - 16
    me = lax.axis_index("feat")
    for i in range(feat):
        weighted[pl.ds(pl.multiple_of((me ^ i) * kf, kf), kf), :] = parts[i][...]
    total = jnp.dot(weighted[...], dosages[:, start : start + width], preferred_element_type=F32)
    encode(total.T, out)


def gradients(parts, dosages, start, variants):
    feat = len(parts)
    kf, persons = parts[0].shape
    k = kf * feat
    return pl.pallas_call(
        functools.partial(gradient_kernel, feat, kf, start),
        in_specs=[VMEM] * (feat + 1),
        out_shape=jax.ShapeDtypeStruct((variants + 16, k), jnp.int16),
        out_specs=VMEM,
        scratch_shapes=[pltpu.VMEM((k, persons), BF16)],
        compiler_params=pltpu.CompilerParams(**PARAMS),
        cost_estimate=pl.CostEstimate(
            flops=2 * persons * variants * k, bytes_accessed=persons * (variants * 2 + k * 2), transcendentals=0
        ),
        name="gradients",
    )(*parts, dosages)


def merge_kernel(mine, other, out):
    height = mine.shape[0] - 16
    encode(decode(mine, height) + decode(other, height), out)


def merge(mine, other):
    return pl.pallas_call(
        merge_kernel,
        in_specs=[VMEM] * 2,
        out_shape=jax.ShapeDtypeStruct(mine.shape, jnp.int16),
        out_specs=VMEM,
        compiler_params=pltpu.CompilerParams(**PARAMS),
        name="merge",
    )(mine, other)


def finish_kernel(parts, *refs):
    mine, other, count = refs[:parts], refs[parts : 2 * parts], refs[2 * parts]
    out, total, sems = refs[2 * parts + 1 :]
    step = mine[0].shape[0] - 16
    block = min(BLOCK, step)
    scale = count[1:2, 0:1]
    copies = []
    for i in range(parts):
        messages = (mine[i], other[i])
        powers = [jnp.exp2(from_short(message[step:])) for message in messages]
        for j in range(step // block):
            at = slice(j * block, (j + 1) * block)
            terms = [from_short(m[at]) * p[j : j + 1] for m, p in zip(messages, powers)]
            total[i * step + j * block : i * step + (j + 1) * block] = (terms[0] + terms[1]) / scale
        copies.append(
            pltpu.make_async_copy(
                total.at[pl.ds(i * step, step)], out.at[pl.ds(i * step, step)], sems.at[i]
            )
        )
        copies[i].start()
    for copy in copies:
        copy.wait()


def finish(mine, other, count):
    parts = len(mine)
    height, k = parts * (mine[0].shape[0] - 16), mine[0].shape[1]
    return pl.pallas_call(
        functools.partial(finish_kernel, parts),
        in_specs=[VMEM] * (2 * parts + 1),
        out_shape=jax.ShapeDtypeStruct((height, k), F32),
        out_specs=HBM,
        scratch_shapes=[pltpu.VMEM((height, k), F32), pltpu.SemaphoreType.DMA((parts,))],
        compiler_params=pltpu.CompilerParams(**PARAMS),
        name="finish",
    )(*mine, *other, count)


def local(dosages, coefficients, directions, event_rank, events):
    feat, ex = lax.axis_size("feat"), lax.axis_size("ex")
    rows = dosages.shape[0]
    variants, k = directions.shape
    each = k // feat
    padded = -(-each // 16) * 16
    if padded != each:
        directions = jnp.pad(directions.reshape(variants, feat, each), ((0, 0), (0, 0), (0, padded - each)))
        directions = directions.reshape(variants, feat * padded)
    rank, event_row = event_rank[None], events[None]

    linear, keep, send = products(dosages, coefficients, directions, feat)
    order = list(reversed(range(1, feat // 2)))
    received = {q: swap(send[q], "feat", 1) for q in order + [0]}
    paired = pair(linear, received[order[0]])
    middle = rows // 2
    firsts = [
        swap(join(keep[q], received[q], 0, middle, paired, []), "feat", 2 * q) for q in order
    ]
    rests = [
        swap(join(keep[q], received[q], middle, middle, paired, [received[0]]), "feat", 2 * q)
        for q in order
    ]
    table = tables(rank, paired, rows)

    risk, sums, ordered_events, total = risks(paired, firsts, rank, event_row, table, rows)
    later = jnp.zeros_like(total)
    bit = 1
    while bit < ex:
        total, later = ranges(bit, total, swap(total, "ex", bit), later, rests if bit == 1 else [])
        bit *= 2
    tangent, later_sums, plain = suffix_sums(keep[0], received[0], firsts + rests, risk, rank, table)
    hazard, ordered_squares, message = shares(later, sums, ordered_events, plain, later_sums)
    messages = [message] + [swap(message, "ex", i) for i in range(1, ex)]
    cumulative, squares = hazards(hazard, ordered_squares, rank, rows)
    summed = prefix_sums(later_sums, ordered_squares, rank, padded)
    own = weights(messages, tangent, summed, risk, cumulative, squares)

    chips = {0: own}
    for q in reversed(range(1, feat // 2)):
        chips[q] = swap(own, "feat", 2 * q)
    parts = []
    for q in range(feat // 2):
        parts += [chips[q], swap(chips[q], "feat", 1)]

    half = variants // 2
    partial_sums = [gradients(parts, dosages, start, half) for start in (0, half)]
    bit = 1
    while 2 * bit < ex:
        received = [swap(message, "ex", bit) for message in partial_sums]
        partial_sums = [merge(mine, other) for mine, other in zip(partial_sums, received)]
        bit *= 2
    received = [swap(message, "ex", bit) for message in partial_sums]
    result = finish(partial_sums, received, total)
    if padded != each:
        result = result.reshape(variants, feat, padded)[:, :, :each].reshape(variants, k)
    return result


def solution(mesh):
    placed = (P("ex", "feat"), P("feat"), P("feat", None), P("ex"), P("ex"))
    return jax.shard_map(
        local, mesh=mesh, in_specs=placed, out_specs=P("feat", None), check_vma=False
    )
```

```python
import functools

import jax
import jax.numpy as jnp
from jax import lax
from jax.experimental import pallas as pl
from jax.experimental.pallas import tpu as pltpu
from jax.sharding import PartitionSpec as P

F32 = jnp.float32
BF16 = jnp.bfloat16
LO = 256
NT = (((1,), (1,)), ((), ()))
BLOCK = 64
SPAN = 512
VMEM = pl.BlockSpec(memory_space=pltpu.VMEM)
HBM = pl.BlockSpec(memory_space=pltpu.HBM)
PARAMS = dict(vmem_limit_bytes=24 * 1024 * 1024)


def swap(x, axis, i):
    count = lax.axis_size(axis)
    return lax.ppermute(x, axis, [(s, s ^ i) for s in range(count)])


def split_two(x):
    high = x.astype(BF16).astype(F32)
    return high, x - high


def split_three(x):
    first, rest = split_two(x)
    second, third = split_two(rest)
    return first, second, third


def one_hot(values, count, kind=BF16):
    shape = (count, values.shape[1])
    return jnp.where(lax.broadcasted_iota(jnp.int32, shape, 0) == values, 1.0, 0.0).astype(kind)


def triangle(n, keep):
    first = lax.broadcasted_iota(jnp.int32, (n, n), 0)
    second = lax.broadcasted_iota(jnp.int32, (n, n), 1)
    return jnp.where(keep(first, second), 1.0, 0.0)


def stacked(parts):
    return jnp.concatenate(parts, axis=0).astype(BF16)


def unstacked(values, count):
    height = values.shape[0] // count
    return sum(values[i * height : (i + 1) * height] for i in range(count))


def dot_binary(a, b):
    parts = jnp.dot(stacked(split_three(a)), b.astype(BF16), preferred_element_type=F32)
    return unstacked(parts, 3)


def binary_dot(a, b):
    a = a.astype(BF16)
    total = None
    for part in split_three(b):
        term = jnp.dot(a, part.astype(BF16), preferred_element_type=F32)
        total = term if total is None else total + term
    return total


def product_kernel(feat, kf, chunk, directions, coefficients, dosages, *refs):
    linear, keep, send = refs[0], refs[1 : 1 + feat // 2], refs[1 + feat // 2 : 1 + feat]
    table, own_directions, own_coefficients, lhs, turned, sems = refs[1 + feat :]
    me = lax.axis_index("feat")
    width = feat * kf
    persons, variants = table.shape
    steps = persons // chunk
    small = [
        pltpu.make_async_copy(directions, own_directions, sems.at[steps]),
        pltpu.make_async_copy(coefficients, own_coefficients, sems.at[steps + 1]),
    ]
    large = [
        pltpu.make_async_copy(
            dosages.at[pl.ds(i * chunk, chunk)], table.at[pl.ds(i * chunk, chunk)], sems.at[i]
        )
        for i in range(steps)
    ]
    for copy in small + large:
        copy.start()
    for copy in small:
        copy.wait()
    turned[...] = own_directions[...].astype(F32).T.reshape(turned.shape)
    for j in range(feat):
        lhs[j * kf : (j + 1) * kf] = turned[me ^ j].astype(BF16)
    lhs[width:] = jnp.broadcast_to(own_coefficients[...].astype(F32)[None, :], (16, variants)).astype(BF16)
    for i in range(steps):
        large[i].wait()
        first = i * chunk
        result = lax.dot_general(
            lhs[...], table[first : first + chunk], NT, preferred_element_type=F32
        )
        for j in range(feat):
            (send if j % 2 else keep)[j // 2][:, first : first + chunk] = result[j * kf : (j + 1) * kf]
        for start in range(0, chunk, LO):
            row = result[width : width + 1, start : start + LO]
            group = (first + start) // LO
            linear[group : group + 1, :] = row
            send[-1][group : group + 1, persons:] = row


def products(dosages, coefficients, directions, feat):
    persons, variants = dosages.shape
    k = directions.shape[1]
    kf = k // feat
    chunk = min(512, persons)
    piece = jax.ShapeDtypeStruct((kf, persons), F32)
    first = jax.ShapeDtypeStruct((kf, persons + LO), F32)
    out = pl.pallas_call(
        functools.partial(product_kernel, feat, kf, chunk),
        in_specs=[HBM, HBM, HBM],
        out_shape=[jax.ShapeDtypeStruct((kf, LO), F32)]
        + [piece] * (feat - 1)
        + [first],
        out_specs=[VMEM] * (feat + 1),
        scratch_shapes=[
            pltpu.VMEM((persons, variants), BF16),
            pltpu.VMEM((variants, k), BF16),
            pltpu.VMEM((variants,), BF16),
            pltpu.VMEM((k + 16, variants), BF16),
            pltpu.VMEM((feat, kf, variants), F32),
            pltpu.SemaphoreType.DMA((persons // chunk + 2,)),
        ],
        compiler_params=pltpu.CompilerParams(**PARAMS),
        cost_estimate=pl.CostEstimate(
            flops=2 * persons * variants * k, bytes_accessed=persons * (variants * 2 + k * 4), transcendentals=0
        ),
        name="products",
    )(*[pltpu.with_memory_space_constraint(x, pltpu.HBM) for x in (directions, coefficients, dosages)])
    return out[0], out[1 : 1 + feat // 2], out[1 + feat // 2 :]


def power_of(largest):
    return jnp.ceil(jnp.log2(jnp.maximum(largest, 1e-30))) - 14.0


def to_short(values):
    return jnp.round(values).astype(jnp.int32).astype(jnp.int16)


def from_short(values):
    return values.astype(jnp.int32).astype(F32)


def pair_kernel(linear, received, out):
    out[...] = linear[...] + received[:, received.shape[1] - LO :]


def pair(linear, received):
    return pl.pallas_call(
        pair_kernel,
        in_specs=[VMEM] * 2,
        out_shape=jax.ShapeDtypeStruct(linear.shape, F32),
        out_specs=VMEM,
        compiler_params=pltpu.CompilerParams(**PARAMS),
        name="pair",
    )(linear, received)


def join_kernel(start, width, mine, other, *refs):
    linear, out = refs[0], refs[-1]
    kf = mine.shape[0]
    span = min(SPAN, width)
    lane = lax.broadcasted_iota(jnp.int32, (kf, 128), 1)
    powers = jnp.zeros((kf, 128), F32)
    for i in range(width // span):
        at = slice(start + i * span, start + (i + 1) * span)
        total = mine[:, at] + other[:, at]
        power = power_of(jnp.max(jnp.abs(total), axis=1, keepdims=True))
        out[:, i * span : (i + 1) * span] = to_short(total * jnp.exp2(-power))
        powers = jnp.where(lane == i, power, powers)
    if start == 0:
        power = power_of(jnp.max(jnp.abs(linear[...]), axis=1, keepdims=True))
        scaled = linear[...] * jnp.exp2(-power)
        whole = jnp.round(scaled)
        out[:, width : width + LO] = to_short(whole)
        out[:, width + LO : width + 2 * LO] = to_short((scaled - whole) * 32768.0)
        powers = jnp.where(lane == 127, power, powers)
    out[:, out.shape[1] - 128 :] = to_short(powers)


def join(keep, received, start, width, linear, waited):
    kf, rows = keep.shape
    extra = 2 * LO if start == 0 else 0
    return pl.pallas_call(
        functools.partial(join_kernel, start, width),
        in_specs=[VMEM] * 3 + [pl.BlockSpec(memory_space=pl.ANY)] * len(waited),
        out_shape=jax.ShapeDtypeStruct((kf, width + extra + 128), jnp.int16),
        out_specs=VMEM,
        compiler_params=pltpu.CompilerParams(**PARAMS),
        name="join",
    )(keep, received, linear, *waited)


def table_kernel(rows, rank, waited, table):
    chunk = min(512, rows)
    lane = lax.broadcasted_iota(jnp.int32, (chunk, 128), 1)
    for start in range(0, rows, chunk):
        at = slice(start, start + chunk)
        inner = lax.rem(rank[:, at], LO)
        column = jnp.broadcast_to(inner.astype(F32), (128, chunk)).T.astype(jnp.int32)
        for first in range(0, LO, 128):
            table[at, first : first + 128] = jnp.where(column == lane + first, 1.0, 0.0).astype(BF16)


def tables(rank, waited, rows):
    return pl.pallas_call(
        functools.partial(table_kernel, rows),
        in_specs=[VMEM, pl.BlockSpec(memory_space=pl.ANY)],
        out_shape=jax.ShapeDtypeStruct((rows, LO), BF16),
        out_specs=VMEM,
        compiler_params=pltpu.CompilerParams(**PARAMS),
        cost_estimate=pl.CostEstimate(flops=rows * LO * 8, bytes_accessed=rows * LO * 2, transcendentals=0),
        name="tables",
    )(rank, waited)


def risk_kernel(rows, parts, linear, *refs):
    messages, (rank, events, table) = refs[:parts], refs[parts : parts + 3]
    risk_out, sums_out, events_out, message = refs[-4:]
    groups = rows // LO
    total = linear[...]
    for part in messages:
        end = part.shape[1] - 128
        power = from_short(part[:, end:])[:, 127:]
        high, low = from_short(part[:, end - 2 * LO : end - LO]), from_short(part[:, end - LO : end])
        total = total + (high + low * (1.0 / 32768.0)) * jnp.exp2(power)
    risk = jnp.exp(total)
    for g in range(groups):
        risk_out[:, g * LO : (g + 1) * LO] = risk[g : g + 1]
    mask = one_hot(lax.rem(rank[...], rows) // LO, groups, F32)
    pieces = [mask * part for part in split_three(risk_out[...])] + [mask * events[...].astype(F32)]
    lhs = jnp.concatenate(pieces, axis=0).astype(BF16)
    sorted_all = jnp.dot(lhs, table[...], preferred_element_type=F32)
    ordered = sorted_all[:groups] + sorted_all[groups : 2 * groups] + sorted_all[2 * groups : 3 * groups]
    happened = sorted_all[3 * groups :]
    inside = dot_binary(ordered, triangle(LO, lambda a, b: a >= b))
    totals = jnp.broadcast_to(inside[:, :1], inside.shape)
    carried = binary_dot(triangle(groups, lambda a, b: a < b), totals)
    sums_out[...] = inside + carried
    events_out[...] = happened
    everything = jnp.sum(totals, axis=0, keepdims=True)[:, :128]
    count = jnp.sum(dot_binary(happened, jnp.ones((LO, 128), F32)), axis=0, keepdims=True)
    message[...] = jnp.concatenate([everything, count, jnp.zeros((6, 128), F32)], axis=0)


def risks(linear, messages, rank, events, table, rows):
    groups = rows // LO
    return pl.pallas_call(
        functools.partial(risk_kernel, rows, len(messages)),
        in_specs=[VMEM] * (len(messages) + 4),
        out_shape=[
            jax.ShapeDtypeStruct((1, rows), F32),
            jax.ShapeDtypeStruct((groups, LO), F32),
            jax.ShapeDtypeStruct((groups, LO), F32),
            jax.ShapeDtypeStruct((8, 128), F32),
        ],
        out_specs=[VMEM] * 4,
        compiler_params=pltpu.CompilerParams(**PARAMS),
        cost_estimate=pl.CostEstimate(flops=rows * LO * 128, bytes_accessed=rows * 64, transcendentals=rows),
        name="risks",
    )(linear, *messages, rank, events, table)


def share_kernel(later, sums, events, plain, ordered, hazard_out, squares, message):
    kf = plain.shape[0]
    groups = sums.shape[0]
    risk_sum = sums[...] + later[0:1, 0:1]
    hazard = events[...] / risk_sum
    square = events[...] / (risk_sum * risk_sum)
    hazard_out[...] = hazard
    squares[...] = square
    scaled = jnp.zeros((kf, LO), F32)
    for g in range(groups):
        scaled = scaled + ordered[g * kf : (g + 1) * kf] * square[g : g + 1]
    message[:kf] = plain[...]
    message[kf : 2 * kf] = sum(scaled[:, start : start + 128] for start in range(0, LO, 128))
    totals = [jnp.sum(jnp.sum(v, axis=0, keepdims=True), axis=1, keepdims=True) for v in (hazard, square)]
    rows = [jnp.broadcast_to(v, (1, 128)) for v in totals]
    message[2 * kf :] = jnp.concatenate(rows + [jnp.zeros((6, 128), F32)], axis=0)


def shares(later, sums, events, plain, ordered):
    flat = jax.ShapeDtypeStruct(sums.shape, F32)
    return pl.pallas_call(
        share_kernel,
        in_specs=[VMEM] * 5,
        out_shape=[flat, flat, jax.ShapeDtypeStruct((2 * plain.shape[0] + 8, 128), F32)],
        out_specs=[VMEM] * 3,
        compiler_params=pltpu.CompilerParams(**PARAMS),
        name="shares",
    )(later, sums, events, plain, ordered)


def hazard_kernel(rows, hazard, square, rank, cumulative, squares):
    groups = rows // LO
    inside = dot_binary(
        jnp.concatenate([hazard[...], square[...]], axis=0), triangle(LO, lambda a, b: a <= b)
    )
    totals = jnp.broadcast_to(inside[:, LO - 1 :], (2 * groups, 128))
    place = lax.rem(rank[...], rows)
    mask = one_hot(place // LO, groups, F32)
    placed = dot_binary(inside, one_hot(lax.rem(place, LO), LO))
    before = triangle(groups, lambda a, b: a > b)
    for first, out in ((0, cumulative), (groups, squares)):
        carried = binary_dot(before, totals[first : first + groups])[:, :1]
        out[...] = jnp.sum(mask * (placed[first : first + groups] + carried), axis=0, keepdims=True)


def hazards(hazard, square, rank, rows):
    row = jax.ShapeDtypeStruct((1, rows), F32)
    return pl.pallas_call(
        functools.partial(hazard_kernel, rows),
        in_specs=[VMEM] * 3,
        out_shape=[row, row],
        out_specs=[VMEM] * 2,
        compiler_params=pltpu.CompilerParams(**PARAMS),
        cost_estimate=pl.CostEstimate(flops=rows * LO * 200, bytes_accessed=rows * 64, transcendentals=0),
        name="hazards",
    )(hazard, square, rank)


def range_kernel(bit, count, *refs):
    total, other, later = refs[:3]
    total_out, later_out = refs[3 + count :]
    is_later = (lax.axis_index("ex") & bit) == 0
    later_out[...] = later[...] + jnp.where(is_later, other[...], 0.0)
    total_out[...] = total[...] + other[...]


def ranges(bit, total, other, later, waited):
    return pl.pallas_call(
        functools.partial(range_kernel, bit, len(waited)),
        in_specs=[VMEM] * 3 + [pl.BlockSpec(memory_space=pl.ANY)] * len(waited),
        out_shape=[jax.ShapeDtypeStruct(total.shape, F32)] * 2,
        out_specs=[VMEM] * 2,
        compiler_params=pltpu.CompilerParams(**PARAMS),
        name="ranges",
    )(total, other, later, *waited)


def suffix_kernel(parts, own, other, *refs):
    messages, (risk, rank, table) = refs[:parts], refs[parts : parts + 3]
    tangent_out, sums, plain, lhs = refs[parts + 3 :]
    kf, rows = own.shape
    folded = jnp.zeros((kf, 128), F32)
    groups = rows // LO
    span = min(SPAN, rows)
    powers = [jnp.exp2(from_short(part[:, part.shape[1] - 128 :])) for part in messages]
    later = len(messages) // 2
    half = messages[0].shape[1] - 2 * LO - 128
    for i in range(rows // span):
        at = slice(i * span, (i + 1) * span)
        tangent = own[:, at] + other[:, at]
        first = 0 if i * span < half else later
        here = i - (first and half // span)
        for part, power in zip(messages[first : first + later], powers[first : first + later]):
            tangent = tangent + from_short(part[:, here * span : (here + 1) * span]) * power[:, here : here + 1]
        tangent_out[:, at] = tangent
        weighted = tangent * risk[:, at]
        folded = folded + sum(weighted[:, j : j + 128] for j in range(0, span, 128))
        high, low = split_two(weighted)
        high, low = high.astype(BF16), low.astype(BF16)
        group = jnp.broadcast_to(lax.rem(rank[:, at], rows) // LO, (kf, span))
        for g in range(groups):
            mask = jnp.where(group == g, 1.0, 0.0).astype(BF16)
            lhs[2 * g * kf : (2 * g + 1) * kf, at] = high * mask
            lhs[(2 * g + 1) * kf : (2 * g + 2) * kf, at] = low * mask
    plain[...] = folded
    ordered = jnp.dot(lhs[...], table[...], preferred_element_type=F32)
    ordered = jnp.concatenate(
        [
            ordered[2 * g * kf : (2 * g + 1) * kf] + ordered[(2 * g + 1) * kf : (2 * g + 2) * kf]
            for g in range(groups)
        ],
        axis=0,
    )
    inside = dot_binary(ordered, triangle(LO, lambda a, b: a >= b))
    carried = jnp.zeros((kf, 1), F32)
    for g in reversed(range(groups)):
        rows_of = slice(g * kf, (g + 1) * kf)
        sums[rows_of] = inside[rows_of] + carried
        carried = carried + inside[rows_of, :1]


def suffix_sums(own, other, messages, risk, rank, table):
    kf, rows = own.shape
    groups = rows // LO
    return pl.pallas_call(
        functools.partial(suffix_kernel, len(messages)),
        in_specs=[VMEM] * (len(messages) + 5),
        out_shape=[
            jax.ShapeDtypeStruct((kf, rows), F32),
            jax.ShapeDtypeStruct((groups * kf, LO), F32),
            jax.ShapeDtypeStruct((kf, 128), F32),
        ],
        out_specs=[VMEM] * 3,
        scratch_shapes=[pltpu.VMEM((groups * 2 * kf, rows), BF16)],
        compiler_params=pltpu.CompilerParams(**PARAMS),
        cost_estimate=pl.CostEstimate(
            flops=2 * rows * LO * groups * 2 * kf, bytes_accessed=rows * kf * 24, transcendentals=0
        ),
        name="suffix_sums",
    )(own, other, *messages, risk, rank, table)


def prefix_kernel(sums, squares, rank, out):
    kf, rows = out.shape
    groups = squares.shape[0]
    chunk = min(512, rows)
    hazard = [sums[g * kf : (g + 1) * kf] * squares[g : g + 1, :] for g in range(groups)]
    inside = dot_binary(jnp.concatenate(hazard, axis=0), triangle(LO, lambda a, b: a <= b))
    carried = jnp.zeros((kf, 1), F32)
    summed = [None] * groups
    for g in range(groups):
        rows_of = slice(g * kf, (g + 1) * kf)
        summed[g] = inside[rows_of] + carried
        carried = carried + inside[rows_of, LO - 1 :]
    both = stacked(split_two(jnp.concatenate(summed, axis=0)))
    for start in range(0, rows, chunk):
        at = slice(start, start + chunk)
        place = lax.rem(rank[:, at], rows)
        group = place // LO
        spread = one_hot(lax.rem(place, LO), LO)
        placed = unstacked(jnp.dot(both, spread, preferred_element_type=F32), 2)
        picked = jnp.zeros((kf, chunk), F32)
        for g in range(groups):
            picked = picked + jnp.where(group == g, placed[g * kf : (g + 1) * kf], 0.0)
        out[:, at] = picked


def prefix_sums(sums, squares, rank, kf):
    rows = rank.shape[1]
    return pl.pallas_call(
        prefix_kernel,
        in_specs=[VMEM] * 3,
        out_shape=jax.ShapeDtypeStruct((kf, rows), F32),
        out_specs=VMEM,
        compiler_params=pltpu.CompilerParams(**PARAMS),
        cost_estimate=pl.CostEstimate(
            flops=4 * rows * LO * (rows // LO) * kf, bytes_accessed=rows * kf * 24, transcendentals=0
        ),
        name="prefix_sums",
    )(sums, squares, rank)


def weight_kernel(ex, *refs):
    messages, (tangent, local, risk, cumulative, squares) = refs[:ex], refs[ex : ex + 5]
    weighted, placed = refs[ex + 5 :]
    kf = tangent.shape[0]
    me = lax.axis_index("ex")
    for i in range(ex):
        placed[me ^ i] = messages[i][...]
    later = jnp.zeros((kf, 128), F32)
    own_later, before = later, later
    hazard_before = jnp.zeros((1, 128), F32)
    for b in reversed(range(ex)):
        plain, scaled, square = placed[b, :kf], placed[b, kf : 2 * kf], placed[b, 2 * kf + 1 : 2 * kf + 2]
        own_later = own_later + jnp.where(b > me, plain, 0.0)
        before = before + jnp.where(b < me, scaled + square * later, 0.0)
        hazard_before = hazard_before + jnp.where(b < me, placed[b, 2 * kf : 2 * kf + 1], 0.0)
        later = later + plain
    own_later = jnp.sum(own_later, axis=1, keepdims=True)
    before = jnp.sum(before, axis=1, keepdims=True)
    hazard_before = hazard_before[:, :1]
    value = tangent[...] * (cumulative[...] + hazard_before) - (local[...] + squares[...] * own_later + before)
    weighted[...] = (risk[...] * value).astype(BF16)


def weights(messages, tangent, local, risk, cumulative, squares):
    ex = len(messages)
    return pl.pallas_call(
        functools.partial(weight_kernel, ex),
        in_specs=[VMEM] * (ex + 5),
        out_shape=jax.ShapeDtypeStruct(tangent.shape, BF16),
        out_specs=VMEM,
        scratch_shapes=[pltpu.VMEM((ex,) + messages[0].shape, F32)],
        compiler_params=pltpu.CompilerParams(**PARAMS),
        name="weights",
    )(*messages, tangent, local, risk, cumulative, squares)


def encode(values, message):
    height = values.shape[0]
    block = min(BLOCK, height)
    powers = []
    for start in range(0, height, block):
        part = values[start : start + block]
        largest = jnp.max(jnp.abs(part), axis=0, keepdims=True)
        power = power_of(largest)
        message[start : start + block] = to_short(part * jnp.exp2(-power))
        powers.append(power)
    powers.append(jnp.zeros((message.shape[0] - height - len(powers), values.shape[1]), F32))
    message[height:] = to_short(jnp.concatenate(powers, axis=0))


def decode(message, height):
    block = min(BLOCK, height)
    powers = from_short(message[height:])
    parts = []
    for i in range(height // block):
        part = from_short(message[i * block : (i + 1) * block])
        parts.append(part * jnp.exp2(powers[i : i + 1]))
    return jnp.concatenate(parts, axis=0)


def gradient_kernel(feat, kf, start, *refs):
    parts, dosages, out, weighted = refs[:feat], refs[feat], refs[feat + 1], refs[feat + 2]
    width = out.shape[0] - 16
    me = lax.axis_index("feat")
    for i in range(feat):
        weighted[pl.ds(pl.multiple_of((me ^ i) * kf, kf), kf), :] = parts[i][...]
    total = jnp.dot(weighted[...], dosages[:, start : start + width], preferred_element_type=F32)
    encode(total.T, out)


def gradients(parts, dosages, start, variants):
    feat = len(parts)
    kf, persons = parts[0].shape
    k = kf * feat
    return pl.pallas_call(
        functools.partial(gradient_kernel, feat, kf, start),
        in_specs=[VMEM] * (feat + 1),
        out_shape=jax.ShapeDtypeStruct((variants + 16, k), jnp.int16),
        out_specs=VMEM,
        scratch_shapes=[pltpu.VMEM((k, persons), BF16)],
        compiler_params=pltpu.CompilerParams(**PARAMS),
        cost_estimate=pl.CostEstimate(
            flops=2 * persons * variants * k, bytes_accessed=persons * (variants * 2 + k * 2), transcendentals=0
        ),
        name="gradients",
    )(*parts, dosages)


def merge_kernel(mine, other, out):
    height = mine.shape[0] - 16
    encode(decode(mine, height) + decode(other, height), out)


def merge(mine, other):
    return pl.pallas_call(
        merge_kernel,
        in_specs=[VMEM] * 2,
        out_shape=jax.ShapeDtypeStruct(mine.shape, jnp.int16),
        out_specs=VMEM,
        compiler_params=pltpu.CompilerParams(**PARAMS),
        name="merge",
    )(mine, other)


def finish_kernel(parts, *refs):
    mine, other, count = refs[:parts], refs[parts : 2 * parts], refs[2 * parts]
    out, total, sems = refs[2 * parts + 1 :]
    step = mine[0].shape[0] - 16
    block = min(BLOCK, step)
    scale = count[1:2, 0:1]
    copies = []
    for i in range(parts):
        messages = (mine[i], other[i])
        powers = [jnp.exp2(from_short(message[step:])) for message in messages]
        for j in range(step // block):
            at = slice(j * block, (j + 1) * block)
            terms = [from_short(m[at]) * p[j : j + 1] for m, p in zip(messages, powers)]
            total[i * step + j * block : i * step + (j + 1) * block] = (terms[0] + terms[1]) / scale
        copies.append(
            pltpu.make_async_copy(
                total.at[pl.ds(i * step, step)], out.at[pl.ds(i * step, step)], sems.at[i]
            )
        )
        copies[i].start()
    for copy in copies:
        copy.wait()


def finish(mine, other, count):
    parts = len(mine)
    height, k = parts * (mine[0].shape[0] - 16), mine[0].shape[1]
    return pl.pallas_call(
        functools.partial(finish_kernel, parts),
        in_specs=[VMEM] * (2 * parts + 1),
        out_shape=jax.ShapeDtypeStruct((height, k), F32),
        out_specs=HBM,
        scratch_shapes=[pltpu.VMEM((height, k), F32), pltpu.SemaphoreType.DMA((parts,))],
        compiler_params=pltpu.CompilerParams(**PARAMS),
        name="finish",
    )(*mine, *other, count)


def local(dosages, coefficients, directions, event_rank, events):
    feat, ex = lax.axis_size("feat"), lax.axis_size("ex")
    rows = dosages.shape[0]
    variants, k = directions.shape
    each = k // feat
    padded = -(-each // 16) * 16
    if padded != each:
        directions = jnp.pad(directions.reshape(variants, feat, each), ((0, 0), (0, 0), (0, padded - each)))
        directions = directions.reshape(variants, feat * padded)
    rank, event_row = event_rank[None], events[None]

    linear, keep, send = products(dosages, coefficients, directions, feat)
    order = list(reversed(range(1, feat // 2)))
    received = {q: swap(send[q], "feat", 1) for q in order + [0]}
    paired = pair(linear, received[order[0]])
    middle = min(SPAN, rows // 2)
    firsts = [
        swap(join(keep[q], received[q], 0, middle, paired, []), "feat", 2 * q) for q in order
    ]
    table = tables(rank, paired, rows)

    risk, sums, ordered_events, total = risks(paired, firsts, rank, event_row, table, rows)
    rests = [
        swap(join(keep[q], received[q], middle, rows - middle, paired, [received[0], total]), "feat", 2 * q)
        for q in order
    ]
    later = jnp.zeros_like(total)
    bit = 1
    while bit < ex:
        total, later = ranges(bit, total, swap(total, "ex", bit), later, rests if 2 * bit == ex else [])
        bit *= 2
    tangent, later_sums, plain = suffix_sums(keep[0], received[0], firsts + rests, risk, rank, table)
    hazard, ordered_squares, message = shares(later, sums, ordered_events, plain, later_sums)
    messages = [message] + [swap(message, "ex", i) for i in range(1, ex)]
    cumulative, squares = hazards(hazard, ordered_squares, rank, rows)
    summed = prefix_sums(later_sums, ordered_squares, rank, padded)
    own = weights(messages, tangent, summed, risk, cumulative, squares)

    chips = {0: own}
    for q in reversed(range(1, feat // 2)):
        chips[q] = swap(own, "feat", 2 * q)
    parts = []
    for q in range(feat // 2):
        parts += [chips[q], swap(chips[q], "feat", 1)]

    half = variants // 2
    partial_sums = [gradients(parts, dosages, start, half) for start in (0, half)]
    bit = 1
    while 2 * bit < ex:
        received = [swap(message, "ex", bit) for message in partial_sums]
        partial_sums = [merge(mine, other) for mine, other in zip(partial_sums, received)]
        bit *= 2
    received = [swap(message, "ex", bit) for message in partial_sums]
    result = finish(partial_sums, received, total)
    if padded != each:
        result = result.reshape(variants, feat, padded)[:, :, :each].reshape(variants, k)
    return result


def solution(mesh):
    placed = (P("ex", "feat"), P("feat"), P("feat", None), P("ex"), P("ex"))
    return jax.shard_map(
        local, mesh=mesh, in_specs=placed, out_specs=P("feat", None), check_vma=False
    )
```

```python
import functools

import jax
import jax.numpy as jnp
from jax import lax
from jax.experimental import pallas as pl
from jax.experimental.pallas import tpu as pltpu
from jax.sharding import PartitionSpec as P

F32 = jnp.float32
BF16 = jnp.bfloat16
LO = 256
NT = (((1,), (1,)), ((), ()))
BLOCK = 64
SPAN = 512
AHEAD = 3
VMEM = pl.BlockSpec(memory_space=pltpu.VMEM)
HBM = pl.BlockSpec(memory_space=pltpu.HBM)
PARAMS = dict(vmem_limit_bytes=24 * 1024 * 1024)


def swap(x, axis, i):
    count = lax.axis_size(axis)
    return lax.ppermute(x, axis, [(s, s ^ i) for s in range(count)])


def split_two(x):
    high = x.astype(BF16).astype(F32)
    return high, x - high


def split_three(x):
    first, rest = split_two(x)
    second, third = split_two(rest)
    return first, second, third


def one_hot(values, count, kind=BF16):
    shape = (count, values.shape[1])
    return jnp.where(lax.broadcasted_iota(jnp.int32, shape, 0) == values, 1.0, 0.0).astype(kind)


def triangle(n, keep):
    first = lax.broadcasted_iota(jnp.int32, (n, n), 0)
    second = lax.broadcasted_iota(jnp.int32, (n, n), 1)
    return jnp.where(keep(first, second), 1.0, 0.0)


def stacked(parts):
    return jnp.concatenate(parts, axis=0).astype(BF16)


def unstacked(values, count):
    height = values.shape[0] // count
    return sum(values[i * height : (i + 1) * height] for i in range(count))


def dot_binary(a, b):
    parts = jnp.dot(stacked(split_three(a)), b.astype(BF16), preferred_element_type=F32)
    return unstacked(parts, 3)


def binary_dot(a, b):
    a = a.astype(BF16)
    total = None
    for part in split_three(b):
        term = jnp.dot(a, part.astype(BF16), preferred_element_type=F32)
        total = term if total is None else total + term
    return total


def product_kernel(feat, kf, chunk, directions, coefficients, dosages, *refs):
    linear, keep, send = refs[0], refs[1 : 1 + feat // 2], refs[1 + feat // 2 : 1 + feat]
    table, own_directions, own_coefficients, lhs, turned, sems = refs[1 + feat :]
    me = lax.axis_index("feat")
    width = feat * kf
    persons, variants = table.shape
    steps = persons // chunk
    small = [
        pltpu.make_async_copy(directions, own_directions, sems.at[steps]),
        pltpu.make_async_copy(coefficients, own_coefficients, sems.at[steps + 1]),
    ]
    large = [
        pltpu.make_async_copy(
            dosages.at[pl.ds(i * chunk, chunk)], table.at[pl.ds(i * chunk, chunk)], sems.at[i]
        )
        for i in range(steps)
    ]
    for copy in small + large[:AHEAD]:
        copy.start()
    for copy in small:
        copy.wait()
    turned[...] = own_directions[...].astype(F32).T.reshape(turned.shape)
    for j in range(feat):
        lhs[j * kf : (j + 1) * kf] = turned[me ^ j].astype(BF16)
    lhs[width:] = jnp.broadcast_to(own_coefficients[...].astype(F32)[None, :], (16, variants)).astype(BF16)
    for i in range(steps):
        large[i].wait()
        if i + AHEAD < steps:
            large[i + AHEAD].start()
        first = i * chunk
        result = lax.dot_general(
            lhs[...], table[first : first + chunk], NT, preferred_element_type=F32
        )
        for j in range(feat):
            (send if j % 2 else keep)[j // 2][:, first : first + chunk] = result[j * kf : (j + 1) * kf]
        for start in range(0, chunk, LO):
            row = result[width : width + 1, start : start + LO]
            group = (first + start) // LO
            linear[group : group + 1, :] = row
            send[-1][group : group + 1, persons:] = row


def products(dosages, coefficients, directions, feat):
    persons, variants = dosages.shape
    k = directions.shape[1]
    kf = k // feat
    chunk = min(512, persons)
    piece = jax.ShapeDtypeStruct((kf, persons), F32)
    first = jax.ShapeDtypeStruct((kf, persons + LO), F32)
    out = pl.pallas_call(
        functools.partial(product_kernel, feat, kf, chunk),
        in_specs=[HBM, HBM, HBM],
        out_shape=[jax.ShapeDtypeStruct((kf, LO), F32)]
        + [piece] * (feat - 1)
        + [first],
        out_specs=[VMEM] * (feat + 1),
        scratch_shapes=[
            pltpu.VMEM((persons, variants), BF16),
            pltpu.VMEM((variants, k), BF16),
            pltpu.VMEM((variants,), BF16),
            pltpu.VMEM((k + 16, variants), BF16),
            pltpu.VMEM((feat, kf, variants), F32),
            pltpu.SemaphoreType.DMA((persons // chunk + 2,)),
        ],
        compiler_params=pltpu.CompilerParams(**PARAMS),
        cost_estimate=pl.CostEstimate(
            flops=2 * persons * variants * k, bytes_accessed=persons * (variants * 2 + k * 4), transcendentals=0
        ),
        name="products",
    )(*[pltpu.with_memory_space_constraint(x, pltpu.HBM) for x in (directions, coefficients, dosages)])
    return out[0], out[1 : 1 + feat // 2], out[1 + feat // 2 :]


def power_of(largest):
    return jnp.ceil(jnp.log2(jnp.maximum(largest, 1e-30))) - 14.0


def to_short(values):
    return jnp.round(values).astype(jnp.int32).astype(jnp.int16)


def from_short(values):
    return values.astype(jnp.int32).astype(F32)


def pair_kernel(linear, received, out):
    out[...] = linear[...] + received[:, received.shape[1] - LO :]


def pair(linear, received):
    return pl.pallas_call(
        pair_kernel,
        in_specs=[VMEM] * 2,
        out_shape=jax.ShapeDtypeStruct(linear.shape, F32),
        out_specs=VMEM,
        compiler_params=pltpu.CompilerParams(**PARAMS),
        name="pair",
    )(linear, received)


def join_kernel(start, width, mine, other, *refs):
    linear, out = refs[0], refs[-1]
    kf = mine.shape[0]
    span = min(SPAN, width)
    lane = lax.broadcasted_iota(jnp.int32, (kf, 128), 1)
    powers = jnp.zeros((kf, 128), F32)
    for i in range(width // span):
        at = slice(start + i * span, start + (i + 1) * span)
        total = mine[:, at] + other[:, at]
        power = power_of(jnp.max(jnp.abs(total), axis=1, keepdims=True))
        out[:, i * span : (i + 1) * span] = to_short(total * jnp.exp2(-power))
        powers = jnp.where(lane == i, power, powers)
    if start == 0:
        power = power_of(jnp.max(jnp.abs(linear[...]), axis=1, keepdims=True))
        scaled = linear[...] * jnp.exp2(-power)
        whole = jnp.round(scaled)
        out[:, width : width + LO] = to_short(whole)
        out[:, width + LO : width + 2 * LO] = to_short((scaled - whole) * 32768.0)
        powers = jnp.where(lane == 127, power, powers)
    out[:, out.shape[1] - 128 :] = to_short(powers)


def join(keep, received, start, width, linear, waited):
    kf, rows = keep.shape
    extra = 2 * LO if start == 0 else 0
    return pl.pallas_call(
        functools.partial(join_kernel, start, width),
        in_specs=[VMEM] * 3 + [pl.BlockSpec(memory_space=pl.ANY)] * len(waited),
        out_shape=jax.ShapeDtypeStruct((kf, width + extra + 128), jnp.int16),
        out_specs=VMEM,
        compiler_params=pltpu.CompilerParams(**PARAMS),
        name="join",
    )(keep, received, linear, *waited)


def table_kernel(rows, rank, waited, table):
    chunk = min(512, rows)
    lane = lax.broadcasted_iota(jnp.int32, (chunk, 128), 1)
    for start in range(0, rows, chunk):
        at = slice(start, start + chunk)
        inner = lax.rem(rank[:, at], LO)
        column = jnp.broadcast_to(inner.astype(F32), (128, chunk)).T.astype(jnp.int32)
        for first in range(0, LO, 128):
            table[at, first : first + 128] = jnp.where(column == lane + first, 1.0, 0.0).astype(BF16)


def tables(rank, waited, rows):
    return pl.pallas_call(
        functools.partial(table_kernel, rows),
        in_specs=[VMEM, pl.BlockSpec(memory_space=pl.ANY)],
        out_shape=jax.ShapeDtypeStruct((rows, LO), BF16),
        out_specs=VMEM,
        compiler_params=pltpu.CompilerParams(**PARAMS),
        cost_estimate=pl.CostEstimate(flops=rows * LO * 8, bytes_accessed=rows * LO * 2, transcendentals=0),
        name="tables",
    )(rank, waited)


def risk_kernel(rows, parts, linear, *refs):
    messages, (rank, events, table) = refs[:parts], refs[parts : parts + 3]
    risk_out, sums_out, events_out, message = refs[-4:]
    groups = rows // LO
    total = linear[...]
    for part in messages:
        end = part.shape[1] - 128
        power = from_short(part[:, end:])[:, 127:]
        high, low = from_short(part[:, end - 2 * LO : end - LO]), from_short(part[:, end - LO : end])
        total = total + (high + low * (1.0 / 32768.0)) * jnp.exp2(power)
    risk = jnp.exp(total)
    for g in range(groups):
        risk_out[:, g * LO : (g + 1) * LO] = risk[g : g + 1]
    mask = one_hot(lax.rem(rank[...], rows) // LO, groups, F32)
    pieces = [mask * part for part in split_three(risk_out[...])] + [mask * events[...].astype(F32)]
    lhs = jnp.concatenate(pieces, axis=0).astype(BF16)
    sorted_all = jnp.dot(lhs, table[...], preferred_element_type=F32)
    ordered = sorted_all[:groups] + sorted_all[groups : 2 * groups] + sorted_all[2 * groups : 3 * groups]
    happened = sorted_all[3 * groups :]
    inside = dot_binary(ordered, triangle(LO, lambda a, b: a >= b))
    totals = jnp.broadcast_to(inside[:, :1], inside.shape)
    carried = binary_dot(triangle(groups, lambda a, b: a < b), totals)
    sums_out[...] = inside + carried
    events_out[...] = happened
    everything = jnp.sum(totals, axis=0, keepdims=True)[:, :128]
    count = jnp.sum(dot_binary(happened, jnp.ones((LO, 128), F32)), axis=0, keepdims=True)
    message[...] = jnp.concatenate([everything, count, jnp.zeros((6, 128), F32)], axis=0)


def risks(linear, messages, rank, events, table, rows):
    groups = rows // LO
    return pl.pallas_call(
        functools.partial(risk_kernel, rows, len(messages)),
        in_specs=[VMEM] * (len(messages) + 4),
        out_shape=[
            jax.ShapeDtypeStruct((1, rows), F32),
            jax.ShapeDtypeStruct((groups, LO), F32),
            jax.ShapeDtypeStruct((groups, LO), F32),
            jax.ShapeDtypeStruct((8, 128), F32),
        ],
        out_specs=[VMEM] * 4,
        compiler_params=pltpu.CompilerParams(**PARAMS),
        cost_estimate=pl.CostEstimate(flops=rows * LO * 128, bytes_accessed=rows * 64, transcendentals=rows),
        name="risks",
    )(linear, *messages, rank, events, table)


def share_kernel(later, sums, events, plain, more, ordered, hazard_out, squares, message):
    kf = plain.shape[0]
    groups = sums.shape[0]
    risk_sum = sums[...] + later[0:1, 0:1]
    hazard = events[...] / risk_sum
    square = events[...] / (risk_sum * risk_sum)
    hazard_out[...] = hazard
    squares[...] = square
    scaled = jnp.zeros((kf, LO), F32)
    for g in range(groups):
        scaled = scaled + ordered[g * kf : (g + 1) * kf] * square[g : g + 1]
    message[:kf] = plain[...] + more[...]
    message[kf : 2 * kf] = sum(scaled[:, start : start + 128] for start in range(0, LO, 128))
    totals = [jnp.sum(jnp.sum(v, axis=0, keepdims=True), axis=1, keepdims=True) for v in (hazard, square)]
    rows = [jnp.broadcast_to(v, (1, 128)) for v in totals]
    message[2 * kf :] = jnp.concatenate(rows + [jnp.zeros((6, 128), F32)], axis=0)


def shares(later, sums, events, plain, more, ordered):
    flat = jax.ShapeDtypeStruct(sums.shape, F32)
    return pl.pallas_call(
        share_kernel,
        in_specs=[VMEM] * 6,
        out_shape=[flat, flat, jax.ShapeDtypeStruct((2 * plain.shape[0] + 8, 128), F32)],
        out_specs=[VMEM] * 3,
        compiler_params=pltpu.CompilerParams(**PARAMS),
        name="shares",
    )(later, sums, events, plain, more, ordered)


def hazard_kernel(rows, hazard, square, rank, cumulative, squares):
    groups = rows // LO
    inside = dot_binary(
        jnp.concatenate([hazard[...], square[...]], axis=0), triangle(LO, lambda a, b: a <= b)
    )
    totals = jnp.broadcast_to(inside[:, LO - 1 :], (2 * groups, 128))
    place = lax.rem(rank[...], rows)
    mask = one_hot(place // LO, groups, F32)
    placed = dot_binary(inside, one_hot(lax.rem(place, LO), LO))
    before = triangle(groups, lambda a, b: a > b)
    for first, out in ((0, cumulative), (groups, squares)):
        carried = binary_dot(before, totals[first : first + groups])[:, :1]
        out[...] = jnp.sum(mask * (placed[first : first + groups] + carried), axis=0, keepdims=True)


def hazards(hazard, square, rank, rows):
    row = jax.ShapeDtypeStruct((1, rows), F32)
    return pl.pallas_call(
        functools.partial(hazard_kernel, rows),
        in_specs=[VMEM] * 3,
        out_shape=[row, row],
        out_specs=[VMEM] * 2,
        compiler_params=pltpu.CompilerParams(**PARAMS),
        cost_estimate=pl.CostEstimate(flops=rows * LO * 200, bytes_accessed=rows * 64, transcendentals=0),
        name="hazards",
    )(hazard, square, rank)


def range_kernel(bit, count, *refs):
    total, other, later = refs[:3]
    total_out, later_out = refs[3 + count :]
    is_later = (lax.axis_index("ex") & bit) == 0
    later_out[...] = later[...] + jnp.where(is_later, other[...], 0.0)
    total_out[...] = total[...] + other[...]


def ranges(bit, total, other, later, waited):
    return pl.pallas_call(
        functools.partial(range_kernel, bit, len(waited)),
        in_specs=[VMEM] * 3 + [pl.BlockSpec(memory_space=pl.ANY)] * len(waited),
        out_shape=[jax.ShapeDtypeStruct(total.shape, F32)] * 2,
        out_specs=[VMEM] * 2,
        compiler_params=pltpu.CompilerParams(**PARAMS),
        name="ranges",
    )(total, other, later, *waited)


def order_kernel(start, parts, own, other, *refs):
    messages, (risk, rank, table) = refs[:parts], refs[parts : parts + 3]
    tangent_out, ordered_out, plain, lhs = refs[-4:]
    kf, width = tangent_out.shape
    rows = own.shape[1]
    groups = rows // LO
    span = min(SPAN, width)
    folded = jnp.zeros((kf, 128), F32)
    powers = [jnp.exp2(from_short(part[:, part.shape[1] - 128 :])) for part in messages]
    for i in range(width // span):
        at = slice(start + i * span, start + (i + 1) * span)
        here = slice(i * span, (i + 1) * span)
        tangent = own[:, at] + other[:, at]
        for part, power in zip(messages, powers):
            tangent = tangent + from_short(part[:, here]) * power[:, i : i + 1]
        tangent_out[:, here] = tangent
        weighted = tangent * risk[:, at]
        folded = folded + sum(weighted[:, j : j + 128] for j in range(0, span, 128))
        high, low = split_two(weighted)
        high, low = high.astype(BF16), low.astype(BF16)
        group = jnp.broadcast_to(lax.rem(rank[:, at], rows) // LO, (kf, span))
        for g in range(groups):
            mask = jnp.where(group == g, 1.0, 0.0).astype(BF16)
            lhs[2 * g * kf : (2 * g + 1) * kf, here] = high * mask
            lhs[(2 * g + 1) * kf : (2 * g + 2) * kf, here] = low * mask
    plain[...] = folded
    ordered = jnp.dot(lhs[...], table[start : start + width], preferred_element_type=F32)
    for g in range(groups):
        ordered_out[g * kf : (g + 1) * kf] = (
            ordered[2 * g * kf : (2 * g + 1) * kf] + ordered[(2 * g + 1) * kf : (2 * g + 2) * kf]
        )


def ordered_values(own, other, messages, risk, rank, table, start, width):
    kf, rows = own.shape
    groups = rows // LO
    return pl.pallas_call(
        functools.partial(order_kernel, start, len(messages)),
        in_specs=[VMEM] * (len(messages) + 5),
        out_shape=[
            jax.ShapeDtypeStruct((kf, width), F32),
            jax.ShapeDtypeStruct((groups * kf, LO), F32),
            jax.ShapeDtypeStruct((kf, 128), F32),
        ],
        out_specs=[VMEM] * 3,
        scratch_shapes=[pltpu.VMEM((groups * 2 * kf, width), BF16)],
        compiler_params=pltpu.CompilerParams(**PARAMS),
        cost_estimate=pl.CostEstimate(
            flops=2 * width * LO * groups * 2 * kf, bytes_accessed=width * kf * 24, transcendentals=0
        ),
        name="ordered_values",
    )(own, other, *messages, risk, rank, table)


def suffix_kernel(kf, one, two, sums):
    groups = sums.shape[0] // kf
    inside = dot_binary(one[...] + two[...], triangle(LO, lambda a, b: a >= b))
    carried = jnp.zeros((kf, 1), F32)
    for g in reversed(range(groups)):
        rows_of = slice(g * kf, (g + 1) * kf)
        sums[rows_of] = inside[rows_of] + carried
        carried = carried + inside[rows_of, :1]


def suffix_sums(one, two, kf):
    return pl.pallas_call(
        functools.partial(suffix_kernel, kf),
        in_specs=[VMEM] * 2,
        out_shape=jax.ShapeDtypeStruct(one.shape, F32),
        out_specs=VMEM,
        compiler_params=pltpu.CompilerParams(**PARAMS),
        name="suffix_sums",
    )(one, two)


def prefix_kernel(sums, squares, rank, out):
    kf, rows = out.shape
    groups = squares.shape[0]
    chunk = min(512, rows)
    hazard = [sums[g * kf : (g + 1) * kf] * squares[g : g + 1, :] for g in range(groups)]
    inside = dot_binary(jnp.concatenate(hazard, axis=0), triangle(LO, lambda a, b: a <= b))
    carried = jnp.zeros((kf, 1), F32)
    summed = [None] * groups
    for g in range(groups):
        rows_of = slice(g * kf, (g + 1) * kf)
        summed[g] = inside[rows_of] + carried
        carried = carried + inside[rows_of, LO - 1 :]
    both = stacked(split_two(jnp.concatenate(summed, axis=0)))
    for start in range(0, rows, chunk):
        at = slice(start, start + chunk)
        place = lax.rem(rank[:, at], rows)
        group = place // LO
        spread = one_hot(lax.rem(place, LO), LO)
        placed = unstacked(jnp.dot(both, spread, preferred_element_type=F32), 2)
        picked = jnp.zeros((kf, chunk), F32)
        for g in range(groups):
            picked = picked + jnp.where(group == g, placed[g * kf : (g + 1) * kf], 0.0)
        out[:, at] = picked


def prefix_sums(sums, squares, rank, kf):
    rows = rank.shape[1]
    return pl.pallas_call(
        prefix_kernel,
        in_specs=[VMEM] * 3,
        out_shape=jax.ShapeDtypeStruct((kf, rows), F32),
        out_specs=VMEM,
        compiler_params=pltpu.CompilerParams(**PARAMS),
        cost_estimate=pl.CostEstimate(
            flops=4 * rows * LO * (rows // LO) * kf, bytes_accessed=rows * kf * 24, transcendentals=0
        ),
        name="prefix_sums",
    )(sums, squares, rank)


def weight_kernel(ex, *refs):
    messages, (first, rest, local, risk, cumulative, squares) = refs[:ex], refs[ex : ex + 6]
    weighted, placed = refs[ex + 6 :]
    kf = first.shape[0]
    me = lax.axis_index("ex")
    for i in range(ex):
        placed[me ^ i] = messages[i][...]
    later = jnp.zeros((kf, 128), F32)
    own_later, before = later, later
    hazard_before = jnp.zeros((1, 128), F32)
    for b in reversed(range(ex)):
        plain, scaled, square = placed[b, :kf], placed[b, kf : 2 * kf], placed[b, 2 * kf + 1 : 2 * kf + 2]
        own_later = own_later + jnp.where(b > me, plain, 0.0)
        before = before + jnp.where(b < me, scaled + square * later, 0.0)
        hazard_before = hazard_before + jnp.where(b < me, placed[b, 2 * kf : 2 * kf + 1], 0.0)
        later = later + plain
    own_later = jnp.sum(own_later, axis=1, keepdims=True)
    before = jnp.sum(before, axis=1, keepdims=True)
    hazard_before = hazard_before[:, :1]
    for start, part in ((0, first), (first.shape[1], rest)):
        at = slice(start, start + part.shape[1])
        value = part[...] * (cumulative[:, at] + hazard_before) - (
            local[:, at] + squares[:, at] * own_later + before
        )
        weighted[:, at] = (risk[:, at] * value).astype(BF16)


def weights(messages, first, rest, local, risk, cumulative, squares):
    ex = len(messages)
    return pl.pallas_call(
        functools.partial(weight_kernel, ex),
        in_specs=[VMEM] * (ex + 6),
        out_shape=jax.ShapeDtypeStruct(local.shape, BF16),
        out_specs=VMEM,
        scratch_shapes=[pltpu.VMEM((ex,) + messages[0].shape, F32)],
        compiler_params=pltpu.CompilerParams(**PARAMS),
        name="weights",
    )(*messages, first, rest, local, risk, cumulative, squares)


def encode(values, message):
    height = values.shape[0]
    block = min(BLOCK, height)
    powers = []
    for start in range(0, height, block):
        part = values[start : start + block]
        largest = jnp.max(jnp.abs(part), axis=0, keepdims=True)
        power = power_of(largest)
        message[start : start + block] = to_short(part * jnp.exp2(-power))
        powers.append(power)
    powers.append(jnp.zeros((message.shape[0] - height - len(powers), values.shape[1]), F32))
    message[height:] = to_short(jnp.concatenate(powers, axis=0))


def decode(message, height):
    block = min(BLOCK, height)
    powers = from_short(message[height:])
    parts = []
    for i in range(height // block):
        part = from_short(message[i * block : (i + 1) * block])
        parts.append(part * jnp.exp2(powers[i : i + 1]))
    return jnp.concatenate(parts, axis=0)


def gradient_kernel(feat, kf, start, *refs):
    parts, dosages, out, weighted = refs[:feat], refs[feat], refs[feat + 1], refs[feat + 2]
    width = out.shape[0] - 16
    me = lax.axis_index("feat")
    for i in range(feat):
        weighted[pl.ds(pl.multiple_of((me ^ i) * kf, kf), kf), :] = parts[i][...]
    total = jnp.dot(weighted[...], dosages[:, start : start + width], preferred_element_type=F32)
    encode(total.T, out)


def gradients(parts, dosages, start, variants):
    feat = len(parts)
    kf, persons = parts[0].shape
    k = kf * feat
    return pl.pallas_call(
        functools.partial(gradient_kernel, feat, kf, start),
        in_specs=[VMEM] * (feat + 1),
        out_shape=jax.ShapeDtypeStruct((variants + 16, k), jnp.int16),
        out_specs=VMEM,
        scratch_shapes=[pltpu.VMEM((k, persons), BF16)],
        compiler_params=pltpu.CompilerParams(**PARAMS),
        cost_estimate=pl.CostEstimate(
            flops=2 * persons * variants * k, bytes_accessed=persons * (variants * 2 + k * 2), transcendentals=0
        ),
        name="gradients",
    )(*parts, dosages)


def merge_kernel(mine, other, out):
    height = mine.shape[0] - 16
    encode(decode(mine, height) + decode(other, height), out)


def merge(mine, other):
    return pl.pallas_call(
        merge_kernel,
        in_specs=[VMEM] * 2,
        out_shape=jax.ShapeDtypeStruct(mine.shape, jnp.int16),
        out_specs=VMEM,
        compiler_params=pltpu.CompilerParams(**PARAMS),
        name="merge",
    )(mine, other)


def finish_kernel(parts, *refs):
    mine, other, count = refs[:parts], refs[parts : 2 * parts], refs[2 * parts]
    out, total, sems = refs[2 * parts + 1 :]
    step = mine[0].shape[0] - 16
    block = min(BLOCK, step)
    scale = count[1:2, 0:1]
    copies = []
    for i in range(parts):
        messages = (mine[i], other[i])
        powers = [jnp.exp2(from_short(message[step:])) for message in messages]
        for j in range(step // block):
            at = slice(j * block, (j + 1) * block)
            terms = [from_short(m[at]) * p[j : j + 1] for m, p in zip(messages, powers)]
            total[i * step + j * block : i * step + (j + 1) * block] = (terms[0] + terms[1]) / scale
        copies.append(
            pltpu.make_async_copy(
                total.at[pl.ds(i * step, step)], out.at[pl.ds(i * step, step)], sems.at[i]
            )
        )
        copies[i].start()
    for copy in copies:
        copy.wait()


def finish(mine, other, count):
    parts = len(mine)
    height, k = parts * (mine[0].shape[0] - 16), mine[0].shape[1]
    return pl.pallas_call(
        functools.partial(finish_kernel, parts),
        in_specs=[VMEM] * (2 * parts + 1),
        out_shape=jax.ShapeDtypeStruct((height, k), F32),
        out_specs=HBM,
        scratch_shapes=[pltpu.VMEM((height, k), F32), pltpu.SemaphoreType.DMA((parts,))],
        compiler_params=pltpu.CompilerParams(**PARAMS),
        name="finish",
    )(*mine, *other, count)


def local(dosages, coefficients, directions, event_rank, events):
    feat, ex = lax.axis_size("feat"), lax.axis_size("ex")
    rows = dosages.shape[0]
    variants, k = directions.shape
    each = k // feat
    padded = -(-each // 16) * 16
    if padded != each:
        directions = jnp.pad(directions.reshape(variants, feat, each), ((0, 0), (0, 0), (0, padded - each)))
        directions = directions.reshape(variants, feat * padded)
    rank, event_row = event_rank[None], events[None]

    linear, keep, send = products(dosages, coefficients, directions, feat)
    order = list(reversed(range(1, feat // 2)))
    received = {q: swap(send[q], "feat", 1) for q in order + [0]}
    paired = pair(linear, received[order[0]])
    middle = min(3 * SPAN, rows // 2)
    firsts = [
        swap(join(keep[q], received[q], 0, middle, paired, []), "feat", 2 * q) for q in order
    ]
    rests = [
        swap(join(keep[q], received[q], middle, rows - middle, paired, [received[0]]), "feat", 2 * q)
        for q in order
    ]
    table = tables(rank, paired, rows)

    risk, sums, ordered_events, total = risks(paired, firsts, rank, event_row, table, rows)
    later = jnp.zeros_like(total)
    bit = 1
    while bit < ex:
        total, later = ranges(bit, total, swap(total, "ex", bit), later, rests if bit == 1 else [])
        bit *= 2
    tangent, one, plain = ordered_values(keep[0], received[0], firsts, risk, rank, table, 0, middle)
    more_tangent, two, more = ordered_values(
        keep[0], received[0], rests, risk, rank, table, middle, rows - middle
    )
    later_sums = suffix_sums(one, two, padded)
    hazard, ordered_squares, message = shares(later, sums, ordered_events, plain, more, later_sums)
    messages = [message] + [swap(message, "ex", i) for i in range(1, ex)]
    cumulative, squares = hazards(hazard, ordered_squares, rank, rows)
    summed = prefix_sums(later_sums, ordered_squares, rank, padded)
    own = weights(messages, tangent, more_tangent, summed, risk, cumulative, squares)

    chips = {0: own}
    for q in reversed(range(1, feat // 2)):
        chips[q] = swap(own, "feat", 2 * q)
    parts = []
    for q in range(feat // 2):
        parts += [chips[q], swap(chips[q], "feat", 1)]

    half = variants // 2
    partial_sums = [gradients(parts, dosages, start, half) for start in (0, half)]
    bit = 1
    while 2 * bit < ex:
        received = [swap(message, "ex", bit) for message in partial_sums]
        partial_sums = [merge(mine, other) for mine, other in zip(partial_sums, received)]
        bit *= 2
    received = [swap(message, "ex", bit) for message in partial_sums]
    result = finish(partial_sums, received, total)
    if padded != each:
        result = result.reshape(variants, feat, padded)[:, :, :each].reshape(variants, k)
    return result


def solution(mesh):
    placed = (P("ex", "feat"), P("feat"), P("feat", None), P("ex"), P("ex"))
    return jax.shard_map(
        local, mesh=mesh, in_specs=placed, out_specs=P("feat", None), check_vma=False
    )
```

```python
import functools

import jax
import jax.numpy as jnp
from jax import lax
from jax.experimental import pallas as pl
from jax.experimental.pallas import tpu as pltpu
from jax.sharding import PartitionSpec as P

F32 = jnp.float32
BF16 = jnp.bfloat16
LO = 256
NT = (((1,), (1,)), ((), ()))
BLOCK = 64
SPAN = 512
SPLIT = 2
VMEM = pl.BlockSpec(memory_space=pltpu.VMEM)
HBM = pl.BlockSpec(memory_space=pltpu.HBM)
PARAMS = dict(vmem_limit_bytes=24 * 1024 * 1024)


def swap(x, axis, i):
    count = lax.axis_size(axis)
    return lax.ppermute(x, axis, [(s, s ^ i) for s in range(count)])


def split_two(x):
    high = x.astype(BF16).astype(F32)
    return high, x - high


def split_three(x):
    first, rest = split_two(x)
    second, third = split_two(rest)
    return first, second, third


def one_hot(values, count, kind=BF16):
    shape = (count, values.shape[1])
    return jnp.where(lax.broadcasted_iota(jnp.int32, shape, 0) == values, 1.0, 0.0).astype(kind)


def triangle(n, keep):
    first = lax.broadcasted_iota(jnp.int32, (n, n), 0)
    second = lax.broadcasted_iota(jnp.int32, (n, n), 1)
    return jnp.where(keep(first, second), 1.0, 0.0)


def stacked(parts):
    return jnp.concatenate(parts, axis=0).astype(BF16)


def unstacked(values, count):
    height = values.shape[0] // count
    return sum(values[i * height : (i + 1) * height] for i in range(count))


def dot_binary(a, b):
    parts = jnp.dot(stacked(split_three(a)), b.astype(BF16), preferred_element_type=F32)
    return unstacked(parts, 3)


def binary_dot(a, b):
    a = a.astype(BF16)
    total = None
    for part in split_three(b):
        term = jnp.dot(a, part.astype(BF16), preferred_element_type=F32)
        total = term if total is None else total + term
    return total


def product_kernel(feat, kf, chunk, directions, coefficients, dosages, *refs):
    linear, keep, send = refs[0], refs[1 : 1 + feat // 2], refs[1 + feat // 2 : 1 + feat]
    table, own_directions, own_coefficients, lhs, turned, sems = refs[1 + feat :]
    me = lax.axis_index("feat")
    width = feat * kf
    persons, variants = table.shape
    steps = persons // chunk
    small = [
        pltpu.make_async_copy(directions, own_directions, sems.at[SPLIT * steps]),
        pltpu.make_async_copy(coefficients, own_coefficients, sems.at[SPLIT * steps + 1]),
    ]
    piece = chunk // SPLIT
    large = [
        pltpu.make_async_copy(
            dosages.at[pl.ds(i * piece, piece)], table.at[pl.ds(i * piece, piece)], sems.at[i]
        )
        for i in range(SPLIT * steps)
    ]
    for copy in small + large:
        copy.start()
    for copy in small:
        copy.wait()
    turned[...] = own_directions[...].astype(F32).T.reshape(turned.shape)
    for j in range(feat):
        lhs[j * kf : (j + 1) * kf] = turned[me ^ j].astype(BF16)
    lhs[width:] = jnp.broadcast_to(own_coefficients[...].astype(F32)[None, :], (16, variants)).astype(BF16)
    for i in range(steps):
        for copy in large[i * SPLIT : (i + 1) * SPLIT]:
            copy.wait()
        first = i * chunk
        result = lax.dot_general(
            lhs[...], table[first : first + chunk], NT, preferred_element_type=F32
        )
        for j in range(feat):
            (send if j % 2 else keep)[j // 2][:, first : first + chunk] = result[j * kf : (j + 1) * kf]
        for start in range(0, chunk, LO):
            row = result[width : width + 1, start : start + LO]
            group = (first + start) // LO
            linear[group : group + 1, :] = row
            send[-1][group : group + 1, persons:] = row


def products(dosages, coefficients, directions, feat):
    persons, variants = dosages.shape
    k = directions.shape[1]
    kf = k // feat
    chunk = min(512, persons)
    piece = jax.ShapeDtypeStruct((kf, persons), F32)
    first = jax.ShapeDtypeStruct((kf, persons + LO), F32)
    out = pl.pallas_call(
        functools.partial(product_kernel, feat, kf, chunk),
        in_specs=[HBM, HBM, HBM],
        out_shape=[jax.ShapeDtypeStruct((kf, LO), F32)]
        + [piece] * (feat - 1)
        + [first],
        out_specs=[VMEM] * (feat + 1),
        scratch_shapes=[
            pltpu.VMEM((persons, variants), BF16),
            pltpu.VMEM((variants, k), BF16),
            pltpu.VMEM((variants,), BF16),
            pltpu.VMEM((k + 16, variants), BF16),
            pltpu.VMEM((feat, kf, variants), F32),
            pltpu.SemaphoreType.DMA((SPLIT * (persons // chunk) + 2,)),
        ],
        compiler_params=pltpu.CompilerParams(**PARAMS),
        cost_estimate=pl.CostEstimate(
            flops=2 * persons * variants * k, bytes_accessed=persons * (variants * 2 + k * 4), transcendentals=0
        ),
        name="products",
    )(*[pltpu.with_memory_space_constraint(x, pltpu.HBM) for x in (directions, coefficients, dosages)])
    return out[0], out[1 : 1 + feat // 2], out[1 + feat // 2 :]


def power_of(largest):
    return jnp.ceil(jnp.log2(jnp.maximum(largest, 1e-30))) - 14.0


def to_short(values):
    return jnp.round(values).astype(jnp.int32).astype(jnp.int16)


def from_short(values):
    return values.astype(jnp.int32).astype(F32)


def pair_kernel(linear, received, out):
    out[...] = linear[...] + received[:, received.shape[1] - LO :]


def pair(linear, received):
    return pl.pallas_call(
        pair_kernel,
        in_specs=[VMEM] * 2,
        out_shape=jax.ShapeDtypeStruct(linear.shape, F32),
        out_specs=VMEM,
        compiler_params=pltpu.CompilerParams(**PARAMS),
        name="pair",
    )(linear, received)


def join_kernel(start, width, mine, other, *refs):
    linear, out = refs[0], refs[-1]
    kf = mine.shape[0]
    span = min(SPAN, width)
    lane = lax.broadcasted_iota(jnp.int32, (kf, 128), 1)
    powers = jnp.zeros((kf, 128), F32)
    for i in range(width // span):
        at = slice(start + i * span, start + (i + 1) * span)
        total = mine[:, at] + other[:, at]
        power = power_of(jnp.max(jnp.abs(total), axis=1, keepdims=True))
        out[:, i * span : (i + 1) * span] = to_short(total * jnp.exp2(-power))
        powers = jnp.where(lane == i, power, powers)
    if start == 0:
        power = power_of(jnp.max(jnp.abs(linear[...]), axis=1, keepdims=True))
        scaled = linear[...] * jnp.exp2(-power)
        whole = jnp.round(scaled)
        out[:, width : width + LO] = to_short(whole)
        out[:, width + LO : width + 2 * LO] = to_short((scaled - whole) * 32768.0)
        powers = jnp.where(lane == 127, power, powers)
    out[:, out.shape[1] - 128 :] = to_short(powers)


def join(keep, received, start, width, linear, waited):
    kf, rows = keep.shape
    extra = 2 * LO if start == 0 else 0
    return pl.pallas_call(
        functools.partial(join_kernel, start, width),
        in_specs=[VMEM] * 3 + [pl.BlockSpec(memory_space=pl.ANY)] * len(waited),
        out_shape=jax.ShapeDtypeStruct((kf, width + extra + 128), jnp.int16),
        out_specs=VMEM,
        compiler_params=pltpu.CompilerParams(**PARAMS),
        name="join",
    )(keep, received, linear, *waited)


def table_kernel(rows, rank, waited, table):
    chunk = min(512, rows)
    lane = lax.broadcasted_iota(jnp.int32, (chunk, 128), 1)
    for start in range(0, rows, chunk):
        at = slice(start, start + chunk)
        inner = lax.rem(rank[:, at], LO)
        column = jnp.broadcast_to(inner.astype(F32), (128, chunk)).T.astype(jnp.int32)
        for first in range(0, LO, 128):
            table[at, first : first + 128] = jnp.where(column == lane + first, 1.0, 0.0).astype(BF16)


def tables(rank, waited, rows):
    return pl.pallas_call(
        functools.partial(table_kernel, rows),
        in_specs=[VMEM, pl.BlockSpec(memory_space=pl.ANY)],
        out_shape=jax.ShapeDtypeStruct((rows, LO), BF16),
        out_specs=VMEM,
        compiler_params=pltpu.CompilerParams(**PARAMS),
        cost_estimate=pl.CostEstimate(flops=rows * LO * 8, bytes_accessed=rows * LO * 2, transcendentals=0),
        name="tables",
    )(rank, waited)


def risk_kernel(rows, parts, linear, *refs):
    messages, (rank, events, table) = refs[:parts], refs[parts : parts + 3]
    risk_out, sums_out, events_out, message = refs[-4:]
    groups = rows // LO
    total = linear[...]
    for part in messages:
        end = part.shape[1] - 128
        power = from_short(part[:, end:])[:, 127:]
        high, low = from_short(part[:, end - 2 * LO : end - LO]), from_short(part[:, end - LO : end])
        total = total + (high + low * (1.0 / 32768.0)) * jnp.exp2(power)
    risk = jnp.exp(total)
    for g in range(groups):
        risk_out[:, g * LO : (g + 1) * LO] = risk[g : g + 1]
    mask = one_hot(lax.rem(rank[...], rows) // LO, groups, F32)
    pieces = [mask * part for part in split_three(risk_out[...])] + [mask * events[...].astype(F32)]
    lhs = jnp.concatenate(pieces, axis=0).astype(BF16)
    sorted_all = jnp.dot(lhs, table[...], preferred_element_type=F32)
    ordered = sorted_all[:groups] + sorted_all[groups : 2 * groups] + sorted_all[2 * groups : 3 * groups]
    happened = sorted_all[3 * groups :]
    inside = dot_binary(ordered, triangle(LO, lambda a, b: a >= b))
    totals = jnp.broadcast_to(inside[:, :1], inside.shape)
    carried = binary_dot(triangle(groups, lambda a, b: a < b), totals)
    sums_out[...] = inside + carried
    events_out[...] = happened
    everything = jnp.sum(totals, axis=0, keepdims=True)[:, :128]
    count = jnp.sum(dot_binary(happened, jnp.ones((LO, 128), F32)), axis=0, keepdims=True)
    message[...] = jnp.concatenate([everything, count, jnp.zeros((6, 128), F32)], axis=0)


def risks(linear, messages, rank, events, table, rows):
    groups = rows // LO
    return pl.pallas_call(
        functools.partial(risk_kernel, rows, len(messages)),
        in_specs=[VMEM] * (len(messages) + 4),
        out_shape=[
            jax.ShapeDtypeStruct((1, rows), F32),
            jax.ShapeDtypeStruct((groups, LO), F32),
            jax.ShapeDtypeStruct((groups, LO), F32),
            jax.ShapeDtypeStruct((8, 128), F32),
        ],
        out_specs=[VMEM] * 4,
        compiler_params=pltpu.CompilerParams(**PARAMS),
        cost_estimate=pl.CostEstimate(flops=rows * LO * 128, bytes_accessed=rows * 64, transcendentals=rows),
        name="risks",
    )(linear, *messages, rank, events, table)


def share_kernel(later, sums, events, plain, more, ordered, hazard_out, squares, message):
    kf = plain.shape[0]
    groups = sums.shape[0]
    risk_sum = sums[...] + later[0:1, 0:1]
    hazard = events[...] / risk_sum
    square = events[...] / (risk_sum * risk_sum)
    hazard_out[...] = hazard
    squares[...] = square
    scaled = jnp.zeros((kf, LO), F32)
    for g in range(groups):
        scaled = scaled + ordered[g * kf : (g + 1) * kf] * square[g : g + 1]
    message[:kf] = plain[...] + more[...]
    message[kf : 2 * kf] = sum(scaled[:, start : start + 128] for start in range(0, LO, 128))
    totals = [jnp.sum(jnp.sum(v, axis=0, keepdims=True), axis=1, keepdims=True) for v in (hazard, square)]
    rows = [jnp.broadcast_to(v, (1, 128)) for v in totals]
    message[2 * kf :] = jnp.concatenate(rows + [jnp.zeros((6, 128), F32)], axis=0)


def shares(later, sums, events, plain, more, ordered):
    flat = jax.ShapeDtypeStruct(sums.shape, F32)
    return pl.pallas_call(
        share_kernel,
        in_specs=[VMEM] * 6,
        out_shape=[flat, flat, jax.ShapeDtypeStruct((2 * plain.shape[0] + 8, 128), F32)],
        out_specs=[VMEM] * 3,
        compiler_params=pltpu.CompilerParams(**PARAMS),
        name="shares",
    )(later, sums, events, plain, more, ordered)


def hazard_kernel(rows, hazard, square, rank, cumulative, squares):
    groups = rows // LO
    inside = dot_binary(
        jnp.concatenate([hazard[...], square[...]], axis=0), triangle(LO, lambda a, b: a <= b)
    )
    totals = jnp.broadcast_to(inside[:, LO - 1 :], (2 * groups, 128))
    place = lax.rem(rank[...], rows)
    mask = one_hot(place // LO, groups, F32)
    placed = dot_binary(inside, one_hot(lax.rem(place, LO), LO))
    before = triangle(groups, lambda a, b: a > b)
    for first, out in ((0, cumulative), (groups, squares)):
        carried = binary_dot(before, totals[first : first + groups])[:, :1]
        out[...] = jnp.sum(mask * (placed[first : first + groups] + carried), axis=0, keepdims=True)


def hazards(hazard, square, rank, rows):
    row = jax.ShapeDtypeStruct((1, rows), F32)
    return pl.pallas_call(
        functools.partial(hazard_kernel, rows),
        in_specs=[VMEM] * 3,
        out_shape=[row, row],
        out_specs=[VMEM] * 2,
        compiler_params=pltpu.CompilerParams(**PARAMS),
        cost_estimate=pl.CostEstimate(flops=rows * LO * 200, bytes_accessed=rows * 64, transcendentals=0),
        name="hazards",
    )(hazard, square, rank)


def range_kernel(bit, count, *refs):
    total, other, later = refs[:3]
    total_out, later_out = refs[3 + count :]
    is_later = (lax.axis_index("ex") & bit) == 0
    later_out[...] = later[...] + jnp.where(is_later, other[...], 0.0)
    total_out[...] = total[...] + other[...]


def ranges(bit, total, other, later, waited):
    return pl.pallas_call(
        functools.partial(range_kernel, bit, len(waited)),
        in_specs=[VMEM] * 3 + [pl.BlockSpec(memory_space=pl.ANY)] * len(waited),
        out_shape=[jax.ShapeDtypeStruct(total.shape, F32)] * 2,
        out_specs=[VMEM] * 2,
        compiler_params=pltpu.CompilerParams(**PARAMS),
        name="ranges",
    )(total, other, later, *waited)


def order_kernel(start, parts, own, other, *refs):
    messages, (risk, rank, table) = refs[:parts], refs[parts : parts + 3]
    tangent_out, ordered_out, plain, lhs = refs[-4:]
    kf, width = tangent_out.shape
    rows = own.shape[1]
    groups = rows // LO
    span = min(SPAN, width)
    folded = jnp.zeros((kf, 128), F32)
    powers = [jnp.exp2(from_short(part[:, part.shape[1] - 128 :])) for part in messages]
    for i in range(width // span):
        at = slice(start + i * span, start + (i + 1) * span)
        here = slice(i * span, (i + 1) * span)
        tangent = own[:, at] + other[:, at]
        for part, power in zip(messages, powers):
            tangent = tangent + from_short(part[:, here]) * power[:, i : i + 1]
        tangent_out[:, here] = tangent
        weighted = tangent * risk[:, at]
        folded = folded + sum(weighted[:, j : j + 128] for j in range(0, span, 128))
        high, low = split_two(weighted)
        high, low = high.astype(BF16), low.astype(BF16)
        group = jnp.broadcast_to(lax.rem(rank[:, at], rows) // LO, (kf, span))
        for g in range(groups):
            mask = jnp.where(group == g, 1.0, 0.0).astype(BF16)
            lhs[2 * g * kf : (2 * g + 1) * kf, here] = high * mask
            lhs[(2 * g + 1) * kf : (2 * g + 2) * kf, here] = low * mask
    plain[...] = folded
    ordered = jnp.dot(lhs[...], table[start : start + width], preferred_element_type=F32)
    for g in range(groups):
        ordered_out[g * kf : (g + 1) * kf] = (
            ordered[2 * g * kf : (2 * g + 1) * kf] + ordered[(2 * g + 1) * kf : (2 * g + 2) * kf]
        )


def ordered_values(own, other, messages, risk, rank, table, start, width):
    kf, rows = own.shape
    groups = rows // LO
    return pl.pallas_call(
        functools.partial(order_kernel, start, len(messages)),
        in_specs=[VMEM] * (len(messages) + 5),
        out_shape=[
            jax.ShapeDtypeStruct((kf, width), F32),
            jax.ShapeDtypeStruct((groups * kf, LO), F32),
            jax.ShapeDtypeStruct((kf, 128), F32),
        ],
        out_specs=[VMEM] * 3,
        scratch_shapes=[pltpu.VMEM((groups * 2 * kf, width), BF16)],
        compiler_params=pltpu.CompilerParams(**PARAMS),
        cost_estimate=pl.CostEstimate(
            flops=2 * width * LO * groups * 2 * kf, bytes_accessed=width * kf * 24, transcendentals=0
        ),
        name="ordered_values",
    )(own, other, *messages, risk, rank, table)


def suffix_kernel(kf, one, two, sums):
    groups = sums.shape[0] // kf
    inside = dot_binary(one[...] + two[...], triangle(LO, lambda a, b: a >= b))
    carried = jnp.zeros((kf, 1), F32)
    for g in reversed(range(groups)):
        rows_of = slice(g * kf, (g + 1) * kf)
        sums[rows_of] = inside[rows_of] + carried
        carried = carried + inside[rows_of, :1]


def suffix_sums(one, two, kf):
    return pl.pallas_call(
        functools.partial(suffix_kernel, kf),
        in_specs=[VMEM] * 2,
        out_shape=jax.ShapeDtypeStruct(one.shape, F32),
        out_specs=VMEM,
        compiler_params=pltpu.CompilerParams(**PARAMS),
        name="suffix_sums",
    )(one, two)


def prefix_kernel(sums, squares, rank, out):
    kf, rows = out.shape
    groups = squares.shape[0]
    chunk = min(512, rows)
    hazard = [sums[g * kf : (g + 1) * kf] * squares[g : g + 1, :] for g in range(groups)]
    inside = dot_binary(jnp.concatenate(hazard, axis=0), triangle(LO, lambda a, b: a <= b))
    carried = jnp.zeros((kf, 1), F32)
    summed = [None] * groups
    for g in range(groups):
        rows_of = slice(g * kf, (g + 1) * kf)
        summed[g] = inside[rows_of] + carried
        carried = carried + inside[rows_of, LO - 1 :]
    both = stacked(split_two(jnp.concatenate(summed, axis=0)))
    for start in range(0, rows, chunk):
        at = slice(start, start + chunk)
        place = lax.rem(rank[:, at], rows)
        group = place // LO
        spread = one_hot(lax.rem(place, LO), LO)
        placed = unstacked(jnp.dot(both, spread, preferred_element_type=F32), 2)
        picked = jnp.zeros((kf, chunk), F32)
        for g in range(groups):
            picked = picked + jnp.where(group == g, placed[g * kf : (g + 1) * kf], 0.0)
        out[:, at] = picked


def prefix_sums(sums, squares, rank, kf):
    rows = rank.shape[1]
    return pl.pallas_call(
        prefix_kernel,
        in_specs=[VMEM] * 3,
        out_shape=jax.ShapeDtypeStruct((kf, rows), F32),
        out_specs=VMEM,
        compiler_params=pltpu.CompilerParams(**PARAMS),
        cost_estimate=pl.CostEstimate(
            flops=4 * rows * LO * (rows // LO) * kf, bytes_accessed=rows * kf * 24, transcendentals=0
        ),
        name="prefix_sums",
    )(sums, squares, rank)


def merged(kf, bit, mine, other, state):
    later_other = (lax.axis_index("ex") & bit) == 0
    plain, scaled, rest = mine[:kf], mine[kf : 2 * kf], mine[2 * kf :]
    other_plain, other_scaled, other_rest = other[:kf], other[kf : 2 * kf], other[2 * kf :]
    square, other_square = rest[1:2], other_rest[1:2]
    crossed = jnp.where(later_other, square * other_plain, other_square * plain)
    total = jnp.concatenate([plain + other_plain, scaled + other_scaled + crossed, rest + other_rest], axis=0)
    if state is None:
        state = jnp.zeros_like(mine)
    later, before, before_rest = state[:kf], state[kf : 2 * kf], state[2 * kf :]
    state = jnp.concatenate(
        [
            later + jnp.where(later_other, other_plain, 0.0),
            before + jnp.where(later_other, before_rest[1:2] * other_plain, other_scaled + other_square * plain),
            before_rest + jnp.where(later_other, 0.0, other_rest),
        ],
        axis=0,
    )
    return total, state


def combine_kernel(kf, bit, count, *refs):
    inputs, (total, state) = [ref[...] for ref in refs[:count]], refs[count + 1 :]
    total[...], state[...] = merged(kf, bit, inputs[0], inputs[1], inputs[2] if count > 2 else None)


def combine(kf, bit, inputs, waited):
    shape = jax.ShapeDtypeStruct(inputs[0].shape, F32)
    return pl.pallas_call(
        functools.partial(combine_kernel, kf, bit, len(inputs)),
        in_specs=[VMEM] * len(inputs) + [pl.BlockSpec(memory_space=pl.ANY)],
        out_shape=[shape, shape],
        out_specs=[VMEM] * 2,
        compiler_params=pltpu.CompilerParams(**PARAMS),
        name="combine",
    )(*inputs, waited)


def weight_kernel(kf, bit, count, *refs):
    inputs = [ref[...] for ref in refs[:count]]
    first, rest, local, risk, cumulative, squares, weighted = refs[count:]
    _, state = merged(kf, bit, inputs[0], inputs[1], inputs[2] if count > 2 else None)
    later = jnp.sum(state[:kf], axis=1, keepdims=True)
    before = jnp.sum(state[kf : 2 * kf], axis=1, keepdims=True)
    hazard_before = state[2 * kf : 2 * kf + 1, :1]
    for start, part in ((0, first), (first.shape[1], rest)):
        at = slice(start, start + part.shape[1])
        value = part[...] * (cumulative[:, at] + hazard_before) - (
            local[:, at] + squares[:, at] * later + before
        )
        weighted[:, at] = (risk[:, at] * value).astype(BF16)


def weights(bit, inputs, first, rest, local, risk, cumulative, squares):
    return pl.pallas_call(
        functools.partial(weight_kernel, first.shape[0], bit, len(inputs)),
        in_specs=[VMEM] * (len(inputs) + 6),
        out_shape=jax.ShapeDtypeStruct(local.shape, BF16),
        out_specs=VMEM,
        compiler_params=pltpu.CompilerParams(**PARAMS),
        name="weights",
    )(*inputs, first, rest, local, risk, cumulative, squares)


def encode(values, message):
    height = values.shape[0]
    block = min(BLOCK, height)
    powers = []
    for start in range(0, height, block):
        part = values[start : start + block]
        largest = jnp.max(jnp.abs(part), axis=0, keepdims=True)
        power = power_of(largest)
        message[start : start + block] = to_short(part * jnp.exp2(-power))
        powers.append(power)
    powers.append(jnp.zeros((message.shape[0] - height - len(powers), values.shape[1]), F32))
    message[height:] = to_short(jnp.concatenate(powers, axis=0))


def decode(message, height):
    block = min(BLOCK, height)
    powers = from_short(message[height:])
    parts = []
    for i in range(height // block):
        part = from_short(message[i * block : (i + 1) * block])
        parts.append(part * jnp.exp2(powers[i : i + 1]))
    return jnp.concatenate(parts, axis=0)


def gradient_kernel(feat, kf, start, *refs):
    parts, dosages, out, weighted = refs[:feat], refs[feat], refs[feat + 1], refs[feat + 2]
    width = out.shape[0] - 16
    me = lax.axis_index("feat")
    for i in range(feat):
        weighted[pl.ds(pl.multiple_of((me ^ i) * kf, kf), kf), :] = parts[i][...]
    total = jnp.dot(weighted[...], dosages[:, start : start + width], preferred_element_type=F32)
    encode(total.T, out)


def gradients(parts, dosages, start, variants):
    feat = len(parts)
    kf, persons = parts[0].shape
    k = kf * feat
    return pl.pallas_call(
        functools.partial(gradient_kernel, feat, kf, start),
        in_specs=[VMEM] * (feat + 1),
        out_shape=jax.ShapeDtypeStruct((variants + 16, k), jnp.int16),
        out_specs=VMEM,
        scratch_shapes=[pltpu.VMEM((k, persons), BF16)],
        compiler_params=pltpu.CompilerParams(**PARAMS),
        cost_estimate=pl.CostEstimate(
            flops=2 * persons * variants * k, bytes_accessed=persons * (variants * 2 + k * 2), transcendentals=0
        ),
        name="gradients",
    )(*parts, dosages)


def merge_kernel(mine, other, out):
    height = mine.shape[0] - 16
    encode(decode(mine, height) + decode(other, height), out)


def merge(mine, other):
    return pl.pallas_call(
        merge_kernel,
        in_specs=[VMEM] * 2,
        out_shape=jax.ShapeDtypeStruct(mine.shape, jnp.int16),
        out_specs=VMEM,
        compiler_params=pltpu.CompilerParams(**PARAMS),
        name="merge",
    )(mine, other)


def finish_kernel(parts, *refs):
    mine, other, count = refs[:parts], refs[parts : 2 * parts], refs[2 * parts]
    out, total, sems = refs[2 * parts + 1 :]
    step = mine[0].shape[0] - 16
    block = min(BLOCK, step)
    scale = count[1:2, 0:1]
    copies = []
    for i in range(parts):
        messages = (mine[i], other[i])
        powers = [jnp.exp2(from_short(message[step:])) for message in messages]
        for j in range(step // block):
            at = slice(j * block, (j + 1) * block)
            terms = [from_short(m[at]) * p[j : j + 1] for m, p in zip(messages, powers)]
            total[i * step + j * block : i * step + (j + 1) * block] = (terms[0] + terms[1]) / scale
        copies.append(
            pltpu.make_async_copy(
                total.at[pl.ds(i * step, step)], out.at[pl.ds(i * step, step)], sems.at[i]
            )
        )
        copies[i].start()
    for copy in copies:
        copy.wait()


def finish(mine, other, count):
    parts = len(mine)
    height, k = parts * (mine[0].shape[0] - 16), mine[0].shape[1]
    return pl.pallas_call(
        functools.partial(finish_kernel, parts),
        in_specs=[VMEM] * (2 * parts + 1),
        out_shape=jax.ShapeDtypeStruct((height, k), F32),
        out_specs=HBM,
        scratch_shapes=[pltpu.VMEM((height, k), F32), pltpu.SemaphoreType.DMA((parts,))],
        compiler_params=pltpu.CompilerParams(**PARAMS),
        name="finish",
    )(*mine, *other, count)


def local(dosages, coefficients, directions, event_rank, events):
    feat, ex = lax.axis_size("feat"), lax.axis_size("ex")
    rows = dosages.shape[0]
    variants, k = directions.shape
    each = k // feat
    padded = -(-each // 16) * 16
    if padded != each:
        directions = jnp.pad(directions.reshape(variants, feat, each), ((0, 0), (0, 0), (0, padded - each)))
        directions = directions.reshape(variants, feat * padded)
    rank, event_row = event_rank[None], events[None]

    linear, keep, send = products(dosages, coefficients, directions, feat)
    order = list(reversed(range(1, feat // 2)))
    received = {q: swap(send[q], "feat", 1) for q in order + [0]}
    paired = pair(linear, received[order[0]])
    middle = min(3 * SPAN, rows // 2)
    firsts = [
        swap(join(keep[q], received[q], 0, middle, paired, []), "feat", 2 * q) for q in order
    ]
    rests = [
        swap(join(keep[q], received[q], middle, rows - middle, paired, [received[0]]), "feat", 2 * q)
        for q in order
    ]
    table = tables(rank, paired, rows)

    risk, sums, ordered_events, total = risks(paired, firsts, rank, event_row, table, rows)
    later = jnp.zeros_like(total)
    bit = 1
    while bit < ex:
        total, later = ranges(bit, total, swap(total, "ex", bit), later, rests if bit == 1 else [])
        bit *= 2
    tangent, one, plain = ordered_values(keep[0], received[0], firsts, risk, rank, table, 0, middle)
    more_tangent, two, more = ordered_values(
        keep[0], received[0], rests, risk, rank, table, middle, rows - middle
    )
    later_sums = suffix_sums(one, two, padded)
    hazard, ordered_squares, message = shares(later, sums, ordered_events, plain, more, later_sums)
    cumulative, squares = hazards(hazard, ordered_squares, rank, rows)
    state, bit = [], 1
    while 2 * bit < ex:
        message, *state = combine(padded, bit, [message, swap(message, "ex", bit)] + state, cumulative)
        bit *= 2
    inputs = [message, swap(message, "ex", bit)] + state
    summed = prefix_sums(later_sums, ordered_squares, rank, padded)
    own = weights(bit, inputs, tangent, more_tangent, summed, risk, cumulative, squares)

    chips = {0: own}
    for q in reversed(range(1, feat // 2)):
        chips[q] = swap(own, "feat", 2 * q)
    parts = []
    for q in range(feat // 2):
        parts += [chips[q], swap(chips[q], "feat", 1)]

    half = variants // 2
    partial_sums = [gradients(parts, dosages, start, half) for start in (0, half)]
    bit = 1
    while 2 * bit < ex:
        received = [swap(message, "ex", bit) for message in partial_sums]
        partial_sums = [merge(mine, other) for mine, other in zip(partial_sums, received)]
        bit *= 2
    received = [swap(message, "ex", bit) for message in partial_sums]
    result = finish(partial_sums, received, total)
    if padded != each:
        result = result.reshape(variants, feat, padded)[:, :, :each].reshape(variants, k)
    return result


def solution(mesh):
    placed = (P("ex", "feat"), P("feat"), P("feat", None), P("ex"), P("ex"))
    return jax.shard_map(
        local, mesh=mesh, in_specs=placed, out_specs=P("feat", None), check_vma=False
    )
```

```python
import functools

import jax
import jax.numpy as jnp
from jax import lax
from jax.experimental import pallas as pl
from jax.experimental.pallas import tpu as pltpu
from jax.sharding import PartitionSpec as P

F32 = jnp.float32
BF16 = jnp.bfloat16
LO = 256
NT = (((1,), (1,)), ((), ()))
SPAN = 512
VMEM = pl.BlockSpec(memory_space=pltpu.VMEM)
HBM = pl.BlockSpec(memory_space=pltpu.HBM)
PARAMS = dict(vmem_limit_bytes=24 * 1024 * 1024)


def swap(x, axis, i):
    count = lax.axis_size(axis)
    return lax.ppermute(x, axis, [(s, s ^ i) for s in range(count)])


def split_two(x):
    high = x.astype(BF16).astype(F32)
    return high, x - high


def split_three(x):
    first, rest = split_two(x)
    second, third = split_two(rest)
    return first, second, third


def one_hot(values, count, kind=BF16):
    shape = (count, values.shape[1])
    return jnp.where(lax.broadcasted_iota(jnp.int32, shape, 0) == values, 1.0, 0.0).astype(kind)


def triangle(n, keep):
    first = lax.broadcasted_iota(jnp.int32, (n, n), 0)
    second = lax.broadcasted_iota(jnp.int32, (n, n), 1)
    return jnp.where(keep(first, second), 1.0, 0.0)


def stacked(parts):
    return jnp.concatenate(parts, axis=0).astype(BF16)


def unstacked(values, count):
    height = values.shape[0] // count
    return sum(values[i * height : (i + 1) * height] for i in range(count))


def dot_binary(a, b):
    parts = jnp.dot(stacked(split_three(a)), b.astype(BF16), preferred_element_type=F32)
    return unstacked(parts, 3)


def binary_dot(a, b):
    a = a.astype(BF16)
    total = None
    for part in split_three(b):
        term = jnp.dot(a, part.astype(BF16), preferred_element_type=F32)
        total = term if total is None else total + term
    return total


def product_kernel(feat, kf, chunk, directions, coefficients, dosages, *refs):
    linear, keep, send = refs[0], refs[1 : 1 + feat // 2], refs[1 + feat // 2 : 1 + feat]
    table, own_directions, own_coefficients, lhs, turned, sems = refs[1 + feat :]
    me = lax.axis_index("feat")
    width = feat * kf
    persons, variants = table.shape
    steps = persons // chunk
    small = [
        pltpu.make_async_copy(directions, own_directions, sems.at[steps]),
        pltpu.make_async_copy(coefficients, own_coefficients, sems.at[steps + 1]),
    ]
    large = [
        pltpu.make_async_copy(
            dosages.at[pl.ds(i * chunk, chunk)], table.at[pl.ds(i * chunk, chunk)], sems.at[i]
        )
        for i in range(steps)
    ]
    for copy in small + large:
        copy.start()
    for copy in small:
        copy.wait()
    turned[...] = own_directions[...].astype(F32).T.reshape(turned.shape)
    for j in range(feat):
        lhs[j * kf : (j + 1) * kf] = turned[me ^ j].astype(BF16)
    lhs[width:] = jnp.broadcast_to(own_coefficients[...].astype(F32)[None, :], (16, variants)).astype(BF16)
    for i in range(steps):
        large[i].wait()
        first = i * chunk
        result = lax.dot_general(
            lhs[...], table[first : first + chunk], NT, preferred_element_type=F32
        )
        for j in range(feat):
            (send if j % 2 else keep)[j // 2][:, first : first + chunk] = result[j * kf : (j + 1) * kf]
        for start in range(0, chunk, LO):
            row = result[width : width + 1, start : start + LO]
            group = (first + start) // LO
            linear[group : group + 1, :] = row
            send[-1][group : group + 1, persons:] = row


def products(dosages, coefficients, directions, feat):
    persons, variants = dosages.shape
    k = directions.shape[1]
    kf = k // feat
    chunk = min(512, persons)
    piece = jax.ShapeDtypeStruct((kf, persons), F32)
    first = jax.ShapeDtypeStruct((kf, persons + LO), F32)
    out = pl.pallas_call(
        functools.partial(product_kernel, feat, kf, chunk),
        in_specs=[HBM, HBM, HBM],
        out_shape=[jax.ShapeDtypeStruct((kf, LO), F32)]
        + [piece] * (feat - 1)
        + [first],
        out_specs=[VMEM] * (feat + 1),
        scratch_shapes=[
            pltpu.VMEM((persons, variants), BF16),
            pltpu.VMEM((variants, k), BF16),
            pltpu.VMEM((variants,), BF16),
            pltpu.VMEM((k + 16, variants), BF16),
            pltpu.VMEM((feat, kf, variants), F32),
            pltpu.SemaphoreType.DMA((persons // chunk + 2,)),
        ],
        compiler_params=pltpu.CompilerParams(**PARAMS),
        cost_estimate=pl.CostEstimate(
            flops=2 * persons * variants * k, bytes_accessed=persons * (variants * 2 + k * 4), transcendentals=0
        ),
        name="products",
    )(*[pltpu.with_memory_space_constraint(x, pltpu.HBM) for x in (directions, coefficients, dosages)])
    return out[0], out[1 : 1 + feat // 2], out[1 + feat // 2 :]


def power_of(largest):
    return jnp.ceil(jnp.log2(jnp.maximum(largest, 1e-30))) - 14.0


def to_short(values):
    return jnp.round(values).astype(jnp.int32).astype(jnp.int16)


def from_short(values):
    return values.astype(jnp.int32).astype(F32)


def pair_kernel(linear, received, waited, out):
    out[...] = linear[...] + received[:, received.shape[1] - LO :]


def pair(linear, received, waited):
    return pl.pallas_call(
        pair_kernel,
        in_specs=[VMEM] * 2 + [pl.BlockSpec(memory_space=pl.ANY)],
        out_shape=jax.ShapeDtypeStruct(linear.shape, F32),
        out_specs=VMEM,
        compiler_params=pltpu.CompilerParams(**PARAMS),
        name="pair",
    )(linear, received, waited)


def join_kernel(start, width, mine, other, *refs):
    linear, out = refs[0], refs[-1]
    kf = mine.shape[0]
    span = min(SPAN, width)
    lane = lax.broadcasted_iota(jnp.int32, (kf, 128), 1)
    powers = jnp.zeros((kf, 128), F32)
    for i in range(width // span):
        at = slice(start + i * span, start + (i + 1) * span)
        total = mine[:, at] + other[:, at]
        power = power_of(jnp.max(jnp.abs(total), axis=1, keepdims=True))
        out[:, i * span : (i + 1) * span] = to_short(total * jnp.exp2(-power))
        powers = jnp.where(lane == i, power, powers)
    if start == 0:
        power = power_of(jnp.max(jnp.abs(linear[...]), axis=1, keepdims=True))
        scaled = linear[...] * jnp.exp2(-power)
        whole = jnp.round(scaled)
        out[:, width : width + LO] = to_short(whole)
        out[:, width + LO : width + 2 * LO] = to_short((scaled - whole) * 32768.0)
        powers = jnp.where(lane == 127, power, powers)
    out[:, out.shape[1] - 128 :] = to_short(powers)


def join(keep, received, start, width, linear, waited):
    kf, rows = keep.shape
    extra = 2 * LO if start == 0 else 0
    return pl.pallas_call(
        functools.partial(join_kernel, start, width),
        in_specs=[VMEM] * 3 + [pl.BlockSpec(memory_space=pl.ANY)] * len(waited),
        out_shape=jax.ShapeDtypeStruct((kf, width + extra + 128), jnp.int16),
        out_specs=VMEM,
        compiler_params=pltpu.CompilerParams(**PARAMS),
        name="join",
    )(keep, received, linear, *waited)


def table_kernel(rows, rank, waited, table):
    chunk = min(512, rows)
    lane = lax.broadcasted_iota(jnp.int32, (chunk, 128), 1)
    for start in range(0, rows, chunk):
        at = slice(start, start + chunk)
        inner = lax.rem(rank[:, at], LO)
        column = jnp.broadcast_to(inner.astype(F32), (128, chunk)).T.astype(jnp.int32)
        for first in range(0, LO, 128):
            table[at, first : first + 128] = jnp.where(column == lane + first, 1.0, 0.0).astype(BF16)


def tables(rank, waited, rows):
    return pl.pallas_call(
        functools.partial(table_kernel, rows),
        in_specs=[VMEM, pl.BlockSpec(memory_space=pl.ANY)],
        out_shape=jax.ShapeDtypeStruct((rows, LO), BF16),
        out_specs=VMEM,
        compiler_params=pltpu.CompilerParams(**PARAMS),
        cost_estimate=pl.CostEstimate(flops=rows * LO * 8, bytes_accessed=rows * LO * 2, transcendentals=0),
        name="tables",
    )(rank, waited)


def risk_kernel(rows, parts, linear, *refs):
    messages, (rank, events, table) = refs[:parts], refs[parts : parts + 3]
    risk_out, sums_out, events_out, message = refs[-4:]
    groups = rows // LO
    total = linear[...]
    for part in messages:
        end = part.shape[1] - 128
        power = from_short(part[:, end:])[:, 127:]
        high, low = from_short(part[:, end - 2 * LO : end - LO]), from_short(part[:, end - LO : end])
        total = total + (high + low * (1.0 / 32768.0)) * jnp.exp2(power)
    risk = jnp.exp(total)
    for g in range(groups):
        risk_out[:, g * LO : (g + 1) * LO] = risk[g : g + 1]
    mask = one_hot(lax.rem(rank[...], rows) // LO, groups, F32)
    pieces = [mask * part for part in split_three(risk_out[...])] + [mask * events[...].astype(F32)]
    lhs = jnp.concatenate(pieces, axis=0).astype(BF16)
    sorted_all = jnp.dot(lhs, table[...], preferred_element_type=F32)
    ordered = sorted_all[:groups] + sorted_all[groups : 2 * groups] + sorted_all[2 * groups : 3 * groups]
    happened = sorted_all[3 * groups :]
    inside = dot_binary(ordered, triangle(LO, lambda a, b: a >= b))
    totals = jnp.broadcast_to(inside[:, :1], inside.shape)
    carried = binary_dot(triangle(groups, lambda a, b: a < b), totals)
    sums_out[...] = inside + carried
    events_out[...] = happened
    everything = jnp.sum(totals, axis=0, keepdims=True)[:, :128]
    count = jnp.sum(dot_binary(happened, jnp.ones((LO, 128), F32)), axis=0, keepdims=True)
    message[...] = jnp.concatenate([everything, count, jnp.zeros((6, 128), F32)], axis=0)


def risks(linear, messages, rank, events, table, rows):
    groups = rows // LO
    return pl.pallas_call(
        functools.partial(risk_kernel, rows, len(messages)),
        in_specs=[VMEM] * (len(messages) + 4),
        out_shape=[
            jax.ShapeDtypeStruct((1, rows), F32),
            jax.ShapeDtypeStruct((groups, LO), F32),
            jax.ShapeDtypeStruct((groups, LO), F32),
            jax.ShapeDtypeStruct((8, 128), F32),
        ],
        out_specs=[VMEM] * 4,
        compiler_params=pltpu.CompilerParams(**PARAMS),
        cost_estimate=pl.CostEstimate(flops=rows * LO * 128, bytes_accessed=rows * 64, transcendentals=rows),
        name="risks",
    )(linear, *messages, rank, events, table)


def share_kernel(later, sums, events, plain, more, ordered, hazard_out, squares, message):
    kf = plain.shape[0]
    groups = sums.shape[0]
    risk_sum = sums[...] + later[0:1, 0:1]
    hazard = events[...] / risk_sum
    square = events[...] / (risk_sum * risk_sum)
    hazard_out[...] = hazard
    squares[...] = square
    scaled = jnp.zeros((kf, LO), F32)
    for g in range(groups):
        scaled = scaled + ordered[g * kf : (g + 1) * kf] * square[g : g + 1]
    message[:kf] = plain[...] + more[...]
    message[kf : 2 * kf] = sum(scaled[:, start : start + 128] for start in range(0, LO, 128))
    totals = [jnp.sum(jnp.sum(v, axis=0, keepdims=True), axis=1, keepdims=True) for v in (hazard, square)]
    rows = [jnp.broadcast_to(v, (1, 128)) for v in totals]
    message[2 * kf :] = jnp.concatenate(rows + [jnp.zeros((6, 128), F32)], axis=0)


def shares(later, sums, events, plain, more, ordered):
    flat = jax.ShapeDtypeStruct(sums.shape, F32)
    return pl.pallas_call(
        share_kernel,
        in_specs=[VMEM] * 6,
        out_shape=[flat, flat, jax.ShapeDtypeStruct((2 * plain.shape[0] + 8, 128), F32)],
        out_specs=[VMEM] * 3,
        compiler_params=pltpu.CompilerParams(**PARAMS),
        name="shares",
    )(later, sums, events, plain, more, ordered)


def hazard_kernel(rows, hazard, square, rank, cumulative, squares):
    groups = rows // LO
    inside = dot_binary(
        jnp.concatenate([hazard[...], square[...]], axis=0), triangle(LO, lambda a, b: a <= b)
    )
    totals = jnp.broadcast_to(inside[:, LO - 1 :], (2 * groups, 128))
    place = lax.rem(rank[...], rows)
    mask = one_hot(place // LO, groups, F32)
    placed = dot_binary(inside, one_hot(lax.rem(place, LO), LO))
    before = triangle(groups, lambda a, b: a > b)
    for first, out in ((0, cumulative), (groups, squares)):
        carried = binary_dot(before, totals[first : first + groups])[:, :1]
        out[...] = jnp.sum(mask * (placed[first : first + groups] + carried), axis=0, keepdims=True)


def hazards(hazard, square, rank, rows):
    row = jax.ShapeDtypeStruct((1, rows), F32)
    return pl.pallas_call(
        functools.partial(hazard_kernel, rows),
        in_specs=[VMEM] * 3,
        out_shape=[row, row],
        out_specs=[VMEM] * 2,
        compiler_params=pltpu.CompilerParams(**PARAMS),
        cost_estimate=pl.CostEstimate(flops=rows * LO * 200, bytes_accessed=rows * 64, transcendentals=0),
        name="hazards",
    )(hazard, square, rank)


def range_kernel(bit, count, *refs):
    total, other, later = refs[:3]
    total_out, later_out = refs[3 + count :]
    is_later = (lax.axis_index("ex") & bit) == 0
    later_out[...] = later[...] + jnp.where(is_later, other[...], 0.0)
    total_out[...] = total[...] + other[...]


def ranges(bit, total, other, later, waited):
    return pl.pallas_call(
        functools.partial(range_kernel, bit, len(waited)),
        in_specs=[VMEM] * 3 + [pl.BlockSpec(memory_space=pl.ANY)] * len(waited),
        out_shape=[jax.ShapeDtypeStruct(total.shape, F32)] * 2,
        out_specs=[VMEM] * 2,
        compiler_params=pltpu.CompilerParams(**PARAMS),
        name="ranges",
    )(total, other, later, *waited)


def order_kernel(start, parts, own, other, *refs):
    messages, (risk, rank, table) = refs[:parts], refs[parts : parts + 3]
    tangent_out, ordered_out, plain, lhs = refs[-4:]
    kf, width = tangent_out.shape
    rows = own.shape[1]
    groups = rows // LO
    span = min(SPAN, width)
    folded = jnp.zeros((kf, 128), F32)
    powers = [jnp.exp2(from_short(part[:, part.shape[1] - 128 :])) for part in messages]
    for i in range(width // span):
        at = slice(start + i * span, start + (i + 1) * span)
        here = slice(i * span, (i + 1) * span)
        tangent = own[:, at] + other[:, at]
        for part, power in zip(messages, powers):
            tangent = tangent + from_short(part[:, here]) * power[:, i : i + 1]
        tangent_out[:, here] = tangent
        weighted = tangent * risk[:, at]
        folded = folded + sum(weighted[:, j : j + 128] for j in range(0, span, 128))
        high, low = split_two(weighted)
        high, low = high.astype(BF16), low.astype(BF16)
        group = jnp.broadcast_to(lax.rem(rank[:, at], rows) // LO, (kf, span))
        for g in range(groups):
            mask = jnp.where(group == g, 1.0, 0.0).astype(BF16)
            lhs[2 * g * kf : (2 * g + 1) * kf, here] = high * mask
            lhs[(2 * g + 1) * kf : (2 * g + 2) * kf, here] = low * mask
    plain[...] = folded
    ordered = jnp.dot(lhs[...], table[start : start + width], preferred_element_type=F32)
    for g in range(groups):
        ordered_out[g * kf : (g + 1) * kf] = (
            ordered[2 * g * kf : (2 * g + 1) * kf] + ordered[(2 * g + 1) * kf : (2 * g + 2) * kf]
        )


def ordered_values(own, other, messages, risk, rank, table, start, width):
    kf, rows = own.shape
    groups = rows // LO
    return pl.pallas_call(
        functools.partial(order_kernel, start, len(messages)),
        in_specs=[VMEM] * (len(messages) + 5),
        out_shape=[
            jax.ShapeDtypeStruct((kf, width), F32),
            jax.ShapeDtypeStruct((groups * kf, LO), F32),
            jax.ShapeDtypeStruct((kf, 128), F32),
        ],
        out_specs=[VMEM] * 3,
        scratch_shapes=[pltpu.VMEM((groups * 2 * kf, width), BF16)],
        compiler_params=pltpu.CompilerParams(**PARAMS),
        cost_estimate=pl.CostEstimate(
            flops=2 * width * LO * groups * 2 * kf, bytes_accessed=width * kf * 24, transcendentals=0
        ),
        name="ordered_values",
    )(own, other, *messages, risk, rank, table)


def suffix_kernel(kf, one, two, sums):
    groups = sums.shape[0] // kf
    inside = dot_binary(one[...] + two[...], triangle(LO, lambda a, b: a >= b))
    carried = jnp.zeros((kf, 1), F32)
    for g in reversed(range(groups)):
        rows_of = slice(g * kf, (g + 1) * kf)
        sums[rows_of] = inside[rows_of] + carried
        carried = carried + inside[rows_of, :1]


def suffix_sums(one, two, kf):
    return pl.pallas_call(
        functools.partial(suffix_kernel, kf),
        in_specs=[VMEM] * 2,
        out_shape=jax.ShapeDtypeStruct(one.shape, F32),
        out_specs=VMEM,
        compiler_params=pltpu.CompilerParams(**PARAMS),
        name="suffix_sums",
    )(one, two)


def prefix_kernel(sums, squares, rank, out):
    kf, rows = out.shape
    groups = squares.shape[0]
    chunk = min(512, rows)
    hazard = [sums[g * kf : (g + 1) * kf] * squares[g : g + 1, :] for g in range(groups)]
    inside = dot_binary(jnp.concatenate(hazard, axis=0), triangle(LO, lambda a, b: a <= b))
    carried = jnp.zeros((kf, 1), F32)
    summed = [None] * groups
    for g in range(groups):
        rows_of = slice(g * kf, (g + 1) * kf)
        summed[g] = inside[rows_of] + carried
        carried = carried + inside[rows_of, LO - 1 :]
    both = stacked(split_two(jnp.concatenate(summed, axis=0)))
    for start in range(0, rows, chunk):
        at = slice(start, start + chunk)
        place = lax.rem(rank[:, at], rows)
        group = place // LO
        spread = one_hot(lax.rem(place, LO), LO)
        placed = unstacked(jnp.dot(both, spread, preferred_element_type=F32), 2)
        picked = jnp.zeros((kf, chunk), F32)
        for g in range(groups):
            picked = picked + jnp.where(group == g, placed[g * kf : (g + 1) * kf], 0.0)
        out[:, at] = picked


def prefix_sums(sums, squares, rank, kf):
    rows = rank.shape[1]
    return pl.pallas_call(
        prefix_kernel,
        in_specs=[VMEM] * 3,
        out_shape=jax.ShapeDtypeStruct((kf, rows), F32),
        out_specs=VMEM,
        compiler_params=pltpu.CompilerParams(**PARAMS),
        cost_estimate=pl.CostEstimate(
            flops=4 * rows * LO * (rows // LO) * kf, bytes_accessed=rows * kf * 24, transcendentals=0
        ),
        name="prefix_sums",
    )(sums, squares, rank)


def weight_kernel(ex, *refs):
    messages, (first, rest, local, risk, cumulative, squares) = refs[:ex], refs[ex : ex + 6]
    weighted, placed = refs[ex + 6 :]
    kf = first.shape[0]
    me = lax.axis_index("ex")
    for i in range(ex):
        placed[me ^ i] = messages[i][...]
    later = jnp.zeros((kf, 128), F32)
    own_later, before = later, later
    hazard_before = jnp.zeros((1, 128), F32)
    for b in reversed(range(ex)):
        plain, scaled, square = placed[b, :kf], placed[b, kf : 2 * kf], placed[b, 2 * kf + 1 : 2 * kf + 2]
        own_later = own_later + jnp.where(b > me, plain, 0.0)
        before = before + jnp.where(b < me, scaled + square * later, 0.0)
        hazard_before = hazard_before + jnp.where(b < me, placed[b, 2 * kf : 2 * kf + 1], 0.0)
        later = later + plain
    own_later = jnp.sum(own_later, axis=1, keepdims=True)
    before = jnp.sum(before, axis=1, keepdims=True)
    hazard_before = hazard_before[:, :1]
    for start, part in ((0, first), (first.shape[1], rest)):
        at = slice(start, start + part.shape[1])
        value = part[...] * (cumulative[:, at] + hazard_before) - (
            local[:, at] + squares[:, at] * own_later + before
        )
        weighted[:, at] = (risk[:, at] * value).astype(BF16)


def weights(messages, first, rest, local, risk, cumulative, squares):
    ex = len(messages)
    return pl.pallas_call(
        functools.partial(weight_kernel, ex),
        in_specs=[VMEM] * (ex + 6),
        out_shape=jax.ShapeDtypeStruct(local.shape, BF16),
        out_specs=VMEM,
        scratch_shapes=[pltpu.VMEM((ex,) + messages[0].shape, F32)],
        compiler_params=pltpu.CompilerParams(**PARAMS),
        name="weights",
    )(*messages, first, rest, local, risk, cumulative, squares)


def encode(values, message):
    columns = len(values)
    powers = []
    for i, value in enumerate(values):
        power = power_of(jnp.max(jnp.abs(value), axis=0, keepdims=True))
        scaled = to_short(value * jnp.exp2(-power))
        for j in range(value.shape[0] // 16):
            message[j * columns + i] = scaled[j * 16 : (j + 1) * 16]
        powers.append(power)
    powers.append(jnp.zeros((16 - columns, 128), F32))
    message[message.shape[0] - 1] = to_short(jnp.concatenate(powers, axis=0))


def decode(message, columns):
    last = message.shape[0] - 1
    scales = jnp.exp2(from_short(message[last]))
    values = []
    for i in range(columns):
        value = jnp.concatenate([from_short(message[j]) for j in range(i, last, columns)], axis=0)
        values.append(value * scales[i : i + 1])
    return values


def decode_sum(mine, other, columns):
    return [one + two for one, two in zip(decode(mine, columns), decode(other, columns))]


def gradient_kernel(parts, kf, *refs):
    pieces, dosages, out, weighted = refs[:parts], refs[parts], refs[parts + 1], refs[parts + 2]
    for i in range(parts):
        weighted[i * kf : (i + 1) * kf, :] = pieces[i][...]
    total = jnp.dot(weighted[...], dosages[...], preferred_element_type=F32)
    encode([total[:, at : at + 128] for at in range(0, total.shape[1], 128)], out)


def gradients(pieces, dosages):
    parts = len(pieces)
    kf, persons = pieces[0].shape
    k, variants = kf * parts, dosages.shape[1]
    return pl.pallas_call(
        functools.partial(gradient_kernel, parts, kf),
        in_specs=[VMEM] * (parts + 1),
        out_shape=jax.ShapeDtypeStruct((k * variants // 2048 + 1, 16, 128), jnp.int16),
        out_specs=VMEM,
        scratch_shapes=[pltpu.VMEM((k, persons), BF16)],
        compiler_params=pltpu.CompilerParams(**PARAMS),
        cost_estimate=pl.CostEstimate(
            flops=2 * persons * variants * k, bytes_accessed=persons * (variants * 2 + k * 2), transcendentals=0
        ),
        name="gradients",
    )(*pieces, dosages)


def merge_kernel(columns, mine, other, out):
    encode(decode_sum(mine, other, columns), out)


def merge(mine, other, variants):
    return pl.pallas_call(
        functools.partial(merge_kernel, variants // 128),
        in_specs=[VMEM] * 2,
        out_shape=jax.ShapeDtypeStruct(mine.shape, jnp.int16),
        out_specs=VMEM,
        compiler_params=pltpu.CompilerParams(**PARAMS),
        name="merge",
    )(mine, other)


def add_kernel(mine, other, out):
    for i, value in enumerate(decode_sum(mine, other, out.shape[1] // 128)):
        out[:, i * 128 : (i + 1) * 128] = value


def add(mine, other, variants):
    return pl.pallas_call(
        add_kernel,
        in_specs=[VMEM] * 2,
        out_shape=jax.ShapeDtypeStruct(((mine.shape[0] - 1) * 2048 // variants, variants), F32),
        out_specs=VMEM,
        compiler_params=pltpu.CompilerParams(**PARAMS),
        name="add",
    )(mine, other)


def finish_kernel(feat, kf, first, mine, other, count, out, placed, total, sems):
    me = lax.axis_index("feat")
    variants = out.shape[0]
    scale = count[1:2, 0:1]
    for q in range(feat // 2):
        placed[me ^ (2 * q)] = first[q * kf : (q + 1) * kf]
    for i, value in enumerate(decode_sum(mine, other, variants // 128)):
        for q in range(feat // 2):
            placed[me ^ (2 * q + 1), :, i * 128 : (i + 1) * 128] = value[q * kf : (q + 1) * kf]
    copies = []
    for i in range(variants // 128):
        at = slice(i * 128, (i + 1) * 128)
        total[at] = placed[:, :, at].reshape(feat * kf, 128).T / scale
        copies.append(
            pltpu.make_async_copy(
                total.at[pl.ds(i * 128, 128)], out.at[pl.ds(i * 128, 128)], sems.at[i]
            )
        )
        copies[i].start()
    for copy in copies:
        copy.wait()


def finish(first, mine, other, count, feat):
    k, variants = 2 * first.shape[0], first.shape[1]
    kf = k // feat
    return pl.pallas_call(
        functools.partial(finish_kernel, feat, kf),
        in_specs=[VMEM] * 4,
        out_shape=jax.ShapeDtypeStruct((variants, k), F32),
        out_specs=HBM,
        scratch_shapes=[
            pltpu.VMEM((feat, kf, variants), F32),
            pltpu.VMEM((variants, k), F32),
            pltpu.SemaphoreType.DMA((variants // 128,)),
        ],
        compiler_params=pltpu.CompilerParams(**PARAMS),
        name="finish",
    )(first, mine, other, count)


def local(dosages, coefficients, directions, event_rank, events):
    feat, ex = lax.axis_size("feat"), lax.axis_size("ex")
    rows = dosages.shape[0]
    variants, k = directions.shape
    each = k // feat
    padded = -(-each // 16) * 16
    if padded != each:
        directions = jnp.pad(directions.reshape(variants, feat, each), ((0, 0), (0, 0), (0, padded - each)))
        directions = directions.reshape(variants, feat * padded)
    rank, event_row = event_rank[None], events[None]

    linear, keep, send = products(dosages, coefficients, directions, feat)
    order = list(reversed(range(1, feat // 2)))
    received = {q: swap(send[q], "feat", 1) for q in order + [0]}
    table = tables(rank, linear, rows)
    paired = pair(linear, received[order[0]], table)
    middle = min(3 * SPAN, rows // 2)
    firsts = [
        swap(join(keep[q], received[q], 0, middle, paired, []), "feat", 2 * q) for q in order
    ]
    rests = [
        swap(join(keep[q], received[q], middle, rows - middle, paired, [received[0]]), "feat", 2 * q)
        for q in order
    ]

    risk, sums, ordered_events, total = risks(paired, firsts, rank, event_row, table, rows)
    later = jnp.zeros_like(total)
    bit = 1
    while bit < ex:
        total, later = ranges(bit, total, swap(total, "ex", bit), later, rests if bit == 1 else [])
        bit *= 2
    tangent, one, plain = ordered_values(keep[0], received[0], firsts, risk, rank, table, 0, middle)
    more_tangent, two, more = ordered_values(
        keep[0], received[0], rests, risk, rank, table, middle, rows - middle
    )
    later_sums = suffix_sums(one, two, padded)
    hazard, ordered_squares, message = shares(later, sums, ordered_events, plain, more, later_sums)
    messages = [message] + [swap(message, "ex", i) for i in range(1, ex)]
    cumulative, squares = hazards(hazard, ordered_squares, rank, rows)
    summed = prefix_sums(later_sums, ordered_squares, rank, padded)
    own = weights(messages, tangent, more_tangent, summed, risk, cumulative, squares)

    chips = {0: own}
    for q in reversed(range(1, feat // 2)):
        chips[q] = swap(own, "feat", 2 * q)
    near = [chips[q] for q in range(feat // 2)]
    far = [swap(chips[q], "feat", 1) for q in range(feat // 2)]
    partial_sums = [gradients(pieces, dosages) for pieces in (near, far)]
    bit = 1
    while 2 * bit < ex:
        received = [swap(message, "ex", bit) for message in partial_sums]
        partial_sums = [merge(mine, other, variants) for mine, other in zip(partial_sums, received)]
        bit *= 2
    received = [swap(message, "ex", bit) for message in partial_sums]
    first = add(partial_sums[0], received[0], variants)
    result = finish(first, partial_sums[1], received[1], total, feat)
    if padded != each:
        result = result.reshape(variants, feat, padded)[:, :, :each].reshape(variants, k)
    return result


def solution(mesh):
    placed = (P("ex", "feat"), P("feat"), P("feat", None), P("ex"), P("ex"))
    return jax.shard_map(
        local, mesh=mesh, in_specs=placed, out_specs=P("feat", None), check_vma=False
    )
```

```python
import functools

import jax
import jax.numpy as jnp
from jax import lax
from jax.experimental import pallas as pl
from jax.experimental.pallas import tpu as pltpu
from jax.sharding import PartitionSpec as P

F32 = jnp.float32
BF16 = jnp.bfloat16
LO = 256
NT = (((1,), (1,)), ((), ()))
SPAN = 512
VMEM = pl.BlockSpec(memory_space=pltpu.VMEM)
HBM = pl.BlockSpec(memory_space=pltpu.HBM)
PARAMS = dict(vmem_limit_bytes=24 * 1024 * 1024)


def swap(x, axis, i):
    count = lax.axis_size(axis)
    return lax.ppermute(x, axis, [(s, s ^ i) for s in range(count)])


def split_two(x):
    high = x.astype(BF16).astype(F32)
    return high, x - high


def split_three(x):
    first, rest = split_two(x)
    second, third = split_two(rest)
    return first, second, third


def one_hot(values, count, kind=BF16):
    shape = (count, values.shape[1])
    return jnp.where(lax.broadcasted_iota(jnp.int32, shape, 0) == values, 1.0, 0.0).astype(kind)


def triangle(n, keep):
    first = lax.broadcasted_iota(jnp.int32, (n, n), 0)
    second = lax.broadcasted_iota(jnp.int32, (n, n), 1)
    return jnp.where(keep(first, second), 1.0, 0.0)


def stacked(parts):
    return jnp.concatenate(parts, axis=0).astype(BF16)


def unstacked(values, count):
    height = values.shape[0] // count
    return sum(values[i * height : (i + 1) * height] for i in range(count))


def dot_binary(a, b):
    parts = jnp.dot(stacked(split_three(a)), b.astype(BF16), preferred_element_type=F32)
    return unstacked(parts, 3)


def binary_dot(a, b):
    a = a.astype(BF16)
    total = None
    for part in split_three(b):
        term = jnp.dot(a, part.astype(BF16), preferred_element_type=F32)
        total = term if total is None else total + term
    return total


def product_kernel(feat, kf, chunk, directions, coefficients, dosages, *refs):
    linear, keep, send = refs[0], refs[1 : 1 + feat // 2], refs[1 + feat // 2 : 1 + feat]
    table, own_directions, own_coefficients, lhs, turned, sems = refs[1 + feat :]
    me = lax.axis_index("feat")
    width = feat * kf
    persons, variants = table.shape
    steps = persons // chunk
    small = [
        pltpu.make_async_copy(directions, own_directions, sems.at[steps]),
        pltpu.make_async_copy(coefficients, own_coefficients, sems.at[steps + 1]),
    ]
    large = [
        pltpu.make_async_copy(
            dosages.at[pl.ds(i * chunk, chunk)], table.at[pl.ds(i * chunk, chunk)], sems.at[i]
        )
        for i in range(steps)
    ]
    for i, copy in enumerate(small + large):
        copy.start(priority=i % 2)
    for copy in small:
        copy.wait()
    turned[...] = own_directions[...].astype(F32).T.reshape(turned.shape)
    for j in range(feat):
        lhs[j * kf : (j + 1) * kf] = turned[me ^ j].astype(BF16)
    lhs[width:] = jnp.broadcast_to(own_coefficients[...].astype(F32)[None, :], (16, variants)).astype(BF16)
    for i in range(steps):
        large[i].wait()
        first = i * chunk
        result = lax.dot_general(
            lhs[...], table[first : first + chunk], NT, preferred_element_type=F32
        )
        for j in range(feat):
            (send if j % 2 else keep)[j // 2][:, first : first + chunk] = result[j * kf : (j + 1) * kf]
        for start in range(0, chunk, LO):
            row = result[width : width + 1, start : start + LO]
            group = (first + start) // LO
            linear[group : group + 1, :] = row
            send[-1][group : group + 1, persons:] = row


def products(dosages, coefficients, directions, feat):
    persons, variants = dosages.shape
    k = directions.shape[1]
    kf = k // feat
    chunk = min(512, persons)
    piece = jax.ShapeDtypeStruct((kf, persons), F32)
    first = jax.ShapeDtypeStruct((kf, persons + LO), F32)
    out = pl.pallas_call(
        functools.partial(product_kernel, feat, kf, chunk),
        in_specs=[HBM, HBM, HBM],
        out_shape=[jax.ShapeDtypeStruct((kf, LO), F32)]
        + [piece] * (feat - 1)
        + [first],
        out_specs=[VMEM] * (feat + 1),
        scratch_shapes=[
            pltpu.VMEM((persons, variants), BF16),
            pltpu.VMEM((variants, k), BF16),
            pltpu.VMEM((variants,), BF16),
            pltpu.VMEM((k + 16, variants), BF16),
            pltpu.VMEM((feat, kf, variants), F32),
            pltpu.SemaphoreType.DMA((persons // chunk + 2,)),
        ],
        compiler_params=pltpu.CompilerParams(**PARAMS),
        cost_estimate=pl.CostEstimate(
            flops=2 * persons * variants * k, bytes_accessed=persons * (variants * 2 + k * 4), transcendentals=0
        ),
        name="products",
    )(*[pltpu.with_memory_space_constraint(x, pltpu.HBM) for x in (directions, coefficients, dosages)])
    return out[0], out[1 : 1 + feat // 2], out[1 + feat // 2 :]


def power_of(largest):
    return jnp.ceil(jnp.log2(jnp.maximum(largest, 1e-30))) - 14.0


def to_short(values):
    return jnp.round(values).astype(jnp.int32).astype(jnp.int16)


def from_short(values):
    return values.astype(jnp.int32).astype(F32)


def pair_kernel(linear, received, waited, out):
    out[...] = linear[...] + received[:, received.shape[1] - LO :]


def pair(linear, received, waited):
    return pl.pallas_call(
        pair_kernel,
        in_specs=[VMEM] * 2 + [pl.BlockSpec(memory_space=pl.ANY)],
        out_shape=jax.ShapeDtypeStruct(linear.shape, F32),
        out_specs=VMEM,
        compiler_params=pltpu.CompilerParams(**PARAMS),
        name="pair",
    )(linear, received, waited)


def join_kernel(start, width, mine, other, *refs):
    linear, out = refs[0], refs[-1]
    kf = mine.shape[0]
    span = min(SPAN, width)
    lane = lax.broadcasted_iota(jnp.int32, (kf, 128), 1)
    powers = jnp.zeros((kf, 128), F32)
    for i in range(width // span):
        at = slice(start + i * span, start + (i + 1) * span)
        total = mine[:, at] + other[:, at]
        power = power_of(jnp.max(jnp.abs(total), axis=1, keepdims=True))
        out[:, i * span : (i + 1) * span] = to_short(total * jnp.exp2(-power))
        powers = jnp.where(lane == i, power, powers)
    if start == 0:
        power = power_of(jnp.max(jnp.abs(linear[...]), axis=1, keepdims=True))
        scaled = linear[...] * jnp.exp2(-power)
        whole = jnp.round(scaled)
        out[:, width : width + LO] = to_short(whole)
        out[:, width + LO : width + 2 * LO] = to_short((scaled - whole) * 32768.0)
        powers = jnp.where(lane == 127, power, powers)
    out[:, out.shape[1] - 128 :] = to_short(powers)


def join(keep, received, start, width, linear, waited):
    kf, rows = keep.shape
    extra = 2 * LO if start == 0 else 0
    return pl.pallas_call(
        functools.partial(join_kernel, start, width),
        in_specs=[VMEM] * 3 + [pl.BlockSpec(memory_space=pl.ANY)] * len(waited),
        out_shape=jax.ShapeDtypeStruct((kf, width + extra + 128), jnp.int16),
        out_specs=VMEM,
        compiler_params=pltpu.CompilerParams(**PARAMS),
        name="join",
    )(keep, received, linear, *waited)


def table_kernel(rows, rank, waited, table):
    chunk = min(512, rows)
    lane = lax.broadcasted_iota(jnp.int32, (chunk, 128), 1)
    for start in range(0, rows, chunk):
        at = slice(start, start + chunk)
        inner = lax.rem(rank[:, at], LO)
        column = jnp.broadcast_to(inner.astype(F32), (128, chunk)).T.astype(jnp.int32)
        for first in range(0, LO, 128):
            table[at, first : first + 128] = jnp.where(column == lane + first, 1.0, 0.0).astype(BF16)


def tables(rank, waited, rows):
    return pl.pallas_call(
        functools.partial(table_kernel, rows),
        in_specs=[VMEM, pl.BlockSpec(memory_space=pl.ANY)],
        out_shape=jax.ShapeDtypeStruct((rows, LO), BF16),
        out_specs=VMEM,
        compiler_params=pltpu.CompilerParams(**PARAMS),
        cost_estimate=pl.CostEstimate(flops=rows * LO * 8, bytes_accessed=rows * LO * 2, transcendentals=0),
        name="tables",
    )(rank, waited)


def risk_kernel(rows, parts, linear, *refs):
    messages, (rank, events, table) = refs[:parts], refs[parts : parts + 3]
    risk_out, sums_out, events_out, message = refs[-4:]
    groups = rows // LO
    total = linear[...]
    for part in messages:
        end = part.shape[1] - 128
        power = from_short(part[:, end:])[:, 127:]
        high, low = from_short(part[:, end - 2 * LO : end - LO]), from_short(part[:, end - LO : end])
        total = total + (high + low * (1.0 / 32768.0)) * jnp.exp2(power)
    risk = jnp.exp(total)
    for g in range(groups):
        risk_out[:, g * LO : (g + 1) * LO] = risk[g : g + 1]
    mask = one_hot(lax.rem(rank[...], rows) // LO, groups, F32)
    pieces = [mask * part for part in split_three(risk_out[...])] + [mask * events[...].astype(F32)]
    lhs = jnp.concatenate(pieces, axis=0).astype(BF16)
    sorted_all = jnp.dot(lhs, table[...], preferred_element_type=F32)
    ordered = sorted_all[:groups] + sorted_all[groups : 2 * groups] + sorted_all[2 * groups : 3 * groups]
    happened = sorted_all[3 * groups :]
    inside = dot_binary(ordered, triangle(LO, lambda a, b: a >= b))
    totals = jnp.broadcast_to(inside[:, :1], inside.shape)
    carried = binary_dot(triangle(groups, lambda a, b: a < b), totals)
    sums_out[...] = inside + carried
    events_out[...] = happened
    everything = jnp.sum(totals, axis=0, keepdims=True)[:, :128]
    count = jnp.sum(dot_binary(happened, jnp.ones((LO, 128), F32)), axis=0, keepdims=True)
    message[...] = jnp.concatenate([everything, count, jnp.zeros((6, 128), F32)], axis=0)


def risks(linear, messages, rank, events, table, rows):
    groups = rows // LO
    return pl.pallas_call(
        functools.partial(risk_kernel, rows, len(messages)),
        in_specs=[VMEM] * (len(messages) + 4),
        out_shape=[
            jax.ShapeDtypeStruct((1, rows), F32),
            jax.ShapeDtypeStruct((groups, LO), F32),
            jax.ShapeDtypeStruct((groups, LO), F32),
            jax.ShapeDtypeStruct((8, 128), F32),
        ],
        out_specs=[VMEM] * 4,
        compiler_params=pltpu.CompilerParams(**PARAMS),
        cost_estimate=pl.CostEstimate(flops=rows * LO * 128, bytes_accessed=rows * 64, transcendentals=rows),
        name="risks",
    )(linear, *messages, rank, events, table)


def share_kernel(later, sums, events, plain, more, ordered, hazard_out, squares, message):
    kf = plain.shape[0]
    groups = sums.shape[0]
    risk_sum = sums[...] + later[0:1, 0:1]
    hazard = events[...] / risk_sum
    square = events[...] / (risk_sum * risk_sum)
    hazard_out[...] = hazard
    squares[...] = square
    scaled = jnp.zeros((kf, LO), F32)
    for g in range(groups):
        scaled = scaled + ordered[g * kf : (g + 1) * kf] * square[g : g + 1]
    columns = [plain[...] + more[...], sum(scaled[:, start : start + 128] for start in range(0, LO, 128))]
    columns += [jnp.sum(v, axis=0, keepdims=True) for v in (hazard, square)]
    lane = lax.broadcasted_iota(jnp.int32, (kf, 128), 1)
    packed = jnp.zeros((kf, 128), F32)
    for i, column in enumerate(columns):
        packed = jnp.where(lane == i, jnp.sum(column, axis=1, keepdims=True), packed)
    message[...] = packed


def shares(later, sums, events, plain, more, ordered):
    flat = jax.ShapeDtypeStruct(sums.shape, F32)
    return pl.pallas_call(
        share_kernel,
        in_specs=[VMEM] * 6,
        out_shape=[flat, flat, jax.ShapeDtypeStruct(plain.shape, F32)],
        out_specs=[VMEM] * 3,
        compiler_params=pltpu.CompilerParams(**PARAMS),
        name="shares",
    )(later, sums, events, plain, more, ordered)


def hazard_kernel(rows, hazard, square, rank, cumulative, squares):
    groups = rows // LO
    inside = dot_binary(
        jnp.concatenate([hazard[...], square[...]], axis=0), triangle(LO, lambda a, b: a <= b)
    )
    totals = jnp.broadcast_to(inside[:, LO - 1 :], (2 * groups, 128))
    place = lax.rem(rank[...], rows)
    mask = one_hot(place // LO, groups, F32)
    placed = dot_binary(inside, one_hot(lax.rem(place, LO), LO))
    before = triangle(groups, lambda a, b: a > b)
    for first, out in ((0, cumulative), (groups, squares)):
        carried = binary_dot(before, totals[first : first + groups])[:, :1]
        out[...] = jnp.sum(mask * (placed[first : first + groups] + carried), axis=0, keepdims=True)


def hazards(hazard, square, rank, rows):
    row = jax.ShapeDtypeStruct((1, rows), F32)
    return pl.pallas_call(
        functools.partial(hazard_kernel, rows),
        in_specs=[VMEM] * 3,
        out_shape=[row, row],
        out_specs=[VMEM] * 2,
        compiler_params=pltpu.CompilerParams(**PARAMS),
        cost_estimate=pl.CostEstimate(flops=rows * LO * 200, bytes_accessed=rows * 64, transcendentals=0),
        name="hazards",
    )(hazard, square, rank)


def range_kernel(bit, count, *refs):
    total, other, later = refs[:3]
    total_out, later_out = refs[3 + count :]
    is_later = (lax.axis_index("ex") & bit) == 0
    later_out[...] = later[...] + jnp.where(is_later, other[...], 0.0)
    total_out[...] = total[...] + other[...]


def ranges(bit, total, other, later, waited):
    return pl.pallas_call(
        functools.partial(range_kernel, bit, len(waited)),
        in_specs=[VMEM] * 3 + [pl.BlockSpec(memory_space=pl.ANY)] * len(waited),
        out_shape=[jax.ShapeDtypeStruct(total.shape, F32)] * 2,
        out_specs=[VMEM] * 2,
        compiler_params=pltpu.CompilerParams(**PARAMS),
        name="ranges",
    )(total, other, later, *waited)


def order_kernel(start, parts, own, other, *refs):
    messages, (risk, rank, table) = refs[:parts], refs[parts : parts + 3]
    tangent_out, ordered_out, plain, lhs = refs[-4:]
    kf, width = tangent_out.shape
    rows = own.shape[1]
    groups = rows // LO
    span = min(SPAN, width)
    folded = jnp.zeros((kf, 128), F32)
    powers = [jnp.exp2(from_short(part[:, part.shape[1] - 128 :])) for part in messages]
    for i in range(width // span):
        at = slice(start + i * span, start + (i + 1) * span)
        here = slice(i * span, (i + 1) * span)
        tangent = own[:, at] + other[:, at]
        for part, power in zip(messages, powers):
            tangent = tangent + from_short(part[:, here]) * power[:, i : i + 1]
        tangent_out[:, here] = tangent
        weighted = tangent * risk[:, at]
        folded = folded + sum(weighted[:, j : j + 128] for j in range(0, span, 128))
        high, low = split_two(weighted)
        high, low = high.astype(BF16), low.astype(BF16)
        group = jnp.broadcast_to(lax.rem(rank[:, at], rows) // LO, (kf, span))
        for g in range(groups):
            mask = jnp.where(group == g, 1.0, 0.0).astype(BF16)
            lhs[2 * g * kf : (2 * g + 1) * kf, here] = high * mask
            lhs[(2 * g + 1) * kf : (2 * g + 2) * kf, here] = low * mask
    plain[...] = folded
    ordered = jnp.dot(lhs[...], table[start : start + width], preferred_element_type=F32)
    for g in range(groups):
        ordered_out[g * kf : (g + 1) * kf] = (
            ordered[2 * g * kf : (2 * g + 1) * kf] + ordered[(2 * g + 1) * kf : (2 * g + 2) * kf]
        )


def ordered_values(own, other, messages, risk, rank, table, start, width):
    kf, rows = own.shape
    groups = rows // LO
    return pl.pallas_call(
        functools.partial(order_kernel, start, len(messages)),
        in_specs=[VMEM] * (len(messages) + 5),
        out_shape=[
            jax.ShapeDtypeStruct((kf, width), F32),
            jax.ShapeDtypeStruct((groups * kf, LO), F32),
            jax.ShapeDtypeStruct((kf, 128), F32),
        ],
        out_specs=[VMEM] * 3,
        scratch_shapes=[pltpu.VMEM((groups * 2 * kf, width), BF16)],
        compiler_params=pltpu.CompilerParams(**PARAMS),
        cost_estimate=pl.CostEstimate(
            flops=2 * width * LO * groups * 2 * kf, bytes_accessed=width * kf * 24, transcendentals=0
        ),
        name="ordered_values",
    )(own, other, *messages, risk, rank, table)


def suffix_kernel(kf, one, two, sums):
    groups = sums.shape[0] // kf
    inside = dot_binary(one[...] + two[...], triangle(LO, lambda a, b: a >= b))
    carried = jnp.zeros((kf, 1), F32)
    for g in reversed(range(groups)):
        rows_of = slice(g * kf, (g + 1) * kf)
        sums[rows_of] = inside[rows_of] + carried
        carried = carried + inside[rows_of, :1]


def suffix_sums(one, two, kf):
    return pl.pallas_call(
        functools.partial(suffix_kernel, kf),
        in_specs=[VMEM] * 2,
        out_shape=jax.ShapeDtypeStruct(one.shape, F32),
        out_specs=VMEM,
        compiler_params=pltpu.CompilerParams(**PARAMS),
        name="suffix_sums",
    )(one, two)


def prefix_kernel(sums, squares, rank, out):
    kf, rows = out.shape
    groups = squares.shape[0]
    chunk = min(512, rows)
    hazard = [sums[g * kf : (g + 1) * kf] * squares[g : g + 1, :] for g in range(groups)]
    inside = dot_binary(jnp.concatenate(hazard, axis=0), triangle(LO, lambda a, b: a <= b))
    carried = jnp.zeros((kf, 1), F32)
    summed = [None] * groups
    for g in range(groups):
        rows_of = slice(g * kf, (g + 1) * kf)
        summed[g] = inside[rows_of] + carried
        carried = carried + inside[rows_of, LO - 1 :]
    both = stacked(split_two(jnp.concatenate(summed, axis=0)))
    for start in range(0, rows, chunk):
        at = slice(start, start + chunk)
        place = lax.rem(rank[:, at], rows)
        group = place // LO
        spread = one_hot(lax.rem(place, LO), LO)
        placed = unstacked(jnp.dot(both, spread, preferred_element_type=F32), 2)
        picked = jnp.zeros((kf, chunk), F32)
        for g in range(groups):
            picked = picked + jnp.where(group == g, placed[g * kf : (g + 1) * kf], 0.0)
        out[:, at] = picked


def prefix_sums(sums, squares, rank, kf):
    rows = rank.shape[1]
    return pl.pallas_call(
        prefix_kernel,
        in_specs=[VMEM] * 3,
        out_shape=jax.ShapeDtypeStruct((kf, rows), F32),
        out_specs=VMEM,
        compiler_params=pltpu.CompilerParams(**PARAMS),
        cost_estimate=pl.CostEstimate(
            flops=4 * rows * LO * (rows // LO) * kf, bytes_accessed=rows * kf * 24, transcendentals=0
        ),
        name="prefix_sums",
    )(sums, squares, rank)


def weight_kernel(ex, *refs):
    messages, (first, rest, local, risk, cumulative, squares) = refs[:ex], refs[ex : ex + 6]
    weighted, placed = refs[ex + 6 :]
    kf = first.shape[0]
    me = lax.axis_index("ex")
    for i in range(ex):
        placed[me ^ i] = messages[i][...]
    later = jnp.zeros((kf, 1), F32)
    own_later, before, hazard_before = later, later, later
    for b in reversed(range(ex)):
        plain, scaled, hazard, square = [placed[b, :, i : i + 1] for i in range(4)]
        own_later = own_later + jnp.where(b > me, plain, 0.0)
        before = before + jnp.where(b < me, scaled + square * later, 0.0)
        hazard_before = hazard_before + jnp.where(b < me, hazard, 0.0)
        later = later + plain
    for start, part in ((0, first), (first.shape[1], rest)):
        at = slice(start, start + part.shape[1])
        value = part[...] * (cumulative[:, at] + hazard_before) - (
            local[:, at] + squares[:, at] * own_later + before
        )
        weighted[:, at] = (risk[:, at] * value).astype(BF16)


def weights(messages, first, rest, local, risk, cumulative, squares):
    ex = len(messages)
    return pl.pallas_call(
        functools.partial(weight_kernel, ex),
        in_specs=[VMEM] * (ex + 6),
        out_shape=jax.ShapeDtypeStruct(local.shape, BF16),
        out_specs=VMEM,
        scratch_shapes=[pltpu.VMEM((ex,) + messages[0].shape, F32)],
        compiler_params=pltpu.CompilerParams(**PARAMS),
        name="weights",
    )(*messages, first, rest, local, risk, cumulative, squares)


def encode(values, message):
    columns = len(values)
    powers = []
    for i, value in enumerate(values):
        power = power_of(jnp.max(jnp.abs(value), axis=0, keepdims=True))
        scaled = to_short(value * jnp.exp2(-power))
        for j in range(value.shape[0] // 16):
            message[j * columns + i] = scaled[j * 16 : (j + 1) * 16]
        powers.append(power)
    powers.append(jnp.zeros((16 - columns, 128), F32))
    message[message.shape[0] - 1] = to_short(jnp.concatenate(powers, axis=0))


def decode(message, columns):
    last = message.shape[0] - 1
    scales = jnp.exp2(from_short(message[last]))
    values = []
    for i in range(columns):
        value = jnp.concatenate([from_short(message[j]) for j in range(i, last, columns)], axis=0)
        values.append(value * scales[i : i + 1])
    return values


def decode_sum(mine, other, columns):
    return [one + two for one, two in zip(decode(mine, columns), decode(other, columns))]


def gradient_kernel(parts, kf, *refs):
    pieces, dosages, out, weighted = refs[:parts], refs[parts], refs[parts + 1], refs[parts + 2]
    for i in range(parts):
        weighted[i * kf : (i + 1) * kf, :] = pieces[i][...]
    total = jnp.dot(weighted[...], dosages[...], preferred_element_type=F32)
    encode([total[:, at : at + 128] for at in range(0, total.shape[1], 128)], out)


def gradients(pieces, dosages):
    parts = len(pieces)
    kf, persons = pieces[0].shape
    k, variants = kf * parts, dosages.shape[1]
    return pl.pallas_call(
        functools.partial(gradient_kernel, parts, kf),
        in_specs=[VMEM] * (parts + 1),
        out_shape=jax.ShapeDtypeStruct((k * variants // 2048 + 1, 16, 128), jnp.int16),
        out_specs=VMEM,
        scratch_shapes=[pltpu.VMEM((k, persons), BF16)],
        compiler_params=pltpu.CompilerParams(**PARAMS),
        cost_estimate=pl.CostEstimate(
            flops=2 * persons * variants * k, bytes_accessed=persons * (variants * 2 + k * 2), transcendentals=0
        ),
        name="gradients",
    )(*pieces, dosages)


def merge_kernel(columns, mine, other, out):
    encode(decode_sum(mine, other, columns), out)


def merge(mine, other, variants):
    return pl.pallas_call(
        functools.partial(merge_kernel, variants // 128),
        in_specs=[VMEM] * 2,
        out_shape=jax.ShapeDtypeStruct(mine.shape, jnp.int16),
        out_specs=VMEM,
        compiler_params=pltpu.CompilerParams(**PARAMS),
        name="merge",
    )(mine, other)


def add_kernel(mine, other, out):
    for i, value in enumerate(decode_sum(mine, other, out.shape[1] // 128)):
        out[:, i * 128 : (i + 1) * 128] = value


def add(mine, other, variants):
    return pl.pallas_call(
        add_kernel,
        in_specs=[VMEM] * 2,
        out_shape=jax.ShapeDtypeStruct(((mine.shape[0] - 1) * 2048 // variants, variants), F32),
        out_specs=VMEM,
        compiler_params=pltpu.CompilerParams(**PARAMS),
        name="add",
    )(mine, other)


def finish_kernel(feat, kf, first, mine, other, count, out, placed, total, sems):
    me = lax.axis_index("feat")
    variants = out.shape[0]
    scale = count[1:2, 0:1]
    for q in range(feat // 2):
        placed[me ^ (2 * q)] = first[q * kf : (q + 1) * kf]
    for i, value in enumerate(decode_sum(mine, other, variants // 128)):
        for q in range(feat // 2):
            placed[me ^ (2 * q + 1), :, i * 128 : (i + 1) * 128] = value[q * kf : (q + 1) * kf]
    copies = []
    for i in range(variants // 128):
        at = slice(i * 128, (i + 1) * 128)
        total[at] = placed[:, :, at].reshape(feat * kf, 128).T / scale
        copies.append(
            pltpu.make_async_copy(
                total.at[pl.ds(i * 128, 128)], out.at[pl.ds(i * 128, 128)], sems.at[i]
            )
        )
        copies[i].start()
    for copy in copies:
        copy.wait()


def finish(first, mine, other, count, feat):
    k, variants = 2 * first.shape[0], first.shape[1]
    kf = k // feat
    return pl.pallas_call(
        functools.partial(finish_kernel, feat, kf),
        in_specs=[VMEM] * 4,
        out_shape=jax.ShapeDtypeStruct((variants, k), F32),
        out_specs=HBM,
        scratch_shapes=[
            pltpu.VMEM((feat, kf, variants), F32),
            pltpu.VMEM((variants, k), F32),
            pltpu.SemaphoreType.DMA((variants // 128,)),
        ],
        compiler_params=pltpu.CompilerParams(**PARAMS),
        name="finish",
    )(first, mine, other, count)


def local(dosages, coefficients, directions, event_rank, events):
    feat, ex = lax.axis_size("feat"), lax.axis_size("ex")
    rows = dosages.shape[0]
    variants, k = directions.shape
    each = k // feat
    padded = -(-each // 16) * 16
    if padded != each:
        directions = jnp.pad(directions.reshape(variants, feat, each), ((0, 0), (0, 0), (0, padded - each)))
        directions = directions.reshape(variants, feat * padded)
    rank, event_row = event_rank[None], events[None]

    linear, keep, send = products(dosages, coefficients, directions, feat)
    order = list(reversed(range(1, feat // 2)))
    received = {q: swap(send[q], "feat", 1) for q in order + [0]}
    table = tables(rank, linear, rows)
    paired = pair(linear, received[order[0]], table)
    middle = min(3 * SPAN, rows // 2)
    firsts = [
        swap(join(keep[q], received[q], 0, middle, paired, []), "feat", 2 * q) for q in order
    ]
    rests = [
        swap(join(keep[q], received[q], middle, rows - middle, paired, [received[0]]), "feat", 2 * q)
        for q in order
    ]

    risk, sums, ordered_events, total = risks(paired, firsts, rank, event_row, table, rows)
    later = jnp.zeros_like(total)
    bit = 1
    while bit < ex:
        total, later = ranges(bit, total, swap(total, "ex", bit), later, rests if bit == 1 else [])
        bit *= 2
    tangent, one, plain = ordered_values(keep[0], received[0], firsts, risk, rank, table, 0, middle)
    more_tangent, two, more = ordered_values(
        keep[0], received[0], rests, risk, rank, table, middle, rows - middle
    )
    later_sums = suffix_sums(one, two, padded)
    hazard, ordered_squares, message = shares(later, sums, ordered_events, plain, more, later_sums)
    messages = [message] + [swap(message, "ex", i) for i in range(1, ex)]
    cumulative, squares = hazards(hazard, ordered_squares, rank, rows)
    summed = prefix_sums(later_sums, ordered_squares, rank, padded)
    own = weights(messages, tangent, more_tangent, summed, risk, cumulative, squares)

    chips = {0: own}
    for q in reversed(range(1, feat // 2)):
        chips[q] = swap(own, "feat", 2 * q)
    near = [chips[q] for q in range(feat // 2)]
    far = [swap(chips[q], "feat", 1) for q in range(feat // 2)]
    partial_sums = [gradients(pieces, dosages) for pieces in (near, far)]
    bit = 1
    while 2 * bit < ex:
        received = [swap(message, "ex", bit) for message in partial_sums]
        partial_sums = [merge(mine, other, variants) for mine, other in zip(partial_sums, received)]
        bit *= 2
    received = [swap(message, "ex", bit) for message in partial_sums]
    first = add(partial_sums[0], received[0], variants)
    result = finish(first, partial_sums[1], received[1], total, feat)
    if padded != each:
        result = result.reshape(variants, feat, padded)[:, :, :each].reshape(variants, k)
    return result


def solution(mesh):
    placed = (P("ex", "feat"), P("feat"), P("feat", None), P("ex"), P("ex"))
    return jax.shard_map(
        local, mesh=mesh, in_specs=placed, out_specs=P("feat", None), check_vma=False
    )
```

```python
import functools

import jax
import jax.numpy as jnp
from jax import lax
from jax.experimental import pallas as pl
from jax.experimental.pallas import tpu as pltpu
from jax.sharding import PartitionSpec as P

F32 = jnp.float32
BF16 = jnp.bfloat16
LO = 256
NT = (((1,), (1,)), ((), ()))
SPAN = 512
VMEM = pl.BlockSpec(memory_space=pltpu.VMEM)
HBM = pl.BlockSpec(memory_space=pltpu.HBM)
PARAMS = dict(vmem_limit_bytes=24 * 1024 * 1024)


def swap(x, axis, i):
    count = lax.axis_size(axis)
    return lax.ppermute(x, axis, [(s, s ^ i) for s in range(count)])


def split_two(x):
    high = x.astype(BF16).astype(F32)
    return high, x - high


def split_three(x):
    first, rest = split_two(x)
    second, third = split_two(rest)
    return first, second, third


def one_hot(values, count, kind=BF16):
    shape = (count, values.shape[1])
    return jnp.where(lax.broadcasted_iota(jnp.int32, shape, 0) == values, 1.0, 0.0).astype(kind)


def triangle(n, keep):
    first = lax.broadcasted_iota(jnp.int32, (n, n), 0)
    second = lax.broadcasted_iota(jnp.int32, (n, n), 1)
    return jnp.where(keep(first, second), 1.0, 0.0)


def stacked(parts):
    return jnp.concatenate(parts, axis=0).astype(BF16)


def unstacked(values, count):
    height = values.shape[0] // count
    return sum(values[i * height : (i + 1) * height] for i in range(count))


def dot_binary(a, b):
    parts = jnp.dot(stacked(split_three(a)), b.astype(BF16), preferred_element_type=F32)
    return unstacked(parts, 3)


def binary_dot(a, b):
    a = a.astype(BF16)
    total = None
    for part in split_three(b):
        term = jnp.dot(a, part.astype(BF16), preferred_element_type=F32)
        total = term if total is None else total + term
    return total


def product_kernel(feat, kf, chunk, directions, coefficients, dosages, *refs):
    linear, keep, send = refs[0], refs[1 : 1 + feat // 2], refs[1 + feat // 2 : 1 + feat]
    table, own_directions, own_coefficients, lhs, turned, sems = refs[1 + feat :]
    me = lax.axis_index("feat")
    width = feat * kf
    persons, variants = table.shape
    steps = persons // chunk
    small = [
        pltpu.make_async_copy(directions, own_directions, sems.at[steps]),
        pltpu.make_async_copy(coefficients, own_coefficients, sems.at[steps + 1]),
    ]
    large = [
        pltpu.make_async_copy(
            dosages.at[pl.ds(i * chunk, chunk)], table.at[pl.ds(i * chunk, chunk)], sems.at[i]
        )
        for i in range(steps)
    ]
    for copy in small + large:
        copy.start()
    for copy in small:
        copy.wait()
    turned[...] = own_directions[...].astype(F32).T.reshape(turned.shape)
    for j in range(feat):
        lhs[j * kf : (j + 1) * kf] = turned[me ^ j].astype(BF16)
    lhs[width:] = jnp.broadcast_to(own_coefficients[...].astype(F32)[None, :], (16, variants)).astype(BF16)
    for i in range(steps):
        large[i].wait()
        first = i * chunk
        result = lax.dot_general(
            lhs[...], table[first : first + chunk], NT, preferred_element_type=F32
        )
        for j in range(feat):
            (send if j % 2 else keep)[j // 2][:, first : first + chunk] = result[j * kf : (j + 1) * kf]
        for start in range(0, chunk, LO):
            row = result[width : width + 1, start : start + LO]
            group = (first + start) // LO
            linear[group : group + 1, :] = row
            send[-1][group : group + 1, persons:] = row


def products(dosages, coefficients, directions, feat):
    persons, variants = dosages.shape
    k = directions.shape[1]
    kf = k // feat
    chunk = min(1024, persons)
    piece = jax.ShapeDtypeStruct((kf, persons), F32)
    first = jax.ShapeDtypeStruct((kf, persons + LO), F32)
    out = pl.pallas_call(
        functools.partial(product_kernel, feat, kf, chunk),
        in_specs=[HBM, HBM, HBM],
        out_shape=[jax.ShapeDtypeStruct((kf, LO), F32)]
        + [piece] * (feat - 1)
        + [first],
        out_specs=[VMEM] * (feat + 1),
        scratch_shapes=[
            pltpu.VMEM((persons, variants), BF16),
            pltpu.VMEM((variants, k), BF16),
            pltpu.VMEM((variants,), BF16),
            pltpu.VMEM((k + 16, variants), BF16),
            pltpu.VMEM((feat, kf, variants), F32),
            pltpu.SemaphoreType.DMA((persons // chunk + 2,)),
        ],
        compiler_params=pltpu.CompilerParams(**PARAMS),
        cost_estimate=pl.CostEstimate(
            flops=2 * persons * variants * k, bytes_accessed=persons * (variants * 2 + k * 4), transcendentals=0
        ),
        name="products",
    )(*[pltpu.with_memory_space_constraint(x, pltpu.HBM) for x in (directions, coefficients, dosages)])
    return out[0], out[1 : 1 + feat // 2], out[1 + feat // 2 :]


def power_of(largest):
    return jnp.ceil(jnp.log2(jnp.maximum(largest, 1e-30))) - 14.0


def to_short(values):
    return jnp.round(values).astype(jnp.int32).astype(jnp.int16)


def from_short(values):
    return values.astype(jnp.int32).astype(F32)


def pair_kernel(linear, received, waited, out):
    out[...] = linear[...] + received[:, received.shape[1] - LO :]


def pair(linear, received, waited):
    return pl.pallas_call(
        pair_kernel,
        in_specs=[VMEM] * 2 + [pl.BlockSpec(memory_space=pl.ANY)],
        out_shape=jax.ShapeDtypeStruct(linear.shape, F32),
        out_specs=VMEM,
        compiler_params=pltpu.CompilerParams(**PARAMS),
        name="pair",
    )(linear, received, waited)


def join_kernel(start, width, mine, other, *refs):
    linear, out = refs[0], refs[-1]
    kf = mine.shape[0]
    span = min(SPAN, width)
    lane = lax.broadcasted_iota(jnp.int32, (kf, 128), 1)
    powers = jnp.zeros((kf, 128), F32)
    for i in range(width // span):
        at = slice(start + i * span, start + (i + 1) * span)
        total = mine[:, at] + other[:, at]
        power = power_of(jnp.max(jnp.abs(total), axis=1, keepdims=True))
        out[:, i * span : (i + 1) * span] = to_short(total * jnp.exp2(-power))
        powers = jnp.where(lane == i, power, powers)
    if start == 0:
        power = power_of(jnp.max(jnp.abs(linear[...]), axis=1, keepdims=True))
        scaled = linear[...] * jnp.exp2(-power)
        whole = jnp.round(scaled)
        out[:, width : width + LO] = to_short(whole)
        out[:, width + LO : width + 2 * LO] = to_short((scaled - whole) * 32768.0)
        powers = jnp.where(lane == 127, power, powers)
    out[:, out.shape[1] - 128 :] = to_short(powers)


def join(keep, received, start, width, linear, waited):
    kf, rows = keep.shape
    extra = 2 * LO if start == 0 else 0
    return pl.pallas_call(
        functools.partial(join_kernel, start, width),
        in_specs=[VMEM] * 3 + [pl.BlockSpec(memory_space=pl.ANY)] * len(waited),
        out_shape=jax.ShapeDtypeStruct((kf, width + extra + 128), jnp.int16),
        out_specs=VMEM,
        compiler_params=pltpu.CompilerParams(**PARAMS),
        name="join",
    )(keep, received, linear, *waited)


def table_kernel(rows, rank, waited, table):
    chunk = min(512, rows)
    lane = lax.broadcasted_iota(jnp.int32, (chunk, 128), 1)
    for start in range(0, rows, chunk):
        at = slice(start, start + chunk)
        inner = lax.rem(rank[:, at], LO)
        column = jnp.broadcast_to(inner.astype(F32), (128, chunk)).T.astype(jnp.int32)
        for first in range(0, LO, 128):
            table[at, first : first + 128] = jnp.where(column == lane + first, 1.0, 0.0).astype(BF16)


def tables(rank, waited, rows):
    return pl.pallas_call(
        functools.partial(table_kernel, rows),
        in_specs=[VMEM, pl.BlockSpec(memory_space=pl.ANY)],
        out_shape=jax.ShapeDtypeStruct((rows, LO), BF16),
        out_specs=VMEM,
        compiler_params=pltpu.CompilerParams(**PARAMS),
        cost_estimate=pl.CostEstimate(flops=rows * LO * 8, bytes_accessed=rows * LO * 2, transcendentals=0),
        name="tables",
    )(rank, waited)


def risk_kernel(rows, parts, linear, *refs):
    messages, (rank, events, table) = refs[:parts], refs[parts : parts + 3]
    risk_out, sums_out, events_out, message = refs[-4:]
    groups = rows // LO
    total = linear[...]
    for part in messages:
        end = part.shape[1] - 128
        power = from_short(part[:, end:])[:, 127:]
        high, low = from_short(part[:, end - 2 * LO : end - LO]), from_short(part[:, end - LO : end])
        total = total + (high + low * (1.0 / 32768.0)) * jnp.exp2(power)
    risk = jnp.exp(total)
    for g in range(groups):
        risk_out[:, g * LO : (g + 1) * LO] = risk[g : g + 1]
    mask = one_hot(lax.rem(rank[...], rows) // LO, groups, F32)
    pieces = [mask * part for part in split_three(risk_out[...])] + [mask * events[...].astype(F32)]
    lhs = jnp.concatenate(pieces, axis=0).astype(BF16)
    sorted_all = jnp.dot(lhs, table[...], preferred_element_type=F32)
    ordered = sorted_all[:groups] + sorted_all[groups : 2 * groups] + sorted_all[2 * groups : 3 * groups]
    happened = sorted_all[3 * groups :]
    inside = dot_binary(ordered, triangle(LO, lambda a, b: a >= b))
    totals = jnp.broadcast_to(inside[:, :1], inside.shape)
    carried = binary_dot(triangle(groups, lambda a, b: a < b), totals)
    sums_out[...] = inside + carried
    events_out[...] = happened
    everything = jnp.sum(totals, axis=0, keepdims=True)[:, :128]
    count = jnp.sum(dot_binary(happened, jnp.ones((LO, 128), F32)), axis=0, keepdims=True)
    message[...] = jnp.concatenate([everything, count, jnp.zeros((6, 128), F32)], axis=0)


def risks(linear, messages, rank, events, table, rows):
    groups = rows // LO
    return pl.pallas_call(
        functools.partial(risk_kernel, rows, len(messages)),
        in_specs=[VMEM] * (len(messages) + 4),
        out_shape=[
            jax.ShapeDtypeStruct((1, rows), F32),
            jax.ShapeDtypeStruct((groups, LO), F32),
            jax.ShapeDtypeStruct((groups, LO), F32),
            jax.ShapeDtypeStruct((8, 128), F32),
        ],
        out_specs=[VMEM] * 4,
        compiler_params=pltpu.CompilerParams(**PARAMS),
        cost_estimate=pl.CostEstimate(flops=rows * LO * 128, bytes_accessed=rows * 64, transcendentals=rows),
        name="risks",
    )(linear, *messages, rank, events, table)


def share_kernel(later, sums, events, plain, more, ordered, hazard_out, squares, message):
    kf = plain.shape[0]
    groups = sums.shape[0]
    risk_sum = sums[...] + later[0:1, 0:1]
    hazard = events[...] / risk_sum
    square = events[...] / (risk_sum * risk_sum)
    hazard_out[...] = hazard
    squares[...] = square
    scaled = jnp.zeros((kf, LO), F32)
    for g in range(groups):
        scaled = scaled + ordered[g * kf : (g + 1) * kf] * square[g : g + 1]
    message[:kf] = plain[...] + more[...]
    message[kf : 2 * kf] = sum(scaled[:, start : start + 128] for start in range(0, LO, 128))
    totals = [jnp.sum(jnp.sum(v, axis=0, keepdims=True), axis=1, keepdims=True) for v in (hazard, square)]
    rows = [jnp.broadcast_to(v, (1, 128)) for v in totals]
    message[2 * kf :] = jnp.concatenate(rows + [jnp.zeros((6, 128), F32)], axis=0)


def shares(later, sums, events, plain, more, ordered):
    flat = jax.ShapeDtypeStruct(sums.shape, F32)
    return pl.pallas_call(
        share_kernel,
        in_specs=[VMEM] * 6,
        out_shape=[flat, flat, jax.ShapeDtypeStruct((2 * plain.shape[0] + 8, 128), F32)],
        out_specs=[VMEM] * 3,
        compiler_params=pltpu.CompilerParams(**PARAMS),
        name="shares",
    )(later, sums, events, plain, more, ordered)


def hazard_kernel(rows, hazard, square, rank, cumulative, squares):
    groups = rows // LO
    inside = dot_binary(
        jnp.concatenate([hazard[...], square[...]], axis=0), triangle(LO, lambda a, b: a <= b)
    )
    totals = jnp.broadcast_to(inside[:, LO - 1 :], (2 * groups, 128))
    place = lax.rem(rank[...], rows)
    mask = one_hot(place // LO, groups, F32)
    placed = dot_binary(inside, one_hot(lax.rem(place, LO), LO))
    before = triangle(groups, lambda a, b: a > b)
    for first, out in ((0, cumulative), (groups, squares)):
        carried = binary_dot(before, totals[first : first + groups])[:, :1]
        out[...] = jnp.sum(mask * (placed[first : first + groups] + carried), axis=0, keepdims=True)


def hazards(hazard, square, rank, rows):
    row = jax.ShapeDtypeStruct((1, rows), F32)
    return pl.pallas_call(
        functools.partial(hazard_kernel, rows),
        in_specs=[VMEM] * 3,
        out_shape=[row, row],
        out_specs=[VMEM] * 2,
        compiler_params=pltpu.CompilerParams(**PARAMS),
        cost_estimate=pl.CostEstimate(flops=rows * LO * 200, bytes_accessed=rows * 64, transcendentals=0),
        name="hazards",
    )(hazard, square, rank)


def range_kernel(bit, count, *refs):
    total, other, later = refs[:3]
    total_out, later_out = refs[3 + count :]
    is_later = (lax.axis_index("ex") & bit) == 0
    later_out[...] = later[...] + jnp.where(is_later, other[...], 0.0)
    total_out[...] = total[...] + other[...]


def ranges(bit, total, other, later, waited):
    return pl.pallas_call(
        functools.partial(range_kernel, bit, len(waited)),
        in_specs=[VMEM] * 3 + [pl.BlockSpec(memory_space=pl.ANY)] * len(waited),
        out_shape=[jax.ShapeDtypeStruct(total.shape, F32)] * 2,
        out_specs=[VMEM] * 2,
        compiler_params=pltpu.CompilerParams(**PARAMS),
        name="ranges",
    )(total, other, later, *waited)


def order_kernel(start, parts, own, other, *refs):
    messages, (risk, rank, table) = refs[:parts], refs[parts : parts + 3]
    tangent_out, ordered_out, plain, lhs = refs[-4:]
    kf, width = tangent_out.shape
    rows = own.shape[1]
    groups = rows // LO
    span = min(SPAN, width)
    folded = jnp.zeros((kf, 128), F32)
    powers = [jnp.exp2(from_short(part[:, part.shape[1] - 128 :])) for part in messages]
    for i in range(width // span):
        at = slice(start + i * span, start + (i + 1) * span)
        here = slice(i * span, (i + 1) * span)
        tangent = own[:, at] + other[:, at]
        for part, power in zip(messages, powers):
            tangent = tangent + from_short(part[:, here]) * power[:, i : i + 1]
        tangent_out[:, here] = tangent
        weighted = tangent * risk[:, at]
        folded = folded + sum(weighted[:, j : j + 128] for j in range(0, span, 128))
        high, low = split_two(weighted)
        high, low = high.astype(BF16), low.astype(BF16)
        group = jnp.broadcast_to(lax.rem(rank[:, at], rows) // LO, (kf, span))
        for g in range(groups):
            mask = jnp.where(group == g, 1.0, 0.0).astype(BF16)
            lhs[2 * g * kf : (2 * g + 1) * kf, here] = high * mask
            lhs[(2 * g + 1) * kf : (2 * g + 2) * kf, here] = low * mask
    plain[...] = folded
    ordered = jnp.dot(lhs[...], table[start : start + width], preferred_element_type=F32)
    for g in range(groups):
        ordered_out[g * kf : (g + 1) * kf] = (
            ordered[2 * g * kf : (2 * g + 1) * kf] + ordered[(2 * g + 1) * kf : (2 * g + 2) * kf]
        )


def ordered_values(own, other, messages, risk, rank, table, start, width):
    kf, rows = own.shape
    groups = rows // LO
    return pl.pallas_call(
        functools.partial(order_kernel, start, len(messages)),
        in_specs=[VMEM] * (len(messages) + 5),
        out_shape=[
            jax.ShapeDtypeStruct((kf, width), F32),
            jax.ShapeDtypeStruct((groups * kf, LO), F32),
            jax.ShapeDtypeStruct((kf, 128), F32),
        ],
        out_specs=[VMEM] * 3,
        scratch_shapes=[pltpu.VMEM((groups * 2 * kf, width), BF16)],
        compiler_params=pltpu.CompilerParams(**PARAMS),
        cost_estimate=pl.CostEstimate(
            flops=2 * width * LO * groups * 2 * kf, bytes_accessed=width * kf * 24, transcendentals=0
        ),
        name="ordered_values",
    )(own, other, *messages, risk, rank, table)


def suffix_kernel(kf, one, two, sums):
    groups = sums.shape[0] // kf
    inside = dot_binary(one[...] + two[...], triangle(LO, lambda a, b: a >= b))
    carried = jnp.zeros((kf, 1), F32)
    for g in reversed(range(groups)):
        rows_of = slice(g * kf, (g + 1) * kf)
        sums[rows_of] = inside[rows_of] + carried
        carried = carried + inside[rows_of, :1]


def suffix_sums(one, two, kf):
    return pl.pallas_call(
        functools.partial(suffix_kernel, kf),
        in_specs=[VMEM] * 2,
        out_shape=jax.ShapeDtypeStruct(one.shape, F32),
        out_specs=VMEM,
        compiler_params=pltpu.CompilerParams(**PARAMS),
        name="suffix_sums",
    )(one, two)


def prefix_kernel(sums, squares, rank, out):
    kf, rows = out.shape
    groups = squares.shape[0]
    chunk = min(512, rows)
    hazard = [sums[g * kf : (g + 1) * kf] * squares[g : g + 1, :] for g in range(groups)]
    inside = dot_binary(jnp.concatenate(hazard, axis=0), triangle(LO, lambda a, b: a <= b))
    carried = jnp.zeros((kf, 1), F32)
    summed = [None] * groups
    for g in range(groups):
        rows_of = slice(g * kf, (g + 1) * kf)
        summed[g] = inside[rows_of] + carried
        carried = carried + inside[rows_of, LO - 1 :]
    both = stacked(split_two(jnp.concatenate(summed, axis=0)))
    for start in range(0, rows, chunk):
        at = slice(start, start + chunk)
        place = lax.rem(rank[:, at], rows)
        group = place // LO
        spread = one_hot(lax.rem(place, LO), LO)
        placed = unstacked(jnp.dot(both, spread, preferred_element_type=F32), 2)
        picked = jnp.zeros((kf, chunk), F32)
        for g in range(groups):
            picked = picked + jnp.where(group == g, placed[g * kf : (g + 1) * kf], 0.0)
        out[:, at] = picked


def prefix_sums(sums, squares, rank, kf):
    rows = rank.shape[1]
    return pl.pallas_call(
        prefix_kernel,
        in_specs=[VMEM] * 3,
        out_shape=jax.ShapeDtypeStruct((kf, rows), F32),
        out_specs=VMEM,
        compiler_params=pltpu.CompilerParams(**PARAMS),
        cost_estimate=pl.CostEstimate(
            flops=4 * rows * LO * (rows // LO) * kf, bytes_accessed=rows * kf * 24, transcendentals=0
        ),
        name="prefix_sums",
    )(sums, squares, rank)


def weight_kernel(ex, *refs):
    messages, (first, rest, local, risk, cumulative, squares) = refs[:ex], refs[ex : ex + 6]
    weighted, placed = refs[ex + 6 :]
    kf = first.shape[0]
    me = lax.axis_index("ex")
    for i in range(ex):
        placed[me ^ i] = messages[i][...]
    later = jnp.zeros((kf, 128), F32)
    own_later, before = later, later
    hazard_before = jnp.zeros((1, 128), F32)
    for b in reversed(range(ex)):
        plain, scaled, square = placed[b, :kf], placed[b, kf : 2 * kf], placed[b, 2 * kf + 1 : 2 * kf + 2]
        own_later = own_later + jnp.where(b > me, plain, 0.0)
        before = before + jnp.where(b < me, scaled + square * later, 0.0)
        hazard_before = hazard_before + jnp.where(b < me, placed[b, 2 * kf : 2 * kf + 1], 0.0)
        later = later + plain
    own_later = jnp.sum(own_later, axis=1, keepdims=True)
    before = jnp.sum(before, axis=1, keepdims=True)
    hazard_before = hazard_before[:, :1]
    for start, part in ((0, first), (first.shape[1], rest)):
        at = slice(start, start + part.shape[1])
        value = part[...] * (cumulative[:, at] + hazard_before) - (
            local[:, at] + squares[:, at] * own_later + before
        )
        weighted[:, at] = (risk[:, at] * value).astype(BF16)


def weights(messages, first, rest, local, risk, cumulative, squares):
    ex = len(messages)
    return pl.pallas_call(
        functools.partial(weight_kernel, ex),
        in_specs=[VMEM] * (ex + 6),
        out_shape=jax.ShapeDtypeStruct(local.shape, BF16),
        out_specs=VMEM,
        scratch_shapes=[pltpu.VMEM((ex,) + messages[0].shape, F32)],
        compiler_params=pltpu.CompilerParams(**PARAMS),
        name="weights",
    )(*messages, first, rest, local, risk, cumulative, squares)


def encode(values, message):
    columns = len(values)
    powers = []
    for i, value in enumerate(values):
        power = power_of(jnp.max(jnp.abs(value), axis=0, keepdims=True))
        scaled = to_short(value * jnp.exp2(-power))
        for j in range(value.shape[0] // 16):
            message[j * columns + i] = scaled[j * 16 : (j + 1) * 16]
        powers.append(power)
    powers.append(jnp.zeros((16 - columns, 128), F32))
    message[message.shape[0] - 1] = to_short(jnp.concatenate(powers, axis=0))


def decode(message, columns):
    last = message.shape[0] - 1
    scales = jnp.exp2(from_short(message[last]))
    values = []
    for i in range(columns):
        value = jnp.concatenate([from_short(message[j]) for j in range(i, last, columns)], axis=0)
        values.append(value * scales[i : i + 1])
    return values


def decode_sum(mine, other, columns):
    return [one + two for one, two in zip(decode(mine, columns), decode(other, columns))]


def gradient_kernel(parts, kf, *refs):
    pieces, dosages, out, weighted = refs[:parts], refs[parts], refs[parts + 1], refs[parts + 2]
    for i in range(parts):
        weighted[i * kf : (i + 1) * kf, :] = pieces[i][...]
    total = jnp.dot(weighted[...], dosages[...], preferred_element_type=F32)
    encode([total[:, at : at + 128] for at in range(0, total.shape[1], 128)], out)


def gradients(pieces, dosages):
    parts = len(pieces)
    kf, persons = pieces[0].shape
    k, variants = kf * parts, dosages.shape[1]
    return pl.pallas_call(
        functools.partial(gradient_kernel, parts, kf),
        in_specs=[VMEM] * (parts + 1),
        out_shape=jax.ShapeDtypeStruct((k * variants // 2048 + 1, 16, 128), jnp.int16),
        out_specs=VMEM,
        scratch_shapes=[pltpu.VMEM((k, persons), BF16)],
        compiler_params=pltpu.CompilerParams(**PARAMS),
        cost_estimate=pl.CostEstimate(
            flops=2 * persons * variants * k, bytes_accessed=persons * (variants * 2 + k * 2), transcendentals=0
        ),
        name="gradients",
    )(*pieces, dosages)


def merge_kernel(columns, mine, other, out):
    encode(decode_sum(mine, other, columns), out)


def merge(mine, other, variants):
    return pl.pallas_call(
        functools.partial(merge_kernel, variants // 128),
        in_specs=[VMEM] * 2,
        out_shape=jax.ShapeDtypeStruct(mine.shape, jnp.int16),
        out_specs=VMEM,
        compiler_params=pltpu.CompilerParams(**PARAMS),
        name="merge",
    )(mine, other)


def add_kernel(mine, other, out):
    for i, value in enumerate(decode_sum(mine, other, out.shape[1] // 128)):
        out[:, i * 128 : (i + 1) * 128] = value


def add(mine, other, variants):
    return pl.pallas_call(
        add_kernel,
        in_specs=[VMEM] * 2,
        out_shape=jax.ShapeDtypeStruct(((mine.shape[0] - 1) * 2048 // variants, variants), F32),
        out_specs=VMEM,
        compiler_params=pltpu.CompilerParams(**PARAMS),
        name="add",
    )(mine, other)


def finish_kernel(feat, kf, first, mine, other, count, out, placed, total, sems):
    me = lax.axis_index("feat")
    variants = out.shape[0]
    scale = count[1:2, 0:1]
    for q in range(feat // 2):
        placed[me ^ (2 * q)] = first[q * kf : (q + 1) * kf]
    for i, value in enumerate(decode_sum(mine, other, variants // 128)):
        for q in range(feat // 2):
            placed[me ^ (2 * q + 1), :, i * 128 : (i + 1) * 128] = value[q * kf : (q + 1) * kf]
    copies = []
    for i in range(variants // 128):
        at = slice(i * 128, (i + 1) * 128)
        total[at] = placed[:, :, at].reshape(feat * kf, 128).T / scale
        copies.append(
            pltpu.make_async_copy(
                total.at[pl.ds(i * 128, 128)], out.at[pl.ds(i * 128, 128)], sems.at[i]
            )
        )
        copies[i].start()
    for copy in copies:
        copy.wait()


def finish(first, mine, other, count, feat):
    k, variants = 2 * first.shape[0], first.shape[1]
    kf = k // feat
    return pl.pallas_call(
        functools.partial(finish_kernel, feat, kf),
        in_specs=[VMEM] * 4,
        out_shape=jax.ShapeDtypeStruct((variants, k), F32),
        out_specs=HBM,
        scratch_shapes=[
            pltpu.VMEM((feat, kf, variants), F32),
            pltpu.VMEM((variants, k), F32),
            pltpu.SemaphoreType.DMA((variants // 128,)),
        ],
        compiler_params=pltpu.CompilerParams(**PARAMS),
        name="finish",
    )(first, mine, other, count)


def local(dosages, coefficients, directions, event_rank, events):
    feat, ex = lax.axis_size("feat"), lax.axis_size("ex")
    rows = dosages.shape[0]
    variants, k = directions.shape
    each = k // feat
    padded = -(-each // 16) * 16
    if padded != each:
        directions = jnp.pad(directions.reshape(variants, feat, each), ((0, 0), (0, 0), (0, padded - each)))
        directions = directions.reshape(variants, feat * padded)
    rank, event_row = event_rank[None], events[None]

    linear, keep, send = products(dosages, coefficients, directions, feat)
    order = list(reversed(range(1, feat // 2)))
    received = {q: swap(send[q], "feat", 1) for q in order + [0]}
    table = tables(rank, linear, rows)
    paired = pair(linear, received[order[0]], table)
    middle = min(3 * SPAN, rows // 2)
    firsts = [
        swap(join(keep[q], received[q], 0, middle, paired, []), "feat", 2 * q) for q in order
    ]
    rests = [
        swap(join(keep[q], received[q], middle, rows - middle, paired, [received[0]]), "feat", 2 * q)
        for q in order
    ]

    risk, sums, ordered_events, total = risks(paired, firsts, rank, event_row, table, rows)
    later = jnp.zeros_like(total)
    bit = 1
    while bit < ex:
        total, later = ranges(bit, total, swap(total, "ex", bit), later, rests if bit == 1 else [])
        bit *= 2
    tangent, one, plain = ordered_values(keep[0], received[0], firsts, risk, rank, table, 0, middle)
    more_tangent, two, more = ordered_values(
        keep[0], received[0], rests, risk, rank, table, middle, rows - middle
    )
    later_sums = suffix_sums(one, two, padded)
    hazard, ordered_squares, message = shares(later, sums, ordered_events, plain, more, later_sums)
    messages = [message] + [swap(message, "ex", i) for i in range(1, ex)]
    cumulative, squares = hazards(hazard, ordered_squares, rank, rows)
    summed = prefix_sums(later_sums, ordered_squares, rank, padded)
    own = weights(messages, tangent, more_tangent, summed, risk, cumulative, squares)

    chips = {0: own}
    for q in range(1, feat // 2):
        chips[q] = swap(own, "feat", 2 * q)
    near = [chips[q] for q in range(feat // 2)]
    far = [swap(chips[q], "feat", 1) for q in range(feat // 2)]
    partial_sums = [gradients(pieces, dosages) for pieces in (near, far)]
    bit = 1
    while 2 * bit < ex:
        received = [swap(message, "ex", bit) for message in partial_sums]
        partial_sums = [merge(mine, other, variants) for mine, other in zip(partial_sums, received)]
        bit *= 2
    received = [swap(message, "ex", bit) for message in partial_sums]
    first = add(partial_sums[0], received[0], variants)
    result = finish(first, partial_sums[1], received[1], total, feat)
    if padded != each:
        result = result.reshape(variants, feat, padded)[:, :, :each].reshape(variants, k)
    return result


def solution(mesh):
    placed = (P("ex", "feat"), P("feat"), P("feat", None), P("ex"), P("ex"))
    return jax.shard_map(
        local, mesh=mesh, in_specs=placed, out_specs=P("feat", None), check_vma=False
    )
```

```python
import functools

import jax
import jax.numpy as jnp
from jax import lax
from jax.experimental import pallas as pl
from jax.experimental.pallas import tpu as pltpu
from jax.sharding import PartitionSpec as P

F32 = jnp.float32
BF16 = jnp.bfloat16
LO = 256
NT = (((1,), (1,)), ((), ()))
SPAN = 512
VMEM = pl.BlockSpec(memory_space=pltpu.VMEM)
HBM = pl.BlockSpec(memory_space=pltpu.HBM)
PARAMS = dict(vmem_limit_bytes=24 * 1024 * 1024)


def swap(x, axis, i):
    count = lax.axis_size(axis)
    return lax.ppermute(x, axis, [(s, s ^ i) for s in range(count)])


def swap_odd(x, i):
    ex, feat = lax.axis_size("ex"), lax.axis_size("feat")
    pairs = [(e * feat + f, (e ^ i) * feat + f) for e in range(ex) for f in range(1, feat, 2)]
    return lax.ppermute(x, ("ex", "feat"), pairs)


def hand_over(x):
    return lax.ppermute(x, "feat", [(f, f - 1) for f in range(1, lax.axis_size("feat"), 2)])


def split_two(x):
    high = x.astype(BF16).astype(F32)
    return high, x - high


def split_three(x):
    first, rest = split_two(x)
    second, third = split_two(rest)
    return first, second, third


def one_hot(values, count, kind=BF16):
    shape = (count, values.shape[1])
    return jnp.where(lax.broadcasted_iota(jnp.int32, shape, 0) == values, 1.0, 0.0).astype(kind)


def triangle(n, keep):
    first = lax.broadcasted_iota(jnp.int32, (n, n), 0)
    second = lax.broadcasted_iota(jnp.int32, (n, n), 1)
    return jnp.where(keep(first, second), 1.0, 0.0)


def stacked(parts):
    return jnp.concatenate(parts, axis=0).astype(BF16)


def unstacked(values, count):
    height = values.shape[0] // count
    return sum(values[i * height : (i + 1) * height] for i in range(count))


def dot_binary(a, b):
    parts = jnp.dot(stacked(split_three(a)), b.astype(BF16), preferred_element_type=F32)
    return unstacked(parts, 3)


def binary_dot(a, b):
    a = a.astype(BF16)
    total = None
    for part in split_three(b):
        term = jnp.dot(a, part.astype(BF16), preferred_element_type=F32)
        total = term if total is None else total + term
    return total


def product_kernel(feat, kf, chunk, directions, coefficients, dosages, *refs):
    linear, keep, send = refs[0], refs[1 : 1 + feat // 2], refs[1 + feat // 2 : 1 + feat]
    table, own_directions, own_coefficients, lhs, turned, sems = refs[1 + feat :]
    me = lax.axis_index("feat")
    width = feat * kf
    persons, variants = table.shape
    steps = persons // chunk
    small = [
        pltpu.make_async_copy(directions, own_directions, sems.at[steps]),
        pltpu.make_async_copy(coefficients, own_coefficients, sems.at[steps + 1]),
    ]
    large = [
        pltpu.make_async_copy(
            dosages.at[pl.ds(i * chunk, chunk)], table.at[pl.ds(i * chunk, chunk)], sems.at[i]
        )
        for i in range(steps)
    ]
    for copy in small + large:
        copy.start()
    for copy in small:
        copy.wait()
    turned[...] = own_directions[...].astype(F32).T.reshape(turned.shape)
    for j in range(feat):
        lhs[j * kf : (j + 1) * kf] = turned[me ^ j].astype(BF16)
    lhs[width:] = jnp.broadcast_to(own_coefficients[...].astype(F32)[None, :], (16, variants)).astype(BF16)
    for i in range(steps):
        large[i].wait()
        first = i * chunk
        result = lax.dot_general(
            lhs[...], table[first : first + chunk], NT, preferred_element_type=F32
        )
        for j in range(feat):
            (send if j % 2 else keep)[j // 2][:, first : first + chunk] = result[j * kf : (j + 1) * kf]
        for start in range(0, chunk, LO):
            row = result[width : width + 1, start : start + LO]
            group = (first + start) // LO
            linear[group : group + 1, :] = row
            send[-1][group : group + 1, persons:] = row


def products(dosages, coefficients, directions, feat):
    persons, variants = dosages.shape
    k = directions.shape[1]
    kf = k // feat
    chunk = min(1024, persons)
    piece = jax.ShapeDtypeStruct((kf, persons), F32)
    first = jax.ShapeDtypeStruct((kf, persons + LO), F32)
    out = pl.pallas_call(
        functools.partial(product_kernel, feat, kf, chunk),
        in_specs=[HBM, HBM, HBM],
        out_shape=[jax.ShapeDtypeStruct((kf, LO), F32)]
        + [piece] * (feat - 1)
        + [first],
        out_specs=[VMEM] * (feat + 1),
        scratch_shapes=[
            pltpu.VMEM((persons, variants), BF16),
            pltpu.VMEM((variants, k), BF16),
            pltpu.VMEM((variants,), BF16),
            pltpu.VMEM((k + 16, variants), BF16),
            pltpu.VMEM((feat, kf, variants), F32),
            pltpu.SemaphoreType.DMA((persons // chunk + 2,)),
        ],
        compiler_params=pltpu.CompilerParams(**PARAMS),
        cost_estimate=pl.CostEstimate(
            flops=2 * persons * variants * k, bytes_accessed=persons * (variants * 2 + k * 4), transcendentals=0
        ),
        name="products",
    )(*[pltpu.with_memory_space_constraint(x, pltpu.HBM) for x in (directions, coefficients, dosages)])
    return out[0], out[1 : 1 + feat // 2], out[1 + feat // 2 :]


def power_of(largest):
    return jnp.ceil(jnp.log2(jnp.maximum(largest, 1e-30))) - 14.0


def to_short(values):
    return jnp.round(values).astype(jnp.int32).astype(jnp.int16)


def from_short(values):
    return values.astype(jnp.int32).astype(F32)


def pair_kernel(linear, received, waited, out):
    out[...] = linear[...] + received[:, received.shape[1] - LO :]


def pair(linear, received, waited):
    return pl.pallas_call(
        pair_kernel,
        in_specs=[VMEM] * 2 + [pl.BlockSpec(memory_space=pl.ANY)],
        out_shape=jax.ShapeDtypeStruct(linear.shape, F32),
        out_specs=VMEM,
        compiler_params=pltpu.CompilerParams(**PARAMS),
        name="pair",
    )(linear, received, waited)


def join_kernel(start, width, mine, other, *refs):
    linear, out = refs[0], refs[-1]
    kf = mine.shape[0]
    span = min(SPAN, width)
    lane = lax.broadcasted_iota(jnp.int32, (kf, 128), 1)
    powers = jnp.zeros((kf, 128), F32)
    for i in range(width // span):
        at = slice(start + i * span, start + (i + 1) * span)
        total = mine[:, at] + other[:, at]
        power = power_of(jnp.max(jnp.abs(total), axis=1, keepdims=True))
        out[:, i * span : (i + 1) * span] = to_short(total * jnp.exp2(-power))
        powers = jnp.where(lane == i, power, powers)
    if start == 0:
        power = power_of(jnp.max(jnp.abs(linear[...]), axis=1, keepdims=True))
        scaled = linear[...] * jnp.exp2(-power)
        whole = jnp.round(scaled)
        out[:, width : width + LO] = to_short(whole)
        out[:, width + LO : width + 2 * LO] = to_short((scaled - whole) * 32768.0)
        powers = jnp.where(lane == 127, power, powers)
    out[:, out.shape[1] - 128 :] = to_short(powers)


def join(keep, received, start, width, linear, waited):
    kf, rows = keep.shape
    extra = 2 * LO if start == 0 else 0
    return pl.pallas_call(
        functools.partial(join_kernel, start, width),
        in_specs=[VMEM] * 3 + [pl.BlockSpec(memory_space=pl.ANY)] * len(waited),
        out_shape=jax.ShapeDtypeStruct((kf, width + extra + 128), jnp.int16),
        out_specs=VMEM,
        compiler_params=pltpu.CompilerParams(**PARAMS),
        name="join",
    )(keep, received, linear, *waited)


def table_kernel(rows, rank, waited, table):
    chunk = min(512, rows)
    lane = lax.broadcasted_iota(jnp.int32, (chunk, 128), 1)
    for start in range(0, rows, chunk):
        at = slice(start, start + chunk)
        inner = lax.rem(rank[:, at], LO)
        column = jnp.broadcast_to(inner.astype(F32), (128, chunk)).T.astype(jnp.int32)
        for first in range(0, LO, 128):
            table[at, first : first + 128] = jnp.where(column == lane + first, 1.0, 0.0).astype(BF16)


def tables(rank, waited, rows):
    return pl.pallas_call(
        functools.partial(table_kernel, rows),
        in_specs=[VMEM, pl.BlockSpec(memory_space=pl.ANY)],
        out_shape=jax.ShapeDtypeStruct((rows, LO), BF16),
        out_specs=VMEM,
        compiler_params=pltpu.CompilerParams(**PARAMS),
        cost_estimate=pl.CostEstimate(flops=rows * LO * 8, bytes_accessed=rows * LO * 2, transcendentals=0),
        name="tables",
    )(rank, waited)


def risk_kernel(rows, parts, linear, *refs):
    messages, (rank, events, table) = refs[:parts], refs[parts : parts + 3]
    risk_out, sums_out, events_out, message = refs[-4:]
    groups = rows // LO
    total = linear[...]
    for part in messages:
        end = part.shape[1] - 128
        power = from_short(part[:, end:])[:, 127:]
        high, low = from_short(part[:, end - 2 * LO : end - LO]), from_short(part[:, end - LO : end])
        total = total + (high + low * (1.0 / 32768.0)) * jnp.exp2(power)
    risk = jnp.exp(total)
    for g in range(groups):
        risk_out[:, g * LO : (g + 1) * LO] = risk[g : g + 1]
    mask = one_hot(lax.rem(rank[...], rows) // LO, groups, F32)
    pieces = [mask * part for part in split_three(risk_out[...])] + [mask * events[...].astype(F32)]
    lhs = jnp.concatenate(pieces, axis=0).astype(BF16)
    sorted_all = jnp.dot(lhs, table[...], preferred_element_type=F32)
    ordered = sorted_all[:groups] + sorted_all[groups : 2 * groups] + sorted_all[2 * groups : 3 * groups]
    happened = sorted_all[3 * groups :]
    inside = dot_binary(ordered, triangle(LO, lambda a, b: a >= b))
    totals = jnp.broadcast_to(inside[:, :1], inside.shape)
    carried = binary_dot(triangle(groups, lambda a, b: a < b), totals)
    sums_out[...] = inside + carried
    events_out[...] = happened
    everything = jnp.sum(totals, axis=0, keepdims=True)[:, :128]
    count = jnp.sum(dot_binary(happened, jnp.ones((LO, 128), F32)), axis=0, keepdims=True)
    message[0] = jnp.concatenate([everything, count, jnp.zeros((6, 128), F32)], axis=0)
    message[1] = jnp.zeros((8, 128), F32)


def risks(linear, messages, rank, events, table, rows):
    groups = rows // LO
    return pl.pallas_call(
        functools.partial(risk_kernel, rows, len(messages)),
        in_specs=[VMEM] * (len(messages) + 4),
        out_shape=[
            jax.ShapeDtypeStruct((1, rows), F32),
            jax.ShapeDtypeStruct((groups, LO), F32),
            jax.ShapeDtypeStruct((groups, LO), F32),
            jax.ShapeDtypeStruct((2, 8, 128), F32),
        ],
        out_specs=[VMEM] * 4,
        compiler_params=pltpu.CompilerParams(**PARAMS),
        cost_estimate=pl.CostEstimate(flops=rows * LO * 128, bytes_accessed=rows * 64, transcendentals=rows),
        name="risks",
    )(linear, *messages, rank, events, table)


def share_kernel(state, handed, sums, events, plain, more, ordered, *outs):
    hazard_out, squares, message, total = outs
    kf = plain.shape[0]
    groups = sums.shape[0]
    odd = (lax.axis_index("feat") & 1) == 1
    total[...] = jnp.where(odd, state[0], handed[0])
    later = jnp.where(odd, state[1], handed[1])
    risk_sum = sums[...] + later[0:1, 0:1]
    hazard = events[...] / risk_sum
    square = events[...] / (risk_sum * risk_sum)
    hazard_out[...] = hazard
    squares[...] = square
    scaled = jnp.zeros((kf, LO), F32)
    for g in range(groups):
        scaled = scaled + ordered[g * kf : (g + 1) * kf] * square[g : g + 1]
    message[:kf] = plain[...] + more[...]
    message[kf : 2 * kf] = sum(scaled[:, start : start + 128] for start in range(0, LO, 128))
    totals = [jnp.sum(jnp.sum(v, axis=0, keepdims=True), axis=1, keepdims=True) for v in (hazard, square)]
    rows = [jnp.broadcast_to(v, (1, 128)) for v in totals]
    message[2 * kf :] = jnp.concatenate(rows + [jnp.zeros((6, 128), F32)], axis=0)


def shares(state, handed, sums, events, plain, more, ordered):
    flat = jax.ShapeDtypeStruct(sums.shape, F32)
    return pl.pallas_call(
        share_kernel,
        in_specs=[VMEM] * 7,
        out_shape=[
            flat,
            flat,
            jax.ShapeDtypeStruct((2 * plain.shape[0] + 8, 128), F32),
            jax.ShapeDtypeStruct((8, 128), F32),
        ],
        out_specs=[VMEM] * 4,
        compiler_params=pltpu.CompilerParams(**PARAMS),
        name="shares",
    )(state, handed, sums, events, plain, more, ordered)


def hazard_kernel(rows, hazard, square, rank, cumulative, squares):
    groups = rows // LO
    inside = dot_binary(
        jnp.concatenate([hazard[...], square[...]], axis=0), triangle(LO, lambda a, b: a <= b)
    )
    totals = jnp.broadcast_to(inside[:, LO - 1 :], (2 * groups, 128))
    place = lax.rem(rank[...], rows)
    mask = one_hot(place // LO, groups, F32)
    placed = dot_binary(inside, one_hot(lax.rem(place, LO), LO))
    before = triangle(groups, lambda a, b: a > b)
    for first, out in ((0, cumulative), (groups, squares)):
        carried = binary_dot(before, totals[first : first + groups])[:, :1]
        out[...] = jnp.sum(mask * (placed[first : first + groups] + carried), axis=0, keepdims=True)


def hazards(hazard, square, rank, rows):
    row = jax.ShapeDtypeStruct((1, rows), F32)
    return pl.pallas_call(
        functools.partial(hazard_kernel, rows),
        in_specs=[VMEM] * 3,
        out_shape=[row, row],
        out_specs=[VMEM] * 2,
        compiler_params=pltpu.CompilerParams(**PARAMS),
        cost_estimate=pl.CostEstimate(flops=rows * LO * 200, bytes_accessed=rows * 64, transcendentals=0),
        name="hazards",
    )(hazard, square, rank)


def range_kernel(bit, count, *refs):
    state, other, out = refs[0], refs[1], refs[2 + count]
    is_later = (lax.axis_index("ex") & bit) == 0
    out[0] = state[0] + other[0]
    out[1] = state[1] + jnp.where(is_later, other[0], 0.0)


def ranges(bit, state, other, waited):
    return pl.pallas_call(
        functools.partial(range_kernel, bit, len(waited)),
        in_specs=[VMEM] * 2 + [pl.BlockSpec(memory_space=pl.ANY)] * len(waited),
        out_shape=jax.ShapeDtypeStruct(state.shape, F32),
        out_specs=VMEM,
        compiler_params=pltpu.CompilerParams(**PARAMS),
        name="ranges",
    )(state, other, *waited)


def order_kernel(start, parts, own, other, *refs):
    messages, (risk, rank, table) = refs[:parts], refs[parts : parts + 3]
    tangent_out, ordered_out, plain, lhs = refs[-4:]
    kf, width = tangent_out.shape
    rows = own.shape[1]
    groups = rows // LO
    span = min(SPAN, width)
    folded = jnp.zeros((kf, 128), F32)
    powers = [jnp.exp2(from_short(part[:, part.shape[1] - 128 :])) for part in messages]
    for i in range(width // span):
        at = slice(start + i * span, start + (i + 1) * span)
        here = slice(i * span, (i + 1) * span)
        tangent = own[:, at] + other[:, at]
        for part, power in zip(messages, powers):
            tangent = tangent + from_short(part[:, here]) * power[:, i : i + 1]
        tangent_out[:, here] = tangent
        weighted = tangent * risk[:, at]
        folded = folded + sum(weighted[:, j : j + 128] for j in range(0, span, 128))
        high, low = split_two(weighted)
        high, low = high.astype(BF16), low.astype(BF16)
        group = jnp.broadcast_to(lax.rem(rank[:, at], rows) // LO, (kf, span))
        for g in range(groups):
            mask = jnp.where(group == g, 1.0, 0.0).astype(BF16)
            lhs[2 * g * kf : (2 * g + 1) * kf, here] = high * mask
            lhs[(2 * g + 1) * kf : (2 * g + 2) * kf, here] = low * mask
    plain[...] = folded
    ordered = jnp.dot(lhs[...], table[start : start + width], preferred_element_type=F32)
    for g in range(groups):
        ordered_out[g * kf : (g + 1) * kf] = (
            ordered[2 * g * kf : (2 * g + 1) * kf] + ordered[(2 * g + 1) * kf : (2 * g + 2) * kf]
        )


def ordered_values(own, other, messages, risk, rank, table, start, width):
    kf, rows = own.shape
    groups = rows // LO
    return pl.pallas_call(
        functools.partial(order_kernel, start, len(messages)),
        in_specs=[VMEM] * (len(messages) + 5),
        out_shape=[
            jax.ShapeDtypeStruct((kf, width), F32),
            jax.ShapeDtypeStruct((groups * kf, LO), F32),
            jax.ShapeDtypeStruct((kf, 128), F32),
        ],
        out_specs=[VMEM] * 3,
        scratch_shapes=[pltpu.VMEM((groups * 2 * kf, width), BF16)],
        compiler_params=pltpu.CompilerParams(**PARAMS),
        cost_estimate=pl.CostEstimate(
            flops=2 * width * LO * groups * 2 * kf, bytes_accessed=width * kf * 24, transcendentals=0
        ),
        name="ordered_values",
    )(own, other, *messages, risk, rank, table)


def suffix_kernel(kf, one, two, sums):
    groups = sums.shape[0] // kf
    inside = dot_binary(one[...] + two[...], triangle(LO, lambda a, b: a >= b))
    carried = jnp.zeros((kf, 1), F32)
    for g in reversed(range(groups)):
        rows_of = slice(g * kf, (g + 1) * kf)
        sums[rows_of] = inside[rows_of] + carried
        carried = carried + inside[rows_of, :1]


def suffix_sums(one, two, kf):
    return pl.pallas_call(
        functools.partial(suffix_kernel, kf),
        in_specs=[VMEM] * 2,
        out_shape=jax.ShapeDtypeStruct(one.shape, F32),
        out_specs=VMEM,
        compiler_params=pltpu.CompilerParams(**PARAMS),
        name="suffix_sums",
    )(one, two)


def prefix_kernel(sums, squares, rank, out):
    kf, rows = out.shape
    groups = squares.shape[0]
    chunk = min(512, rows)
    hazard = [sums[g * kf : (g + 1) * kf] * squares[g : g + 1, :] for g in range(groups)]
    inside = dot_binary(jnp.concatenate(hazard, axis=0), triangle(LO, lambda a, b: a <= b))
    carried = jnp.zeros((kf, 1), F32)
    summed = [None] * groups
    for g in range(groups):
        rows_of = slice(g * kf, (g + 1) * kf)
        summed[g] = inside[rows_of] + carried
        carried = carried + inside[rows_of, LO - 1 :]
    both = stacked(split_two(jnp.concatenate(summed, axis=0)))
    for start in range(0, rows, chunk):
        at = slice(start, start + chunk)
        place = lax.rem(rank[:, at], rows)
        group = place // LO
        spread = one_hot(lax.rem(place, LO), LO)
        placed = unstacked(jnp.dot(both, spread, preferred_element_type=F32), 2)
        picked = jnp.zeros((kf, chunk), F32)
        for g in range(groups):
            picked = picked + jnp.where(group == g, placed[g * kf : (g + 1) * kf], 0.0)
        out[:, at] = picked


def prefix_sums(sums, squares, rank, kf):
    rows = rank.shape[1]
    return pl.pallas_call(
        prefix_kernel,
        in_specs=[VMEM] * 3,
        out_shape=jax.ShapeDtypeStruct((kf, rows), F32),
        out_specs=VMEM,
        compiler_params=pltpu.CompilerParams(**PARAMS),
        cost_estimate=pl.CostEstimate(
            flops=4 * rows * LO * (rows // LO) * kf, bytes_accessed=rows * kf * 24, transcendentals=0
        ),
        name="prefix_sums",
    )(sums, squares, rank)


def weight_kernel(ex, *refs):
    messages, (first, rest, local, risk, cumulative, squares) = refs[:ex], refs[ex : ex + 6]
    weighted, placed = refs[ex + 6 :]
    kf = first.shape[0]
    me = lax.axis_index("ex")
    for i in range(ex):
        placed[me ^ i] = messages[i][...]
    later = jnp.zeros((kf, 128), F32)
    own_later, before = later, later
    hazard_before = jnp.zeros((1, 128), F32)
    for b in reversed(range(ex)):
        plain, scaled, square = placed[b, :kf], placed[b, kf : 2 * kf], placed[b, 2 * kf + 1 : 2 * kf + 2]
        own_later = own_later + jnp.where(b > me, plain, 0.0)
        before = before + jnp.where(b < me, scaled + square * later, 0.0)
        hazard_before = hazard_before + jnp.where(b < me, placed[b, 2 * kf : 2 * kf + 1], 0.0)
        later = later + plain
    own_later = jnp.sum(own_later, axis=1, keepdims=True)
    before = jnp.sum(before, axis=1, keepdims=True)
    hazard_before = hazard_before[:, :1]
    for start, part in ((0, first), (first.shape[1], rest)):
        at = slice(start, start + part.shape[1])
        value = part[...] * (cumulative[:, at] + hazard_before) - (
            local[:, at] + squares[:, at] * own_later + before
        )
        weighted[:, at] = (risk[:, at] * value).astype(BF16)


def weights(messages, first, rest, local, risk, cumulative, squares):
    ex = len(messages)
    return pl.pallas_call(
        functools.partial(weight_kernel, ex),
        in_specs=[VMEM] * (ex + 6),
        out_shape=jax.ShapeDtypeStruct(local.shape, BF16),
        out_specs=VMEM,
        scratch_shapes=[pltpu.VMEM((ex,) + messages[0].shape, F32)],
        compiler_params=pltpu.CompilerParams(**PARAMS),
        name="weights",
    )(*messages, first, rest, local, risk, cumulative, squares)


def encode(values, message):
    columns = len(values)
    powers = []
    for i, value in enumerate(values):
        power = power_of(jnp.max(jnp.abs(value), axis=0, keepdims=True))
        scaled = to_short(value * jnp.exp2(-power))
        for j in range(value.shape[0] // 16):
            message[j * columns + i] = scaled[j * 16 : (j + 1) * 16]
        powers.append(power)
    powers.append(jnp.zeros((16 - columns, 128), F32))
    message[message.shape[0] - 1] = to_short(jnp.concatenate(powers, axis=0))


def decode(message, columns):
    last = message.shape[0] - 1
    scales = jnp.exp2(from_short(message[last]))
    values = []
    for i in range(columns):
        value = jnp.concatenate([from_short(message[j]) for j in range(i, last, columns)], axis=0)
        values.append(value * scales[i : i + 1])
    return values


def decode_sum(mine, other, columns):
    return [one + two for one, two in zip(decode(mine, columns), decode(other, columns))]


def gradient_kernel(parts, kf, *refs):
    pieces, dosages, out, weighted = refs[:parts], refs[parts], refs[parts + 1], refs[parts + 2]
    for i in range(parts):
        weighted[i * kf : (i + 1) * kf, :] = pieces[i][...]
    total = jnp.dot(weighted[...], dosages[...], preferred_element_type=F32)
    encode([total[:, at : at + 128] for at in range(0, total.shape[1], 128)], out)


def gradients(pieces, dosages):
    parts = len(pieces)
    kf, persons = pieces[0].shape
    k, variants = kf * parts, dosages.shape[1]
    return pl.pallas_call(
        functools.partial(gradient_kernel, parts, kf),
        in_specs=[VMEM] * (parts + 1),
        out_shape=jax.ShapeDtypeStruct((k * variants // 2048 + 1, 16, 128), jnp.int16),
        out_specs=VMEM,
        scratch_shapes=[pltpu.VMEM((k, persons), BF16)],
        compiler_params=pltpu.CompilerParams(**PARAMS),
        cost_estimate=pl.CostEstimate(
            flops=2 * persons * variants * k, bytes_accessed=persons * (variants * 2 + k * 2), transcendentals=0
        ),
        name="gradients",
    )(*pieces, dosages)


def merge_kernel(columns, mine, other, out):
    encode(decode_sum(mine, other, columns), out)


def merge(mine, other, variants):
    return pl.pallas_call(
        functools.partial(merge_kernel, variants // 128),
        in_specs=[VMEM] * 2,
        out_shape=jax.ShapeDtypeStruct(mine.shape, jnp.int16),
        out_specs=VMEM,
        compiler_params=pltpu.CompilerParams(**PARAMS),
        name="merge",
    )(mine, other)


def add_kernel(mine, other, out):
    for i, value in enumerate(decode_sum(mine, other, out.shape[1] // 128)):
        out[:, i * 128 : (i + 1) * 128] = value


def add(mine, other, variants):
    return pl.pallas_call(
        add_kernel,
        in_specs=[VMEM] * 2,
        out_shape=jax.ShapeDtypeStruct(((mine.shape[0] - 1) * 2048 // variants, variants), F32),
        out_specs=VMEM,
        compiler_params=pltpu.CompilerParams(**PARAMS),
        name="add",
    )(mine, other)


def finish_kernel(feat, kf, first, mine, other, count, out, placed, total, sems):
    me = lax.axis_index("feat")
    variants = out.shape[0]
    scale = count[1:2, 0:1]
    for q in range(feat // 2):
        placed[me ^ (2 * q)] = first[q * kf : (q + 1) * kf]
    for i, value in enumerate(decode_sum(mine, other, variants // 128)):
        for q in range(feat // 2):
            placed[me ^ (2 * q + 1), :, i * 128 : (i + 1) * 128] = value[q * kf : (q + 1) * kf]
    copies = []
    for i in range(variants // 128):
        at = slice(i * 128, (i + 1) * 128)
        total[at] = placed[:, :, at].reshape(feat * kf, 128).T / scale
        copies.append(
            pltpu.make_async_copy(
                total.at[pl.ds(i * 128, 128)], out.at[pl.ds(i * 128, 128)], sems.at[i]
            )
        )
        copies[i].start()
    for copy in copies:
        copy.wait()


def finish(first, mine, other, count, feat):
    k, variants = 2 * first.shape[0], first.shape[1]
    kf = k // feat
    return pl.pallas_call(
        functools.partial(finish_kernel, feat, kf),
        in_specs=[VMEM] * 4,
        out_shape=jax.ShapeDtypeStruct((variants, k), F32),
        out_specs=HBM,
        scratch_shapes=[
            pltpu.VMEM((feat, kf, variants), F32),
            pltpu.VMEM((variants, k), F32),
            pltpu.SemaphoreType.DMA((variants // 128,)),
        ],
        compiler_params=pltpu.CompilerParams(**PARAMS),
        name="finish",
    )(first, mine, other, count)


def local(dosages, coefficients, directions, event_rank, events):
    feat, ex = lax.axis_size("feat"), lax.axis_size("ex")
    rows = dosages.shape[0]
    variants, k = directions.shape
    each = k // feat
    padded = -(-each // 16) * 16
    if padded != each:
        directions = jnp.pad(directions.reshape(variants, feat, each), ((0, 0), (0, 0), (0, padded - each)))
        directions = directions.reshape(variants, feat * padded)
    rank, event_row = event_rank[None], events[None]

    linear, keep, send = products(dosages, coefficients, directions, feat)
    order = list(reversed(range(1, feat // 2)))
    received = {q: swap(send[q], "feat", 1) for q in order + [0]}
    table = tables(rank, linear, rows)
    paired = pair(linear, received[order[0]], table)
    middle = min(3 * SPAN, rows // 2)
    firsts = [
        swap(join(keep[q], received[q], 0, middle, paired, []), "feat", 2 * q) for q in order
    ]
    rests = [
        swap(join(keep[q], received[q], middle, rows - middle, paired, [received[0]]), "feat", 2 * q)
        for q in order
    ]

    risk, sums, ordered_events, state = risks(paired, firsts, rank, event_row, table, rows)
    bit = 1
    while bit < ex:
        state = ranges(bit, state, swap_odd(state, bit), rests if bit == 1 else [])
        bit *= 2
    tangent, one, plain = ordered_values(keep[0], received[0], firsts, risk, rank, table, 0, middle)
    more_tangent, two, more = ordered_values(
        keep[0], received[0], rests, risk, rank, table, middle, rows - middle
    )
    later_sums = suffix_sums(one, two, padded)
    hazard, ordered_squares, message, total = shares(
        state, hand_over(state), sums, ordered_events, plain, more, later_sums
    )
    messages = [message] + [swap(message, "ex", i) for i in range(1, ex)]
    cumulative, squares = hazards(hazard, ordered_squares, rank, rows)
    summed = prefix_sums(later_sums, ordered_squares, rank, padded)
    own = weights(messages, tangent, more_tangent, summed, risk, cumulative, squares)

    chips = {0: own}
    for q in range(1, feat // 2):
        chips[q] = swap(own, "feat", 2 * q)
    near = [chips[q] for q in range(feat // 2)]
    far = [swap(chips[q], "feat", 1) for q in range(feat // 2)]
    partial_sums = [gradients(pieces, dosages) for pieces in (near, far)]
    bit = 1
    while 2 * bit < ex:
        received = [swap(message, "ex", bit) for message in partial_sums]
        partial_sums = [merge(mine, other, variants) for mine, other in zip(partial_sums, received)]
        bit *= 2
    received = [swap(message, "ex", bit) for message in partial_sums]
    first = add(partial_sums[0], received[0], variants)
    result = finish(first, partial_sums[1], received[1], total, feat)
    if padded != each:
        result = result.reshape(variants, feat, padded)[:, :, :each].reshape(variants, k)
    return result


def solution(mesh):
    placed = (P("ex", "feat"), P("feat"), P("feat", None), P("ex"), P("ex"))
    return jax.shard_map(
        local, mesh=mesh, in_specs=placed, out_specs=P("feat", None), check_vma=False
    )
```

```python
import functools

import jax
import jax.numpy as jnp
from jax import lax
from jax.experimental import pallas as pl
from jax.experimental.pallas import tpu as pltpu
from jax.sharding import PartitionSpec as P

F32 = jnp.float32
BF16 = jnp.bfloat16
LO = 256
NT = (((1,), (1,)), ((), ()))
SPAN = 256
VMEM = pl.BlockSpec(memory_space=pltpu.VMEM)
HBM = pl.BlockSpec(memory_space=pltpu.HBM)
PARAMS = dict(vmem_limit_bytes=24 * 1024 * 1024)


def swap(x, axis, i):
    count = lax.axis_size(axis)
    return lax.ppermute(x, axis, [(s, s ^ i) for s in range(count)])


def split_two(x):
    high = x.astype(BF16).astype(F32)
    return high, x - high


def split_three(x):
    first, rest = split_two(x)
    second, third = split_two(rest)
    return first, second, third


def one_hot(values, count, kind=BF16):
    shape = (count, values.shape[1])
    return jnp.where(lax.broadcasted_iota(jnp.int32, shape, 0) == values, 1.0, 0.0).astype(kind)


def triangle(n, keep):
    first = lax.broadcasted_iota(jnp.int32, (n, n), 0)
    second = lax.broadcasted_iota(jnp.int32, (n, n), 1)
    return jnp.where(keep(first, second), 1.0, 0.0)


def stacked(parts):
    return jnp.concatenate(parts, axis=0).astype(BF16)


def unstacked(values, count):
    height = values.shape[0] // count
    return sum(values[i * height : (i + 1) * height] for i in range(count))


def dot_binary(a, b):
    parts = jnp.dot(stacked(split_three(a)), b.astype(BF16), preferred_element_type=F32)
    return unstacked(parts, 3)


def binary_dot(a, b):
    a = a.astype(BF16)
    total = None
    for part in split_three(b):
        term = jnp.dot(a, part.astype(BF16), preferred_element_type=F32)
        total = term if total is None else total + term
    return total


def product_kernel(feat, kf, chunk, directions, coefficients, dosages, *refs):
    linear, keep, send = refs[0], refs[1 : 1 + feat // 2], refs[1 + feat // 2 : 1 + feat]
    table, own_directions, own_coefficients, lhs, turned, sems = refs[1 + feat :]
    me = lax.axis_index("feat")
    width = feat * kf
    persons, variants = table.shape
    steps = persons // chunk
    small = [
        pltpu.make_async_copy(directions, own_directions, sems.at[steps]),
        pltpu.make_async_copy(coefficients, own_coefficients, sems.at[steps + 1]),
    ]
    large = [
        pltpu.make_async_copy(
            dosages.at[pl.ds(i * chunk, chunk)], table.at[pl.ds(i * chunk, chunk)], sems.at[i]
        )
        for i in range(steps)
    ]
    for copy in small + large:
        copy.start()
    for copy in small:
        copy.wait()
    turned[...] = own_directions[...].astype(F32).T.reshape(turned.shape)
    for j in range(feat):
        lhs[j * kf : (j + 1) * kf] = turned[me ^ j].astype(BF16)
    lhs[width:] = jnp.broadcast_to(own_coefficients[...].astype(F32)[None, :], (16, variants)).astype(BF16)
    for i in range(steps):
        large[i].wait()
        first = i * chunk
        result = lax.dot_general(
            lhs[...], table[first : first + chunk], NT, preferred_element_type=F32
        )
        for j in range(feat):
            (send if j % 2 else keep)[j // 2][:, first : first + chunk] = result[j * kf : (j + 1) * kf]
        for start in range(0, chunk, LO):
            row = result[width : width + 1, start : start + LO]
            group = (first + start) // LO
            linear[group : group + 1, :] = row
            send[-1][group : group + 1, persons:] = row


def products(dosages, coefficients, directions, feat):
    persons, variants = dosages.shape
    k = directions.shape[1]
    kf = k // feat
    chunk = min(2048, persons)
    piece = jax.ShapeDtypeStruct((kf, persons), F32)
    first = jax.ShapeDtypeStruct((kf, persons + LO), F32)
    out = pl.pallas_call(
        functools.partial(product_kernel, feat, kf, chunk),
        in_specs=[HBM, HBM, HBM],
        out_shape=[jax.ShapeDtypeStruct((kf, LO), F32)]
        + [piece] * (feat - 1)
        + [first],
        out_specs=[VMEM] * (feat + 1),
        scratch_shapes=[
            pltpu.VMEM((persons, variants), BF16),
            pltpu.VMEM((variants, k), BF16),
            pltpu.VMEM((variants,), BF16),
            pltpu.VMEM((k + 16, variants), BF16),
            pltpu.VMEM((feat, kf, variants), F32),
            pltpu.SemaphoreType.DMA((persons // chunk + 2,)),
        ],
        compiler_params=pltpu.CompilerParams(**PARAMS),
        cost_estimate=pl.CostEstimate(
            flops=2 * persons * variants * k, bytes_accessed=persons * (variants * 2 + k * 4), transcendentals=0
        ),
        name="products",
    )(*[pltpu.with_memory_space_constraint(x, pltpu.HBM) for x in (directions, coefficients, dosages)])
    return out[0], out[1 : 1 + feat // 2], out[1 + feat // 2 :]


def power_of(largest):
    return jnp.ceil(jnp.log2(jnp.maximum(largest, 1e-30))) - 14.0


def to_short(values):
    return jnp.round(values).astype(jnp.int32).astype(jnp.int16)


def from_short(values):
    return values.astype(jnp.int32).astype(F32)


def pair_kernel(linear, received, waited, out):
    out[...] = linear[...] + received[:, received.shape[1] - LO :]


def pair(linear, received, waited):
    return pl.pallas_call(
        pair_kernel,
        in_specs=[VMEM] * 2 + [pl.BlockSpec(memory_space=pl.ANY)],
        out_shape=jax.ShapeDtypeStruct(linear.shape, F32),
        out_specs=VMEM,
        compiler_params=pltpu.CompilerParams(**PARAMS),
        name="pair",
    )(linear, received, waited)


def join_kernel(start, width, mine, other, *refs):
    linear, out = refs[0], refs[-1]
    kf = mine.shape[0]
    span = min(SPAN, width)
    lane = lax.broadcasted_iota(jnp.int32, (kf, 128), 1)
    powers = jnp.zeros((kf, 128), F32)
    for i in range(width // span):
        at = slice(start + i * span, start + (i + 1) * span)
        total = mine[:, at] + other[:, at]
        power = power_of(jnp.max(jnp.abs(total), axis=1, keepdims=True))
        out[:, i * span : (i + 1) * span] = to_short(total * jnp.exp2(-power))
        powers = jnp.where(lane == i, power, powers)
    if start == 0:
        power = power_of(jnp.max(jnp.abs(linear[...]), axis=1, keepdims=True))
        scaled = linear[...] * jnp.exp2(-power)
        whole = jnp.round(scaled)
        out[:, width : width + LO] = to_short(whole)
        out[:, width + LO : width + 2 * LO] = to_short((scaled - whole) * 32768.0)
        powers = jnp.where(lane == 127, power, powers)
    out[:, out.shape[1] - 128 :] = to_short(powers)


def join(keep, received, start, width, linear, waited):
    kf, rows = keep.shape
    extra = 2 * LO if start == 0 else 0
    return pl.pallas_call(
        functools.partial(join_kernel, start, width),
        in_specs=[VMEM] * 3 + [pl.BlockSpec(memory_space=pl.ANY)] * len(waited),
        out_shape=jax.ShapeDtypeStruct((kf, width + extra + 128), jnp.int16),
        out_specs=VMEM,
        compiler_params=pltpu.CompilerParams(**PARAMS),
        name="join",
    )(keep, received, linear, *waited)


def table_kernel(rows, rank, waited, table):
    chunk = min(512, rows)
    lane = lax.broadcasted_iota(jnp.int32, (chunk, 128), 1)
    for start in range(0, rows, chunk):
        at = slice(start, start + chunk)
        inner = lax.rem(rank[:, at], LO)
        column = jnp.broadcast_to(inner.astype(F32), (128, chunk)).T.astype(jnp.int32)
        for first in range(0, LO, 128):
            table[at, first : first + 128] = jnp.where(column == lane + first, 1.0, 0.0).astype(BF16)


def tables(rank, waited, rows):
    return pl.pallas_call(
        functools.partial(table_kernel, rows),
        in_specs=[VMEM, pl.BlockSpec(memory_space=pl.ANY)],
        out_shape=jax.ShapeDtypeStruct((rows, LO), BF16),
        out_specs=VMEM,
        compiler_params=pltpu.CompilerParams(**PARAMS),
        cost_estimate=pl.CostEstimate(flops=rows * LO * 8, bytes_accessed=rows * LO * 2, transcendentals=0),
        name="tables",
    )(rank, waited)


def risk_kernel(rows, parts, linear, *refs):
    messages, (rank, events, table) = refs[:parts], refs[parts : parts + 3]
    risk_out, sums_out, events_out, message = refs[-4:]
    groups = rows // LO
    total = linear[...]
    for part in messages:
        end = part.shape[1] - 128
        power = from_short(part[:, end:])[:, 127:]
        high, low = from_short(part[:, end - 2 * LO : end - LO]), from_short(part[:, end - LO : end])
        total = total + (high + low * (1.0 / 32768.0)) * jnp.exp2(power)
    risk = jnp.exp(total)
    for g in range(groups):
        risk_out[:, g * LO : (g + 1) * LO] = risk[g : g + 1]
    mask = one_hot(lax.rem(rank[...], rows) // LO, groups, F32)
    pieces = [mask * part for part in split_three(risk_out[...])] + [mask * events[...].astype(F32)]
    lhs = jnp.concatenate(pieces, axis=0).astype(BF16)
    sorted_all = jnp.dot(lhs, table[...], preferred_element_type=F32)
    ordered = sorted_all[:groups] + sorted_all[groups : 2 * groups] + sorted_all[2 * groups : 3 * groups]
    happened = sorted_all[3 * groups :]
    inside = dot_binary(ordered, triangle(LO, lambda a, b: a >= b))
    totals = jnp.broadcast_to(inside[:, :1], inside.shape)
    carried = binary_dot(triangle(groups, lambda a, b: a < b), totals)
    sums_out[...] = inside + carried
    events_out[...] = happened
    everything = jnp.sum(totals, axis=0, keepdims=True)[:, :128]
    count = jnp.sum(dot_binary(happened, jnp.ones((LO, 128), F32)), axis=0, keepdims=True)
    message[...] = jnp.concatenate([everything, count, jnp.zeros((6, 128), F32)], axis=0)


def risks(linear, messages, rank, events, table, rows):
    groups = rows // LO
    return pl.pallas_call(
        functools.partial(risk_kernel, rows, len(messages)),
        in_specs=[VMEM] * (len(messages) + 4),
        out_shape=[
            jax.ShapeDtypeStruct((1, rows), F32),
            jax.ShapeDtypeStruct((groups, LO), F32),
            jax.ShapeDtypeStruct((groups, LO), F32),
            jax.ShapeDtypeStruct((8, 128), F32),
        ],
        out_specs=[VMEM] * 4,
        compiler_params=pltpu.CompilerParams(**PARAMS),
        cost_estimate=pl.CostEstimate(flops=rows * LO * 128, bytes_accessed=rows * 64, transcendentals=rows),
        name="risks",
    )(linear, *messages, rank, events, table)


def share_kernel(later, sums, events, plain, more, ordered, hazard_out, squares, message):
    kf = plain.shape[0]
    groups = sums.shape[0]
    risk_sum = sums[...] + later[0:1, 0:1]
    hazard = events[...] / risk_sum
    square = events[...] / (risk_sum * risk_sum)
    hazard_out[...] = hazard
    squares[...] = square
    scaled = jnp.zeros((kf, LO), F32)
    for g in range(groups):
        scaled = scaled + ordered[g * kf : (g + 1) * kf] * square[g : g + 1]
    message[:kf] = plain[...] + more[...]
    message[kf : 2 * kf] = sum(scaled[:, start : start + 128] for start in range(0, LO, 128))
    totals = [jnp.sum(jnp.sum(v, axis=0, keepdims=True), axis=1, keepdims=True) for v in (hazard, square)]
    rows = [jnp.broadcast_to(v, (1, 128)) for v in totals]
    message[2 * kf :] = jnp.concatenate(rows + [jnp.zeros((6, 128), F32)], axis=0)


def shares(later, sums, events, plain, more, ordered):
    flat = jax.ShapeDtypeStruct(sums.shape, F32)
    return pl.pallas_call(
        share_kernel,
        in_specs=[VMEM] * 6,
        out_shape=[flat, flat, jax.ShapeDtypeStruct((2 * plain.shape[0] + 8, 128), F32)],
        out_specs=[VMEM] * 3,
        compiler_params=pltpu.CompilerParams(**PARAMS),
        name="shares",
    )(later, sums, events, plain, more, ordered)


def hazard_kernel(rows, hazard, square, rank, cumulative, squares):
    groups = rows // LO
    inside = dot_binary(
        jnp.concatenate([hazard[...], square[...]], axis=0), triangle(LO, lambda a, b: a <= b)
    )
    totals = jnp.broadcast_to(inside[:, LO - 1 :], (2 * groups, 128))
    place = lax.rem(rank[...], rows)
    mask = one_hot(place // LO, groups, F32)
    placed = dot_binary(inside, one_hot(lax.rem(place, LO), LO))
    before = triangle(groups, lambda a, b: a > b)
    for first, out in ((0, cumulative), (groups, squares)):
        carried = binary_dot(before, totals[first : first + groups])[:, :1]
        out[...] = jnp.sum(mask * (placed[first : first + groups] + carried), axis=0, keepdims=True)


def hazards(hazard, square, rank, rows):
    row = jax.ShapeDtypeStruct((1, rows), F32)
    return pl.pallas_call(
        functools.partial(hazard_kernel, rows),
        in_specs=[VMEM] * 3,
        out_shape=[row, row],
        out_specs=[VMEM] * 2,
        compiler_params=pltpu.CompilerParams(**PARAMS),
        cost_estimate=pl.CostEstimate(flops=rows * LO * 200, bytes_accessed=rows * 64, transcendentals=0),
        name="hazards",
    )(hazard, square, rank)


def range_kernel(bit, count, *refs):
    total, other, later = refs[:3]
    total_out, later_out = refs[3 + count :]
    is_later = (lax.axis_index("ex") & bit) == 0
    later_out[...] = later[...] + jnp.where(is_later, other[...], 0.0)
    total_out[...] = total[...] + other[...]


def ranges(bit, total, other, later, waited):
    return pl.pallas_call(
        functools.partial(range_kernel, bit, len(waited)),
        in_specs=[VMEM] * 3 + [pl.BlockSpec(memory_space=pl.ANY)] * len(waited),
        out_shape=[jax.ShapeDtypeStruct(total.shape, F32)] * 2,
        out_specs=[VMEM] * 2,
        compiler_params=pltpu.CompilerParams(**PARAMS),
        name="ranges",
    )(total, other, later, *waited)


def order_kernel(start, parts, own, other, *refs):
    messages, (risk, rank, table) = refs[:parts], refs[parts : parts + 3]
    tangent_out, ordered_out, plain, lhs = refs[-4:]
    kf, width = tangent_out.shape
    rows = own.shape[1]
    groups = rows // LO
    span = min(SPAN, width)
    folded = jnp.zeros((kf, 128), F32)
    powers = [jnp.exp2(from_short(part[:, part.shape[1] - 128 :])) for part in messages]
    for i in range(width // span):
        at = slice(start + i * span, start + (i + 1) * span)
        here = slice(i * span, (i + 1) * span)
        tangent = own[:, at] + other[:, at]
        for part, power in zip(messages, powers):
            tangent = tangent + from_short(part[:, here]) * power[:, i : i + 1]
        tangent_out[:, here] = tangent
        weighted = tangent * risk[:, at]
        folded = folded + sum(weighted[:, j : j + 128] for j in range(0, span, 128))
        high, low = split_two(weighted)
        high, low = high.astype(BF16), low.astype(BF16)
        group = jnp.broadcast_to(lax.rem(rank[:, at], rows) // LO, (kf, span))
        for g in range(groups):
            mask = jnp.where(group == g, 1.0, 0.0).astype(BF16)
            lhs[2 * g * kf : (2 * g + 1) * kf, here] = high * mask
            lhs[(2 * g + 1) * kf : (2 * g + 2) * kf, here] = low * mask
    plain[...] = folded
    ordered = jnp.dot(lhs[...], table[start : start + width], preferred_element_type=F32)
    for g in range(groups):
        ordered_out[g * kf : (g + 1) * kf] = (
            ordered[2 * g * kf : (2 * g + 1) * kf] + ordered[(2 * g + 1) * kf : (2 * g + 2) * kf]
        )


def ordered_values(own, other, messages, risk, rank, table, start, width):
    kf, rows = own.shape
    groups = rows // LO
    return pl.pallas_call(
        functools.partial(order_kernel, start, len(messages)),
        in_specs=[VMEM] * (len(messages) + 5),
        out_shape=[
            jax.ShapeDtypeStruct((kf, width), F32),
            jax.ShapeDtypeStruct((groups * kf, LO), F32),
            jax.ShapeDtypeStruct((kf, 128), F32),
        ],
        out_specs=[VMEM] * 3,
        scratch_shapes=[pltpu.VMEM((groups * 2 * kf, width), BF16)],
        compiler_params=pltpu.CompilerParams(**PARAMS),
        cost_estimate=pl.CostEstimate(
            flops=2 * width * LO * groups * 2 * kf, bytes_accessed=width * kf * 24, transcendentals=0
        ),
        name="ordered_values",
    )(own, other, *messages, risk, rank, table)


def suffix_kernel(kf, one, two, sums):
    groups = sums.shape[0] // kf
    inside = dot_binary(one[...] + two[...], triangle(LO, lambda a, b: a >= b))
    carried = jnp.zeros((kf, 1), F32)
    for g in reversed(range(groups)):
        rows_of = slice(g * kf, (g + 1) * kf)
        sums[rows_of] = inside[rows_of] + carried
        carried = carried + inside[rows_of, :1]


def suffix_sums(one, two, kf):
    return pl.pallas_call(
        functools.partial(suffix_kernel, kf),
        in_specs=[VMEM] * 2,
        out_shape=jax.ShapeDtypeStruct(one.shape, F32),
        out_specs=VMEM,
        compiler_params=pltpu.CompilerParams(**PARAMS),
        name="suffix_sums",
    )(one, two)


def prefix_kernel(sums, squares, rank, out):
    kf, rows = out.shape
    groups = squares.shape[0]
    chunk = min(512, rows)
    hazard = [sums[g * kf : (g + 1) * kf] * squares[g : g + 1, :] for g in range(groups)]
    inside = dot_binary(jnp.concatenate(hazard, axis=0), triangle(LO, lambda a, b: a <= b))
    carried = jnp.zeros((kf, 1), F32)
    summed = [None] * groups
    for g in range(groups):
        rows_of = slice(g * kf, (g + 1) * kf)
        summed[g] = inside[rows_of] + carried
        carried = carried + inside[rows_of, LO - 1 :]
    both = stacked(split_two(jnp.concatenate(summed, axis=0)))
    for start in range(0, rows, chunk):
        at = slice(start, start + chunk)
        place = lax.rem(rank[:, at], rows)
        group = place // LO
        spread = one_hot(lax.rem(place, LO), LO)
        placed = unstacked(jnp.dot(both, spread, preferred_element_type=F32), 2)
        picked = jnp.zeros((kf, chunk), F32)
        for g in range(groups):
            picked = picked + jnp.where(group == g, placed[g * kf : (g + 1) * kf], 0.0)
        out[:, at] = picked


def prefix_sums(sums, squares, rank, kf):
    rows = rank.shape[1]
    return pl.pallas_call(
        prefix_kernel,
        in_specs=[VMEM] * 3,
        out_shape=jax.ShapeDtypeStruct((kf, rows), F32),
        out_specs=VMEM,
        compiler_params=pltpu.CompilerParams(**PARAMS),
        cost_estimate=pl.CostEstimate(
            flops=4 * rows * LO * (rows // LO) * kf, bytes_accessed=rows * kf * 24, transcendentals=0
        ),
        name="prefix_sums",
    )(sums, squares, rank)


def weight_kernel(ex, *refs):
    messages, (first, rest, local, risk, cumulative, squares) = refs[:ex], refs[ex : ex + 6]
    weighted, placed = refs[ex + 6 :]
    kf = first.shape[0]
    me = lax.axis_index("ex")
    for i in range(ex):
        placed[me ^ i] = messages[i][...]
    later = jnp.zeros((kf, 128), F32)
    own_later, before = later, later
    hazard_before = jnp.zeros((1, 128), F32)
    for b in reversed(range(ex)):
        plain, scaled, square = placed[b, :kf], placed[b, kf : 2 * kf], placed[b, 2 * kf + 1 : 2 * kf + 2]
        own_later = own_later + jnp.where(b > me, plain, 0.0)
        before = before + jnp.where(b < me, scaled + square * later, 0.0)
        hazard_before = hazard_before + jnp.where(b < me, placed[b, 2 * kf : 2 * kf + 1], 0.0)
        later = later + plain
    own_later = jnp.sum(own_later, axis=1, keepdims=True)
    before = jnp.sum(before, axis=1, keepdims=True)
    hazard_before = hazard_before[:, :1]
    for start, part in ((0, first), (first.shape[1], rest)):
        at = slice(start, start + part.shape[1])
        value = part[...] * (cumulative[:, at] + hazard_before) - (
            local[:, at] + squares[:, at] * own_later + before
        )
        weighted[:, at] = (risk[:, at] * value).astype(BF16)


def weights(messages, first, rest, local, risk, cumulative, squares):
    ex = len(messages)
    return pl.pallas_call(
        functools.partial(weight_kernel, ex),
        in_specs=[VMEM] * (ex + 6),
        out_shape=jax.ShapeDtypeStruct(local.shape, BF16),
        out_specs=VMEM,
        scratch_shapes=[pltpu.VMEM((ex,) + messages[0].shape, F32)],
        compiler_params=pltpu.CompilerParams(**PARAMS),
        name="weights",
    )(*messages, first, rest, local, risk, cumulative, squares)


def encode(values, message):
    columns = len(values)
    powers = []
    for i, value in enumerate(values):
        power = power_of(jnp.max(jnp.abs(value), axis=0, keepdims=True))
        scaled = to_short(value * jnp.exp2(-power))
        for j in range(value.shape[0] // 16):
            message[j * columns + i] = scaled[j * 16 : (j + 1) * 16]
        powers.append(power)
    powers.append(jnp.zeros((16 - columns, 128), F32))
    message[message.shape[0] - 1] = to_short(jnp.concatenate(powers, axis=0))


def decode(message, columns):
    last = message.shape[0] - 1
    scales = jnp.exp2(from_short(message[last]))
    values = []
    for i in range(columns):
        value = jnp.concatenate([from_short(message[j]) for j in range(i, last, columns)], axis=0)
        values.append(value * scales[i : i + 1])
    return values


def decode_sum(mine, other, columns):
    return [one + two for one, two in zip(decode(mine, columns), decode(other, columns))]


def gradient_kernel(parts, kf, *refs):
    pieces, dosages, out, weighted = refs[:parts], refs[parts], refs[parts + 1], refs[parts + 2]
    for i in range(parts):
        weighted[i * kf : (i + 1) * kf, :] = pieces[i][...]
    total = jnp.dot(weighted[...], dosages[...], preferred_element_type=F32)
    encode([total[:, at : at + 128] for at in range(0, total.shape[1], 128)], out)


def gradients(pieces, dosages):
    parts = len(pieces)
    kf, persons = pieces[0].shape
    k, variants = kf * parts, dosages.shape[1]
    return pl.pallas_call(
        functools.partial(gradient_kernel, parts, kf),
        in_specs=[VMEM] * (parts + 1),
        out_shape=jax.ShapeDtypeStruct((k * variants // 2048 + 1, 16, 128), jnp.int16),
        out_specs=VMEM,
        scratch_shapes=[pltpu.VMEM((k, persons), BF16)],
        compiler_params=pltpu.CompilerParams(**PARAMS),
        cost_estimate=pl.CostEstimate(
            flops=2 * persons * variants * k, bytes_accessed=persons * (variants * 2 + k * 2), transcendentals=0
        ),
        name="gradients",
    )(*pieces, dosages)


def merge_kernel(columns, mine, other, out):
    encode(decode_sum(mine, other, columns), out)


def merge(mine, other, variants):
    return pl.pallas_call(
        functools.partial(merge_kernel, variants // 128),
        in_specs=[VMEM] * 2,
        out_shape=jax.ShapeDtypeStruct(mine.shape, jnp.int16),
        out_specs=VMEM,
        compiler_params=pltpu.CompilerParams(**PARAMS),
        name="merge",
    )(mine, other)


def add_kernel(mine, other, out):
    for i, value in enumerate(decode_sum(mine, other, out.shape[1] // 128)):
        out[:, i * 128 : (i + 1) * 128] = value


def add(mine, other, variants):
    return pl.pallas_call(
        add_kernel,
        in_specs=[VMEM] * 2,
        out_shape=jax.ShapeDtypeStruct(((mine.shape[0] - 1) * 2048 // variants, variants), F32),
        out_specs=VMEM,
        compiler_params=pltpu.CompilerParams(**PARAMS),
        name="add",
    )(mine, other)


def finish_kernel(feat, kf, first, mine, other, count, out, placed, total, sems):
    me = lax.axis_index("feat")
    variants = out.shape[0]
    scale = count[1:2, 0:1]
    for q in range(feat // 2):
        placed[me ^ (2 * q)] = first[q * kf : (q + 1) * kf]
    for i, value in enumerate(decode_sum(mine, other, variants // 128)):
        for q in range(feat // 2):
            placed[me ^ (2 * q + 1), :, i * 128 : (i + 1) * 128] = value[q * kf : (q + 1) * kf]
    copies = []
    for i in range(variants // 128):
        at = slice(i * 128, (i + 1) * 128)
        total[at] = placed[:, :, at].reshape(feat * kf, 128).T / scale
        copies.append(
            pltpu.make_async_copy(
                total.at[pl.ds(i * 128, 128)], out.at[pl.ds(i * 128, 128)], sems.at[i]
            )
        )
        copies[i].start()
    for copy in copies:
        copy.wait()


def finish(first, mine, other, count, feat):
    k, variants = 2 * first.shape[0], first.shape[1]
    kf = k // feat
    return pl.pallas_call(
        functools.partial(finish_kernel, feat, kf),
        in_specs=[VMEM] * 4,
        out_shape=jax.ShapeDtypeStruct((variants, k), F32),
        out_specs=HBM,
        scratch_shapes=[
            pltpu.VMEM((feat, kf, variants), F32),
            pltpu.VMEM((variants, k), F32),
            pltpu.SemaphoreType.DMA((variants // 128,)),
        ],
        compiler_params=pltpu.CompilerParams(**PARAMS),
        name="finish",
    )(first, mine, other, count)


def local(dosages, coefficients, directions, event_rank, events):
    feat, ex = lax.axis_size("feat"), lax.axis_size("ex")
    rows = dosages.shape[0]
    variants, k = directions.shape
    each = k // feat
    padded = -(-each // 16) * 16
    if padded != each:
        directions = jnp.pad(directions.reshape(variants, feat, each), ((0, 0), (0, 0), (0, padded - each)))
        directions = directions.reshape(variants, feat * padded)
    rank, event_row = event_rank[None], events[None]

    linear, keep, send = products(dosages, coefficients, directions, feat)
    order = list(reversed(range(1, feat // 2)))
    received = {q: swap(send[q], "feat", 1) for q in order + [0]}
    table = tables(rank, linear, rows)
    paired = pair(linear, received[order[0]], table)
    middle = min(5 * SPAN, rows // 2)
    firsts = [
        swap(join(keep[q], received[q], 0, middle, paired, []), "feat", 2 * q) for q in order
    ]
    rests = [
        swap(join(keep[q], received[q], middle, rows - middle, paired, [received[0]]), "feat", 2 * q)
        for q in order
    ]

    risk, sums, ordered_events, total = risks(paired, firsts, rank, event_row, table, rows)
    later = jnp.zeros_like(total)
    bit = 1
    while bit < ex:
        total, later = ranges(bit, total, swap(total, "ex", bit), later, rests if bit == 1 else [])
        bit *= 2
    tangent, one, plain = ordered_values(keep[0], received[0], firsts, risk, rank, table, 0, middle)
    more_tangent, two, more = ordered_values(
        keep[0], received[0], rests, risk, rank, table, middle, rows - middle
    )
    later_sums = suffix_sums(one, two, padded)
    hazard, ordered_squares, message = shares(later, sums, ordered_events, plain, more, later_sums)
    messages = [message] + [swap(message, "ex", i) for i in range(1, ex)]
    cumulative, squares = hazards(hazard, ordered_squares, rank, rows)
    summed = prefix_sums(later_sums, ordered_squares, rank, padded)
    own = weights(messages, tangent, more_tangent, summed, risk, cumulative, squares)

    chips = {0: own}
    for q in range(1, feat // 2):
        chips[q] = swap(own, "feat", 2 * q)
    near = [chips[q] for q in range(feat // 2)]
    far = [swap(chips[q], "feat", 1) for q in range(feat // 2)]
    partial_sums = [gradients(pieces, dosages) for pieces in (near, far)]
    bit = 1
    while 2 * bit < ex:
        received = [swap(message, "ex", bit) for message in partial_sums]
        partial_sums = [merge(mine, other, variants) for mine, other in zip(partial_sums, received)]
        bit *= 2
    received = [swap(message, "ex", bit) for message in partial_sums]
    first = add(partial_sums[0], received[0], variants)
    result = finish(first, partial_sums[1], received[1], total, feat)
    if padded != each:
        result = result.reshape(variants, feat, padded)[:, :, :each].reshape(variants, k)
    return result


def solution(mesh):
    placed = (P("ex", "feat"), P("feat"), P("feat", None), P("ex"), P("ex"))
    return jax.shard_map(
        local, mesh=mesh, in_specs=placed, out_specs=P("feat", None), check_vma=False
    )
```

```python
import functools

import jax
import jax.numpy as jnp
from jax import lax
from jax.experimental import pallas as pl
from jax.experimental.pallas import tpu as pltpu
from jax.sharding import PartitionSpec as P

F32 = jnp.float32
BF16 = jnp.bfloat16
LO = 256
NT = (((1,), (1,)), ((), ()))
SPAN = 512
VMEM = pl.BlockSpec(memory_space=pltpu.VMEM)
HBM = pl.BlockSpec(memory_space=pltpu.HBM)
PARAMS = dict(vmem_limit_bytes=24 * 1024 * 1024)


def swap(x, axis, i):
    count = lax.axis_size(axis)
    return lax.ppermute(x, axis, [(s, s ^ i) for s in range(count)])


def split_two(x):
    high = x.astype(BF16).astype(F32)
    return high, x - high


def split_three(x):
    first, rest = split_two(x)
    second, third = split_two(rest)
    return first, second, third


def one_hot(values, count, kind=BF16):
    shape = (count, values.shape[1])
    return jnp.where(lax.broadcasted_iota(jnp.int32, shape, 0) == values, 1.0, 0.0).astype(kind)


def triangle(n, keep):
    first = lax.broadcasted_iota(jnp.int32, (n, n), 0)
    second = lax.broadcasted_iota(jnp.int32, (n, n), 1)
    return jnp.where(keep(first, second), 1.0, 0.0)


def stacked(parts):
    return jnp.concatenate(parts, axis=0).astype(BF16)


def unstacked(values, count):
    height = values.shape[0] // count
    return sum(values[i * height : (i + 1) * height] for i in range(count))


def dot_binary(a, b):
    parts = jnp.dot(stacked(split_three(a)), b.astype(BF16), preferred_element_type=F32)
    return unstacked(parts, 3)


def binary_dot(a, b):
    a = a.astype(BF16)
    total = None
    for part in split_three(b):
        term = jnp.dot(a, part.astype(BF16), preferred_element_type=F32)
        total = term if total is None else total + term
    return total


def product_kernel(feat, kf, chunk, directions, coefficients, dosages, *refs):
    linear, keep, send = refs[0], refs[1 : 1 + feat // 2], refs[1 + feat // 2 : 1 + feat]
    table, own_directions, own_coefficients, lhs, turned, sems = refs[1 + feat :]
    me = lax.axis_index("feat")
    width = feat * kf
    persons, variants = table.shape
    steps = persons // chunk
    small = [
        pltpu.make_async_copy(directions, own_directions, sems.at[steps]),
        pltpu.make_async_copy(coefficients, own_coefficients, sems.at[steps + 1]),
    ]
    large = [
        pltpu.make_async_copy(
            dosages.at[pl.ds(i * chunk, chunk)], table.at[pl.ds(i * chunk, chunk)], sems.at[i]
        )
        for i in range(steps)
    ]
    for copy in small + large:
        copy.start()
    for copy in small:
        copy.wait()
    turned[...] = own_directions[...].astype(F32).T.reshape(turned.shape)
    for j in range(feat):
        lhs[j * kf : (j + 1) * kf] = turned[me ^ j].astype(BF16)
    lhs[width:] = jnp.broadcast_to(own_coefficients[...].astype(F32)[None, :], (16, variants)).astype(BF16)
    for i in range(steps):
        large[i].wait()
        first = i * chunk
        result = lax.dot_general(
            lhs[...], table[first : first + chunk], NT, preferred_element_type=F32
        )
        for j in range(feat):
            (send if j % 2 else keep)[j // 2][:, first : first + chunk] = result[j * kf : (j + 1) * kf]
        for start in range(0, chunk, LO):
            row = result[width : width + 1, start : start + LO]
            group = (first + start) // LO
            linear[group : group + 1, :] = row
            send[-1][group : group + 1, persons:] = row


def products(dosages, coefficients, directions, feat):
    persons, variants = dosages.shape
    k = directions.shape[1]
    kf = k // feat
    chunk = min(1024, persons)
    piece = jax.ShapeDtypeStruct((kf, persons), F32)
    first = jax.ShapeDtypeStruct((kf, persons + LO), F32)
    out = pl.pallas_call(
        functools.partial(product_kernel, feat, kf, chunk),
        in_specs=[HBM, HBM, HBM],
        out_shape=[jax.ShapeDtypeStruct((kf, LO), F32)]
        + [piece] * (feat - 1)
        + [first],
        out_specs=[VMEM] * (feat + 1),
        scratch_shapes=[
            pltpu.VMEM((persons, variants), BF16),
            pltpu.VMEM((variants, k), BF16),
            pltpu.VMEM((variants,), BF16),
            pltpu.VMEM((k + 16, variants), BF16),
            pltpu.VMEM((feat, kf, variants), F32),
            pltpu.SemaphoreType.DMA((persons // chunk + 2,)),
        ],
        compiler_params=pltpu.CompilerParams(**PARAMS),
        cost_estimate=pl.CostEstimate(
            flops=2 * persons * variants * k, bytes_accessed=persons * (variants * 2 + k * 4), transcendentals=0
        ),
        name="products",
    )(*[pltpu.with_memory_space_constraint(x, pltpu.HBM) for x in (directions, coefficients, dosages)])
    return out[0], out[1 : 1 + feat // 2], out[1 + feat // 2 :]


def power_of(largest):
    return jnp.ceil(jnp.log2(jnp.maximum(largest, 1e-30))) - 14.0


def to_short(values):
    return jnp.round(values).astype(jnp.int32).astype(jnp.int16)


def from_short(values):
    return values.astype(jnp.int32).astype(F32)


def pair_kernel(linear, received, waited, out):
    out[...] = linear[...] + received[:, received.shape[1] - LO :]


def pair(linear, received, waited):
    return pl.pallas_call(
        pair_kernel,
        in_specs=[VMEM] * 2 + [pl.BlockSpec(memory_space=pl.ANY)],
        out_shape=jax.ShapeDtypeStruct(linear.shape, F32),
        out_specs=VMEM,
        compiler_params=pltpu.CompilerParams(**PARAMS),
        name="pair",
    )(linear, received, waited)


def join_kernel(start, width, mine, other, *refs):
    linear, out = refs[0], refs[-1]
    kf = mine.shape[0]
    span = min(SPAN, width)
    lane = lax.broadcasted_iota(jnp.int32, (kf, 128), 1)
    powers = jnp.zeros((kf, 128), F32)
    for i in range(width // span):
        at = slice(start + i * span, start + (i + 1) * span)
        total = mine[:, at] + other[:, at]
        power = power_of(jnp.max(jnp.abs(total), axis=1, keepdims=True))
        out[:, i * span : (i + 1) * span] = to_short(total * jnp.exp2(-power))
        powers = jnp.where(lane == i, power, powers)
    if start == 0:
        power = power_of(jnp.max(jnp.abs(linear[...]), axis=1, keepdims=True))
        scaled = linear[...] * jnp.exp2(-power)
        whole = jnp.round(scaled)
        out[:, width : width + LO] = to_short(whole)
        out[:, width + LO : width + 2 * LO] = to_short((scaled - whole) * 32768.0)
        powers = jnp.where(lane == 127, power, powers)
    out[:, out.shape[1] - 128 :] = to_short(powers)


def join(keep, received, start, width, linear, waited):
    kf, rows = keep.shape
    extra = 2 * LO if start == 0 else 0
    return pl.pallas_call(
        functools.partial(join_kernel, start, width),
        in_specs=[VMEM] * 3 + [pl.BlockSpec(memory_space=pl.ANY)] * len(waited),
        out_shape=jax.ShapeDtypeStruct((kf, width + extra + 128), jnp.int16),
        out_specs=VMEM,
        compiler_params=pltpu.CompilerParams(**PARAMS),
        name="join",
    )(keep, received, linear, *waited)


def table_kernel(rows, rank, waited, table):
    chunk = min(512, rows)
    lane = lax.broadcasted_iota(jnp.int32, (chunk, 128), 1)
    for start in range(0, rows, chunk):
        at = slice(start, start + chunk)
        inner = lax.rem(rank[:, at], LO)
        column = jnp.broadcast_to(inner.astype(F32), (128, chunk)).T.astype(jnp.int32)
        for first in range(0, LO, 128):
            table[at, first : first + 128] = jnp.where(column == lane + first, 1.0, 0.0).astype(BF16)


def tables(rank, waited, rows):
    return pl.pallas_call(
        functools.partial(table_kernel, rows),
        in_specs=[VMEM, pl.BlockSpec(memory_space=pl.ANY)],
        out_shape=jax.ShapeDtypeStruct((rows, LO), BF16),
        out_specs=VMEM,
        compiler_params=pltpu.CompilerParams(**PARAMS),
        cost_estimate=pl.CostEstimate(flops=rows * LO * 8, bytes_accessed=rows * LO * 2, transcendentals=0),
        name="tables",
    )(rank, waited)


def risk_kernel(rows, parts, linear, *refs):
    messages, (rank, events, table) = refs[:parts], refs[parts : parts + 3]
    risk_out, sums_out, events_out, message = refs[-4:]
    groups = rows // LO
    total = linear[...]
    for part in messages:
        end = part.shape[1] - 128
        power = from_short(part[:, end:])[:, 127:]
        high, low = from_short(part[:, end - 2 * LO : end - LO]), from_short(part[:, end - LO : end])
        total = total + (high + low * (1.0 / 32768.0)) * jnp.exp2(power)
    risk = jnp.exp(total)
    for g in range(groups):
        risk_out[:, g * LO : (g + 1) * LO] = risk[g : g + 1]
    mask = one_hot(lax.rem(rank[...], rows) // LO, groups, F32)
    pieces = [mask * part for part in split_three(risk_out[...])] + [mask * events[...].astype(F32)]
    lhs = jnp.concatenate(pieces, axis=0).astype(BF16)
    sorted_all = jnp.dot(lhs, table[...], preferred_element_type=F32)
    ordered = sorted_all[:groups] + sorted_all[groups : 2 * groups] + sorted_all[2 * groups : 3 * groups]
    happened = sorted_all[3 * groups :]
    inside = dot_binary(ordered, triangle(LO, lambda a, b: a >= b))
    totals = jnp.broadcast_to(inside[:, :1], inside.shape)
    carried = binary_dot(triangle(groups, lambda a, b: a < b), totals)
    sums_out[...] = inside + carried
    events_out[...] = happened
    everything = jnp.sum(totals, axis=0, keepdims=True)[:, :128]
    count = jnp.sum(dot_binary(happened, jnp.ones((LO, 128), F32)), axis=0, keepdims=True)
    message[...] = jnp.concatenate([everything, count, jnp.zeros((6, 128), F32)], axis=0)


def risks(linear, messages, rank, events, table, rows):
    groups = rows // LO
    return pl.pallas_call(
        functools.partial(risk_kernel, rows, len(messages)),
        in_specs=[VMEM] * (len(messages) + 4),
        out_shape=[
            jax.ShapeDtypeStruct((1, rows), F32),
            jax.ShapeDtypeStruct((groups, LO), F32),
            jax.ShapeDtypeStruct((groups, LO), F32),
            jax.ShapeDtypeStruct((8, 128), F32),
        ],
        out_specs=[VMEM] * 4,
        compiler_params=pltpu.CompilerParams(**PARAMS),
        cost_estimate=pl.CostEstimate(flops=rows * LO * 128, bytes_accessed=rows * 64, transcendentals=rows),
        name="risks",
    )(linear, *messages, rank, events, table)


def share_kernel(later, sums, events, plain, more, ordered, hazard_out, squares, message):
    kf = plain.shape[0]
    groups = sums.shape[0]
    risk_sum = sums[...] + later[0:1, 0:1]
    hazard = events[...] / risk_sum
    square = events[...] / (risk_sum * risk_sum)
    hazard_out[...] = hazard
    squares[...] = square
    scaled = jnp.zeros((kf, LO), F32)
    for g in range(groups):
        scaled = scaled + ordered[g * kf : (g + 1) * kf] * square[g : g + 1]
    message[:kf] = plain[...] + more[...]
    message[kf : 2 * kf] = sum(scaled[:, start : start + 128] for start in range(0, LO, 128))
    totals = [jnp.sum(jnp.sum(v, axis=0, keepdims=True), axis=1, keepdims=True) for v in (hazard, square)]
    rows = [jnp.broadcast_to(v, (1, 128)) for v in totals]
    message[2 * kf :] = jnp.concatenate(rows + [jnp.zeros((6, 128), F32)], axis=0)


def shares(later, sums, events, plain, more, ordered):
    flat = jax.ShapeDtypeStruct(sums.shape, F32)
    return pl.pallas_call(
        share_kernel,
        in_specs=[VMEM] * 6,
        out_shape=[flat, flat, jax.ShapeDtypeStruct((2 * plain.shape[0] + 8, 128), F32)],
        out_specs=[VMEM] * 3,
        compiler_params=pltpu.CompilerParams(**PARAMS),
        name="shares",
    )(later, sums, events, plain, more, ordered)


def hazard_kernel(rows, hazard, square, rank, cumulative, squares):
    groups = rows // LO
    inside = dot_binary(
        jnp.concatenate([hazard[...], square[...]], axis=0), triangle(LO, lambda a, b: a <= b)
    )
    totals = jnp.broadcast_to(inside[:, LO - 1 :], (2 * groups, 128))
    place = lax.rem(rank[...], rows)
    mask = one_hot(place // LO, groups, F32)
    placed = dot_binary(inside, one_hot(lax.rem(place, LO), LO))
    before = triangle(groups, lambda a, b: a > b)
    for first, out in ((0, cumulative), (groups, squares)):
        carried = binary_dot(before, totals[first : first + groups])[:, :1]
        out[...] = jnp.sum(mask * (placed[first : first + groups] + carried), axis=0, keepdims=True)


def hazards(hazard, square, rank, rows):
    row = jax.ShapeDtypeStruct((1, rows), F32)
    return pl.pallas_call(
        functools.partial(hazard_kernel, rows),
        in_specs=[VMEM] * 3,
        out_shape=[row, row],
        out_specs=[VMEM] * 2,
        compiler_params=pltpu.CompilerParams(**PARAMS),
        cost_estimate=pl.CostEstimate(flops=rows * LO * 200, bytes_accessed=rows * 64, transcendentals=0),
        name="hazards",
    )(hazard, square, rank)


def range_kernel(bit, count, *refs):
    total, other, later = refs[:3]
    total_out, later_out = refs[3 + count :]
    is_later = (lax.axis_index("ex") & bit) == 0
    later_out[...] = later[...] + jnp.where(is_later, other[...], 0.0)
    total_out[...] = total[...] + other[...]


def ranges(bit, total, other, later, waited):
    return pl.pallas_call(
        functools.partial(range_kernel, bit, len(waited)),
        in_specs=[VMEM] * 3 + [pl.BlockSpec(memory_space=pl.ANY)] * len(waited),
        out_shape=[jax.ShapeDtypeStruct(total.shape, F32)] * 2,
        out_specs=[VMEM] * 2,
        compiler_params=pltpu.CompilerParams(**PARAMS),
        name="ranges",
    )(total, other, later, *waited)


def order_kernel(start, parts, own, other, *refs):
    messages, (risk, rank, table) = refs[:parts], refs[parts : parts + 3]
    tangent_out, ordered_out, plain, lhs = refs[-4:]
    kf, width = tangent_out.shape
    rows = own.shape[1]
    groups = rows // LO
    span = min(SPAN, width)
    folded = jnp.zeros((kf, 128), F32)
    powers = [jnp.exp2(from_short(part[:, part.shape[1] - 128 :])) for part in messages]
    for i in range(width // span):
        at = slice(start + i * span, start + (i + 1) * span)
        here = slice(i * span, (i + 1) * span)
        tangent = own[:, at] + other[:, at]
        for part, power in zip(messages, powers):
            tangent = tangent + from_short(part[:, here]) * power[:, i : i + 1]
        tangent_out[:, here] = tangent
        weighted = tangent * risk[:, at]
        folded = folded + sum(weighted[:, j : j + 128] for j in range(0, span, 128))
        high, low = split_two(weighted)
        high, low = high.astype(BF16), low.astype(BF16)
        group = jnp.broadcast_to(lax.rem(rank[:, at], rows) // LO, (kf, span))
        for g in range(groups):
            mask = jnp.where(group == g, 1.0, 0.0).astype(BF16)
            lhs[2 * g * kf : (2 * g + 1) * kf, here] = high * mask
            lhs[(2 * g + 1) * kf : (2 * g + 2) * kf, here] = low * mask
    plain[...] = folded
    ordered = jnp.dot(lhs[...], table[start : start + width], preferred_element_type=F32)
    for g in range(groups):
        ordered_out[g * kf : (g + 1) * kf] = (
            ordered[2 * g * kf : (2 * g + 1) * kf] + ordered[(2 * g + 1) * kf : (2 * g + 2) * kf]
        )


def ordered_values(own, other, messages, risk, rank, table, start, width):
    kf, rows = own.shape
    groups = rows // LO
    return pl.pallas_call(
        functools.partial(order_kernel, start, len(messages)),
        in_specs=[VMEM] * (len(messages) + 5),
        out_shape=[
            jax.ShapeDtypeStruct((kf, width), F32),
            jax.ShapeDtypeStruct((groups * kf, LO), F32),
            jax.ShapeDtypeStruct((kf, 128), F32),
        ],
        out_specs=[VMEM] * 3,
        scratch_shapes=[pltpu.VMEM((groups * 2 * kf, width), BF16)],
        compiler_params=pltpu.CompilerParams(**PARAMS),
        cost_estimate=pl.CostEstimate(
            flops=2 * width * LO * groups * 2 * kf, bytes_accessed=width * kf * 24, transcendentals=0
        ),
        name="ordered_values",
    )(own, other, *messages, risk, rank, table)


def suffix_kernel(kf, one, two, sums):
    groups = sums.shape[0] // kf
    inside = dot_binary(one[...] + two[...], triangle(LO, lambda a, b: a >= b))
    carried = jnp.zeros((kf, 1), F32)
    for g in reversed(range(groups)):
        rows_of = slice(g * kf, (g + 1) * kf)
        sums[rows_of] = inside[rows_of] + carried
        carried = carried + inside[rows_of, :1]


def suffix_sums(one, two, kf):
    return pl.pallas_call(
        functools.partial(suffix_kernel, kf),
        in_specs=[VMEM] * 2,
        out_shape=jax.ShapeDtypeStruct(one.shape, F32),
        out_specs=VMEM,
        compiler_params=pltpu.CompilerParams(**PARAMS),
        name="suffix_sums",
    )(one, two)


def prefix_kernel(sums, squares, rank, out):
    kf, rows = out.shape
    groups = squares.shape[0]
    chunk = min(512, rows)
    hazard = [sums[g * kf : (g + 1) * kf] * squares[g : g + 1, :] for g in range(groups)]
    inside = dot_binary(jnp.concatenate(hazard, axis=0), triangle(LO, lambda a, b: a <= b))
    carried = jnp.zeros((kf, 1), F32)
    summed = [None] * groups
    for g in range(groups):
        rows_of = slice(g * kf, (g + 1) * kf)
        summed[g] = inside[rows_of] + carried
        carried = carried + inside[rows_of, LO - 1 :]
    both = stacked(split_two(jnp.concatenate(summed, axis=0)))
    for start in range(0, rows, chunk):
        at = slice(start, start + chunk)
        place = lax.rem(rank[:, at], rows)
        group = place // LO
        spread = one_hot(lax.rem(place, LO), LO)
        placed = unstacked(jnp.dot(both, spread, preferred_element_type=F32), 2)
        picked = jnp.zeros((kf, chunk), F32)
        for g in range(groups):
            picked = picked + jnp.where(group == g, placed[g * kf : (g + 1) * kf], 0.0)
        out[:, at] = picked


def prefix_sums(sums, squares, rank, kf):
    rows = rank.shape[1]
    return pl.pallas_call(
        prefix_kernel,
        in_specs=[VMEM] * 3,
        out_shape=jax.ShapeDtypeStruct((kf, rows), F32),
        out_specs=VMEM,
        compiler_params=pltpu.CompilerParams(**PARAMS),
        cost_estimate=pl.CostEstimate(
            flops=4 * rows * LO * (rows // LO) * kf, bytes_accessed=rows * kf * 24, transcendentals=0
        ),
        name="prefix_sums",
    )(sums, squares, rank)


def weight_kernel(places, *refs):
    ex = len(places)
    messages, (first, rest, local, risk, cumulative, squares) = refs[:ex], refs[ex : ex + 6]
    weighted, placed = refs[ex + 6 :]
    kf = first.shape[0]
    me = lax.axis_index("ex")
    for i, part in zip(places, messages):
        placed[me ^ i] = part[...]
    later = jnp.zeros((kf, 128), F32)
    own_later, before = later, later
    hazard_before = jnp.zeros((1, 128), F32)
    for b in reversed(range(ex)):
        plain, scaled, square = placed[b, :kf], placed[b, kf : 2 * kf], placed[b, 2 * kf + 1 : 2 * kf + 2]
        own_later = own_later + jnp.where(b > me, plain, 0.0)
        before = before + jnp.where(b < me, scaled + square * later, 0.0)
        hazard_before = hazard_before + jnp.where(b < me, placed[b, 2 * kf : 2 * kf + 1], 0.0)
        later = later + plain
    own_later = jnp.sum(own_later, axis=1, keepdims=True)
    before = jnp.sum(before, axis=1, keepdims=True)
    hazard_before = hazard_before[:, :1]
    for start, part in ((0, first), (first.shape[1], rest)):
        at = slice(start, start + part.shape[1])
        value = part[...] * (cumulative[:, at] + hazard_before) - (
            local[:, at] + squares[:, at] * own_later + before
        )
        weighted[:, at] = (risk[:, at] * value).astype(BF16)


def weights(places, messages, first, rest, local, risk, cumulative, squares):
    ex = len(messages)
    return pl.pallas_call(
        functools.partial(weight_kernel, tuple(places)),
        in_specs=[VMEM] * (ex + 6),
        out_shape=jax.ShapeDtypeStruct(local.shape, BF16),
        out_specs=VMEM,
        scratch_shapes=[pltpu.VMEM((ex,) + messages[0].shape, F32)],
        compiler_params=pltpu.CompilerParams(**PARAMS),
        name="weights",
    )(*messages, first, rest, local, risk, cumulative, squares)


def encode(values, message):
    columns = len(values)
    powers = []
    for i, value in enumerate(values):
        power = power_of(jnp.max(jnp.abs(value), axis=0, keepdims=True))
        scaled = to_short(value * jnp.exp2(-power))
        for j in range(value.shape[0] // 16):
            message[j * columns + i] = scaled[j * 16 : (j + 1) * 16]
        powers.append(power)
    powers.append(jnp.zeros((16 - columns, 128), F32))
    message[message.shape[0] - 1] = to_short(jnp.concatenate(powers, axis=0))


def decode(message, columns):
    last = message.shape[0] - 1
    scales = jnp.exp2(from_short(message[last]))
    values = []
    for i in range(columns):
        value = jnp.concatenate([from_short(message[j]) for j in range(i, last, columns)], axis=0)
        values.append(value * scales[i : i + 1])
    return values


def decode_sum(mine, other, columns):
    return [one + two for one, two in zip(decode(mine, columns), decode(other, columns))]


def gradient_kernel(parts, kf, *refs):
    pieces, dosages, out, weighted = refs[:parts], refs[parts], refs[parts + 1], refs[parts + 2]
    for i in range(parts):
        weighted[i * kf : (i + 1) * kf, :] = pieces[i][...]
    total = jnp.dot(weighted[...], dosages[...], preferred_element_type=F32)
    encode([total[:, at : at + 128] for at in range(0, total.shape[1], 128)], out)


def gradients(pieces, dosages):
    parts = len(pieces)
    kf, persons = pieces[0].shape
    k, variants = kf * parts, dosages.shape[1]
    return pl.pallas_call(
        functools.partial(gradient_kernel, parts, kf),
        in_specs=[VMEM] * (parts + 1),
        out_shape=jax.ShapeDtypeStruct((k * variants // 2048 + 1, 16, 128), jnp.int16),
        out_specs=VMEM,
        scratch_shapes=[pltpu.VMEM((k, persons), BF16)],
        compiler_params=pltpu.CompilerParams(**PARAMS),
        cost_estimate=pl.CostEstimate(
            flops=2 * persons * variants * k, bytes_accessed=persons * (variants * 2 + k * 2), transcendentals=0
        ),
        name="gradients",
    )(*pieces, dosages)


def merge_kernel(columns, mine, other, out):
    encode(decode_sum(mine, other, columns), out)


def merge(mine, other, variants):
    return pl.pallas_call(
        functools.partial(merge_kernel, variants // 128),
        in_specs=[VMEM] * 2,
        out_shape=jax.ShapeDtypeStruct(mine.shape, jnp.int16),
        out_specs=VMEM,
        compiler_params=pltpu.CompilerParams(**PARAMS),
        name="merge",
    )(mine, other)


def add_kernel(mine, other, out):
    for i, value in enumerate(decode_sum(mine, other, out.shape[1] // 128)):
        out[:, i * 128 : (i + 1) * 128] = value


def add(mine, other, variants):
    return pl.pallas_call(
        add_kernel,
        in_specs=[VMEM] * 2,
        out_shape=jax.ShapeDtypeStruct(((mine.shape[0] - 1) * 2048 // variants, variants), F32),
        out_specs=VMEM,
        compiler_params=pltpu.CompilerParams(**PARAMS),
        name="add",
    )(mine, other)


def finish_kernel(feat, kf, ring, first, mine, other, count, out, placed, total, sems):
    me = lax.axis_index("feat")
    variants = out.shape[0]
    scale = count[1:2, 0:1]
    for j, q in enumerate(ring):
        placed[me ^ (2 * q)] = first[j * kf : (j + 1) * kf]
    for i, value in enumerate(decode_sum(mine, other, variants // 128)):
        for j, q in enumerate(ring):
            placed[me ^ (2 * q + 1), :, i * 128 : (i + 1) * 128] = value[j * kf : (j + 1) * kf]
    copies = []
    for i in range(variants // 128):
        at = slice(i * 128, (i + 1) * 128)
        total[at] = placed[:, :, at].reshape(feat * kf, 128).T / scale
        copies.append(
            pltpu.make_async_copy(
                total.at[pl.ds(i * 128, 128)], out.at[pl.ds(i * 128, 128)], sems.at[i]
            )
        )
        copies[i].start()
    for copy in copies:
        copy.wait()


def finish(first, mine, other, count, ring):
    feat = 2 * len(ring)
    k, variants = 2 * first.shape[0], first.shape[1]
    kf = k // feat
    return pl.pallas_call(
        functools.partial(finish_kernel, feat, kf, tuple(ring)),
        in_specs=[VMEM] * 4,
        out_shape=jax.ShapeDtypeStruct((variants, k), F32),
        out_specs=HBM,
        scratch_shapes=[
            pltpu.VMEM((feat, kf, variants), F32),
            pltpu.VMEM((variants, k), F32),
            pltpu.SemaphoreType.DMA((variants // 128,)),
        ],
        compiler_params=pltpu.CompilerParams(**PARAMS),
        name="finish",
    )(first, mine, other, count)


def local(dosages, coefficients, directions, event_rank, events):
    feat, ex = lax.axis_size("feat"), lax.axis_size("ex")
    rows = dosages.shape[0]
    variants, k = directions.shape
    each = k // feat
    padded = -(-each // 16) * 16
    if padded != each:
        directions = jnp.pad(directions.reshape(variants, feat, each), ((0, 0), (0, 0), (0, padded - each)))
        directions = directions.reshape(variants, feat * padded)
    rank, event_row = event_rank[None], events[None]

    linear, keep, send = products(dosages, coefficients, directions, feat)
    order = list(reversed(range(1, feat // 2)))
    received = {q: swap(send[q], "feat", 1) for q in order + [0]}
    table = tables(rank, linear, rows)
    paired = pair(linear, received[order[0]], table)
    middle = min(3 * SPAN, rows // 2)
    firsts = [
        swap(join(keep[q], received[q], 0, middle, paired, []), "feat", 2 * q) for q in order
    ]
    rests = [
        swap(join(keep[q], received[q], middle, rows - middle, paired, [received[0]]), "feat", 2 * q)
        for q in order
    ]

    risk, sums, ordered_events, total = risks(paired, firsts, rank, event_row, table, rows)
    later = jnp.zeros_like(total)
    bit = 1
    while bit < ex:
        total, later = ranges(bit, total, swap(total, "ex", bit), later, rests if bit == 1 else [])
        bit *= 2
    tangent, one, plain = ordered_values(keep[0], received[0], firsts, risk, rank, table, 0, middle)
    more_tangent, two, more = ordered_values(
        keep[0], received[0], rests, risk, rank, table, middle, rows - middle
    )
    later_sums = suffix_sums(one, two, padded)
    hazard, ordered_squares, message = shares(later, sums, ordered_events, plain, more, later_sums)
    places = list(range(ex))
    places[-2:] = places[:-3:-1]
    messages = [swap(message, "ex", i) if i else message for i in places]
    cumulative, squares = hazards(hazard, ordered_squares, rank, rows)
    summed = prefix_sums(later_sums, ordered_squares, rank, padded)
    own = weights(places, messages, tangent, more_tangent, summed, risk, cumulative, squares)

    chips = {0: own}
    for q in range(1, feat // 2):
        chips[q] = swap(own, "feat", 2 * q)
    ring = [0] + list(reversed(range(1, feat // 2)))
    near = [chips[q] for q in ring]
    far = [swap(chips[q], "feat", 1) for q in ring]
    partial_sums = [gradients(pieces, dosages) for pieces in (near, far)]
    bit = 1
    while 2 * bit < ex:
        received = [swap(message, "ex", bit) for message in partial_sums]
        partial_sums = [merge(mine, other, variants) for mine, other in zip(partial_sums, received)]
        bit *= 2
    received = [swap(message, "ex", bit) for message in partial_sums]
    first = add(partial_sums[0], received[0], variants)
    result = finish(first, partial_sums[1], received[1], total, ring)
    if padded != each:
        result = result.reshape(variants, feat, padded)[:, :, :each].reshape(variants, k)
    return result


def solution(mesh):
    placed = (P("ex", "feat"), P("feat"), P("feat", None), P("ex"), P("ex"))
    return jax.shard_map(
        local, mesh=mesh, in_specs=placed, out_specs=P("feat", None), check_vma=False
    )
```

```python
import functools

import jax
import jax.numpy as jnp
from jax import lax
from jax.experimental import pallas as pl
from jax.experimental.pallas import tpu as pltpu
from jax.sharding import PartitionSpec as P

F32 = jnp.float32
BF16 = jnp.bfloat16
LO = 256
NT = (((1,), (1,)), ((), ()))
SPAN = 512
VMEM = pl.BlockSpec(memory_space=pltpu.VMEM)
HBM = pl.BlockSpec(memory_space=pltpu.HBM)
PARAMS = dict(vmem_limit_bytes=24 * 1024 * 1024)


def swap(x, axis, i):
    count = lax.axis_size(axis)
    return lax.ppermute(x, axis, [(s, s ^ i) for s in range(count)])


def split_two(x):
    high = x.astype(BF16).astype(F32)
    return high, x - high


def split_three(x):
    first, rest = split_two(x)
    second, third = split_two(rest)
    return first, second, third


def one_hot(values, count, kind=BF16):
    shape = (count, values.shape[1])
    return jnp.where(lax.broadcasted_iota(jnp.int32, shape, 0) == values, 1.0, 0.0).astype(kind)


def triangle(n, keep):
    first = lax.broadcasted_iota(jnp.int32, (n, n), 0)
    second = lax.broadcasted_iota(jnp.int32, (n, n), 1)
    return jnp.where(keep(first, second), 1.0, 0.0)


def stacked(parts):
    return jnp.concatenate(parts, axis=0).astype(BF16)


def unstacked(values, count):
    height = values.shape[0] // count
    return sum(values[i * height : (i + 1) * height] for i in range(count))


def dot_binary(a, b):
    parts = jnp.dot(stacked(split_three(a)), b.astype(BF16), preferred_element_type=F32)
    return unstacked(parts, 3)


def binary_dot(a, b):
    a = a.astype(BF16)
    total = None
    for part in split_three(b):
        term = jnp.dot(a, part.astype(BF16), preferred_element_type=F32)
        total = term if total is None else total + term
    return total


def product_kernel(feat, kf, chunk, directions, coefficients, dosages, *refs):
    linear, keep, send = refs[0], refs[1 : 1 + feat // 2], refs[1 + feat // 2 : 1 + feat]
    table, own_directions, own_coefficients, lhs, turned, sems = refs[1 + feat :]
    me = lax.axis_index("feat")
    width = feat * kf
    persons, variants = table.shape
    steps = persons // chunk
    small = [
        pltpu.make_async_copy(directions, own_directions, sems.at[steps]),
        pltpu.make_async_copy(coefficients, own_coefficients, sems.at[steps + 1]),
    ]
    large = [
        pltpu.make_async_copy(
            dosages.at[pl.ds(i * chunk, chunk)], table.at[pl.ds(i * chunk, chunk)], sems.at[i]
        )
        for i in range(steps)
    ]
    for copy in small + large:
        copy.start()
    for copy in small:
        copy.wait()
    turned[...] = own_directions[...].astype(F32).T.reshape(turned.shape)
    for j in range(feat):
        lhs[j * kf : (j + 1) * kf] = turned[me ^ j].astype(BF16)
    lhs[width:] = jnp.broadcast_to(own_coefficients[...].astype(F32)[None, :], (16, variants)).astype(BF16)
    for i in range(steps):
        large[i].wait()
        first = i * chunk
        result = lax.dot_general(
            lhs[...], table[first : first + chunk], NT, preferred_element_type=F32
        )
        for j in range(feat):
            (send if j % 2 else keep)[j // 2][:, first : first + chunk] = result[j * kf : (j + 1) * kf]
        for start in range(0, chunk, LO):
            row = result[width : width + 1, start : start + LO]
            group = (first + start) // LO
            linear[group : group + 1, :] = row
            send[-1][group : group + 1, persons:] = row


def products(dosages, coefficients, directions, feat):
    persons, variants = dosages.shape
    k = directions.shape[1]
    kf = k // feat
    chunk = min(1024, persons)
    piece = jax.ShapeDtypeStruct((kf, persons), F32)
    first = jax.ShapeDtypeStruct((kf, persons + LO), F32)
    out = pl.pallas_call(
        functools.partial(product_kernel, feat, kf, chunk),
        in_specs=[HBM, HBM, HBM],
        out_shape=[jax.ShapeDtypeStruct((kf, LO), F32)]
        + [piece] * (feat - 1)
        + [first],
        out_specs=[VMEM] * (feat + 1),
        scratch_shapes=[
            pltpu.VMEM((persons, variants), BF16),
            pltpu.VMEM((variants, k), BF16),
            pltpu.VMEM((variants,), BF16),
            pltpu.VMEM((k + 16, variants), BF16),
            pltpu.VMEM((feat, kf, variants), F32),
            pltpu.SemaphoreType.DMA((persons // chunk + 2,)),
        ],
        compiler_params=pltpu.CompilerParams(**PARAMS),
        cost_estimate=pl.CostEstimate(
            flops=2 * persons * variants * k, bytes_accessed=persons * (variants * 2 + k * 4), transcendentals=0
        ),
        name="products",
    )(*[pltpu.with_memory_space_constraint(x, pltpu.HBM) for x in (directions, coefficients, dosages)])
    return out[0], out[1 : 1 + feat // 2], out[1 + feat // 2 :]


def power_of(largest):
    return jnp.ceil(jnp.log2(jnp.maximum(largest, 1e-30))) - 14.0


def to_short(values):
    return jnp.round(values).astype(jnp.int32).astype(jnp.int16)


def from_short(values):
    return values.astype(jnp.int32).astype(F32)


def pair_kernel(linear, received, waited, out):
    out[...] = linear[...] + received[:, received.shape[1] - LO :]


def pair(linear, received, waited):
    return pl.pallas_call(
        pair_kernel,
        in_specs=[VMEM] * 2 + [pl.BlockSpec(memory_space=pl.ANY)],
        out_shape=jax.ShapeDtypeStruct(linear.shape, F32),
        out_specs=VMEM,
        compiler_params=pltpu.CompilerParams(**PARAMS),
        name="pair",
    )(linear, received, waited)


def join_kernel(start, width, mine, other, *refs):
    linear, out = refs[0], refs[-1]
    kf = mine.shape[0]
    span = min(SPAN, width)
    lane = lax.broadcasted_iota(jnp.int32, (kf, 128), 1)
    powers = jnp.zeros((kf, 128), F32)
    for i in range(width // span):
        at = slice(start + i * span, start + (i + 1) * span)
        total = mine[:, at] + other[:, at]
        power = power_of(jnp.max(jnp.abs(total), axis=1, keepdims=True))
        out[:, i * span : (i + 1) * span] = to_short(total * jnp.exp2(-power))
        powers = jnp.where(lane == i, power, powers)
    if start == 0:
        power = power_of(jnp.max(jnp.abs(linear[...]), axis=1, keepdims=True))
        scaled = linear[...] * jnp.exp2(-power)
        whole = jnp.round(scaled)
        out[:, width : width + LO] = to_short(whole)
        out[:, width + LO : width + 2 * LO] = to_short((scaled - whole) * 32768.0)
        powers = jnp.where(lane == 127, power, powers)
    out[:, out.shape[1] - 128 :] = to_short(powers)


def join(keep, received, start, width, linear, waited):
    kf, rows = keep.shape
    extra = 2 * LO if start == 0 else 0
    return pl.pallas_call(
        functools.partial(join_kernel, start, width),
        in_specs=[VMEM] * 3 + [pl.BlockSpec(memory_space=pl.ANY)] * len(waited),
        out_shape=jax.ShapeDtypeStruct((kf, width + extra + 128), jnp.int16),
        out_specs=VMEM,
        compiler_params=pltpu.CompilerParams(**PARAMS),
        name="join",
    )(keep, received, linear, *waited)


def table_kernel(rows, rank, waited, table):
    chunk = min(512, rows)
    lane = lax.broadcasted_iota(jnp.int32, (chunk, 128), 1)
    for start in range(0, rows, chunk):
        at = slice(start, start + chunk)
        inner = lax.rem(rank[:, at], LO)
        column = jnp.broadcast_to(inner.astype(F32), (128, chunk)).T.astype(jnp.int32)
        for first in range(0, LO, 128):
            table[at, first : first + 128] = jnp.where(column == lane + first, 1.0, 0.0).astype(BF16)


def tables(rank, waited, rows):
    return pl.pallas_call(
        functools.partial(table_kernel, rows),
        in_specs=[VMEM, pl.BlockSpec(memory_space=pl.ANY)],
        out_shape=jax.ShapeDtypeStruct((rows, LO), BF16),
        out_specs=VMEM,
        compiler_params=pltpu.CompilerParams(**PARAMS),
        cost_estimate=pl.CostEstimate(flops=rows * LO * 8, bytes_accessed=rows * LO * 2, transcendentals=0),
        name="tables",
    )(rank, waited)


def risk_kernel(rows, parts, linear, *refs):
    messages, events = refs[:parts], refs[parts]
    risk_out, message = refs[parts + 1 :]
    groups = rows // LO
    total = linear[...]
    for part in messages:
        end = part.shape[1] - 128
        power = from_short(part[:, end:])[:, 127:]
        high, low = from_short(part[:, end - 2 * LO : end - LO]), from_short(part[:, end - LO : end])
        total = total + (high + low * (1.0 / 32768.0)) * jnp.exp2(power)
    risk = jnp.exp(total[:groups])
    for g in range(groups):
        risk_out[:, g * LO : (g + 1) * LO] = risk[g : g + 1]
    everything = jnp.sum(jnp.sum(risk, axis=0, keepdims=True), axis=1, keepdims=True)
    count = jnp.sum(events[...].astype(F32), axis=1, keepdims=True)
    totals = [jnp.broadcast_to(value, (1, 128)) for value in (everything, count)]
    message[...] = jnp.concatenate(totals + [jnp.zeros((6, 128), F32)], axis=0)


def risks(linear, messages, events, rows):
    return pl.pallas_call(
        functools.partial(risk_kernel, rows, len(messages)),
        in_specs=[VMEM] * (len(messages) + 2),
        out_shape=[jax.ShapeDtypeStruct((1, rows), F32), jax.ShapeDtypeStruct((8, 128), F32)],
        out_specs=[VMEM] * 2,
        compiler_params=pltpu.CompilerParams(**PARAMS),
        cost_estimate=pl.CostEstimate(flops=rows * 64, bytes_accessed=rows * 64, transcendentals=rows),
        name="risks",
    )(linear, *messages, events)


def risk_sum_kernel(rows, risk, rank, events, table, sums_out, events_out):
    groups = rows // LO
    mask = one_hot(lax.rem(rank[...], rows) // LO, groups, F32)
    pieces = [mask * part for part in split_three(risk[...])] + [mask * events[...].astype(F32)]
    lhs = jnp.concatenate(pieces, axis=0).astype(BF16)
    sorted_all = jnp.dot(lhs, table[...], preferred_element_type=F32)
    ordered = sorted_all[:groups] + sorted_all[groups : 2 * groups] + sorted_all[2 * groups : 3 * groups]
    inside = dot_binary(ordered, triangle(LO, lambda a, b: a >= b))
    totals = jnp.broadcast_to(inside[:, :1], inside.shape)
    carried = binary_dot(triangle(groups, lambda a, b: a < b), totals)
    sums_out[...] = inside + carried
    events_out[...] = sorted_all[3 * groups :]


def risk_sums(risk, rank, events, table, rows):
    flat = jax.ShapeDtypeStruct((rows // LO, LO), F32)
    return pl.pallas_call(
        functools.partial(risk_sum_kernel, rows),
        in_specs=[VMEM] * 4,
        out_shape=[flat, flat],
        out_specs=[VMEM] * 2,
        compiler_params=pltpu.CompilerParams(**PARAMS),
        cost_estimate=pl.CostEstimate(flops=rows * LO * 128, bytes_accessed=rows * 64, transcendentals=0),
        name="risk_sums",
    )(risk, rank, events, table)


def share_kernel(later, sums, events, plain, more, ordered, hazard_out, squares, message):
    kf = plain.shape[0]
    groups = sums.shape[0]
    risk_sum = sums[...] + later[0:1, 0:1]
    hazard = events[...] / risk_sum
    square = events[...] / (risk_sum * risk_sum)
    hazard_out[...] = hazard
    squares[...] = square
    scaled = jnp.zeros((kf, LO), F32)
    for g in range(groups):
        scaled = scaled + ordered[g * kf : (g + 1) * kf] * square[g : g + 1]
    message[:kf] = plain[...] + more[...]
    message[kf : 2 * kf] = sum(scaled[:, start : start + 128] for start in range(0, LO, 128))
    totals = [jnp.sum(jnp.sum(v, axis=0, keepdims=True), axis=1, keepdims=True) for v in (hazard, square)]
    rows = [jnp.broadcast_to(v, (1, 128)) for v in totals]
    message[2 * kf :] = jnp.concatenate(rows + [jnp.zeros((6, 128), F32)], axis=0)


def shares(later, sums, events, plain, more, ordered):
    flat = jax.ShapeDtypeStruct(sums.shape, F32)
    return pl.pallas_call(
        share_kernel,
        in_specs=[VMEM] * 6,
        out_shape=[flat, flat, jax.ShapeDtypeStruct((2 * plain.shape[0] + 8, 128), F32)],
        out_specs=[VMEM] * 3,
        compiler_params=pltpu.CompilerParams(**PARAMS),
        name="shares",
    )(later, sums, events, plain, more, ordered)


def hazard_kernel(rows, hazard, square, rank, cumulative, squares):
    groups = rows // LO
    inside = dot_binary(
        jnp.concatenate([hazard[...], square[...]], axis=0), triangle(LO, lambda a, b: a <= b)
    )
    totals = jnp.broadcast_to(inside[:, LO - 1 :], (2 * groups, 128))
    place = lax.rem(rank[...], rows)
    mask = one_hot(place // LO, groups, F32)
    placed = dot_binary(inside, one_hot(lax.rem(place, LO), LO))
    before = triangle(groups, lambda a, b: a > b)
    for first, out in ((0, cumulative), (groups, squares)):
        carried = binary_dot(before, totals[first : first + groups])[:, :1]
        out[...] = jnp.sum(mask * (placed[first : first + groups] + carried), axis=0, keepdims=True)


def hazards(hazard, square, rank, rows):
    row = jax.ShapeDtypeStruct((1, rows), F32)
    return pl.pallas_call(
        functools.partial(hazard_kernel, rows),
        in_specs=[VMEM] * 3,
        out_shape=[row, row],
        out_specs=[VMEM] * 2,
        compiler_params=pltpu.CompilerParams(**PARAMS),
        cost_estimate=pl.CostEstimate(flops=rows * LO * 200, bytes_accessed=rows * 64, transcendentals=0),
        name="hazards",
    )(hazard, square, rank)


def range_kernel(bit, count, *refs):
    total, other, later = refs[:3]
    total_out, later_out = refs[3 + count :]
    is_later = (lax.axis_index("ex") & bit) == 0
    later_out[...] = later[...] + jnp.where(is_later, other[...], 0.0)
    total_out[...] = total[...] + other[...]


def ranges(bit, total, other, later, waited):
    return pl.pallas_call(
        functools.partial(range_kernel, bit, len(waited)),
        in_specs=[VMEM] * 3 + [pl.BlockSpec(memory_space=pl.ANY)] * len(waited),
        out_shape=[jax.ShapeDtypeStruct(total.shape, F32)] * 2,
        out_specs=[VMEM] * 2,
        compiler_params=pltpu.CompilerParams(**PARAMS),
        name="ranges",
    )(total, other, later, *waited)


def order_kernel(start, parts, own, other, *refs):
    messages, (risk, rank, table) = refs[:parts], refs[parts : parts + 3]
    tangent_out, ordered_out, plain, lhs = refs[-4:]
    kf, width = tangent_out.shape
    rows = own.shape[1]
    groups = rows // LO
    span = min(SPAN, width)
    folded = jnp.zeros((kf, 128), F32)
    powers = [jnp.exp2(from_short(part[:, part.shape[1] - 128 :])) for part in messages]
    for i in range(width // span):
        at = slice(start + i * span, start + (i + 1) * span)
        here = slice(i * span, (i + 1) * span)
        tangent = own[:, at] + other[:, at]
        for part, power in zip(messages, powers):
            tangent = tangent + from_short(part[:, here]) * power[:, i : i + 1]
        tangent_out[:, here] = tangent
        weighted = tangent * risk[:, at]
        folded = folded + sum(weighted[:, j : j + 128] for j in range(0, span, 128))
        high, low = split_two(weighted)
        high, low = high.astype(BF16), low.astype(BF16)
        group = jnp.broadcast_to(lax.rem(rank[:, at], rows) // LO, (kf, span))
        for g in range(groups):
            mask = jnp.where(group == g, 1.0, 0.0).astype(BF16)
            lhs[2 * g * kf : (2 * g + 1) * kf, here] = high * mask
            lhs[(2 * g + 1) * kf : (2 * g + 2) * kf, here] = low * mask
    plain[...] = folded
    ordered = jnp.dot(lhs[...], table[start : start + width], preferred_element_type=F32)
    for g in range(groups):
        ordered_out[g * kf : (g + 1) * kf] = (
            ordered[2 * g * kf : (2 * g + 1) * kf] + ordered[(2 * g + 1) * kf : (2 * g + 2) * kf]
        )


def ordered_values(own, other, messages, risk, rank, table, start, width):
    kf, rows = own.shape
    groups = rows // LO
    return pl.pallas_call(
        functools.partial(order_kernel, start, len(messages)),
        in_specs=[VMEM] * (len(messages) + 5),
        out_shape=[
            jax.ShapeDtypeStruct((kf, width), F32),
            jax.ShapeDtypeStruct((groups * kf, LO), F32),
            jax.ShapeDtypeStruct((kf, 128), F32),
        ],
        out_specs=[VMEM] * 3,
        scratch_shapes=[pltpu.VMEM((groups * 2 * kf, width), BF16)],
        compiler_params=pltpu.CompilerParams(**PARAMS),
        cost_estimate=pl.CostEstimate(
            flops=2 * width * LO * groups * 2 * kf, bytes_accessed=width * kf * 24, transcendentals=0
        ),
        name="ordered_values",
    )(own, other, *messages, risk, rank, table)


def suffix_kernel(kf, one, two, sums):
    groups = sums.shape[0] // kf
    inside = dot_binary(one[...] + two[...], triangle(LO, lambda a, b: a >= b))
    carried = jnp.zeros((kf, 1), F32)
    for g in reversed(range(groups)):
        rows_of = slice(g * kf, (g + 1) * kf)
        sums[rows_of] = inside[rows_of] + carried
        carried = carried + inside[rows_of, :1]


def suffix_sums(one, two, kf):
    return pl.pallas_call(
        functools.partial(suffix_kernel, kf),
        in_specs=[VMEM] * 2,
        out_shape=jax.ShapeDtypeStruct(one.shape, F32),
        out_specs=VMEM,
        compiler_params=pltpu.CompilerParams(**PARAMS),
        name="suffix_sums",
    )(one, two)


def prefix_kernel(sums, squares, rank, out):
    kf, rows = out.shape
    groups = squares.shape[0]
    chunk = min(512, rows)
    hazard = [sums[g * kf : (g + 1) * kf] * squares[g : g + 1, :] for g in range(groups)]
    inside = dot_binary(jnp.concatenate(hazard, axis=0), triangle(LO, lambda a, b: a <= b))
    carried = jnp.zeros((kf, 1), F32)
    summed = [None] * groups
    for g in range(groups):
        rows_of = slice(g * kf, (g + 1) * kf)
        summed[g] = inside[rows_of] + carried
        carried = carried + inside[rows_of, LO - 1 :]
    both = stacked(split_two(jnp.concatenate(summed, axis=0)))
    for start in range(0, rows, chunk):
        at = slice(start, start + chunk)
        place = lax.rem(rank[:, at], rows)
        group = place // LO
        spread = one_hot(lax.rem(place, LO), LO)
        placed = unstacked(jnp.dot(both, spread, preferred_element_type=F32), 2)
        picked = jnp.zeros((kf, chunk), F32)
        for g in range(groups):
            picked = picked + jnp.where(group == g, placed[g * kf : (g + 1) * kf], 0.0)
        out[:, at] = picked


def prefix_sums(sums, squares, rank, kf):
    rows = rank.shape[1]
    return pl.pallas_call(
        prefix_kernel,
        in_specs=[VMEM] * 3,
        out_shape=jax.ShapeDtypeStruct((kf, rows), F32),
        out_specs=VMEM,
        compiler_params=pltpu.CompilerParams(**PARAMS),
        cost_estimate=pl.CostEstimate(
            flops=4 * rows * LO * (rows // LO) * kf, bytes_accessed=rows * kf * 24, transcendentals=0
        ),
        name="prefix_sums",
    )(sums, squares, rank)


def weight_kernel(ex, *refs):
    messages, (first, rest, local, risk, cumulative, squares) = refs[:ex], refs[ex : ex + 6]
    weighted, placed = refs[ex + 6 :]
    kf = first.shape[0]
    me = lax.axis_index("ex")
    for i in range(ex):
        placed[me ^ i] = messages[i][...]
    later = jnp.zeros((kf, 128), F32)
    own_later, before = later, later
    hazard_before = jnp.zeros((1, 128), F32)
    for b in reversed(range(ex)):
        plain, scaled, square = placed[b, :kf], placed[b, kf : 2 * kf], placed[b, 2 * kf + 1 : 2 * kf + 2]
        own_later = own_later + jnp.where(b > me, plain, 0.0)
        before = before + jnp.where(b < me, scaled + square * later, 0.0)
        hazard_before = hazard_before + jnp.where(b < me, placed[b, 2 * kf : 2 * kf + 1], 0.0)
        later = later + plain
    own_later = jnp.sum(own_later, axis=1, keepdims=True)
    before = jnp.sum(before, axis=1, keepdims=True)
    hazard_before = hazard_before[:, :1]
    for start, part in ((0, first), (first.shape[1], rest)):
        at = slice(start, start + part.shape[1])
        value = part[...] * (cumulative[:, at] + hazard_before) - (
            local[:, at] + squares[:, at] * own_later + before
        )
        weighted[:, at] = (risk[:, at] * value).astype(BF16)


def weights(messages, first, rest, local, risk, cumulative, squares):
    ex = len(messages)
    return pl.pallas_call(
        functools.partial(weight_kernel, ex),
        in_specs=[VMEM] * (ex + 6),
        out_shape=jax.ShapeDtypeStruct(local.shape, BF16),
        out_specs=VMEM,
        scratch_shapes=[pltpu.VMEM((ex,) + messages[0].shape, F32)],
        compiler_params=pltpu.CompilerParams(**PARAMS),
        name="weights",
    )(*messages, first, rest, local, risk, cumulative, squares)


def encode(values, message):
    columns = len(values)
    powers = []
    for i, value in enumerate(values):
        power = power_of(jnp.max(jnp.abs(value), axis=0, keepdims=True))
        scaled = to_short(value * jnp.exp2(-power))
        for j in range(value.shape[0] // 16):
            message[j * columns + i] = scaled[j * 16 : (j + 1) * 16]
        powers.append(power)
    powers.append(jnp.zeros((16 - columns, 128), F32))
    message[message.shape[0] - 1] = to_short(jnp.concatenate(powers, axis=0))


def decode(message, columns):
    last = message.shape[0] - 1
    scales = jnp.exp2(from_short(message[last]))
    values = []
    for i in range(columns):
        value = jnp.concatenate([from_short(message[j]) for j in range(i, last, columns)], axis=0)
        values.append(value * scales[i : i + 1])
    return values


def decode_sum(mine, other, columns):
    return [one + two for one, two in zip(decode(mine, columns), decode(other, columns))]


def gradient_kernel(parts, kf, *refs):
    pieces, dosages, out, weighted = refs[:parts], refs[parts], refs[parts + 1], refs[parts + 2]
    for i in range(parts):
        weighted[i * kf : (i + 1) * kf, :] = pieces[i][...]
    total = jnp.dot(weighted[...], dosages[...], preferred_element_type=F32)
    encode([total[:, at : at + 128] for at in range(0, total.shape[1], 128)], out)


def gradients(pieces, dosages):
    parts = len(pieces)
    kf, persons = pieces[0].shape
    k, variants = kf * parts, dosages.shape[1]
    return pl.pallas_call(
        functools.partial(gradient_kernel, parts, kf),
        in_specs=[VMEM] * (parts + 1),
        out_shape=jax.ShapeDtypeStruct((k * variants // 2048 + 1, 16, 128), jnp.int16),
        out_specs=VMEM,
        scratch_shapes=[pltpu.VMEM((k, persons), BF16)],
        compiler_params=pltpu.CompilerParams(**PARAMS),
        cost_estimate=pl.CostEstimate(
            flops=2 * persons * variants * k, bytes_accessed=persons * (variants * 2 + k * 2), transcendentals=0
        ),
        name="gradients",
    )(*pieces, dosages)


def merge_kernel(columns, mine, other, out):
    encode(decode_sum(mine, other, columns), out)


def merge(mine, other, variants):
    return pl.pallas_call(
        functools.partial(merge_kernel, variants // 128),
        in_specs=[VMEM] * 2,
        out_shape=jax.ShapeDtypeStruct(mine.shape, jnp.int16),
        out_specs=VMEM,
        compiler_params=pltpu.CompilerParams(**PARAMS),
        name="merge",
    )(mine, other)


def add_kernel(mine, other, out):
    for i, value in enumerate(decode_sum(mine, other, out.shape[1] // 128)):
        out[:, i * 128 : (i + 1) * 128] = value


def add(mine, other, variants):
    return pl.pallas_call(
        add_kernel,
        in_specs=[VMEM] * 2,
        out_shape=jax.ShapeDtypeStruct(((mine.shape[0] - 1) * 2048 // variants, variants), F32),
        out_specs=VMEM,
        compiler_params=pltpu.CompilerParams(**PARAMS),
        name="add",
    )(mine, other)


def finish_kernel(feat, kf, first, mine, other, count, out, placed, total, sems):
    me = lax.axis_index("feat")
    variants = out.shape[0]
    scale = count[1:2, 0:1]
    for q in range(feat // 2):
        placed[me ^ (2 * q)] = first[q * kf : (q + 1) * kf]
    for i, value in enumerate(decode_sum(mine, other, variants // 128)):
        for q in range(feat // 2):
            placed[me ^ (2 * q + 1), :, i * 128 : (i + 1) * 128] = value[q * kf : (q + 1) * kf]
    copies = []
    for i in range(variants // 128):
        at = slice(i * 128, (i + 1) * 128)
        total[at] = placed[:, :, at].reshape(feat * kf, 128).T / scale
        copies.append(
            pltpu.make_async_copy(
                total.at[pl.ds(i * 128, 128)], out.at[pl.ds(i * 128, 128)], sems.at[i]
            )
        )
        copies[i].start()
    for copy in copies:
        copy.wait()


def finish(first, mine, other, count, feat):
    k, variants = 2 * first.shape[0], first.shape[1]
    kf = k // feat
    return pl.pallas_call(
        functools.partial(finish_kernel, feat, kf),
        in_specs=[VMEM] * 4,
        out_shape=jax.ShapeDtypeStruct((variants, k), F32),
        out_specs=HBM,
        scratch_shapes=[
            pltpu.VMEM((feat, kf, variants), F32),
            pltpu.VMEM((variants, k), F32),
            pltpu.SemaphoreType.DMA((variants // 128,)),
        ],
        compiler_params=pltpu.CompilerParams(**PARAMS),
        name="finish",
    )(first, mine, other, count)


def local(dosages, coefficients, directions, event_rank, events):
    feat, ex = lax.axis_size("feat"), lax.axis_size("ex")
    rows = dosages.shape[0]
    variants, k = directions.shape
    each = k // feat
    padded = -(-each // 16) * 16
    if padded != each:
        directions = jnp.pad(directions.reshape(variants, feat, each), ((0, 0), (0, 0), (0, padded - each)))
        directions = directions.reshape(variants, feat * padded)
    rank, event_row = event_rank[None], events[None]

    linear, keep, send = products(dosages, coefficients, directions, feat)
    order = list(reversed(range(1, feat // 2)))
    received = {q: swap(send[q], "feat", 1) for q in order + [0]}
    table = tables(rank, linear, rows)
    paired = pair(linear, received[order[0]], table)
    middle = min(3 * SPAN, rows // 2)
    firsts = [
        swap(join(keep[q], received[q], 0, middle, paired, []), "feat", 2 * q) for q in order
    ]
    rests = [
        swap(join(keep[q], received[q], middle, rows - middle, paired, [received[0]]), "feat", 2 * q)
        for q in order
    ]

    risk, total = risks(paired, firsts, event_row, rows)
    sums, ordered_events = risk_sums(risk, rank, event_row, table, rows)
    later = jnp.zeros_like(total)
    bit = 1
    while bit < ex:
        total, later = ranges(bit, total, swap(total, "ex", bit), later, rests + [sums] if bit == 1 else [])
        bit *= 2
    tangent, one, plain = ordered_values(keep[0], received[0], firsts, risk, rank, table, 0, middle)
    more_tangent, two, more = ordered_values(
        keep[0], received[0], rests, risk, rank, table, middle, rows - middle
    )
    later_sums = suffix_sums(one, two, padded)
    hazard, ordered_squares, message = shares(later, sums, ordered_events, plain, more, later_sums)
    messages = [message] + [swap(message, "ex", i) for i in range(1, ex)]
    cumulative, squares = hazards(hazard, ordered_squares, rank, rows)
    summed = prefix_sums(later_sums, ordered_squares, rank, padded)
    own = weights(messages, tangent, more_tangent, summed, risk, cumulative, squares)

    chips = {0: own}
    for q in range(1, feat // 2):
        chips[q] = swap(own, "feat", 2 * q)
    near = [chips[q] for q in range(feat // 2)]
    far = [swap(chips[q], "feat", 1) for q in range(feat // 2)]
    partial_sums = [gradients(pieces, dosages) for pieces in (near, far)]
    bit = 1
    while 2 * bit < ex:
        received = [swap(message, "ex", bit) for message in partial_sums]
        partial_sums = [merge(mine, other, variants) for mine, other in zip(partial_sums, received)]
        bit *= 2
    received = [swap(message, "ex", bit) for message in partial_sums]
    first = add(partial_sums[0], received[0], variants)
    result = finish(first, partial_sums[1], received[1], total, feat)
    if padded != each:
        result = result.reshape(variants, feat, padded)[:, :, :each].reshape(variants, k)
    return result


def solution(mesh):
    placed = (P("ex", "feat"), P("feat"), P("feat", None), P("ex"), P("ex"))
    return jax.shard_map(
        local, mesh=mesh, in_specs=placed, out_specs=P("feat", None), check_vma=False
    )
```

```python
import functools

import jax
import jax.numpy as jnp
from jax import lax
from jax.experimental import pallas as pl
from jax.experimental.pallas import tpu as pltpu
from jax.sharding import PartitionSpec as P

F32 = jnp.float32
BF16 = jnp.bfloat16
LO = 256
NT = (((1,), (1,)), ((), ()))
SPAN = 512
VMEM = pl.BlockSpec(memory_space=pltpu.VMEM)
HBM = pl.BlockSpec(memory_space=pltpu.HBM)
PARAMS = dict(vmem_limit_bytes=24 * 1024 * 1024)


def swap(x, axis, i):
    count = lax.axis_size(axis)
    return lax.ppermute(x, axis, [(s, s ^ i) for s in range(count)])


def split_two(x):
    high = x.astype(BF16).astype(F32)
    return high, x - high


def split_three(x):
    first, rest = split_two(x)
    second, third = split_two(rest)
    return first, second, third


def one_hot(values, count, kind=BF16):
    shape = (count, values.shape[1])
    return jnp.where(lax.broadcasted_iota(jnp.int32, shape, 0) == values, 1.0, 0.0).astype(kind)


def triangle(n, keep):
    first = lax.broadcasted_iota(jnp.int32, (n, n), 0)
    second = lax.broadcasted_iota(jnp.int32, (n, n), 1)
    return jnp.where(keep(first, second), 1.0, 0.0)


def stacked(parts):
    return jnp.concatenate(parts, axis=0).astype(BF16)


def unstacked(values, count):
    height = values.shape[0] // count
    return sum(values[i * height : (i + 1) * height] for i in range(count))


def dot_binary(a, b):
    parts = jnp.dot(stacked(split_three(a)), b.astype(BF16), preferred_element_type=F32)
    return unstacked(parts, 3)


def binary_dot(a, b):
    a = a.astype(BF16)
    total = None
    for part in split_three(b):
        term = jnp.dot(a, part.astype(BF16), preferred_element_type=F32)
        total = term if total is None else total + term
    return total


def product_kernel(feat, kf, sizes, directions, coefficients, dosages, *refs):
    linear, keep, send = refs[0], refs[1 : 1 + feat // 2], refs[1 + feat // 2 : 1 + feat]
    table, own_directions, own_coefficients, lhs, turned, sems = refs[1 + feat :]
    me = lax.axis_index("feat")
    width = feat * kf
    persons, variants = table.shape
    steps = len(sizes)
    starts = [sum(sizes[:i]) for i in range(steps)]
    small = [
        pltpu.make_async_copy(directions, own_directions, sems.at[steps]),
        pltpu.make_async_copy(coefficients, own_coefficients, sems.at[steps + 1]),
    ]
    large = [
        pltpu.make_async_copy(
            dosages.at[pl.ds(first, chunk)], table.at[pl.ds(first, chunk)], sems.at[i]
        )
        for i, (first, chunk) in enumerate(zip(starts, sizes))
    ]
    for copy in small + large:
        copy.start()
    for copy in small:
        copy.wait()
    turned[...] = own_directions[...].astype(F32).T.reshape(turned.shape)
    for j in range(feat):
        lhs[j * kf : (j + 1) * kf] = turned[me ^ j].astype(BF16)
    lhs[width:] = jnp.broadcast_to(own_coefficients[...].astype(F32)[None, :], (16, variants)).astype(BF16)
    for copy, first, chunk in zip(large, starts, sizes):
        copy.wait()
        result = lax.dot_general(
            lhs[...], table[first : first + chunk], NT, preferred_element_type=F32
        )
        for j in range(feat):
            (send if j % 2 else keep)[j // 2][:, first : first + chunk] = result[j * kf : (j + 1) * kf]
        for start in range(0, chunk, LO):
            row = result[width : width + 1, start : start + LO]
            group = (first + start) // LO
            linear[group : group + 1, :] = row
            send[-1][group : group + 1, persons:] = row


def products(dosages, coefficients, directions, feat):
    persons, variants = dosages.shape
    k = directions.shape[1]
    kf = k // feat
    chunk = min(1024, persons)
    sizes = [chunk] * (persons // chunk - 1) + [chunk // 2] * 2
    piece = jax.ShapeDtypeStruct((kf, persons), F32)
    first = jax.ShapeDtypeStruct((kf, persons + LO), F32)
    out = pl.pallas_call(
        functools.partial(product_kernel, feat, kf, tuple(sizes)),
        in_specs=[HBM, HBM, HBM],
        out_shape=[jax.ShapeDtypeStruct((kf, LO), F32)]
        + [piece] * (feat - 1)
        + [first],
        out_specs=[VMEM] * (feat + 1),
        scratch_shapes=[
            pltpu.VMEM((persons, variants), BF16),
            pltpu.VMEM((variants, k), BF16),
            pltpu.VMEM((variants,), BF16),
            pltpu.VMEM((k + 16, variants), BF16),
            pltpu.VMEM((feat, kf, variants), F32),
            pltpu.SemaphoreType.DMA((len(sizes) + 2,)),
        ],
        compiler_params=pltpu.CompilerParams(**PARAMS),
        cost_estimate=pl.CostEstimate(
            flops=2 * persons * variants * k, bytes_accessed=persons * (variants * 2 + k * 4), transcendentals=0
        ),
        name="products",
    )(*[pltpu.with_memory_space_constraint(x, pltpu.HBM) for x in (directions, coefficients, dosages)])
    return out[0], out[1 : 1 + feat // 2], out[1 + feat // 2 :]


def power_of(largest):
    return jnp.ceil(jnp.log2(jnp.maximum(largest, 1e-30))) - 14.0


def to_short(values):
    return jnp.round(values).astype(jnp.int32).astype(jnp.int16)


def from_short(values):
    return values.astype(jnp.int32).astype(F32)


def pair_kernel(linear, received, waited, out):
    out[...] = linear[...] + received[:, received.shape[1] - LO :]


def pair(linear, received, waited):
    return pl.pallas_call(
        pair_kernel,
        in_specs=[VMEM] * 2 + [pl.BlockSpec(memory_space=pl.ANY)],
        out_shape=jax.ShapeDtypeStruct(linear.shape, F32),
        out_specs=VMEM,
        compiler_params=pltpu.CompilerParams(**PARAMS),
        name="pair",
    )(linear, received, waited)


def join_kernel(start, width, mine, other, *refs):
    linear, out = refs[0], refs[-1]
    kf = mine.shape[0]
    span = min(SPAN, width)
    lane = lax.broadcasted_iota(jnp.int32, (kf, 128), 1)
    powers = jnp.zeros((kf, 128), F32)
    for i in range(width // span):
        at = slice(start + i * span, start + (i + 1) * span)
        total = mine[:, at] + other[:, at]
        power = power_of(jnp.max(jnp.abs(total), axis=1, keepdims=True))
        out[:, i * span : (i + 1) * span] = to_short(total * jnp.exp2(-power))
        powers = jnp.where(lane == i, power, powers)
    if start == 0:
        power = power_of(jnp.max(jnp.abs(linear[...]), axis=1, keepdims=True))
        scaled = linear[...] * jnp.exp2(-power)
        whole = jnp.round(scaled)
        out[:, width : width + LO] = to_short(whole)
        out[:, width + LO : width + 2 * LO] = to_short((scaled - whole) * 32768.0)
        powers = jnp.where(lane == 127, power, powers)
    out[:, out.shape[1] - 128 :] = to_short(powers)


def join(keep, received, start, width, linear, waited):
    kf, rows = keep.shape
    extra = 2 * LO if start == 0 else 0
    return pl.pallas_call(
        functools.partial(join_kernel, start, width),
        in_specs=[VMEM] * 3 + [pl.BlockSpec(memory_space=pl.ANY)] * len(waited),
        out_shape=jax.ShapeDtypeStruct((kf, width + extra + 128), jnp.int16),
        out_specs=VMEM,
        compiler_params=pltpu.CompilerParams(**PARAMS),
        name="join",
    )(keep, received, linear, *waited)


def table_kernel(rows, rank, waited, table):
    chunk = min(512, rows)
    lane = lax.broadcasted_iota(jnp.int32, (chunk, 128), 1)
    for start in range(0, rows, chunk):
        at = slice(start, start + chunk)
        inner = lax.rem(rank[:, at], LO)
        column = jnp.broadcast_to(inner.astype(F32), (128, chunk)).T.astype(jnp.int32)
        for first in range(0, LO, 128):
            table[at, first : first + 128] = jnp.where(column == lane + first, 1.0, 0.0).astype(BF16)


def tables(rank, waited, rows):
    return pl.pallas_call(
        functools.partial(table_kernel, rows),
        in_specs=[VMEM, pl.BlockSpec(memory_space=pl.ANY)],
        out_shape=jax.ShapeDtypeStruct((rows, LO), BF16),
        out_specs=VMEM,
        compiler_params=pltpu.CompilerParams(**PARAMS),
        cost_estimate=pl.CostEstimate(flops=rows * LO * 8, bytes_accessed=rows * LO * 2, transcendentals=0),
        name="tables",
    )(rank, waited)


def risk_kernel(rows, parts, linear, *refs):
    messages, events = refs[:parts], refs[parts]
    risk_out, message = refs[parts + 1 :]
    groups = rows // LO
    total = linear[...]
    for part in messages:
        end = part.shape[1] - 128
        power = from_short(part[:, end:])[:, 127:]
        high, low = from_short(part[:, end - 2 * LO : end - LO]), from_short(part[:, end - LO : end])
        total = total + (high + low * (1.0 / 32768.0)) * jnp.exp2(power)
    risk = jnp.exp(total[:groups])
    for g in range(groups):
        risk_out[:, g * LO : (g + 1) * LO] = risk[g : g + 1]
    everything = jnp.sum(jnp.sum(risk, axis=0, keepdims=True), axis=1, keepdims=True)
    count = jnp.sum(events[...].astype(F32), axis=1, keepdims=True)
    totals = [jnp.broadcast_to(value, (1, 128)) for value in (everything, count)]
    message[...] = jnp.concatenate(totals + [jnp.zeros((6, 128), F32)], axis=0)


def risks(linear, messages, events, rows):
    return pl.pallas_call(
        functools.partial(risk_kernel, rows, len(messages)),
        in_specs=[VMEM] * (len(messages) + 2),
        out_shape=[jax.ShapeDtypeStruct((1, rows), F32), jax.ShapeDtypeStruct((8, 128), F32)],
        out_specs=[VMEM] * 2,
        compiler_params=pltpu.CompilerParams(**PARAMS),
        cost_estimate=pl.CostEstimate(flops=rows * 64, bytes_accessed=rows * 64, transcendentals=rows),
        name="risks",
    )(linear, *messages, events)


def risk_sum_kernel(rows, risk, rank, events, table, sums_out, events_out):
    groups = rows // LO
    mask = one_hot(lax.rem(rank[...], rows) // LO, groups, F32)
    pieces = [mask * part for part in split_three(risk[...])] + [mask * events[...].astype(F32)]
    lhs = jnp.concatenate(pieces, axis=0).astype(BF16)
    sorted_all = jnp.dot(lhs, table[...], preferred_element_type=F32)
    ordered = sorted_all[:groups] + sorted_all[groups : 2 * groups] + sorted_all[2 * groups : 3 * groups]
    inside = dot_binary(ordered, triangle(LO, lambda a, b: a >= b))
    totals = jnp.broadcast_to(inside[:, :1], inside.shape)
    carried = binary_dot(triangle(groups, lambda a, b: a < b), totals)
    sums_out[...] = inside + carried
    events_out[...] = sorted_all[3 * groups :]


def risk_sums(risk, rank, events, table, rows):
    flat = jax.ShapeDtypeStruct((rows // LO, LO), F32)
    return pl.pallas_call(
        functools.partial(risk_sum_kernel, rows),
        in_specs=[VMEM] * 4,
        out_shape=[flat, flat],
        out_specs=[VMEM] * 2,
        compiler_params=pltpu.CompilerParams(**PARAMS),
        cost_estimate=pl.CostEstimate(flops=rows * LO * 128, bytes_accessed=rows * 64, transcendentals=0),
        name="risk_sums",
    )(risk, rank, events, table)


def share_kernel(later, sums, events, plain, more, ordered, hazard_out, squares, message):
    kf = plain.shape[0]
    groups = sums.shape[0]
    risk_sum = sums[...] + later[0:1, 0:1]
    hazard = events[...] / risk_sum
    square = events[...] / (risk_sum * risk_sum)
    hazard_out[...] = hazard
    squares[...] = square
    scaled = jnp.zeros((kf, LO), F32)
    for g in range(groups):
        scaled = scaled + ordered[g * kf : (g + 1) * kf] * square[g : g + 1]
    message[:kf] = plain[...] + more[...]
    message[kf : 2 * kf] = sum(scaled[:, start : start + 128] for start in range(0, LO, 128))
    totals = [jnp.sum(jnp.sum(v, axis=0, keepdims=True), axis=1, keepdims=True) for v in (hazard, square)]
    rows = [jnp.broadcast_to(v, (1, 128)) for v in totals]
    message[2 * kf :] = jnp.concatenate(rows + [jnp.zeros((6, 128), F32)], axis=0)


def shares(later, sums, events, plain, more, ordered):
    flat = jax.ShapeDtypeStruct(sums.shape, F32)
    return pl.pallas_call(
        share_kernel,
        in_specs=[VMEM] * 6,
        out_shape=[flat, flat, jax.ShapeDtypeStruct((2 * plain.shape[0] + 8, 128), F32)],
        out_specs=[VMEM] * 3,
        compiler_params=pltpu.CompilerParams(**PARAMS),
        name="shares",
    )(later, sums, events, plain, more, ordered)


def hazard_kernel(rows, hazard, square, rank, cumulative, squares):
    groups = rows // LO
    inside = dot_binary(
        jnp.concatenate([hazard[...], square[...]], axis=0), triangle(LO, lambda a, b: a <= b)
    )
    totals = jnp.broadcast_to(inside[:, LO - 1 :], (2 * groups, 128))
    place = lax.rem(rank[...], rows)
    mask = one_hot(place // LO, groups, F32)
    placed = dot_binary(inside, one_hot(lax.rem(place, LO), LO))
    before = triangle(groups, lambda a, b: a > b)
    for first, out in ((0, cumulative), (groups, squares)):
        carried = binary_dot(before, totals[first : first + groups])[:, :1]
        out[...] = jnp.sum(mask * (placed[first : first + groups] + carried), axis=0, keepdims=True)


def hazards(hazard, square, rank, rows):
    row = jax.ShapeDtypeStruct((1, rows), F32)
    return pl.pallas_call(
        functools.partial(hazard_kernel, rows),
        in_specs=[VMEM] * 3,
        out_shape=[row, row],
        out_specs=[VMEM] * 2,
        compiler_params=pltpu.CompilerParams(**PARAMS),
        cost_estimate=pl.CostEstimate(flops=rows * LO * 200, bytes_accessed=rows * 64, transcendentals=0),
        name="hazards",
    )(hazard, square, rank)


def range_kernel(bit, count, *refs):
    total, other, later = refs[:3]
    total_out, later_out = refs[3 + count :]
    is_later = (lax.axis_index("ex") & bit) == 0
    later_out[...] = later[...] + jnp.where(is_later, other[...], 0.0)
    total_out[...] = total[...] + other[...]


def ranges(bit, total, other, later, waited):
    return pl.pallas_call(
        functools.partial(range_kernel, bit, len(waited)),
        in_specs=[VMEM] * 3 + [pl.BlockSpec(memory_space=pl.ANY)] * len(waited),
        out_shape=[jax.ShapeDtypeStruct(total.shape, F32)] * 2,
        out_specs=[VMEM] * 2,
        compiler_params=pltpu.CompilerParams(**PARAMS),
        name="ranges",
    )(total, other, later, *waited)


def order_kernel(start, parts, own, other, *refs):
    messages, (risk, rank, table) = refs[:parts], refs[parts : parts + 3]
    tangent_out, ordered_out, plain, lhs = refs[-4:]
    kf, width = tangent_out.shape
    rows = own.shape[1]
    groups = rows // LO
    span = min(SPAN, width)
    folded = jnp.zeros((kf, 128), F32)
    powers = [jnp.exp2(from_short(part[:, part.shape[1] - 128 :])) for part in messages]
    for i in range(width // span):
        at = slice(start + i * span, start + (i + 1) * span)
        here = slice(i * span, (i + 1) * span)
        tangent = own[:, at] + other[:, at]
        for part, power in zip(messages, powers):
            tangent = tangent + from_short(part[:, here]) * power[:, i : i + 1]
        tangent_out[:, here] = tangent
        weighted = tangent * risk[:, at]
        folded = folded + sum(weighted[:, j : j + 128] for j in range(0, span, 128))
        high, low = split_two(weighted)
        high, low = high.astype(BF16), low.astype(BF16)
        group = jnp.broadcast_to(lax.rem(rank[:, at], rows) // LO, (kf, span))
        for g in range(groups):
            mask = jnp.where(group == g, 1.0, 0.0).astype(BF16)
            lhs[2 * g * kf : (2 * g + 1) * kf, here] = high * mask
            lhs[(2 * g + 1) * kf : (2 * g + 2) * kf, here] = low * mask
    plain[...] = folded
    ordered = jnp.dot(lhs[...], table[start : start + width], preferred_element_type=F32)
    for g in range(groups):
        ordered_out[g * kf : (g + 1) * kf] = (
            ordered[2 * g * kf : (2 * g + 1) * kf] + ordered[(2 * g + 1) * kf : (2 * g + 2) * kf]
        )


def ordered_values(own, other, messages, risk, rank, table, start, width):
    kf, rows = own.shape
    groups = rows // LO
    return pl.pallas_call(
        functools.partial(order_kernel, start, len(messages)),
        in_specs=[VMEM] * (len(messages) + 5),
        out_shape=[
            jax.ShapeDtypeStruct((kf, width), F32),
            jax.ShapeDtypeStruct((groups * kf, LO), F32),
            jax.ShapeDtypeStruct((kf, 128), F32),
        ],
        out_specs=[VMEM] * 3,
        scratch_shapes=[pltpu.VMEM((groups * 2 * kf, width), BF16)],
        compiler_params=pltpu.CompilerParams(**PARAMS),
        cost_estimate=pl.CostEstimate(
            flops=2 * width * LO * groups * 2 * kf, bytes_accessed=width * kf * 24, transcendentals=0
        ),
        name="ordered_values",
    )(own, other, *messages, risk, rank, table)


def suffix_kernel(kf, one, two, sums):
    groups = sums.shape[0] // kf
    inside = dot_binary(one[...] + two[...], triangle(LO, lambda a, b: a >= b))
    carried = jnp.zeros((kf, 1), F32)
    for g in reversed(range(groups)):
        rows_of = slice(g * kf, (g + 1) * kf)
        sums[rows_of] = inside[rows_of] + carried
        carried = carried + inside[rows_of, :1]


def suffix_sums(one, two, kf):
    return pl.pallas_call(
        functools.partial(suffix_kernel, kf),
        in_specs=[VMEM] * 2,
        out_shape=jax.ShapeDtypeStruct(one.shape, F32),
        out_specs=VMEM,
        compiler_params=pltpu.CompilerParams(**PARAMS),
        name="suffix_sums",
    )(one, two)


def prefix_kernel(sums, squares, rank, out):
    kf, rows = out.shape
    groups = squares.shape[0]
    chunk = min(512, rows)
    hazard = [sums[g * kf : (g + 1) * kf] * squares[g : g + 1, :] for g in range(groups)]
    inside = dot_binary(jnp.concatenate(hazard, axis=0), triangle(LO, lambda a, b: a <= b))
    carried = jnp.zeros((kf, 1), F32)
    summed = [None] * groups
    for g in range(groups):
        rows_of = slice(g * kf, (g + 1) * kf)
        summed[g] = inside[rows_of] + carried
        carried = carried + inside[rows_of, LO - 1 :]
    both = stacked(split_two(jnp.concatenate(summed, axis=0)))
    for start in range(0, rows, chunk):
        at = slice(start, start + chunk)
        place = lax.rem(rank[:, at], rows)
        group = place // LO
        spread = one_hot(lax.rem(place, LO), LO)
        placed = unstacked(jnp.dot(both, spread, preferred_element_type=F32), 2)
        picked = jnp.zeros((kf, chunk), F32)
        for g in range(groups):
            picked = picked + jnp.where(group == g, placed[g * kf : (g + 1) * kf], 0.0)
        out[:, at] = picked


def prefix_sums(sums, squares, rank, kf):
    rows = rank.shape[1]
    return pl.pallas_call(
        prefix_kernel,
        in_specs=[VMEM] * 3,
        out_shape=jax.ShapeDtypeStruct((kf, rows), F32),
        out_specs=VMEM,
        compiler_params=pltpu.CompilerParams(**PARAMS),
        cost_estimate=pl.CostEstimate(
            flops=4 * rows * LO * (rows // LO) * kf, bytes_accessed=rows * kf * 24, transcendentals=0
        ),
        name="prefix_sums",
    )(sums, squares, rank)


def weight_kernel(places, *refs):
    ex = len(places)
    messages, (first, rest, local, risk, cumulative, squares) = refs[:ex], refs[ex : ex + 6]
    weighted, placed = refs[ex + 6 :]
    kf = first.shape[0]
    me = lax.axis_index("ex")
    for i, part in zip(places, messages):
        placed[me ^ i] = part[...]
    later = jnp.zeros((kf, 128), F32)
    own_later, before = later, later
    hazard_before = jnp.zeros((1, 128), F32)
    for b in reversed(range(ex)):
        plain, scaled, square = placed[b, :kf], placed[b, kf : 2 * kf], placed[b, 2 * kf + 1 : 2 * kf + 2]
        own_later = own_later + jnp.where(b > me, plain, 0.0)
        before = before + jnp.where(b < me, scaled + square * later, 0.0)
        hazard_before = hazard_before + jnp.where(b < me, placed[b, 2 * kf : 2 * kf + 1], 0.0)
        later = later + plain
    own_later = jnp.sum(own_later, axis=1, keepdims=True)
    before = jnp.sum(before, axis=1, keepdims=True)
    hazard_before = hazard_before[:, :1]
    for start, part in ((0, first), (first.shape[1], rest)):
        at = slice(start, start + part.shape[1])
        value = part[...] * (cumulative[:, at] + hazard_before) - (
            local[:, at] + squares[:, at] * own_later + before
        )
        weighted[:, at] = (risk[:, at] * value).astype(BF16)


def weights(places, messages, first, rest, local, risk, cumulative, squares):
    ex = len(messages)
    return pl.pallas_call(
        functools.partial(weight_kernel, tuple(places)),
        in_specs=[VMEM] * (ex + 6),
        out_shape=jax.ShapeDtypeStruct(local.shape, BF16),
        out_specs=VMEM,
        scratch_shapes=[pltpu.VMEM((ex,) + messages[0].shape, F32)],
        compiler_params=pltpu.CompilerParams(**PARAMS),
        name="weights",
    )(*messages, first, rest, local, risk, cumulative, squares)


def encode(values, message):
    columns = len(values)
    powers = []
    for i, value in enumerate(values):
        power = power_of(jnp.max(jnp.abs(value), axis=0, keepdims=True))
        scaled = to_short(value * jnp.exp2(-power))
        for j in range(value.shape[0] // 16):
            message[j * columns + i] = scaled[j * 16 : (j + 1) * 16]
        powers.append(power)
    powers.append(jnp.zeros((16 - columns, 128), F32))
    message[message.shape[0] - 1] = to_short(jnp.concatenate(powers, axis=0))


def decode(message, columns):
    last = message.shape[0] - 1
    scales = jnp.exp2(from_short(message[last]))
    values = []
    for i in range(columns):
        value = jnp.concatenate([from_short(message[j]) for j in range(i, last, columns)], axis=0)
        values.append(value * scales[i : i + 1])
    return values


def decode_sum(mine, other, columns):
    return [one + two for one, two in zip(decode(mine, columns), decode(other, columns))]


def gradient_kernel(parts, kf, *refs):
    pieces, dosages, out, weighted = refs[:parts], refs[parts], refs[parts + 1], refs[parts + 2]
    for i in range(parts):
        weighted[i * kf : (i + 1) * kf, :] = pieces[i][...]
    total = jnp.dot(weighted[...], dosages[...], preferred_element_type=F32)
    encode([total[:, at : at + 128] for at in range(0, total.shape[1], 128)], out)


def gradients(pieces, dosages):
    parts = len(pieces)
    kf, persons = pieces[0].shape
    k, variants = kf * parts, dosages.shape[1]
    return pl.pallas_call(
        functools.partial(gradient_kernel, parts, kf),
        in_specs=[VMEM] * (parts + 1),
        out_shape=jax.ShapeDtypeStruct((k * variants // 2048 + 1, 16, 128), jnp.int16),
        out_specs=VMEM,
        scratch_shapes=[pltpu.VMEM((k, persons), BF16)],
        compiler_params=pltpu.CompilerParams(**PARAMS),
        cost_estimate=pl.CostEstimate(
            flops=2 * persons * variants * k, bytes_accessed=persons * (variants * 2 + k * 2), transcendentals=0
        ),
        name="gradients",
    )(*pieces, dosages)


def merge_kernel(columns, mine, other, out):
    encode(decode_sum(mine, other, columns), out)


def merge(mine, other, variants):
    return pl.pallas_call(
        functools.partial(merge_kernel, variants // 128),
        in_specs=[VMEM] * 2,
        out_shape=jax.ShapeDtypeStruct(mine.shape, jnp.int16),
        out_specs=VMEM,
        compiler_params=pltpu.CompilerParams(**PARAMS),
        name="merge",
    )(mine, other)


def add_kernel(mine, other, out):
    for i, value in enumerate(decode_sum(mine, other, out.shape[1] // 128)):
        out[:, i * 128 : (i + 1) * 128] = value


def add(mine, other, variants):
    return pl.pallas_call(
        add_kernel,
        in_specs=[VMEM] * 2,
        out_shape=jax.ShapeDtypeStruct(((mine.shape[0] - 1) * 2048 // variants, variants), F32),
        out_specs=VMEM,
        compiler_params=pltpu.CompilerParams(**PARAMS),
        name="add",
    )(mine, other)


def finish_kernel(feat, kf, first, mine, other, count, out, placed, total, sems):
    me = lax.axis_index("feat")
    variants = out.shape[0]
    scale = count[1:2, 0:1]
    copies = []
    for i, value in enumerate(decode_sum(mine, other, variants // 128)):
        at = slice(i * 128, (i + 1) * 128)
        for q in range(feat // 2):
            rows = slice(q * kf, (q + 1) * kf)
            placed[i, me ^ (2 * q)] = first[rows, at]
            placed[i, me ^ (2 * q + 1)] = value[rows]
        total[at] = placed[i].reshape(feat * kf, 128).T / scale
        copies.append(
            pltpu.make_async_copy(
                total.at[pl.ds(i * 128, 128)], out.at[pl.ds(i * 128, 128)], sems.at[i]
            )
        )
        copies[i].start()
    for copy in copies:
        copy.wait()


def finish(first, mine, other, count, feat):
    k, variants = 2 * first.shape[0], first.shape[1]
    kf = k // feat
    return pl.pallas_call(
        functools.partial(finish_kernel, feat, kf),
        in_specs=[VMEM] * 4,
        out_shape=jax.ShapeDtypeStruct((variants, k), F32),
        out_specs=HBM,
        scratch_shapes=[
            pltpu.VMEM((variants // 128, feat, kf, 128), F32),
            pltpu.VMEM((variants, k), F32),
            pltpu.SemaphoreType.DMA((variants // 128,)),
        ],
        compiler_params=pltpu.CompilerParams(**PARAMS),
        name="finish",
    )(first, mine, other, count)


def local(dosages, coefficients, directions, event_rank, events):
    feat, ex = lax.axis_size("feat"), lax.axis_size("ex")
    rows = dosages.shape[0]
    variants, k = directions.shape
    each = k // feat
    padded = -(-each // 16) * 16
    if padded != each:
        directions = jnp.pad(directions.reshape(variants, feat, each), ((0, 0), (0, 0), (0, padded - each)))
        directions = directions.reshape(variants, feat * padded)
    rank, event_row = event_rank[None], events[None]

    linear, keep, send = products(dosages, coefficients, directions, feat)
    order = list(reversed(range(1, feat // 2)))
    received = {q: swap(send[q], "feat", 1) for q in order + [0]}
    table = tables(rank, linear, rows)
    paired = pair(linear, received[order[0]], table)
    middle = min(3 * SPAN, rows // 2)
    firsts = [
        swap(join(keep[q], received[q], 0, middle, paired, []), "feat", 2 * q) for q in order
    ]
    rests = [
        swap(join(keep[q], received[q], middle, rows - middle, paired, [received[0]]), "feat", 2 * q)
        for q in order
    ]

    risk, total = risks(paired, firsts, event_row, rows)
    sums, ordered_events = risk_sums(risk, rank, event_row, table, rows)
    later = jnp.zeros_like(total)
    bit = 1
    while bit < ex:
        total, later = ranges(bit, total, swap(total, "ex", bit), later, rests + [sums] if bit == 1 else [])
        bit *= 2
    tangent, one, plain = ordered_values(keep[0], received[0], firsts, risk, rank, table, 0, middle)
    more_tangent, two, more = ordered_values(
        keep[0], received[0], rests, risk, rank, table, middle, rows - middle
    )
    later_sums = suffix_sums(one, two, padded)
    hazard, ordered_squares, message = shares(later, sums, ordered_events, plain, more, later_sums)
    places = list(range(ex))
    places[-2:] = places[:-3:-1]
    messages = [swap(message, "ex", i) if i else message for i in places]
    cumulative, squares = hazards(hazard, ordered_squares, rank, rows)
    summed = prefix_sums(later_sums, ordered_squares, rank, padded)
    own = weights(places, messages, tangent, more_tangent, summed, risk, cumulative, squares)

    chips = {0: own}
    for q in range(1, feat // 2):
        chips[q] = swap(own, "feat", 2 * q)
    near = [chips[q] for q in range(feat // 2)]
    far = [swap(chips[q], "feat", 1) for q in range(feat // 2)]
    partial_sums = [gradients(pieces, dosages) for pieces in (near, far)]
    bit = 1
    while 2 * bit < ex:
        received = [swap(message, "ex", bit) for message in partial_sums]
        partial_sums = [merge(mine, other, variants) for mine, other in zip(partial_sums, received)]
        bit *= 2
    received = [swap(message, "ex", bit) for message in partial_sums]
    first = add(partial_sums[0], received[0], variants)
    result = finish(first, partial_sums[1], received[1], total, feat)
    if padded != each:
        result = result.reshape(variants, feat, padded)[:, :, :each].reshape(variants, k)
    return result


def solution(mesh):
    placed = (P("ex", "feat"), P("feat"), P("feat", None), P("ex"), P("ex"))
    return jax.shard_map(
        local, mesh=mesh, in_specs=placed, out_specs=P("feat", None), check_vma=False
    )
```

```python
import functools

import jax
import jax.numpy as jnp
from jax import lax
from jax.experimental import pallas as pl
from jax.experimental.pallas import tpu as pltpu
from jax.sharding import PartitionSpec as P

F32 = jnp.float32
BF16 = jnp.bfloat16
LO = 256
NT = (((1,), (1,)), ((), ()))
SPAN = 512
VMEM = pl.BlockSpec(memory_space=pltpu.VMEM)
HBM = pl.BlockSpec(memory_space=pltpu.HBM)
PARAMS = dict(vmem_limit_bytes=24 * 1024 * 1024)


def swap(x, axis, i):
    count = lax.axis_size(axis)
    return lax.ppermute(x, axis, [(s, s ^ i) for s in range(count)])


def split_two(x):
    high = x.astype(BF16).astype(F32)
    return high, x - high


def split_three(x):
    first, rest = split_two(x)
    second, third = split_two(rest)
    return first, second, third


def one_hot(values, count, kind=BF16):
    shape = (count, values.shape[1])
    return jnp.where(lax.broadcasted_iota(jnp.int32, shape, 0) == values, 1.0, 0.0).astype(kind)


def triangle(n, keep):
    first = lax.broadcasted_iota(jnp.int32, (n, n), 0)
    second = lax.broadcasted_iota(jnp.int32, (n, n), 1)
    return jnp.where(keep(first, second), 1.0, 0.0)


def stacked(parts):
    return jnp.concatenate(parts, axis=0).astype(BF16)


def unstacked(values, count):
    height = values.shape[0] // count
    return sum(values[i * height : (i + 1) * height] for i in range(count))


def dot_binary(a, b):
    parts = jnp.dot(stacked(split_three(a)), b.astype(BF16), preferred_element_type=F32)
    return unstacked(parts, 3)


def binary_dot(a, b):
    a = a.astype(BF16)
    total = None
    for part in split_three(b):
        term = jnp.dot(a, part.astype(BF16), preferred_element_type=F32)
        total = term if total is None else total + term
    return total


def product_kernel(feat, kf, sizes, directions, coefficients, dosages, *refs):
    linear, keep, send = refs[0], refs[1 : 1 + feat // 2], refs[1 + feat // 2 : 1 + feat]
    table, own_directions, own_coefficients, lhs, turned, sems = refs[1 + feat :]
    me = lax.axis_index("feat")
    width = feat * kf
    persons, variants = table.shape
    steps = len(sizes)
    starts = [sum(sizes[:i]) for i in range(steps)]
    small = [
        pltpu.make_async_copy(directions, own_directions, sems.at[steps]),
        pltpu.make_async_copy(coefficients, own_coefficients, sems.at[steps + 1]),
    ]
    large = [
        pltpu.make_async_copy(
            dosages.at[pl.ds(first, chunk)], table.at[pl.ds(first, chunk)], sems.at[i]
        )
        for i, (first, chunk) in enumerate(zip(starts, sizes))
    ]
    for copy in small + large:
        copy.start()
    for copy in small:
        copy.wait()
    turned[...] = own_directions[...].astype(F32).T.reshape(turned.shape)
    for j in range(feat):
        lhs[j * kf : (j + 1) * kf] = turned[me ^ j].astype(BF16)
    lhs[width:] = jnp.broadcast_to(own_coefficients[...].astype(F32)[None, :], (16, variants)).astype(BF16)
    for copy, first, chunk in zip(large, starts, sizes):
        copy.wait()
        result = lax.dot_general(
            lhs[...], table[first : first + chunk], NT, preferred_element_type=F32
        )
        for j in range(feat):
            (send if j % 2 else keep)[j // 2][:, first : first + chunk] = result[j * kf : (j + 1) * kf]
        for start in range(0, chunk, LO):
            row = result[width : width + 1, start : start + LO]
            group = (first + start) // LO
            linear[group : group + 1, :] = row
            send[-1][group : group + 1, persons:] = row


def products(dosages, coefficients, directions, feat):
    persons, variants = dosages.shape
    k = directions.shape[1]
    kf = k // feat
    chunk = min(1024, persons)
    sizes = [chunk] * (persons // chunk)
    piece = jax.ShapeDtypeStruct((kf, persons), F32)
    first = jax.ShapeDtypeStruct((kf, persons + LO), F32)
    out = pl.pallas_call(
        functools.partial(product_kernel, feat, kf, tuple(sizes)),
        in_specs=[HBM, HBM, HBM],
        out_shape=[jax.ShapeDtypeStruct((kf, LO), F32)]
        + [piece] * (feat - 1)
        + [first],
        out_specs=[VMEM] * (feat + 1),
        scratch_shapes=[
            pltpu.VMEM((persons, variants), BF16),
            pltpu.VMEM((variants, k), BF16),
            pltpu.VMEM((variants,), BF16),
            pltpu.VMEM((k + 16, variants), BF16),
            pltpu.VMEM((feat, kf, variants), F32),
            pltpu.SemaphoreType.DMA((len(sizes) + 2,)),
        ],
        compiler_params=pltpu.CompilerParams(**PARAMS),
        cost_estimate=pl.CostEstimate(
            flops=2 * persons * variants * k, bytes_accessed=persons * (variants * 2 + k * 4), transcendentals=0
        ),
        name="products",
    )(*[pltpu.with_memory_space_constraint(x, pltpu.HBM) for x in (directions, coefficients, dosages)])
    return out[0], out[1 : 1 + feat // 2], out[1 + feat // 2 :]


def power_of(largest):
    return jnp.ceil(jnp.log2(jnp.maximum(largest, 1e-30))) - 14.0


def to_short(values):
    return jnp.round(values).astype(jnp.int32).astype(jnp.int16)


def from_short(values):
    return values.astype(jnp.int32).astype(F32)


def pair_kernel(linear, received, waited, out):
    out[...] = linear[...] + received[:, received.shape[1] - LO :]


def pair(linear, received, waited):
    return pl.pallas_call(
        pair_kernel,
        in_specs=[VMEM] * 2 + [pl.BlockSpec(memory_space=pl.ANY)],
        out_shape=jax.ShapeDtypeStruct(linear.shape, F32),
        out_specs=VMEM,
        compiler_params=pltpu.CompilerParams(**PARAMS),
        name="pair",
    )(linear, received, waited)


def join_kernel(start, width, mine, other, *refs):
    linear, out = refs[0], refs[-1]
    kf = mine.shape[0]
    span = min(SPAN, width)
    lane = lax.broadcasted_iota(jnp.int32, (kf, 128), 1)
    powers = jnp.zeros((kf, 128), F32)
    for i in range(width // span):
        at = slice(start + i * span, start + (i + 1) * span)
        total = mine[:, at] + other[:, at]
        power = power_of(jnp.max(jnp.abs(total), axis=1, keepdims=True))
        out[:, i * span : (i + 1) * span] = to_short(total * jnp.exp2(-power))
        powers = jnp.where(lane == i, power, powers)
    if start == 0:
        power = power_of(jnp.max(jnp.abs(linear[...]), axis=1, keepdims=True))
        scaled = linear[...] * jnp.exp2(-power)
        whole = jnp.round(scaled)
        out[:, width : width + LO] = to_short(whole)
        out[:, width + LO : width + 2 * LO] = to_short((scaled - whole) * 32768.0)
        powers = jnp.where(lane == 127, power, powers)
    out[:, out.shape[1] - 128 :] = to_short(powers)


def join(keep, received, start, width, linear, waited):
    kf, rows = keep.shape
    extra = 2 * LO if start == 0 else 0
    return pl.pallas_call(
        functools.partial(join_kernel, start, width),
        in_specs=[VMEM] * 3 + [pl.BlockSpec(memory_space=pl.ANY)] * len(waited),
        out_shape=jax.ShapeDtypeStruct((kf, width + extra + 128), jnp.int16),
        out_specs=VMEM,
        compiler_params=pltpu.CompilerParams(**PARAMS),
        name="join",
    )(keep, received, linear, *waited)


def table_kernel(rows, rank, waited, table):
    chunk = min(512, rows)
    lane = lax.broadcasted_iota(jnp.int32, (chunk, 128), 1)
    for start in range(0, rows, chunk):
        at = slice(start, start + chunk)
        inner = lax.rem(rank[:, at], LO)
        column = jnp.broadcast_to(inner.astype(F32), (128, chunk)).T.astype(jnp.int32)
        for first in range(0, LO, 128):
            table[at, first : first + 128] = jnp.where(column == lane + first, 1.0, 0.0).astype(BF16)


def tables(rank, waited, rows):
    return pl.pallas_call(
        functools.partial(table_kernel, rows),
        in_specs=[VMEM, pl.BlockSpec(memory_space=pl.ANY)],
        out_shape=jax.ShapeDtypeStruct((rows, LO), BF16),
        out_specs=VMEM,
        compiler_params=pltpu.CompilerParams(**PARAMS),
        cost_estimate=pl.CostEstimate(flops=rows * LO * 8, bytes_accessed=rows * LO * 2, transcendentals=0),
        name="tables",
    )(rank, waited)


def risk_kernel(rows, parts, linear, *refs):
    messages, events = refs[:parts], refs[parts]
    risk_out, message = refs[parts + 1 :]
    groups = rows // LO
    total = linear[...]
    for part in messages:
        end = part.shape[1] - 128
        power = from_short(part[:, end:])[:, 127:]
        high, low = from_short(part[:, end - 2 * LO : end - LO]), from_short(part[:, end - LO : end])
        total = total + (high + low * (1.0 / 32768.0)) * jnp.exp2(power)
    risk = jnp.exp(total[:groups])
    for g in range(groups):
        risk_out[:, g * LO : (g + 1) * LO] = risk[g : g + 1]
    everything = jnp.sum(jnp.sum(risk, axis=0, keepdims=True), axis=1, keepdims=True)
    count = jnp.sum(events[...].astype(F32), axis=1, keepdims=True)
    totals = [jnp.broadcast_to(value, (1, 128)) for value in (everything, count)]
    message[...] = jnp.concatenate(totals + [jnp.zeros((6, 128), F32)], axis=0)


def risks(linear, messages, events, rows):
    return pl.pallas_call(
        functools.partial(risk_kernel, rows, len(messages)),
        in_specs=[VMEM] * (len(messages) + 2),
        out_shape=[jax.ShapeDtypeStruct((1, rows), F32), jax.ShapeDtypeStruct((8, 128), F32)],
        out_specs=[VMEM] * 2,
        compiler_params=pltpu.CompilerParams(**PARAMS),
        cost_estimate=pl.CostEstimate(flops=rows * 64, bytes_accessed=rows * 64, transcendentals=rows),
        name="risks",
    )(linear, *messages, events)


def risk_sum_kernel(rows, risk, rank, events, table, sums_out, events_out):
    groups = rows // LO
    mask = one_hot(lax.rem(rank[...], rows) // LO, groups, F32)
    pieces = [mask * part for part in split_three(risk[...])] + [mask * events[...].astype(F32)]
    lhs = jnp.concatenate(pieces, axis=0).astype(BF16)
    sorted_all = jnp.dot(lhs, table[...], preferred_element_type=F32)
    ordered = sorted_all[:groups] + sorted_all[groups : 2 * groups] + sorted_all[2 * groups : 3 * groups]
    inside = dot_binary(ordered, triangle(LO, lambda a, b: a >= b))
    totals = jnp.broadcast_to(inside[:, :1], inside.shape)
    carried = binary_dot(triangle(groups, lambda a, b: a < b), totals)
    sums_out[...] = inside + carried
    events_out[...] = sorted_all[3 * groups :]


def risk_sums(risk, rank, events, table, rows):
    flat = jax.ShapeDtypeStruct((rows // LO, LO), F32)
    return pl.pallas_call(
        functools.partial(risk_sum_kernel, rows),
        in_specs=[VMEM] * 4,
        out_shape=[flat, flat],
        out_specs=[VMEM] * 2,
        compiler_params=pltpu.CompilerParams(**PARAMS),
        cost_estimate=pl.CostEstimate(flops=rows * LO * 128, bytes_accessed=rows * 64, transcendentals=0),
        name="risk_sums",
    )(risk, rank, events, table)


def share_kernel(later, sums, events, plain, more, ordered, hazard_out, squares, message):
    kf = plain.shape[0]
    groups = sums.shape[0]
    risk_sum = sums[...] + later[0:1, 0:1]
    hazard = events[...] / risk_sum
    square = events[...] / (risk_sum * risk_sum)
    hazard_out[...] = hazard
    squares[...] = square
    scaled = jnp.zeros((kf, LO), F32)
    for g in range(groups):
        scaled = scaled + ordered[g * kf : (g + 1) * kf] * square[g : g + 1]
    message[:kf] = plain[...] + more[...]
    message[kf : 2 * kf] = sum(scaled[:, start : start + 128] for start in range(0, LO, 128))
    totals = [jnp.sum(jnp.sum(v, axis=0, keepdims=True), axis=1, keepdims=True) for v in (hazard, square)]
    rows = [jnp.broadcast_to(v, (1, 128)) for v in totals]
    message[2 * kf :] = jnp.concatenate(rows + [jnp.zeros((6, 128), F32)], axis=0)


def shares(later, sums, events, plain, more, ordered):
    flat = jax.ShapeDtypeStruct(sums.shape, F32)
    return pl.pallas_call(
        share_kernel,
        in_specs=[VMEM] * 6,
        out_shape=[flat, flat, jax.ShapeDtypeStruct((2 * plain.shape[0] + 8, 128), F32)],
        out_specs=[VMEM] * 3,
        compiler_params=pltpu.CompilerParams(**PARAMS),
        name="shares",
    )(later, sums, events, plain, more, ordered)


def hazard_kernel(rows, hazard, square, rank, cumulative, squares):
    groups = rows // LO
    inside = dot_binary(
        jnp.concatenate([hazard[...], square[...]], axis=0), triangle(LO, lambda a, b: a <= b)
    )
    totals = jnp.broadcast_to(inside[:, LO - 1 :], (2 * groups, 128))
    place = lax.rem(rank[...], rows)
    mask = one_hot(place // LO, groups, F32)
    placed = dot_binary(inside, one_hot(lax.rem(place, LO), LO))
    before = triangle(groups, lambda a, b: a > b)
    for first, out in ((0, cumulative), (groups, squares)):
        carried = binary_dot(before, totals[first : first + groups])[:, :1]
        out[...] = jnp.sum(mask * (placed[first : first + groups] + carried), axis=0, keepdims=True)


def hazards(hazard, square, rank, rows):
    row = jax.ShapeDtypeStruct((1, rows), F32)
    return pl.pallas_call(
        functools.partial(hazard_kernel, rows),
        in_specs=[VMEM] * 3,
        out_shape=[row, row],
        out_specs=[VMEM] * 2,
        compiler_params=pltpu.CompilerParams(**PARAMS),
        cost_estimate=pl.CostEstimate(flops=rows * LO * 200, bytes_accessed=rows * 64, transcendentals=0),
        name="hazards",
    )(hazard, square, rank)


def range_kernel(bit, count, *refs):
    total, other, later = refs[:3]
    total_out, later_out = refs[3 + count :]
    is_later = (lax.axis_index("ex") & bit) == 0
    later_out[...] = later[...] + jnp.where(is_later, other[...], 0.0)
    total_out[...] = total[...] + other[...]


def ranges(bit, total, other, later, waited):
    return pl.pallas_call(
        functools.partial(range_kernel, bit, len(waited)),
        in_specs=[VMEM] * 3 + [pl.BlockSpec(memory_space=pl.ANY)] * len(waited),
        out_shape=[jax.ShapeDtypeStruct(total.shape, F32)] * 2,
        out_specs=[VMEM] * 2,
        compiler_params=pltpu.CompilerParams(**PARAMS),
        name="ranges",
    )(total, other, later, *waited)


def order_kernel(start, parts, own, other, *refs):
    messages, (risk, rank, table) = refs[:parts], refs[parts : parts + 3]
    tangent_out, ordered_out, plain, lhs = refs[-4:]
    kf, width = tangent_out.shape
    rows = own.shape[1]
    groups = rows // LO
    span = min(SPAN, width)
    folded = jnp.zeros((kf, 128), F32)
    powers = [jnp.exp2(from_short(part[:, part.shape[1] - 128 :])) for part in messages]
    for i in range(width // span):
        at = slice(start + i * span, start + (i + 1) * span)
        here = slice(i * span, (i + 1) * span)
        tangent = own[:, at] + other[:, at]
        for part, power in zip(messages, powers):
            tangent = tangent + from_short(part[:, here]) * power[:, i : i + 1]
        tangent_out[:, here] = tangent
        weighted = tangent * risk[:, at]
        folded = folded + sum(weighted[:, j : j + 128] for j in range(0, span, 128))
        high, low = split_two(weighted)
        high, low = high.astype(BF16), low.astype(BF16)
        group = jnp.broadcast_to(lax.rem(rank[:, at], rows) // LO, (kf, span))
        for g in range(groups):
            mask = jnp.where(group == g, 1.0, 0.0).astype(BF16)
            lhs[2 * g * kf : (2 * g + 1) * kf, here] = high * mask
            lhs[(2 * g + 1) * kf : (2 * g + 2) * kf, here] = low * mask
    plain[...] = folded
    ordered = jnp.dot(lhs[...], table[start : start + width], preferred_element_type=F32)
    for g in range(groups):
        ordered_out[g * kf : (g + 1) * kf] = (
            ordered[2 * g * kf : (2 * g + 1) * kf] + ordered[(2 * g + 1) * kf : (2 * g + 2) * kf]
        )


def ordered_values(own, other, messages, risk, rank, table, start, width):
    kf, rows = own.shape
    groups = rows // LO
    return pl.pallas_call(
        functools.partial(order_kernel, start, len(messages)),
        in_specs=[VMEM] * (len(messages) + 5),
        out_shape=[
            jax.ShapeDtypeStruct((kf, width), F32),
            jax.ShapeDtypeStruct((groups * kf, LO), F32),
            jax.ShapeDtypeStruct((kf, 128), F32),
        ],
        out_specs=[VMEM] * 3,
        scratch_shapes=[pltpu.VMEM((groups * 2 * kf, width), BF16)],
        compiler_params=pltpu.CompilerParams(**PARAMS),
        cost_estimate=pl.CostEstimate(
            flops=2 * width * LO * groups * 2 * kf, bytes_accessed=width * kf * 24, transcendentals=0
        ),
        name="ordered_values",
    )(own, other, *messages, risk, rank, table)


def suffix_kernel(kf, one, two, sums):
    groups = sums.shape[0] // kf
    inside = dot_binary(one[...] + two[...], triangle(LO, lambda a, b: a >= b))
    carried = jnp.zeros((kf, 1), F32)
    for g in reversed(range(groups)):
        rows_of = slice(g * kf, (g + 1) * kf)
        sums[rows_of] = inside[rows_of] + carried
        carried = carried + inside[rows_of, :1]


def suffix_sums(one, two, kf):
    return pl.pallas_call(
        functools.partial(suffix_kernel, kf),
        in_specs=[VMEM] * 2,
        out_shape=jax.ShapeDtypeStruct(one.shape, F32),
        out_specs=VMEM,
        compiler_params=pltpu.CompilerParams(**PARAMS),
        name="suffix_sums",
    )(one, two)


def prefix_kernel(sums, squares, rank, out):
    kf, rows = out.shape
    groups = squares.shape[0]
    chunk = min(512, rows)
    hazard = [sums[g * kf : (g + 1) * kf] * squares[g : g + 1, :] for g in range(groups)]
    inside = dot_binary(jnp.concatenate(hazard, axis=0), triangle(LO, lambda a, b: a <= b))
    carried = jnp.zeros((kf, 1), F32)
    summed = [None] * groups
    for g in range(groups):
        rows_of = slice(g * kf, (g + 1) * kf)
        summed[g] = inside[rows_of] + carried
        carried = carried + inside[rows_of, LO - 1 :]
    both = stacked(split_two(jnp.concatenate(summed, axis=0)))
    for start in range(0, rows, chunk):
        at = slice(start, start + chunk)
        place = lax.rem(rank[:, at], rows)
        group = place // LO
        spread = one_hot(lax.rem(place, LO), LO)
        placed = unstacked(jnp.dot(both, spread, preferred_element_type=F32), 2)
        picked = jnp.zeros((kf, chunk), F32)
        for g in range(groups):
            picked = picked + jnp.where(group == g, placed[g * kf : (g + 1) * kf], 0.0)
        out[:, at] = picked


def prefix_sums(sums, squares, rank, kf):
    rows = rank.shape[1]
    return pl.pallas_call(
        prefix_kernel,
        in_specs=[VMEM] * 3,
        out_shape=jax.ShapeDtypeStruct((kf, rows), F32),
        out_specs=VMEM,
        compiler_params=pltpu.CompilerParams(**PARAMS),
        cost_estimate=pl.CostEstimate(
            flops=4 * rows * LO * (rows // LO) * kf, bytes_accessed=rows * kf * 24, transcendentals=0
        ),
        name="prefix_sums",
    )(sums, squares, rank)


def weight_kernel(places, *refs):
    ex = len(places)
    messages, (first, rest, local, risk, cumulative, squares) = refs[:ex], refs[ex : ex + 6]
    weighted, placed = refs[ex + 6 :]
    kf = first.shape[0]
    me = lax.axis_index("ex")
    for i, part in zip(places, messages):
        placed[me ^ i] = part[...]
    later = jnp.zeros((kf, 128), F32)
    own_later, before = later, later
    hazard_before = jnp.zeros((1, 128), F32)
    for b in reversed(range(ex)):
        plain, scaled, square = placed[b, :kf], placed[b, kf : 2 * kf], placed[b, 2 * kf + 1 : 2 * kf + 2]
        own_later = own_later + jnp.where(b > me, plain, 0.0)
        before = before + jnp.where(b < me, scaled + square * later, 0.0)
        hazard_before = hazard_before + jnp.where(b < me, placed[b, 2 * kf : 2 * kf + 1], 0.0)
        later = later + plain
    own_later = jnp.sum(own_later, axis=1, keepdims=True)
    before = jnp.sum(before, axis=1, keepdims=True)
    hazard_before = hazard_before[:, :1]
    for start, part in ((0, first), (first.shape[1], rest)):
        at = slice(start, start + part.shape[1])
        value = part[...] * (cumulative[:, at] + hazard_before) - (
            local[:, at] + squares[:, at] * own_later + before
        )
        weighted[:, at] = (risk[:, at] * value).astype(BF16)


def weights(places, messages, first, rest, local, risk, cumulative, squares):
    ex = len(messages)
    return pl.pallas_call(
        functools.partial(weight_kernel, tuple(places)),
        in_specs=[VMEM] * (ex + 6),
        out_shape=jax.ShapeDtypeStruct(local.shape, BF16),
        out_specs=VMEM,
        scratch_shapes=[pltpu.VMEM((ex,) + messages[0].shape, F32)],
        compiler_params=pltpu.CompilerParams(**PARAMS),
        name="weights",
    )(*messages, first, rest, local, risk, cumulative, squares)


def encode(values, message):
    columns = len(values)
    powers = []
    for i, value in enumerate(values):
        power = power_of(jnp.max(jnp.abs(value), axis=0, keepdims=True))
        scaled = to_short(value * jnp.exp2(-power))
        for j in range(value.shape[0] // 16):
            message[j * columns + i] = scaled[j * 16 : (j + 1) * 16]
        powers.append(power)
    powers.append(jnp.zeros((16 - columns, 128), F32))
    message[message.shape[0] - 1] = to_short(jnp.concatenate(powers, axis=0))


def decode(message, columns):
    last = message.shape[0] - 1
    scales = jnp.exp2(from_short(message[last]))
    values = []
    for i in range(columns):
        value = jnp.concatenate([from_short(message[j]) for j in range(i, last, columns)], axis=0)
        values.append(value * scales[i : i + 1])
    return values


def decode_sum(mine, other, columns):
    return [one + two for one, two in zip(decode(mine, columns), decode(other, columns))]


def gradient_kernel(parts, kf, *refs):
    pieces, dosages, out, weighted = refs[:parts], refs[parts], refs[parts + 1], refs[parts + 2]
    for i in range(parts):
        weighted[i * kf : (i + 1) * kf, :] = pieces[i][...]
    variants = dosages.shape[1]
    block = min(256, variants)
    values = []
    for start in range(0, variants, block):
        total = jnp.dot(weighted[...], dosages[:, start : start + block], preferred_element_type=F32)
        values += [total[:, at : at + 128] for at in range(0, block, 128)]
    encode(values, out)


def gradients(pieces, dosages):
    parts = len(pieces)
    kf, persons = pieces[0].shape
    k, variants = kf * parts, dosages.shape[1]
    return pl.pallas_call(
        functools.partial(gradient_kernel, parts, kf),
        in_specs=[VMEM] * (parts + 1),
        out_shape=jax.ShapeDtypeStruct((k * variants // 2048 + 1, 16, 128), jnp.int16),
        out_specs=VMEM,
        scratch_shapes=[pltpu.VMEM((k, persons), BF16)],
        compiler_params=pltpu.CompilerParams(**PARAMS),
        cost_estimate=pl.CostEstimate(
            flops=2 * persons * variants * k, bytes_accessed=persons * (variants * 2 + k * 2), transcendentals=0
        ),
        name="gradients",
    )(*pieces, dosages)


def merge_kernel(columns, mine, other, out):
    encode(decode_sum(mine, other, columns), out)


def merge(mine, other, variants):
    return pl.pallas_call(
        functools.partial(merge_kernel, variants // 128),
        in_specs=[VMEM] * 2,
        out_shape=jax.ShapeDtypeStruct(mine.shape, jnp.int16),
        out_specs=VMEM,
        compiler_params=pltpu.CompilerParams(**PARAMS),
        name="merge",
    )(mine, other)


def add_kernel(mine, other, out):
    for i, value in enumerate(decode_sum(mine, other, out.shape[1] // 128)):
        out[:, i * 128 : (i + 1) * 128] = value


def add(mine, other, variants):
    return pl.pallas_call(
        add_kernel,
        in_specs=[VMEM] * 2,
        out_shape=jax.ShapeDtypeStruct(((mine.shape[0] - 1) * 2048 // variants, variants), F32),
        out_specs=VMEM,
        compiler_params=pltpu.CompilerParams(**PARAMS),
        name="add",
    )(mine, other)


def finish_kernel(feat, kf, first, mine, other, count, out, placed, total, sems):
    me = lax.axis_index("feat")
    variants = out.shape[0]
    scale = count[1:2, 0:1]
    copies = []
    for i, value in enumerate(decode_sum(mine, other, variants // 128)):
        at = slice(i * 128, (i + 1) * 128)
        for q in range(feat // 2):
            rows = slice(q * kf, (q + 1) * kf)
            placed[i, me ^ (2 * q)] = first[rows, at]
            placed[i, me ^ (2 * q + 1)] = value[rows]
        total[at] = placed[i].reshape(feat * kf, 128).T / scale
        copies.append(
            pltpu.make_async_copy(
                total.at[pl.ds(i * 128, 128)], out.at[pl.ds(i * 128, 128)], sems.at[i]
            )
        )
        copies[i].start()
    for copy in copies:
        copy.wait()


def finish(first, mine, other, count, feat):
    k, variants = 2 * first.shape[0], first.shape[1]
    kf = k // feat
    return pl.pallas_call(
        functools.partial(finish_kernel, feat, kf),
        in_specs=[VMEM] * 4,
        out_shape=jax.ShapeDtypeStruct((variants, k), F32),
        out_specs=HBM,
        scratch_shapes=[
            pltpu.VMEM((variants // 128, feat, kf, 128), F32),
            pltpu.VMEM((variants, k), F32),
            pltpu.SemaphoreType.DMA((variants // 128,)),
        ],
        compiler_params=pltpu.CompilerParams(**PARAMS),
        name="finish",
    )(first, mine, other, count)


def local(dosages, coefficients, directions, event_rank, events):
    feat, ex = lax.axis_size("feat"), lax.axis_size("ex")
    rows = dosages.shape[0]
    variants, k = directions.shape
    each = k // feat
    padded = -(-each // 16) * 16
    if padded != each:
        directions = jnp.pad(directions.reshape(variants, feat, each), ((0, 0), (0, 0), (0, padded - each)))
        directions = directions.reshape(variants, feat * padded)
    rank, event_row = event_rank[None], events[None]

    linear, keep, send = products(dosages, coefficients, directions, feat)
    order = list(reversed(range(1, feat // 2)))
    received = {q: swap(send[q], "feat", 1) for q in order + [0]}
    table = tables(rank, linear, rows)
    paired = pair(linear, received[order[0]], table)
    middle = min(3 * SPAN, rows // 2)
    firsts = [
        swap(join(keep[q], received[q], 0, middle, paired, []), "feat", 2 * q) for q in order
    ]
    rests = [
        swap(join(keep[q], received[q], middle, rows - middle, paired, [received[0]]), "feat", 2 * q)
        for q in order
    ]

    risk, total = risks(paired, firsts, event_row, rows)
    sums, ordered_events = risk_sums(risk, rank, event_row, table, rows)
    later = jnp.zeros_like(total)
    bit = 1
    while bit < ex:
        total, later = ranges(bit, total, swap(total, "ex", bit), later, rests + [sums] if bit == 1 else [])
        bit *= 2
    tangent, one, plain = ordered_values(keep[0], received[0], firsts, risk, rank, table, 0, middle)
    more_tangent, two, more = ordered_values(
        keep[0], received[0], rests, risk, rank, table, middle, rows - middle
    )
    later_sums = suffix_sums(one, two, padded)
    hazard, ordered_squares, message = shares(later, sums, ordered_events, plain, more, later_sums)
    places = list(range(ex))
    places[-2:] = places[:-3:-1]
    messages = [swap(message, "ex", i) if i else message for i in places]
    cumulative, squares = hazards(hazard, ordered_squares, rank, rows)
    summed = prefix_sums(later_sums, ordered_squares, rank, padded)
    own = weights(places, messages, tangent, more_tangent, summed, risk, cumulative, squares)

    chips = {0: own}
    for q in range(1, feat // 2):
        chips[q] = swap(own, "feat", 2 * q)
    near = [chips[q] for q in range(feat // 2)]
    far = [swap(chips[q], "feat", 1) for q in range(feat // 2)]
    partial_sums = [gradients(pieces, dosages) for pieces in (near, far)]
    bit = 1
    while 2 * bit < ex:
        received = [swap(message, "ex", bit) for message in partial_sums]
        partial_sums = [merge(mine, other, variants) for mine, other in zip(partial_sums, received)]
        bit *= 2
    received = [swap(message, "ex", bit) for message in partial_sums]
    first = add(partial_sums[0], received[0], variants)
    result = finish(first, partial_sums[1], received[1], total, feat)
    if padded != each:
        result = result.reshape(variants, feat, padded)[:, :, :each].reshape(variants, k)
    return result


def solution(mesh):
    placed = (P("ex", "feat"), P("feat"), P("feat", None), P("ex"), P("ex"))
    return jax.shard_map(
        local, mesh=mesh, in_specs=placed, out_specs=P("feat", None), check_vma=False
    )
```

```python
import functools

import jax
import jax.numpy as jnp
from jax import lax
from jax.experimental import pallas as pl
from jax.experimental.pallas import tpu as pltpu
from jax.sharding import PartitionSpec as P

F32 = jnp.float32
BF16 = jnp.bfloat16
LO = 256
NT = (((1,), (1,)), ((), ()))
SPAN = 512
VMEM = pl.BlockSpec(memory_space=pltpu.VMEM)
HBM = pl.BlockSpec(memory_space=pltpu.HBM)
PARAMS = dict(vmem_limit_bytes=24 * 1024 * 1024)


def swap(x, axis, i):
    count = lax.axis_size(axis)
    return lax.ppermute(x, axis, [(s, s ^ i) for s in range(count)])


def split_two(x):
    high = x.astype(BF16).astype(F32)
    return high, x - high


def split_three(x):
    first, rest = split_two(x)
    second, third = split_two(rest)
    return first, second, third


def one_hot(values, count, kind=BF16):
    shape = (count, values.shape[1])
    return jnp.where(lax.broadcasted_iota(jnp.int32, shape, 0) == values, 1.0, 0.0).astype(kind)


def triangle(n, keep):
    first = lax.broadcasted_iota(jnp.int32, (n, n), 0)
    second = lax.broadcasted_iota(jnp.int32, (n, n), 1)
    return jnp.where(keep(first, second), 1.0, 0.0)


def stacked(parts):
    return jnp.concatenate(parts, axis=0).astype(BF16)


def unstacked(values, count):
    height = values.shape[0] // count
    return sum(values[i * height : (i + 1) * height] for i in range(count))


def dot_binary(a, b):
    parts = jnp.dot(stacked(split_three(a)), b.astype(BF16), preferred_element_type=F32)
    return unstacked(parts, 3)


def binary_dot(a, b):
    a = a.astype(BF16)
    total = None
    for part in split_three(b):
        term = jnp.dot(a, part.astype(BF16), preferred_element_type=F32)
        total = term if total is None else total + term
    return total


def product_kernel(feat, kf, chunk, directions, coefficients, dosages, *refs):
    linear, keep, send = refs[0], refs[1 : 1 + feat // 2], refs[1 + feat // 2 : 1 + feat]
    table, own_directions, own_coefficients, lhs, turned, sems = refs[1 + feat :]
    me = lax.axis_index("feat")
    width = feat * kf
    persons, variants = table.shape
    steps = persons // chunk
    small = [
        pltpu.make_async_copy(directions, own_directions, sems.at[steps]),
        pltpu.make_async_copy(coefficients, own_coefficients, sems.at[steps + 1]),
    ]
    large = [
        pltpu.make_async_copy(
            dosages.at[pl.ds(i * chunk, chunk)], table.at[pl.ds(i * chunk, chunk)], sems.at[i]
        )
        for i in range(steps)
    ]
    for copy in small + large:
        copy.start()
    for copy in small:
        copy.wait()
    turned[...] = own_directions[...].astype(F32).T.reshape(turned.shape)
    for j in range(feat):
        lhs[j * kf : (j + 1) * kf] = turned[me ^ j].astype(BF16)
    lhs[width:] = jnp.broadcast_to(own_coefficients[...].astype(F32)[None, :], (16, variants)).astype(BF16)
    for i in range(steps):
        large[i].wait()
        first = i * chunk
        result = lax.dot_general(
            lhs[...], table[first : first + chunk], NT, preferred_element_type=F32
        )
        for j in range(feat):
            (send if j % 2 else keep)[j // 2][:, first : first + chunk] = result[j * kf : (j + 1) * kf]
        for start in range(0, chunk, LO):
            row = result[width : width + 1, start : start + LO]
            group = (first + start) // LO
            linear[group : group + 1, :] = row
            send[-1][group : group + 1, persons:] = row


def products(dosages, coefficients, directions, feat):
    persons, variants = dosages.shape
    k = directions.shape[1]
    kf = k // feat
    chunk = min(1024, persons)
    piece = jax.ShapeDtypeStruct((kf, persons), F32)
    first = jax.ShapeDtypeStruct((kf, persons + LO), F32)
    out = pl.pallas_call(
        functools.partial(product_kernel, feat, kf, chunk),
        in_specs=[HBM, HBM, HBM],
        out_shape=[jax.ShapeDtypeStruct((kf, LO), F32)]
        + [piece] * (feat - 1)
        + [first],
        out_specs=[VMEM] * (feat + 1),
        scratch_shapes=[
            pltpu.VMEM((persons, variants), BF16),
            pltpu.VMEM((variants, k), BF16),
            pltpu.VMEM((variants,), BF16),
            pltpu.VMEM((k + 16, variants), BF16),
            pltpu.VMEM((feat, kf, variants), F32),
            pltpu.SemaphoreType.DMA((persons // chunk + 2,)),
        ],
        compiler_params=pltpu.CompilerParams(**PARAMS),
        cost_estimate=pl.CostEstimate(
            flops=2 * persons * variants * k, bytes_accessed=persons * (variants * 2 + k * 4), transcendentals=0
        ),
        name="products",
    )(*[pltpu.with_memory_space_constraint(x, pltpu.HBM) for x in (directions, coefficients, dosages)])
    return out[0], out[1 : 1 + feat // 2], out[1 + feat // 2 :]


def power_of(largest):
    return jnp.ceil(jnp.log2(jnp.maximum(largest, 1e-30))) - 14.0


def to_short(values):
    return jnp.round(values).astype(jnp.int32).astype(jnp.int16)


def from_short(values):
    return values.astype(jnp.int32).astype(F32)


def pair_kernel(linear, received, waited, out):
    out[...] = linear[...] + received[:, received.shape[1] - LO :]


def pair(linear, received, waited):
    return pl.pallas_call(
        pair_kernel,
        in_specs=[VMEM] * 2 + [pl.BlockSpec(memory_space=pl.ANY)],
        out_shape=jax.ShapeDtypeStruct(linear.shape, F32),
        out_specs=VMEM,
        compiler_params=pltpu.CompilerParams(**PARAMS),
        name="pair",
    )(linear, received, waited)


def join_kernel(start, width, mine, other, *refs):
    linear, out = refs[0], refs[-1]
    kf = mine.shape[0]
    span = min(SPAN, width)
    lane = lax.broadcasted_iota(jnp.int32, (kf, 128), 1)
    powers = jnp.zeros((kf, 128), F32)
    for i in range(width // span):
        at = slice(start + i * span, start + (i + 1) * span)
        total = mine[:, at] + other[:, at]
        power = power_of(jnp.max(jnp.abs(total), axis=1, keepdims=True))
        out[:, i * span : (i + 1) * span] = to_short(total * jnp.exp2(-power))
        powers = jnp.where(lane == i, power, powers)
    if start == 0:
        power = power_of(jnp.max(jnp.abs(linear[...]), axis=1, keepdims=True))
        scaled = linear[...] * jnp.exp2(-power)
        whole = jnp.round(scaled)
        out[:, width : width + LO] = to_short(whole)
        out[:, width + LO : width + 2 * LO] = to_short((scaled - whole) * 32768.0)
        powers = jnp.where(lane == 127, power, powers)
    out[:, out.shape[1] - 128 :] = to_short(powers)


def join(keep, received, start, width, linear, waited):
    kf, rows = keep.shape
    extra = 2 * LO if start == 0 else 0
    return pl.pallas_call(
        functools.partial(join_kernel, start, width),
        in_specs=[VMEM] * 3 + [pl.BlockSpec(memory_space=pl.ANY)] * len(waited),
        out_shape=jax.ShapeDtypeStruct((kf, width + extra + 128), jnp.int16),
        out_specs=VMEM,
        compiler_params=pltpu.CompilerParams(**PARAMS),
        name="join",
    )(keep, received, linear, *waited)


def table_kernel(rows, rank, waited, table):
    chunk = min(512, rows)
    lane = lax.broadcasted_iota(jnp.int32, (chunk, 128), 1)
    for start in range(0, rows, chunk):
        at = slice(start, start + chunk)
        inner = lax.rem(rank[:, at], LO)
        column = jnp.broadcast_to(inner.astype(F32), (128, chunk)).T.astype(jnp.int32)
        for first in range(0, LO, 128):
            table[at, first : first + 128] = jnp.where(column == lane + first, 1.0, 0.0).astype(BF16)


def tables(rank, waited, rows):
    return pl.pallas_call(
        functools.partial(table_kernel, rows),
        in_specs=[VMEM, pl.BlockSpec(memory_space=pl.ANY)],
        out_shape=jax.ShapeDtypeStruct((rows, LO), BF16),
        out_specs=VMEM,
        compiler_params=pltpu.CompilerParams(**PARAMS),
        cost_estimate=pl.CostEstimate(flops=rows * LO * 8, bytes_accessed=rows * LO * 2, transcendentals=0),
        name="tables",
    )(rank, waited)


def risk_kernel(rows, parts, linear, *refs):
    messages, events = refs[:parts], refs[parts]
    risk_out, message = refs[parts + 1 :]
    groups = rows // LO
    total = linear[...]
    for part in messages:
        end = part.shape[1] - 128
        power = from_short(part[:, end:])[:, 127:]
        high, low = from_short(part[:, end - 2 * LO : end - LO]), from_short(part[:, end - LO : end])
        total = total + (high + low * (1.0 / 32768.0)) * jnp.exp2(power)
    risk = jnp.exp(total[:groups])
    for g in range(groups):
        risk_out[:, g * LO : (g + 1) * LO] = risk[g : g + 1]
    everything = jnp.sum(jnp.sum(risk, axis=0, keepdims=True), axis=1, keepdims=True)
    count = jnp.sum(events[...].astype(F32), axis=1, keepdims=True)
    totals = [jnp.broadcast_to(value, (1, 128)) for value in (everything, count)]
    message[...] = jnp.concatenate(totals + [jnp.zeros((6, 128), F32)], axis=0)


def risks(linear, messages, events, rows):
    return pl.pallas_call(
        functools.partial(risk_kernel, rows, len(messages)),
        in_specs=[VMEM] * (len(messages) + 2),
        out_shape=[jax.ShapeDtypeStruct((1, rows), F32), jax.ShapeDtypeStruct((8, 128), F32)],
        out_specs=[VMEM] * 2,
        compiler_params=pltpu.CompilerParams(**PARAMS),
        cost_estimate=pl.CostEstimate(flops=rows * 64, bytes_accessed=rows * 64, transcendentals=rows),
        name="risks",
    )(linear, *messages, events)


def risk_sum_kernel(rows, risk, rank, events, table, sums_out, events_out):
    groups = rows // LO
    mask = one_hot(lax.rem(rank[...], rows) // LO, groups, F32)
    pieces = [mask * part for part in split_three(risk[...])] + [mask * events[...].astype(F32)]
    lhs = jnp.concatenate(pieces, axis=0).astype(BF16)
    sorted_all = jnp.dot(lhs, table[...], preferred_element_type=F32)
    ordered = sorted_all[:groups] + sorted_all[groups : 2 * groups] + sorted_all[2 * groups : 3 * groups]
    inside = dot_binary(ordered, triangle(LO, lambda a, b: a >= b))
    totals = jnp.broadcast_to(inside[:, :1], inside.shape)
    carried = binary_dot(triangle(groups, lambda a, b: a < b), totals)
    sums_out[...] = inside + carried
    events_out[...] = sorted_all[3 * groups :]


def risk_sums(risk, rank, events, table, rows):
    flat = jax.ShapeDtypeStruct((rows // LO, LO), F32)
    return pl.pallas_call(
        functools.partial(risk_sum_kernel, rows),
        in_specs=[VMEM] * 4,
        out_shape=[flat, flat],
        out_specs=[VMEM] * 2,
        compiler_params=pltpu.CompilerParams(**PARAMS),
        cost_estimate=pl.CostEstimate(flops=rows * LO * 128, bytes_accessed=rows * 64, transcendentals=0),
        name="risk_sums",
    )(risk, rank, events, table)


def share_kernel(later, sums, events, plain, more, ordered, hazard_out, squares, message):
    kf = plain.shape[0]
    groups = sums.shape[0]
    risk_sum = sums[...] + later[0:1, 0:1]
    hazard = events[...] / risk_sum
    square = events[...] / (risk_sum * risk_sum)
    hazard_out[...] = hazard
    squares[...] = square
    scaled = jnp.zeros((kf, LO), F32)
    for g in range(groups):
        scaled = scaled + ordered[g * kf : (g + 1) * kf] * square[g : g + 1]
    message[:kf] = plain[...] + more[...]
    message[kf : 2 * kf] = sum(scaled[:, start : start + 128] for start in range(0, LO, 128))
    totals = [jnp.sum(jnp.sum(v, axis=0, keepdims=True), axis=1, keepdims=True) for v in (hazard, square)]
    rows = [jnp.broadcast_to(v, (1, 128)) for v in totals]
    message[2 * kf :] = jnp.concatenate(rows + [jnp.zeros((6, 128), F32)], axis=0)


def shares(later, sums, events, plain, more, ordered):
    flat = jax.ShapeDtypeStruct(sums.shape, F32)
    return pl.pallas_call(
        share_kernel,
        in_specs=[VMEM] * 6,
        out_shape=[flat, flat, jax.ShapeDtypeStruct((2 * plain.shape[0] + 8, 128), F32)],
        out_specs=[VMEM] * 3,
        compiler_params=pltpu.CompilerParams(**PARAMS),
        name="shares",
    )(later, sums, events, plain, more, ordered)


def hazard_kernel(rows, hazard, square, rank, cumulative, squares):
    groups = rows // LO
    inside = dot_binary(
        jnp.concatenate([hazard[...], square[...]], axis=0), triangle(LO, lambda a, b: a <= b)
    )
    totals = jnp.broadcast_to(inside[:, LO - 1 :], (2 * groups, 128))
    place = lax.rem(rank[...], rows)
    mask = one_hot(place // LO, groups, F32)
    placed = dot_binary(inside, one_hot(lax.rem(place, LO), LO))
    before = triangle(groups, lambda a, b: a > b)
    for first, out in ((0, cumulative), (groups, squares)):
        carried = binary_dot(before, totals[first : first + groups])[:, :1]
        out[...] = jnp.sum(mask * (placed[first : first + groups] + carried), axis=0, keepdims=True)


def hazards(hazard, square, rank, rows):
    row = jax.ShapeDtypeStruct((1, rows), F32)
    return pl.pallas_call(
        functools.partial(hazard_kernel, rows),
        in_specs=[VMEM] * 3,
        out_shape=[row, row],
        out_specs=[VMEM] * 2,
        compiler_params=pltpu.CompilerParams(**PARAMS),
        cost_estimate=pl.CostEstimate(flops=rows * LO * 200, bytes_accessed=rows * 64, transcendentals=0),
        name="hazards",
    )(hazard, square, rank)


def range_kernel(bit, count, *refs):
    total, other, later = refs[:3]
    total_out, later_out = refs[3 + count :]
    is_later = (lax.axis_index("ex") & bit) == 0
    later_out[...] = later[...] + jnp.where(is_later, other[...], 0.0)
    total_out[...] = total[...] + other[...]


def ranges(bit, total, other, later, waited):
    return pl.pallas_call(
        functools.partial(range_kernel, bit, len(waited)),
        in_specs=[VMEM] * 3 + [pl.BlockSpec(memory_space=pl.ANY)] * len(waited),
        out_shape=[jax.ShapeDtypeStruct(total.shape, F32)] * 2,
        out_specs=[VMEM] * 2,
        compiler_params=pltpu.CompilerParams(**PARAMS),
        name="ranges",
    )(total, other, later, *waited)


def order_kernel(start, parts, own, other, *refs):
    messages, (risk, rank, table) = refs[:parts], refs[parts : parts + 3]
    tangent_out, ordered_out, plain, lhs = refs[-4:]
    kf, width = tangent_out.shape
    rows = own.shape[1]
    groups = rows // LO
    span = min(SPAN, width)
    folded = jnp.zeros((kf, 128), F32)
    powers = [jnp.exp2(from_short(part[:, part.shape[1] - 128 :])) for part in messages]
    for i in range(width // span):
        at = slice(start + i * span, start + (i + 1) * span)
        here = slice(i * span, (i + 1) * span)
        tangent = own[:, at] + other[:, at]
        for part, power in zip(messages, powers):
            tangent = tangent + from_short(part[:, here]) * power[:, i : i + 1]
        tangent_out[:, here] = tangent
        weighted = tangent * risk[:, at]
        folded = folded + sum(weighted[:, j : j + 128] for j in range(0, span, 128))
        high, low = split_two(weighted)
        high, low = high.astype(BF16), low.astype(BF16)
        group = jnp.broadcast_to(lax.rem(rank[:, at], rows) // LO, (kf, span))
        for g in range(groups):
            mask = jnp.where(group == g, 1.0, 0.0).astype(BF16)
            lhs[2 * g * kf : (2 * g + 1) * kf, here] = high * mask
            lhs[(2 * g + 1) * kf : (2 * g + 2) * kf, here] = low * mask
    plain[...] = folded
    ordered = jnp.dot(lhs[...], table[start : start + width], preferred_element_type=F32)
    for g in range(groups):
        ordered_out[g * kf : (g + 1) * kf] = (
            ordered[2 * g * kf : (2 * g + 1) * kf] + ordered[(2 * g + 1) * kf : (2 * g + 2) * kf]
        )


def ordered_values(own, other, messages, risk, rank, table, start, width):
    kf, rows = own.shape
    groups = rows // LO
    return pl.pallas_call(
        functools.partial(order_kernel, start, len(messages)),
        in_specs=[VMEM] * (len(messages) + 5),
        out_shape=[
            jax.ShapeDtypeStruct((kf, width), F32),
            jax.ShapeDtypeStruct((groups * kf, LO), F32),
            jax.ShapeDtypeStruct((kf, 128), F32),
        ],
        out_specs=[VMEM] * 3,
        scratch_shapes=[pltpu.VMEM((groups * 2 * kf, width), BF16)],
        compiler_params=pltpu.CompilerParams(**PARAMS),
        cost_estimate=pl.CostEstimate(
            flops=2 * width * LO * groups * 2 * kf, bytes_accessed=width * kf * 24, transcendentals=0
        ),
        name="ordered_values",
    )(own, other, *messages, risk, rank, table)


def suffix_kernel(kf, one, two, sums):
    groups = sums.shape[0] // kf
    inside = dot_binary(one[...] + two[...], triangle(LO, lambda a, b: a >= b))
    carried = jnp.zeros((kf, 1), F32)
    for g in reversed(range(groups)):
        rows_of = slice(g * kf, (g + 1) * kf)
        sums[rows_of] = inside[rows_of] + carried
        carried = carried + inside[rows_of, :1]


def suffix_sums(one, two, kf):
    return pl.pallas_call(
        functools.partial(suffix_kernel, kf),
        in_specs=[VMEM] * 2,
        out_shape=jax.ShapeDtypeStruct(one.shape, F32),
        out_specs=VMEM,
        compiler_params=pltpu.CompilerParams(**PARAMS),
        name="suffix_sums",
    )(one, two)


def prefix_kernel(sums, squares, rank, out):
    kf, rows = out.shape
    groups = squares.shape[0]
    chunk = min(512, rows)
    hazard = [sums[g * kf : (g + 1) * kf] * squares[g : g + 1, :] for g in range(groups)]
    inside = dot_binary(jnp.concatenate(hazard, axis=0), triangle(LO, lambda a, b: a <= b))
    carried = jnp.zeros((kf, 1), F32)
    summed = [None] * groups
    for g in range(groups):
        rows_of = slice(g * kf, (g + 1) * kf)
        summed[g] = inside[rows_of] + carried
        carried = carried + inside[rows_of, LO - 1 :]
    both = stacked(split_two(jnp.concatenate(summed, axis=0)))
    for start in range(0, rows, chunk):
        at = slice(start, start + chunk)
        place = lax.rem(rank[:, at], rows)
        group = place // LO
        spread = one_hot(lax.rem(place, LO), LO)
        placed = unstacked(jnp.dot(both, spread, preferred_element_type=F32), 2)
        picked = jnp.zeros((kf, chunk), F32)
        for g in range(groups):
            picked = picked + jnp.where(group == g, placed[g * kf : (g + 1) * kf], 0.0)
        out[:, at] = picked


def prefix_sums(sums, squares, rank, kf):
    rows = rank.shape[1]
    return pl.pallas_call(
        prefix_kernel,
        in_specs=[VMEM] * 3,
        out_shape=jax.ShapeDtypeStruct((kf, rows), F32),
        out_specs=VMEM,
        compiler_params=pltpu.CompilerParams(**PARAMS),
        cost_estimate=pl.CostEstimate(
            flops=4 * rows * LO * (rows // LO) * kf, bytes_accessed=rows * kf * 24, transcendentals=0
        ),
        name="prefix_sums",
    )(sums, squares, rank)


def weight_kernel(ex, *refs):
    messages, (first, rest, local, risk, cumulative, squares) = refs[:ex], refs[ex : ex + 6]
    weighted, placed = refs[ex + 6 :]
    kf = first.shape[0]
    me = lax.axis_index("ex")
    for i in range(ex):
        placed[me ^ i] = messages[i][...]
    later = jnp.zeros((kf, 128), F32)
    own_later, before = later, later
    hazard_before = jnp.zeros((1, 128), F32)
    for b in reversed(range(ex)):
        plain, scaled, square = placed[b, :kf], placed[b, kf : 2 * kf], placed[b, 2 * kf + 1 : 2 * kf + 2]
        own_later = own_later + jnp.where(b > me, plain, 0.0)
        before = before + jnp.where(b < me, scaled + square * later, 0.0)
        hazard_before = hazard_before + jnp.where(b < me, placed[b, 2 * kf : 2 * kf + 1], 0.0)
        later = later + plain
    own_later = jnp.sum(own_later, axis=1, keepdims=True)
    before = jnp.sum(before, axis=1, keepdims=True)
    hazard_before = hazard_before[:, :1]
    for start, part in ((0, first), (first.shape[1], rest)):
        at = slice(start, start + part.shape[1])
        value = part[...] * (cumulative[:, at] + hazard_before) - (
            local[:, at] + squares[:, at] * own_later + before
        )
        weighted[:, at] = (risk[:, at] * value).astype(BF16)


def weights(messages, first, rest, local, risk, cumulative, squares):
    ex = len(messages)
    return pl.pallas_call(
        functools.partial(weight_kernel, ex),
        in_specs=[VMEM] * (ex + 6),
        out_shape=jax.ShapeDtypeStruct(local.shape, BF16),
        out_specs=VMEM,
        scratch_shapes=[pltpu.VMEM((ex,) + messages[0].shape, F32)],
        compiler_params=pltpu.CompilerParams(**PARAMS),
        name="weights",
    )(*messages, first, rest, local, risk, cumulative, squares)


def encode(values, message):
    columns = len(values)
    powers = []
    for i, value in enumerate(values):
        power = power_of(jnp.max(jnp.abs(value), axis=0, keepdims=True))
        scaled = to_short(value * jnp.exp2(-power))
        for j in range(value.shape[0] // 16):
            message[j * columns + i] = scaled[j * 16 : (j + 1) * 16]
        powers.append(power)
    powers.append(jnp.zeros((16 - columns, 128), F32))
    message[message.shape[0] - 1] = to_short(jnp.concatenate(powers, axis=0))


def decode(message, columns):
    last = message.shape[0] - 1
    scales = jnp.exp2(from_short(message[last]))
    values = []
    for i in range(columns):
        value = jnp.concatenate([from_short(message[j]) for j in range(i, last, columns)], axis=0)
        values.append(value * scales[i : i + 1])
    return values


def decode_sum(mine, other, columns):
    return [one + two for one, two in zip(decode(mine, columns), decode(other, columns))]


def gradient_kernel(parts, kf, *refs):
    pieces, dosages, out, weighted = refs[:parts], refs[parts], refs[parts + 1], refs[parts + 2]
    for i in range(parts):
        weighted[i * kf : (i + 1) * kf, :] = pieces[i][...]
    total = jnp.dot(weighted[...], dosages[...], preferred_element_type=F32)
    encode([total[:, at : at + 128] for at in range(0, total.shape[1], 128)], out)


def gradients(pieces, dosages):
    parts = len(pieces)
    kf, persons = pieces[0].shape
    k, variants = kf * parts, dosages.shape[1]
    return pl.pallas_call(
        functools.partial(gradient_kernel, parts, kf),
        in_specs=[VMEM] * (parts + 1),
        out_shape=jax.ShapeDtypeStruct((k * variants // 2048 + 1, 16, 128), jnp.int16),
        out_specs=VMEM,
        scratch_shapes=[pltpu.VMEM((k, persons), BF16)],
        compiler_params=pltpu.CompilerParams(**PARAMS),
        cost_estimate=pl.CostEstimate(
            flops=2 * persons * variants * k, bytes_accessed=persons * (variants * 2 + k * 2), transcendentals=0
        ),
        name="gradients",
    )(*pieces, dosages)


def hold_kernel(parts, *refs):
    for piece, out in zip(refs[:parts], refs[parts + 1 :]):
        out[...] = piece[...]


def hold(pieces, waited):
    parts = len(pieces)
    return pl.pallas_call(
        functools.partial(hold_kernel, parts),
        in_specs=[VMEM] * parts + [pl.BlockSpec(memory_space=pl.ANY)],
        out_shape=[jax.ShapeDtypeStruct(piece.shape, piece.dtype) for piece in pieces],
        out_specs=[VMEM] * parts,
        compiler_params=pltpu.CompilerParams(**PARAMS),
        name="hold",
    )(*pieces, waited)


def merge_kernel(columns, mine, other, out):
    encode(decode_sum(mine, other, columns), out)


def merge(mine, other, variants):
    return pl.pallas_call(
        functools.partial(merge_kernel, variants // 128),
        in_specs=[VMEM] * 2,
        out_shape=jax.ShapeDtypeStruct(mine.shape, jnp.int16),
        out_specs=VMEM,
        compiler_params=pltpu.CompilerParams(**PARAMS),
        name="merge",
    )(mine, other)


def add_kernel(mine, other, out):
    for i, value in enumerate(decode_sum(mine, other, out.shape[1] // 128)):
        out[:, i * 128 : (i + 1) * 128] = value


def add(mine, other, variants):
    return pl.pallas_call(
        add_kernel,
        in_specs=[VMEM] * 2,
        out_shape=jax.ShapeDtypeStruct(((mine.shape[0] - 1) * 2048 // variants, variants), F32),
        out_specs=VMEM,
        compiler_params=pltpu.CompilerParams(**PARAMS),
        name="add",
    )(mine, other)


def finish_kernel(feat, kf, first, mine, other, count, out, placed, total, sems):
    me = lax.axis_index("feat")
    variants = out.shape[0]
    scale = count[1:2, 0:1]
    for q in range(feat // 2):
        placed[me ^ (2 * q)] = first[q * kf : (q + 1) * kf]
    for i, value in enumerate(decode_sum(mine, other, variants // 128)):
        for q in range(feat // 2):
            placed[me ^ (2 * q + 1), :, i * 128 : (i + 1) * 128] = value[q * kf : (q + 1) * kf]
    copies = []
    for i in range(variants // 128):
        at = slice(i * 128, (i + 1) * 128)
        total[at] = placed[:, :, at].reshape(feat * kf, 128).T / scale
        copies.append(
            pltpu.make_async_copy(
                total.at[pl.ds(i * 128, 128)], out.at[pl.ds(i * 128, 128)], sems.at[i]
            )
        )
        copies[i].start()
    for copy in copies:
        copy.wait()


def finish(first, mine, other, count, feat):
    k, variants = 2 * first.shape[0], first.shape[1]
    kf = k // feat
    return pl.pallas_call(
        functools.partial(finish_kernel, feat, kf),
        in_specs=[VMEM] * 4,
        out_shape=jax.ShapeDtypeStruct((variants, k), F32),
        out_specs=HBM,
        scratch_shapes=[
            pltpu.VMEM((feat, kf, variants), F32),
            pltpu.VMEM((variants, k), F32),
            pltpu.SemaphoreType.DMA((variants // 128,)),
        ],
        compiler_params=pltpu.CompilerParams(**PARAMS),
        name="finish",
    )(first, mine, other, count)


def local(dosages, coefficients, directions, event_rank, events):
    feat, ex = lax.axis_size("feat"), lax.axis_size("ex")
    rows = dosages.shape[0]
    variants, k = directions.shape
    each = k // feat
    padded = -(-each // 16) * 16
    if padded != each:
        directions = jnp.pad(directions.reshape(variants, feat, each), ((0, 0), (0, 0), (0, padded - each)))
        directions = directions.reshape(variants, feat * padded)
    rank, event_row = event_rank[None], events[None]

    linear, keep, send = products(dosages, coefficients, directions, feat)
    order = list(reversed(range(1, feat // 2)))
    received = {q: swap(send[q], "feat", 1) for q in order + [0]}
    table = tables(rank, linear, rows)
    paired = pair(linear, received[order[0]], table)
    middle = min(3 * SPAN, rows // 2)
    firsts = [
        swap(join(keep[q], received[q], 0, middle, paired, []), "feat", 2 * q) for q in order
    ]
    rests = [
        swap(join(keep[q], received[q], middle, rows - middle, paired, [received[0]]), "feat", 2 * q)
        for q in order
    ]

    risk, total = risks(paired, firsts, event_row, rows)
    sums, ordered_events = risk_sums(risk, rank, event_row, table, rows)
    later = jnp.zeros_like(total)
    bit = 1
    while bit < ex:
        total, later = ranges(bit, total, swap(total, "ex", bit), later, rests + [sums] if bit == 1 else [])
        bit *= 2
    tangent, one, plain = ordered_values(keep[0], received[0], firsts, risk, rank, table, 0, middle)
    more_tangent, two, more = ordered_values(
        keep[0], received[0], rests, risk, rank, table, middle, rows - middle
    )
    later_sums = suffix_sums(one, two, padded)
    hazard, ordered_squares, message = shares(later, sums, ordered_events, plain, more, later_sums)
    messages = [message] + [swap(message, "ex", i) for i in range(1, ex)]
    cumulative, squares = hazards(hazard, ordered_squares, rank, rows)
    summed = prefix_sums(later_sums, ordered_squares, rank, padded)
    own = weights(messages, tangent, more_tangent, summed, risk, cumulative, squares)

    chips = {0: own}
    for q in range(1, feat // 2):
        chips[q] = swap(own, "feat", 2 * q)
    near = [chips[q] for q in range(feat // 2)]
    first_sum = gradients(near, dosages)
    far = [swap(piece, "feat", 1) for piece in hold(near, first_sum)]
    partial_sums = [first_sum, gradients(far, dosages)]
    bit = 1
    while 2 * bit < ex:
        received = [swap(message, "ex", bit) for message in partial_sums]
        partial_sums = [merge(mine, other, variants) for mine, other in zip(partial_sums, received)]
        bit *= 2
    received = [swap(message, "ex", bit) for message in partial_sums]
    first = add(partial_sums[0], received[0], variants)
    result = finish(first, partial_sums[1], received[1], total, feat)
    if padded != each:
        result = result.reshape(variants, feat, padded)[:, :, :each].reshape(variants, k)
    return result


def solution(mesh):
    placed = (P("ex", "feat"), P("feat"), P("feat", None), P("ex"), P("ex"))
    return jax.shard_map(
        local, mesh=mesh, in_specs=placed, out_specs=P("feat", None), check_vma=False
    )
```

```python
import functools

import jax
import jax.numpy as jnp
from jax import lax
from jax.experimental import pallas as pl
from jax.experimental.pallas import tpu as pltpu
from jax.sharding import PartitionSpec as P

F32 = jnp.float32
BF16 = jnp.bfloat16
LO = 256
NT = (((1,), (1,)), ((), ()))
SPAN = 512
VMEM = pl.BlockSpec(memory_space=pltpu.VMEM)
HBM = pl.BlockSpec(memory_space=pltpu.HBM)
PARAMS = dict(vmem_limit_bytes=24 * 1024 * 1024)


def swap(x, axis, i):
    count = lax.axis_size(axis)
    return lax.ppermute(x, axis, [(s, s ^ i) for s in range(count)])


def split_two(x):
    high = x.astype(BF16).astype(F32)
    return high, x - high


def split_three(x):
    first, rest = split_two(x)
    second, third = split_two(rest)
    return first, second, third


def one_hot(values, count, kind=BF16):
    shape = (count, values.shape[1])
    return jnp.where(lax.broadcasted_iota(jnp.int32, shape, 0) == values, 1.0, 0.0).astype(kind)


def triangle(n, keep):
    first = lax.broadcasted_iota(jnp.int32, (n, n), 0)
    second = lax.broadcasted_iota(jnp.int32, (n, n), 1)
    return jnp.where(keep(first, second), 1.0, 0.0)


def stacked(parts):
    return jnp.concatenate(parts, axis=0).astype(BF16)


def unstacked(values, count):
    height = values.shape[0] // count
    return sum(values[i * height : (i + 1) * height] for i in range(count))


def dot_binary(a, b):
    parts = jnp.dot(stacked(split_three(a)), b.astype(BF16), preferred_element_type=F32)
    return unstacked(parts, 3)


def binary_dot(a, b):
    a = a.astype(BF16)
    total = None
    for part in split_three(b):
        term = jnp.dot(a, part.astype(BF16), preferred_element_type=F32)
        total = term if total is None else total + term
    return total


def product_kernel(feat, kf, chunk, directions, coefficients, dosages, *refs):
    linear, keep, send = refs[0], refs[1 : 1 + feat // 2], refs[1 + feat // 2 : 1 + feat]
    table, own_directions, own_coefficients, lhs, turned, sems = refs[1 + feat :]
    me = lax.axis_index("feat")
    width = feat * kf
    persons, variants = table.shape
    steps = persons // chunk
    small = [
        pltpu.make_async_copy(directions, own_directions, sems.at[steps]),
        pltpu.make_async_copy(coefficients, own_coefficients, sems.at[steps + 1]),
    ]
    large = [
        pltpu.make_async_copy(
            dosages.at[pl.ds(i * chunk, chunk)], table.at[pl.ds(i * chunk, chunk)], sems.at[i]
        )
        for i in range(steps)
    ]
    for copy in small + large:
        copy.start()
    for copy in small:
        copy.wait()
    turned[...] = own_directions[...].astype(F32).T.reshape(turned.shape)
    for j in range(feat):
        lhs[j * kf : (j + 1) * kf] = turned[me ^ j].astype(BF16)
    lhs[width:] = jnp.broadcast_to(own_coefficients[...].astype(F32)[None, :], (16, variants)).astype(BF16)
    for i in range(steps):
        large[i].wait()
        first = i * chunk
        result = lax.dot_general(
            lhs[...], table[first : first + chunk], NT, preferred_element_type=F32
        )
        for j in range(feat):
            (send if j % 2 else keep)[j // 2][:, first : first + chunk] = result[j * kf : (j + 1) * kf]
        for start in range(0, chunk, LO):
            row = result[width : width + 1, start : start + LO]
            group = (first + start) // LO
            linear[group : group + 1, :] = row
            send[-1][group : group + 1, persons:] = row


def products(dosages, coefficients, directions, feat):
    persons, variants = dosages.shape
    k = directions.shape[1]
    kf = k // feat
    chunk = min(1024, persons)
    piece = jax.ShapeDtypeStruct((kf, persons), F32)
    first = jax.ShapeDtypeStruct((kf, persons + LO), F32)
    out = pl.pallas_call(
        functools.partial(product_kernel, feat, kf, chunk),
        in_specs=[HBM, HBM, HBM],
        out_shape=[jax.ShapeDtypeStruct((kf, LO), F32)]
        + [piece] * (feat - 1)
        + [first],
        out_specs=[VMEM] * (feat + 1),
        scratch_shapes=[
            pltpu.VMEM((persons, variants), BF16),
            pltpu.VMEM((variants, k), BF16),
            pltpu.VMEM((variants,), BF16),
            pltpu.VMEM((k + 16, variants), BF16),
            pltpu.VMEM((feat, kf, variants), F32),
            pltpu.SemaphoreType.DMA((persons // chunk + 2,)),
        ],
        compiler_params=pltpu.CompilerParams(**PARAMS),
        cost_estimate=pl.CostEstimate(
            flops=2 * persons * variants * k, bytes_accessed=persons * (variants * 2 + k * 4), transcendentals=0
        ),
        name="products",
    )(*[pltpu.with_memory_space_constraint(x, pltpu.HBM) for x in (directions, coefficients, dosages)])
    return out[0], out[1 : 1 + feat // 2], out[1 + feat // 2 :]


def power_of(largest):
    return jnp.ceil(jnp.log2(jnp.maximum(largest, 1e-30))) - 14.0


def to_short(values):
    return jnp.round(values).astype(jnp.int32).astype(jnp.int16)


def from_short(values):
    return values.astype(jnp.int32).astype(F32)


def pair_kernel(linear, received, waited, out):
    out[...] = linear[...] + received[:, received.shape[1] - LO :]


def pair(linear, received, waited):
    return pl.pallas_call(
        pair_kernel,
        in_specs=[VMEM] * 2 + [pl.BlockSpec(memory_space=pl.ANY)],
        out_shape=jax.ShapeDtypeStruct(linear.shape, F32),
        out_specs=VMEM,
        compiler_params=pltpu.CompilerParams(**PARAMS),
        name="pair",
    )(linear, received, waited)


def join_kernel(start, width, mine, other, *refs):
    linear, out = refs[0], refs[-1]
    kf = mine.shape[0]
    span = min(SPAN, width)
    lane = lax.broadcasted_iota(jnp.int32, (kf, 128), 1)
    powers = jnp.zeros((kf, 128), F32)
    for i in range(width // span):
        at = slice(start + i * span, start + (i + 1) * span)
        total = mine[:, at] + other[:, at]
        power = power_of(jnp.max(jnp.abs(total), axis=1, keepdims=True))
        out[:, i * span : (i + 1) * span] = to_short(total * jnp.exp2(-power))
        powers = jnp.where(lane == i, power, powers)
    if start == 0:
        power = power_of(jnp.max(jnp.abs(linear[...]), axis=1, keepdims=True))
        scaled = linear[...] * jnp.exp2(-power)
        whole = jnp.round(scaled)
        out[:, width : width + LO] = to_short(whole)
        out[:, width + LO : width + 2 * LO] = to_short((scaled - whole) * 32768.0)
        powers = jnp.where(lane == 127, power, powers)
    out[:, out.shape[1] - 128 :] = to_short(powers)


def join(keep, received, start, width, linear, waited):
    kf, rows = keep.shape
    extra = 2 * LO if start == 0 else 0
    return pl.pallas_call(
        functools.partial(join_kernel, start, width),
        in_specs=[VMEM] * 3 + [pl.BlockSpec(memory_space=pl.ANY)] * len(waited),
        out_shape=jax.ShapeDtypeStruct((kf, width + extra + 128), jnp.int16),
        out_specs=VMEM,
        compiler_params=pltpu.CompilerParams(**PARAMS),
        name="join",
    )(keep, received, linear, *waited)


def table_kernel(rows, rank, waited, table):
    chunk = min(512, rows)
    lane = lax.broadcasted_iota(jnp.int32, (chunk, 128), 1)
    for start in range(0, rows, chunk):
        at = slice(start, start + chunk)
        inner = lax.rem(rank[:, at], LO)
        column = jnp.broadcast_to(inner.astype(F32), (128, chunk)).T.astype(jnp.int32)
        for first in range(0, LO, 128):
            table[at, first : first + 128] = jnp.where(column == lane + first, 1.0, 0.0).astype(BF16)


def tables(rank, waited, rows):
    return pl.pallas_call(
        functools.partial(table_kernel, rows),
        in_specs=[VMEM, pl.BlockSpec(memory_space=pl.ANY)],
        out_shape=jax.ShapeDtypeStruct((rows, LO), BF16),
        out_specs=VMEM,
        compiler_params=pltpu.CompilerParams(**PARAMS),
        cost_estimate=pl.CostEstimate(flops=rows * LO * 8, bytes_accessed=rows * LO * 2, transcendentals=0),
        name="tables",
    )(rank, waited)


def risk_kernel(rows, parts, linear, *refs):
    messages, events = refs[:parts], refs[parts]
    risk_out, message = refs[parts + 1 :]
    groups = rows // LO
    total = linear[...]
    for part in messages:
        end = part.shape[1] - 128
        power = from_short(part[:, end:])[:, 127:]
        high, low = from_short(part[:, end - 2 * LO : end - LO]), from_short(part[:, end - LO : end])
        total = total + (high + low * (1.0 / 32768.0)) * jnp.exp2(power)
    risk = jnp.exp(total[:groups])
    for g in range(groups):
        risk_out[:, g * LO : (g + 1) * LO] = risk[g : g + 1]
    everything = jnp.sum(jnp.sum(risk, axis=0, keepdims=True), axis=1, keepdims=True)
    count = jnp.sum(events[...].astype(F32), axis=1, keepdims=True)
    totals = [jnp.broadcast_to(value, (1, 128)) for value in (everything, count)]
    message[...] = jnp.concatenate(totals + [jnp.zeros((6, 128), F32)], axis=0)


def risks(linear, messages, events, rows):
    return pl.pallas_call(
        functools.partial(risk_kernel, rows, len(messages)),
        in_specs=[VMEM] * (len(messages) + 2),
        out_shape=[jax.ShapeDtypeStruct((1, rows), F32), jax.ShapeDtypeStruct((8, 128), F32)],
        out_specs=[VMEM] * 2,
        compiler_params=pltpu.CompilerParams(**PARAMS),
        cost_estimate=pl.CostEstimate(flops=rows * 64, bytes_accessed=rows * 64, transcendentals=rows),
        name="risks",
    )(linear, *messages, events)


def risk_sum_kernel(rows, risk, rank, events, table, sums_out, events_out):
    groups = rows // LO
    mask = one_hot(lax.rem(rank[...], rows) // LO, groups, F32)
    pieces = [mask * part for part in split_three(risk[...])] + [mask * events[...].astype(F32)]
    lhs = jnp.concatenate(pieces, axis=0).astype(BF16)
    sorted_all = jnp.dot(lhs, table[...], preferred_element_type=F32)
    ordered = sorted_all[:groups] + sorted_all[groups : 2 * groups] + sorted_all[2 * groups : 3 * groups]
    inside = dot_binary(ordered, triangle(LO, lambda a, b: a >= b))
    totals = jnp.broadcast_to(inside[:, :1], inside.shape)
    carried = binary_dot(triangle(groups, lambda a, b: a < b), totals)
    sums_out[...] = inside + carried
    events_out[...] = sorted_all[3 * groups :]


def risk_sums(risk, rank, events, table, rows):
    flat = jax.ShapeDtypeStruct((rows // LO, LO), F32)
    return pl.pallas_call(
        functools.partial(risk_sum_kernel, rows),
        in_specs=[VMEM] * 4,
        out_shape=[flat, flat],
        out_specs=[VMEM] * 2,
        compiler_params=pltpu.CompilerParams(**PARAMS),
        cost_estimate=pl.CostEstimate(flops=rows * LO * 128, bytes_accessed=rows * 64, transcendentals=0),
        name="risk_sums",
    )(risk, rank, events, table)


def share_kernel(later, sums, events, plain, more, ordered, hazard_out, squares, message):
    kf = plain.shape[0]
    groups = sums.shape[0]
    risk_sum = sums[...] + later[0:1, 0:1]
    hazard = events[...] / risk_sum
    square = events[...] / (risk_sum * risk_sum)
    hazard_out[...] = hazard
    squares[...] = square
    scaled = jnp.zeros((kf, LO), F32)
    for g in range(groups):
        scaled = scaled + ordered[g * kf : (g + 1) * kf] * square[g : g + 1]
    message[:kf] = plain[...] + more[...]
    message[kf : 2 * kf] = sum(scaled[:, start : start + 128] for start in range(0, LO, 128))
    totals = [jnp.sum(jnp.sum(v, axis=0, keepdims=True), axis=1, keepdims=True) for v in (hazard, square)]
    rows = [jnp.broadcast_to(v, (1, 128)) for v in totals]
    message[2 * kf :] = jnp.concatenate(rows + [jnp.zeros((6, 128), F32)], axis=0)


def shares(later, sums, events, plain, more, ordered):
    flat = jax.ShapeDtypeStruct(sums.shape, F32)
    return pl.pallas_call(
        share_kernel,
        in_specs=[VMEM] * 6,
        out_shape=[flat, flat, jax.ShapeDtypeStruct((2 * plain.shape[0] + 8, 128), F32)],
        out_specs=[VMEM] * 3,
        compiler_params=pltpu.CompilerParams(**PARAMS),
        name="shares",
    )(later, sums, events, plain, more, ordered)


def hazard_kernel(rows, hazard, square, rank, cumulative, squares):
    groups = rows // LO
    inside = dot_binary(
        jnp.concatenate([hazard[...], square[...]], axis=0), triangle(LO, lambda a, b: a <= b)
    )
    totals = jnp.broadcast_to(inside[:, LO - 1 :], (2 * groups, 128))
    place = lax.rem(rank[...], rows)
    mask = one_hot(place // LO, groups, F32)
    placed = dot_binary(inside, one_hot(lax.rem(place, LO), LO))
    before = triangle(groups, lambda a, b: a > b)
    for first, out in ((0, cumulative), (groups, squares)):
        carried = binary_dot(before, totals[first : first + groups])[:, :1]
        out[...] = jnp.sum(mask * (placed[first : first + groups] + carried), axis=0, keepdims=True)


def hazards(hazard, square, rank, rows):
    row = jax.ShapeDtypeStruct((1, rows), F32)
    return pl.pallas_call(
        functools.partial(hazard_kernel, rows),
        in_specs=[VMEM] * 3,
        out_shape=[row, row],
        out_specs=[VMEM] * 2,
        compiler_params=pltpu.CompilerParams(**PARAMS),
        cost_estimate=pl.CostEstimate(flops=rows * LO * 200, bytes_accessed=rows * 64, transcendentals=0),
        name="hazards",
    )(hazard, square, rank)


def range_kernel(bit, count, *refs):
    total, other, later = refs[:3]
    total_out, later_out = refs[3 + count :]
    is_later = (lax.axis_index("ex") & bit) == 0
    later_out[...] = later[...] + jnp.where(is_later, other[...], 0.0)
    total_out[...] = total[...] + other[...]


def ranges(bit, total, other, later, waited):
    return pl.pallas_call(
        functools.partial(range_kernel, bit, len(waited)),
        in_specs=[VMEM] * 3 + [pl.BlockSpec(memory_space=pl.ANY)] * len(waited),
        out_shape=[jax.ShapeDtypeStruct(total.shape, F32)] * 2,
        out_specs=[VMEM] * 2,
        compiler_params=pltpu.CompilerParams(**PARAMS),
        name="ranges",
    )(total, other, later, *waited)


def order_kernel(start, parts, own, other, *refs):
    messages, (risk, rank, table) = refs[:parts], refs[parts : parts + 3]
    tangent_out, ordered_out, plain, lhs = refs[-4:]
    kf, width = tangent_out.shape
    rows = own.shape[1]
    groups = rows // LO
    span = min(SPAN, width)
    folded = jnp.zeros((kf, 128), F32)
    powers = [jnp.exp2(from_short(part[:, part.shape[1] - 128 :])) for part in messages]
    for i in range(width // span):
        at = slice(start + i * span, start + (i + 1) * span)
        here = slice(i * span, (i + 1) * span)
        tangent = own[:, at] + other[:, at]
        for part, power in zip(messages, powers):
            tangent = tangent + from_short(part[:, here]) * power[:, i : i + 1]
        tangent_out[:, here] = tangent
        weighted = tangent * risk[:, at]
        folded = folded + sum(weighted[:, j : j + 128] for j in range(0, span, 128))
        high, low = split_two(weighted)
        high, low = high.astype(BF16), low.astype(BF16)
        group = jnp.broadcast_to(lax.rem(rank[:, at], rows) // LO, (kf, span))
        for g in range(groups):
            mask = jnp.where(group == g, 1.0, 0.0).astype(BF16)
            lhs[2 * g * kf : (2 * g + 1) * kf, here] = high * mask
            lhs[(2 * g + 1) * kf : (2 * g + 2) * kf, here] = low * mask
    plain[...] = folded
    ordered = jnp.dot(lhs[...], table[start : start + width], preferred_element_type=F32)
    for g in range(groups):
        ordered_out[g * kf : (g + 1) * kf] = (
            ordered[2 * g * kf : (2 * g + 1) * kf] + ordered[(2 * g + 1) * kf : (2 * g + 2) * kf]
        )


def ordered_values(own, other, messages, risk, rank, table, start, width):
    kf, rows = own.shape
    groups = rows // LO
    return pl.pallas_call(
        functools.partial(order_kernel, start, len(messages)),
        in_specs=[VMEM] * (len(messages) + 5),
        out_shape=[
            jax.ShapeDtypeStruct((kf, width), F32),
            jax.ShapeDtypeStruct((groups * kf, LO), F32),
            jax.ShapeDtypeStruct((kf, 128), F32),
        ],
        out_specs=[VMEM] * 3,
        scratch_shapes=[pltpu.VMEM((groups * 2 * kf, width), BF16)],
        compiler_params=pltpu.CompilerParams(**PARAMS),
        cost_estimate=pl.CostEstimate(
            flops=2 * width * LO * groups * 2 * kf, bytes_accessed=width * kf * 24, transcendentals=0
        ),
        name="ordered_values",
    )(own, other, *messages, risk, rank, table)


def suffix_kernel(kf, one, two, sums):
    groups = sums.shape[0] // kf
    inside = dot_binary(one[...] + two[...], triangle(LO, lambda a, b: a >= b))
    carried = jnp.zeros((kf, 1), F32)
    for g in reversed(range(groups)):
        rows_of = slice(g * kf, (g + 1) * kf)
        sums[rows_of] = inside[rows_of] + carried
        carried = carried + inside[rows_of, :1]


def suffix_sums(one, two, kf):
    return pl.pallas_call(
        functools.partial(suffix_kernel, kf),
        in_specs=[VMEM] * 2,
        out_shape=jax.ShapeDtypeStruct(one.shape, F32),
        out_specs=VMEM,
        compiler_params=pltpu.CompilerParams(**PARAMS),
        name="suffix_sums",
    )(one, two)


def prefix_kernel(sums, squares, rank, out):
    kf, rows = out.shape
    groups = squares.shape[0]
    chunk = min(512, rows)
    hazard = [sums[g * kf : (g + 1) * kf] * squares[g : g + 1, :] for g in range(groups)]
    inside = dot_binary(jnp.concatenate(hazard, axis=0), triangle(LO, lambda a, b: a <= b))
    carried = jnp.zeros((kf, 1), F32)
    summed = [None] * groups
    for g in range(groups):
        rows_of = slice(g * kf, (g + 1) * kf)
        summed[g] = inside[rows_of] + carried
        carried = carried + inside[rows_of, LO - 1 :]
    both = stacked(split_two(jnp.concatenate(summed, axis=0)))
    for start in range(0, rows, chunk):
        at = slice(start, start + chunk)
        place = lax.rem(rank[:, at], rows)
        group = place // LO
        spread = one_hot(lax.rem(place, LO), LO)
        placed = unstacked(jnp.dot(both, spread, preferred_element_type=F32), 2)
        picked = jnp.zeros((kf, chunk), F32)
        for g in range(groups):
            picked = picked + jnp.where(group == g, placed[g * kf : (g + 1) * kf], 0.0)
        out[:, at] = picked


def prefix_sums(sums, squares, rank, kf):
    rows = rank.shape[1]
    return pl.pallas_call(
        prefix_kernel,
        in_specs=[VMEM] * 3,
        out_shape=jax.ShapeDtypeStruct((kf, rows), F32),
        out_specs=VMEM,
        compiler_params=pltpu.CompilerParams(**PARAMS),
        cost_estimate=pl.CostEstimate(
            flops=4 * rows * LO * (rows // LO) * kf, bytes_accessed=rows * kf * 24, transcendentals=0
        ),
        name="prefix_sums",
    )(sums, squares, rank)


def weight_kernel(ex, *refs):
    messages, (first, rest, local, risk, cumulative, squares) = refs[:ex], refs[ex : ex + 6]
    weighted, placed = refs[ex + 6 :]
    kf = first.shape[0]
    me = lax.axis_index("ex")
    for i in range(ex):
        placed[me ^ i] = messages[i][...]
    later = jnp.zeros((kf, 128), F32)
    own_later, before = later, later
    hazard_before = jnp.zeros((1, 128), F32)
    for b in reversed(range(ex)):
        plain, scaled, square = placed[b, :kf], placed[b, kf : 2 * kf], placed[b, 2 * kf + 1 : 2 * kf + 2]
        own_later = own_later + jnp.where(b > me, plain, 0.0)
        before = before + jnp.where(b < me, scaled + square * later, 0.0)
        hazard_before = hazard_before + jnp.where(b < me, placed[b, 2 * kf : 2 * kf + 1], 0.0)
        later = later + plain
    own_later = jnp.sum(own_later, axis=1, keepdims=True)
    before = jnp.sum(before, axis=1, keepdims=True)
    hazard_before = hazard_before[:, :1]
    for start, part in ((0, first), (first.shape[1], rest)):
        at = slice(start, start + part.shape[1])
        value = part[...] * (cumulative[:, at] + hazard_before) - (
            local[:, at] + squares[:, at] * own_later + before
        )
        weighted[:, at] = (risk[:, at] * value).astype(BF16)


def weights(messages, first, rest, local, risk, cumulative, squares):
    ex = len(messages)
    return pl.pallas_call(
        functools.partial(weight_kernel, ex),
        in_specs=[VMEM] * (ex + 6),
        out_shape=jax.ShapeDtypeStruct(local.shape, BF16),
        out_specs=VMEM,
        scratch_shapes=[pltpu.VMEM((ex,) + messages[0].shape, F32)],
        compiler_params=pltpu.CompilerParams(**PARAMS),
        name="weights",
    )(*messages, first, rest, local, risk, cumulative, squares)


def encode(values, message):
    columns = len(values)
    powers = []
    for i, value in enumerate(values):
        power = power_of(jnp.max(jnp.abs(value), axis=0, keepdims=True))
        scaled = to_short(value * jnp.exp2(-power))
        for j in range(value.shape[0] // 16):
            message[j * columns + i] = scaled[j * 16 : (j + 1) * 16]
        powers.append(power)
    powers.append(jnp.zeros((16 - columns, 128), F32))
    message[message.shape[0] - 1] = to_short(jnp.concatenate(powers, axis=0))


def decode(message, columns):
    last = message.shape[0] - 1
    scales = jnp.exp2(from_short(message[last]))
    values = []
    for i in range(columns):
        value = jnp.concatenate([from_short(message[j]) for j in range(i, last, columns)], axis=0)
        values.append(value * scales[i : i + 1])
    return values


def decode_sum(mine, other, columns):
    return [one + two for one, two in zip(decode(mine, columns), decode(other, columns))]


def gradient_kernel(parts, kf, *refs):
    pieces, dosages, out, weighted = refs[:parts], refs[parts], refs[parts + 1], refs[parts + 2]
    for i in range(parts):
        weighted[i * kf : (i + 1) * kf, :] = pieces[i][...]
    total = jnp.dot(weighted[...], dosages[...], preferred_element_type=F32)
    encode([total[:, at : at + 128] for at in range(0, total.shape[1], 128)], out)


def gradients(pieces, dosages):
    parts = len(pieces)
    kf, persons = pieces[0].shape
    k, variants = kf * parts, dosages.shape[1]
    return pl.pallas_call(
        functools.partial(gradient_kernel, parts, kf),
        in_specs=[VMEM] * (parts + 1),
        out_shape=jax.ShapeDtypeStruct((k * variants // 2048 + 1, 16, 128), jnp.int16),
        out_specs=VMEM,
        scratch_shapes=[pltpu.VMEM((k, persons), BF16)],
        compiler_params=pltpu.CompilerParams(**PARAMS),
        cost_estimate=pl.CostEstimate(
            flops=2 * persons * variants * k, bytes_accessed=persons * (variants * 2 + k * 2), transcendentals=0
        ),
        name="gradients",
    )(*pieces, dosages)


def merge_kernel(columns, mine, other, out):
    encode(decode_sum(mine, other, columns), out)


def merge(mine, other, variants):
    return pl.pallas_call(
        functools.partial(merge_kernel, variants // 128),
        in_specs=[VMEM] * 2,
        out_shape=jax.ShapeDtypeStruct(mine.shape, jnp.int16),
        out_specs=VMEM,
        compiler_params=pltpu.CompilerParams(**PARAMS),
        name="merge",
    )(mine, other)


def add_kernel(mine, other, out):
    for i, value in enumerate(decode_sum(mine, other, out.shape[1] // 128)):
        out[:, i * 128 : (i + 1) * 128] = value


def add(mine, other, variants):
    return pl.pallas_call(
        add_kernel,
        in_specs=[VMEM] * 2,
        out_shape=jax.ShapeDtypeStruct(((mine.shape[0] - 1) * 2048 // variants, variants), F32),
        out_specs=VMEM,
        compiler_params=pltpu.CompilerParams(**PARAMS),
        name="add",
    )(mine, other)


def finish_kernel(feat, kf, first, mine, other, count, out, placed, total, sems):
    me = lax.axis_index("feat")
    variants = out.shape[0]
    scale = count[1:2, 0:1]
    for q in range(feat // 2):
        placed[me ^ (2 * q)] = first[q * kf : (q + 1) * kf]
    for i, value in enumerate(decode_sum(mine, other, variants // 128)):
        for q in range(feat // 2):
            placed[me ^ (2 * q + 1), :, i * 128 : (i + 1) * 128] = value[q * kf : (q + 1) * kf]
    copies = []
    for i in range(variants // 128):
        at = slice(i * 128, (i + 1) * 128)
        total[at] = placed[:, :, at].reshape(feat * kf, 128).T / scale
        copies.append(
            pltpu.make_async_copy(
                total.at[pl.ds(i * 128, 128)], out.at[pl.ds(i * 128, 128)], sems.at[i]
            )
        )
        copies[i].start()
    for copy in copies:
        copy.wait()


def finish(first, mine, other, count, feat):
    k, variants = 2 * first.shape[0], first.shape[1]
    kf = k // feat
    return pl.pallas_call(
        functools.partial(finish_kernel, feat, kf),
        in_specs=[VMEM] * 4,
        out_shape=jax.ShapeDtypeStruct((variants, k), F32),
        out_specs=HBM,
        scratch_shapes=[
            pltpu.VMEM((feat, kf, variants), F32),
            pltpu.VMEM((variants, k), F32),
            pltpu.SemaphoreType.DMA((variants // 128,)),
        ],
        compiler_params=pltpu.CompilerParams(**PARAMS),
        name="finish",
    )(first, mine, other, count)


def local(dosages, coefficients, directions, event_rank, events):
    feat, ex = lax.axis_size("feat"), lax.axis_size("ex")
    rows = dosages.shape[0]
    variants, k = directions.shape
    each = k // feat
    padded = -(-each // 16) * 16
    if padded != each:
        directions = jnp.pad(directions.reshape(variants, feat, each), ((0, 0), (0, 0), (0, padded - each)))
        directions = directions.reshape(variants, feat * padded)
    rank, event_row = event_rank[None], events[None]

    linear, keep, send = products(dosages, coefficients, directions, feat)
    order = list(range(1, feat // 2))
    received = {q: swap(send[q], "feat", 1) for q in order[::-1] + [0]}
    table = tables(rank, linear, rows)
    paired = pair(linear, received[order[-1]], table)
    middle = min(3 * SPAN, rows // 2)
    firsts = [
        swap(join(keep[q], received[q], 0, middle, paired, []), "feat", 2 * q) for q in order
    ]
    rests = [
        swap(join(keep[q], received[q], middle, rows - middle, paired, [received[0]]), "feat", 2 * q)
        for q in order
    ]

    risk, total = risks(paired, firsts, event_row, rows)
    sums, ordered_events = risk_sums(risk, rank, event_row, table, rows)
    later = jnp.zeros_like(total)
    bit = 1
    while bit < ex:
        total, later = ranges(bit, total, swap(total, "ex", bit), later, rests + [sums] if bit == 1 else [])
        bit *= 2
    tangent, one, plain = ordered_values(keep[0], received[0], firsts, risk, rank, table, 0, middle)
    more_tangent, two, more = ordered_values(
        keep[0], received[0], rests, risk, rank, table, middle, rows - middle
    )
    later_sums = suffix_sums(one, two, padded)
    hazard, ordered_squares, message = shares(later, sums, ordered_events, plain, more, later_sums)
    messages = [message] + [swap(message, "ex", i) for i in range(1, ex)]
    cumulative, squares = hazards(hazard, ordered_squares, rank, rows)
    summed = prefix_sums(later_sums, ordered_squares, rank, padded)
    own = weights(messages, tangent, more_tangent, summed, risk, cumulative, squares)

    chips = {0: own}
    for q in range(1, feat // 2):
        chips[q] = swap(own, "feat", 2 * q)
    near = [chips[q] for q in range(feat // 2)]
    far = [swap(chips[q], "feat", 1) for q in range(feat // 2)]
    partial_sums = [gradients(pieces, dosages) for pieces in (near, far)]
    bit = 1
    while 2 * bit < ex:
        received = [swap(message, "ex", bit) for message in partial_sums]
        partial_sums = [merge(mine, other, variants) for mine, other in zip(partial_sums, received)]
        bit *= 2
    received = [swap(message, "ex", bit) for message in partial_sums]
    first = add(partial_sums[0], received[0], variants)
    result = finish(first, partial_sums[1], received[1], total, feat)
    if padded != each:
        result = result.reshape(variants, feat, padded)[:, :, :each].reshape(variants, k)
    return result


def solution(mesh):
    placed = (P("ex", "feat"), P("feat"), P("feat", None), P("ex"), P("ex"))
    return jax.shard_map(
        local, mesh=mesh, in_specs=placed, out_specs=P("feat", None), check_vma=False
    )
```

```python
import functools

import jax
import jax.numpy as jnp
from jax import lax
from jax.experimental import pallas as pl
from jax.experimental.pallas import tpu as pltpu
from jax.sharding import PartitionSpec as P

F32 = jnp.float32
BF16 = jnp.bfloat16
LO = 256
NT = (((1,), (1,)), ((), ()))
SPAN = 512
VMEM = pl.BlockSpec(memory_space=pltpu.VMEM)
HBM = pl.BlockSpec(memory_space=pltpu.HBM)
PARAMS = dict(vmem_limit_bytes=24 * 1024 * 1024)


def swap(x, axis, i):
    count = lax.axis_size(axis)
    return lax.ppermute(x, axis, [(s, s ^ i) for s in range(count)])


def split_two(x):
    high = x.astype(BF16).astype(F32)
    return high, x - high


def split_three(x):
    first, rest = split_two(x)
    second, third = split_two(rest)
    return first, second, third


def one_hot(values, count, kind=BF16):
    shape = (count, values.shape[1])
    return jnp.where(lax.broadcasted_iota(jnp.int32, shape, 0) == values, 1.0, 0.0).astype(kind)


def triangle(n, keep):
    first = lax.broadcasted_iota(jnp.int32, (n, n), 0)
    second = lax.broadcasted_iota(jnp.int32, (n, n), 1)
    return jnp.where(keep(first, second), 1.0, 0.0)


def stacked(parts):
    return jnp.concatenate(parts, axis=0).astype(BF16)


def unstacked(values, count):
    height = values.shape[0] // count
    return sum(values[i * height : (i + 1) * height] for i in range(count))


def dot_binary(a, b):
    parts = jnp.dot(stacked(split_three(a)), b.astype(BF16), preferred_element_type=F32)
    return unstacked(parts, 3)


def binary_dot(a, b):
    a = a.astype(BF16)
    total = None
    for part in split_three(b):
        term = jnp.dot(a, part.astype(BF16), preferred_element_type=F32)
        total = term if total is None else total + term
    return total


def product_kernel(feat, kf, sizes, directions, coefficients, dosages, *refs):
    linear, keep, send = refs[0], refs[1 : 1 + feat // 2], refs[1 + feat // 2 : 1 + feat]
    table, own_directions, own_coefficients, lhs, turned, sems = refs[1 + feat :]
    me = lax.axis_index("feat")
    width = feat * kf
    persons, variants = table.shape
    steps = len(sizes)
    starts = [sum(sizes[:i]) for i in range(steps)]
    small = [
        pltpu.make_async_copy(directions, own_directions, sems.at[steps]),
        pltpu.make_async_copy(coefficients, own_coefficients, sems.at[steps + 1]),
    ]
    large = [
        pltpu.make_async_copy(
            dosages.at[pl.ds(first, chunk)], table.at[pl.ds(first, chunk)], sems.at[i]
        )
        for i, (first, chunk) in enumerate(zip(starts, sizes))
    ]
    for copy in small + large:
        copy.start()
    for copy in small:
        copy.wait()
    turned[...] = own_directions[...].astype(F32).T.reshape(turned.shape)
    for j in range(feat):
        lhs[j * kf : (j + 1) * kf] = turned[me ^ j].astype(BF16)
    lhs[width:] = jnp.broadcast_to(own_coefficients[...].astype(F32)[None, :], (16, variants)).astype(BF16)
    for copy, first, chunk in zip(large, starts, sizes):
        copy.wait()
        result = lax.dot_general(
            lhs[...], table[first : first + chunk], NT, preferred_element_type=F32
        )
        for j in range(feat):
            (send if j % 2 else keep)[j // 2][:, first : first + chunk] = result[j * kf : (j + 1) * kf]
        for start in range(0, chunk, LO):
            row = result[width : width + 1, start : start + LO]
            group = (first + start) // LO
            linear[group : group + 1, :] = row
            send[-1][group : group + 1, persons:] = row


def products(dosages, coefficients, directions, feat):
    persons, variants = dosages.shape
    k = directions.shape[1]
    kf = k // feat
    chunk = min(1024, persons)
    sizes = [chunk] * (persons // chunk)
    piece = jax.ShapeDtypeStruct((kf, persons), F32)
    first = jax.ShapeDtypeStruct((kf, persons + LO), F32)
    out = pl.pallas_call(
        functools.partial(product_kernel, feat, kf, tuple(sizes)),
        in_specs=[HBM, HBM, HBM],
        out_shape=[jax.ShapeDtypeStruct((kf, LO), F32)]
        + [piece] * (feat - 1)
        + [first],
        out_specs=[VMEM] * (feat + 1),
        scratch_shapes=[
            pltpu.VMEM((persons, variants), BF16),
            pltpu.VMEM((variants, k), BF16),
            pltpu.VMEM((variants,), BF16),
            pltpu.VMEM((k + 16, variants), BF16),
            pltpu.VMEM((feat, kf, variants), F32),
            pltpu.SemaphoreType.DMA((len(sizes) + 2,)),
        ],
        compiler_params=pltpu.CompilerParams(**PARAMS),
        cost_estimate=pl.CostEstimate(
            flops=2 * persons * variants * k, bytes_accessed=persons * (variants * 2 + k * 4), transcendentals=0
        ),
        name="products",
    )(*[pltpu.with_memory_space_constraint(x, pltpu.HBM) for x in (directions, coefficients, dosages)])
    return out[0], out[1 : 1 + feat // 2], out[1 + feat // 2 :]


def power_of(largest):
    return jnp.ceil(jnp.log2(jnp.maximum(largest, 1e-30))) - 14.0


def to_short(values):
    return jnp.round(values).astype(jnp.int32).astype(jnp.int16)


def from_short(values):
    return values.astype(jnp.int32).astype(F32)


def pair_kernel(linear, received, waited, out):
    out[...] = linear[...] + received[:, received.shape[1] - LO :]


def pair(linear, received, waited):
    return pl.pallas_call(
        pair_kernel,
        in_specs=[VMEM] * 2 + [pl.BlockSpec(memory_space=pl.ANY)],
        out_shape=jax.ShapeDtypeStruct(linear.shape, F32),
        out_specs=VMEM,
        compiler_params=pltpu.CompilerParams(**PARAMS),
        name="pair",
    )(linear, received, waited)


def join_kernel(start, width, mine, other, *refs):
    linear, out = refs[0], refs[-1]
    kf = mine.shape[0]
    span = min(SPAN, width)
    lane = lax.broadcasted_iota(jnp.int32, (kf, 128), 1)
    powers = jnp.zeros((kf, 128), F32)
    for i in range(width // span):
        at = slice(start + i * span, start + (i + 1) * span)
        total = mine[:, at] + other[:, at]
        power = power_of(jnp.max(jnp.abs(total), axis=1, keepdims=True))
        out[:, i * span : (i + 1) * span] = to_short(total * jnp.exp2(-power))
        powers = jnp.where(lane == i, power, powers)
    if start == 0:
        power = power_of(jnp.max(jnp.abs(linear[...]), axis=1, keepdims=True))
        scaled = linear[...] * jnp.exp2(-power)
        whole = jnp.round(scaled)
        out[:, width : width + LO] = to_short(whole)
        out[:, width + LO : width + 2 * LO] = to_short((scaled - whole) * 32768.0)
        powers = jnp.where(lane == 127, power, powers)
    out[:, out.shape[1] - 128 :] = to_short(powers)


def join(keep, received, start, width, linear, waited):
    kf, rows = keep.shape
    extra = 2 * LO if start == 0 else 0
    return pl.pallas_call(
        functools.partial(join_kernel, start, width),
        in_specs=[VMEM] * 3 + [pl.BlockSpec(memory_space=pl.ANY)] * len(waited),
        out_shape=jax.ShapeDtypeStruct((kf, width + extra + 128), jnp.int16),
        out_specs=VMEM,
        compiler_params=pltpu.CompilerParams(**PARAMS),
        name="join",
    )(keep, received, linear, *waited)


def table_kernel(rows, rank, waited, table):
    chunk = min(512, rows)
    lane = lax.broadcasted_iota(jnp.int32, (chunk, 128), 1)
    for start in range(0, rows, chunk):
        at = slice(start, start + chunk)
        inner = lax.rem(rank[:, at], LO)
        column = jnp.broadcast_to(inner.astype(F32), (128, chunk)).T.astype(jnp.int32)
        for first in range(0, LO, 128):
            table[at, first : first + 128] = jnp.where(column == lane + first, 1.0, 0.0).astype(BF16)


def tables(rank, waited, rows):
    return pl.pallas_call(
        functools.partial(table_kernel, rows),
        in_specs=[VMEM, pl.BlockSpec(memory_space=pl.ANY)],
        out_shape=jax.ShapeDtypeStruct((rows, LO), BF16),
        out_specs=VMEM,
        compiler_params=pltpu.CompilerParams(**PARAMS),
        cost_estimate=pl.CostEstimate(flops=rows * LO * 8, bytes_accessed=rows * LO * 2, transcendentals=0),
        name="tables",
    )(rank, waited)


def risk_kernel(rows, parts, linear, *refs):
    messages, events = refs[:parts], refs[parts]
    risk_out, message = refs[parts + 1 :]
    groups = rows // LO
    total = linear[...]
    for part in messages:
        end = part.shape[1] - 128
        power = from_short(part[:, end:])[:, 127:]
        high, low = from_short(part[:, end - 2 * LO : end - LO]), from_short(part[:, end - LO : end])
        total = total + (high + low * (1.0 / 32768.0)) * jnp.exp2(power)
    risk = jnp.exp(total[:groups])
    for g in range(groups):
        risk_out[:, g * LO : (g + 1) * LO] = risk[g : g + 1]
    everything = jnp.sum(jnp.sum(risk, axis=0, keepdims=True), axis=1, keepdims=True)
    count = jnp.sum(events[...].astype(F32), axis=1, keepdims=True)
    totals = [jnp.broadcast_to(value, (1, 128)) for value in (everything, count)]
    message[...] = jnp.concatenate(totals + [jnp.zeros((6, 128), F32)], axis=0)


def risks(linear, messages, events, rows):
    return pl.pallas_call(
        functools.partial(risk_kernel, rows, len(messages)),
        in_specs=[VMEM] * (len(messages) + 2),
        out_shape=[jax.ShapeDtypeStruct((1, rows), F32), jax.ShapeDtypeStruct((8, 128), F32)],
        out_specs=[VMEM] * 2,
        compiler_params=pltpu.CompilerParams(**PARAMS),
        cost_estimate=pl.CostEstimate(flops=rows * 64, bytes_accessed=rows * 64, transcendentals=rows),
        name="risks",
    )(linear, *messages, events)


def risk_sum_kernel(rows, risk, rank, events, table, sums_out, events_out):
    groups = rows // LO
    mask = one_hot(lax.rem(rank[...], rows) // LO, groups, F32)
    pieces = [mask * part for part in split_three(risk[...])] + [mask * events[...].astype(F32)]
    lhs = jnp.concatenate(pieces, axis=0).astype(BF16)
    sorted_all = jnp.dot(lhs, table[...], preferred_element_type=F32)
    ordered = sorted_all[:groups] + sorted_all[groups : 2 * groups] + sorted_all[2 * groups : 3 * groups]
    inside = dot_binary(ordered, triangle(LO, lambda a, b: a >= b))
    totals = jnp.broadcast_to(inside[:, :1], inside.shape)
    carried = binary_dot(triangle(groups, lambda a, b: a < b), totals)
    sums_out[...] = inside + carried
    events_out[...] = sorted_all[3 * groups :]


def risk_sums(risk, rank, events, table, rows):
    flat = jax.ShapeDtypeStruct((rows // LO, LO), F32)
    return pl.pallas_call(
        functools.partial(risk_sum_kernel, rows),
        in_specs=[VMEM] * 4,
        out_shape=[flat, flat],
        out_specs=[VMEM] * 2,
        compiler_params=pltpu.CompilerParams(**PARAMS),
        cost_estimate=pl.CostEstimate(flops=rows * LO * 128, bytes_accessed=rows * 64, transcendentals=0),
        name="risk_sums",
    )(risk, rank, events, table)


def share_kernel(later, sums, events, plain, more, ordered, hazard_out, squares, message):
    kf = plain.shape[0]
    groups = sums.shape[0]
    risk_sum = sums[...] + later[0:1, 0:1]
    hazard = events[...] / risk_sum
    square = events[...] / (risk_sum * risk_sum)
    hazard_out[...] = hazard
    squares[...] = square
    scaled = jnp.zeros((kf, LO), F32)
    for g in range(groups):
        scaled = scaled + ordered[g * kf : (g + 1) * kf] * square[g : g + 1]
    message[:kf] = plain[...] + more[...]
    message[kf : 2 * kf] = sum(scaled[:, start : start + 128] for start in range(0, LO, 128))
    totals = [jnp.sum(jnp.sum(v, axis=0, keepdims=True), axis=1, keepdims=True) for v in (hazard, square)]
    rows = [jnp.broadcast_to(v, (1, 128)) for v in totals]
    message[2 * kf :] = jnp.concatenate(rows + [jnp.zeros((6, 128), F32)], axis=0)


def shares(later, sums, events, plain, more, ordered):
    flat = jax.ShapeDtypeStruct(sums.shape, F32)
    return pl.pallas_call(
        share_kernel,
        in_specs=[VMEM] * 6,
        out_shape=[flat, flat, jax.ShapeDtypeStruct((2 * plain.shape[0] + 8, 128), F32)],
        out_specs=[VMEM] * 3,
        compiler_params=pltpu.CompilerParams(**PARAMS),
        name="shares",
    )(later, sums, events, plain, more, ordered)


def hazard_kernel(rows, hazard, square, rank, cumulative, squares):
    groups = rows // LO
    inside = dot_binary(
        jnp.concatenate([hazard[...], square[...]], axis=0), triangle(LO, lambda a, b: a <= b)
    )
    totals = jnp.broadcast_to(inside[:, LO - 1 :], (2 * groups, 128))
    place = lax.rem(rank[...], rows)
    mask = one_hot(place // LO, groups, F32)
    placed = dot_binary(inside, one_hot(lax.rem(place, LO), LO))
    before = triangle(groups, lambda a, b: a > b)
    for first, out in ((0, cumulative), (groups, squares)):
        carried = binary_dot(before, totals[first : first + groups])[:, :1]
        out[...] = jnp.sum(mask * (placed[first : first + groups] + carried), axis=0, keepdims=True)


def hazards(hazard, square, rank, rows):
    row = jax.ShapeDtypeStruct((1, rows), F32)
    return pl.pallas_call(
        functools.partial(hazard_kernel, rows),
        in_specs=[VMEM] * 3,
        out_shape=[row, row],
        out_specs=[VMEM] * 2,
        compiler_params=pltpu.CompilerParams(**PARAMS),
        cost_estimate=pl.CostEstimate(flops=rows * LO * 200, bytes_accessed=rows * 64, transcendentals=0),
        name="hazards",
    )(hazard, square, rank)


def range_kernel(bit, count, *refs):
    total, other, later = refs[:3]
    total_out, later_out = refs[3 + count :]
    is_later = (lax.axis_index("ex") & bit) == 0
    later_out[...] = later[...] + jnp.where(is_later, other[...], 0.0)
    total_out[...] = total[...] + other[...]


def ranges(bit, total, other, later, waited):
    return pl.pallas_call(
        functools.partial(range_kernel, bit, len(waited)),
        in_specs=[VMEM] * 3 + [pl.BlockSpec(memory_space=pl.ANY)] * len(waited),
        out_shape=[jax.ShapeDtypeStruct(total.shape, F32)] * 2,
        out_specs=[VMEM] * 2,
        compiler_params=pltpu.CompilerParams(**PARAMS),
        name="ranges",
    )(total, other, later, *waited)


def order_kernel(start, parts, own, other, *refs):
    messages, (risk, rank, table) = refs[:parts], refs[parts : parts + 3]
    tangent_out, ordered_out, plain, lhs = refs[-4:]
    kf, width = tangent_out.shape
    rows = own.shape[1]
    groups = rows // LO
    span = min(SPAN, width)
    folded = jnp.zeros((kf, 128), F32)
    powers = [jnp.exp2(from_short(part[:, part.shape[1] - 128 :])) for part in messages]
    for i in range(width // span):
        at = slice(start + i * span, start + (i + 1) * span)
        here = slice(i * span, (i + 1) * span)
        tangent = own[:, at] + other[:, at]
        for part, power in zip(messages, powers):
            tangent = tangent + from_short(part[:, here]) * power[:, i : i + 1]
        tangent_out[:, here] = tangent
        weighted = tangent * risk[:, at]
        folded = folded + sum(weighted[:, j : j + 128] for j in range(0, span, 128))
        high, low = split_two(weighted)
        high, low = high.astype(BF16), low.astype(BF16)
        group = jnp.broadcast_to(lax.rem(rank[:, at], rows) // LO, (kf, span))
        for g in range(groups):
            mask = jnp.where(group == g, 1.0, 0.0).astype(BF16)
            lhs[2 * g * kf : (2 * g + 1) * kf, here] = high * mask
            lhs[(2 * g + 1) * kf : (2 * g + 2) * kf, here] = low * mask
    plain[...] = folded
    ordered = jnp.dot(lhs[...], table[start : start + width], preferred_element_type=F32)
    for g in range(groups):
        ordered_out[g * kf : (g + 1) * kf] = (
            ordered[2 * g * kf : (2 * g + 1) * kf] + ordered[(2 * g + 1) * kf : (2 * g + 2) * kf]
        )


def ordered_values(own, other, messages, risk, rank, table, start, width):
    kf, rows = own.shape
    groups = rows // LO
    return pl.pallas_call(
        functools.partial(order_kernel, start, len(messages)),
        in_specs=[VMEM] * (len(messages) + 5),
        out_shape=[
            jax.ShapeDtypeStruct((kf, width), F32),
            jax.ShapeDtypeStruct((groups * kf, LO), F32),
            jax.ShapeDtypeStruct((kf, 128), F32),
        ],
        out_specs=[VMEM] * 3,
        scratch_shapes=[pltpu.VMEM((groups * 2 * kf, width), BF16)],
        compiler_params=pltpu.CompilerParams(**PARAMS),
        cost_estimate=pl.CostEstimate(
            flops=2 * width * LO * groups * 2 * kf, bytes_accessed=width * kf * 24, transcendentals=0
        ),
        name="ordered_values",
    )(own, other, *messages, risk, rank, table)


def suffix_kernel(kf, one, two, sums):
    groups = sums.shape[0] // kf
    inside = dot_binary(one[...] + two[...], triangle(LO, lambda a, b: a >= b))
    carried = jnp.zeros((kf, 1), F32)
    for g in reversed(range(groups)):
        rows_of = slice(g * kf, (g + 1) * kf)
        sums[rows_of] = inside[rows_of] + carried
        carried = carried + inside[rows_of, :1]


def suffix_sums(one, two, kf):
    return pl.pallas_call(
        functools.partial(suffix_kernel, kf),
        in_specs=[VMEM] * 2,
        out_shape=jax.ShapeDtypeStruct(one.shape, F32),
        out_specs=VMEM,
        compiler_params=pltpu.CompilerParams(**PARAMS),
        name="suffix_sums",
    )(one, two)


def prefix_kernel(sums, squares, rank, out):
    kf, rows = out.shape
    groups = squares.shape[0]
    chunk = min(512, rows)
    hazard = [sums[g * kf : (g + 1) * kf] * squares[g : g + 1, :] for g in range(groups)]
    inside = dot_binary(jnp.concatenate(hazard, axis=0), triangle(LO, lambda a, b: a <= b))
    carried = jnp.zeros((kf, 1), F32)
    summed = [None] * groups
    for g in range(groups):
        rows_of = slice(g * kf, (g + 1) * kf)
        summed[g] = inside[rows_of] + carried
        carried = carried + inside[rows_of, LO - 1 :]
    both = stacked(split_two(jnp.concatenate(summed, axis=0)))
    for start in range(0, rows, chunk):
        at = slice(start, start + chunk)
        place = lax.rem(rank[:, at], rows)
        group = place // LO
        spread = one_hot(lax.rem(place, LO), LO)
        placed = unstacked(jnp.dot(both, spread, preferred_element_type=F32), 2)
        picked = jnp.zeros((kf, chunk), F32)
        for g in range(groups):
            picked = picked + jnp.where(group == g, placed[g * kf : (g + 1) * kf], 0.0)
        out[:, at] = picked


def prefix_sums(sums, squares, rank, kf):
    rows = rank.shape[1]
    return pl.pallas_call(
        prefix_kernel,
        in_specs=[VMEM] * 3,
        out_shape=jax.ShapeDtypeStruct((kf, rows), F32),
        out_specs=VMEM,
        compiler_params=pltpu.CompilerParams(**PARAMS),
        cost_estimate=pl.CostEstimate(
            flops=4 * rows * LO * (rows // LO) * kf, bytes_accessed=rows * kf * 24, transcendentals=0
        ),
        name="prefix_sums",
    )(sums, squares, rank)


def weight_kernel(places, *refs):
    ex = len(places)
    messages, (first, rest, local, risk, cumulative, squares) = refs[:ex], refs[ex : ex + 6]
    weighted, placed = refs[ex + 6 :]
    kf = first.shape[0]
    me = lax.axis_index("ex")
    for i, part in zip(places, messages):
        placed[me ^ i] = part[...]
    later = jnp.zeros((kf, 128), F32)
    own_later, before = later, later
    hazard_before = jnp.zeros((1, 128), F32)
    for b in reversed(range(ex)):
        plain, scaled, square = placed[b, :kf], placed[b, kf : 2 * kf], placed[b, 2 * kf + 1 : 2 * kf + 2]
        own_later = own_later + jnp.where(b > me, plain, 0.0)
        before = before + jnp.where(b < me, scaled + square * later, 0.0)
        hazard_before = hazard_before + jnp.where(b < me, placed[b, 2 * kf : 2 * kf + 1], 0.0)
        later = later + plain
    own_later = jnp.sum(own_later, axis=1, keepdims=True)
    before = jnp.sum(before, axis=1, keepdims=True)
    hazard_before = hazard_before[:, :1]
    for start, part in ((0, first), (first.shape[1], rest)):
        at = slice(start, start + part.shape[1])
        value = part[...] * (cumulative[:, at] + hazard_before) - (
            local[:, at] + squares[:, at] * own_later + before
        )
        weighted[:, at] = (risk[:, at] * value).astype(BF16)


def weights(places, messages, first, rest, local, risk, cumulative, squares):
    ex = len(messages)
    return pl.pallas_call(
        functools.partial(weight_kernel, tuple(places)),
        in_specs=[VMEM] * (ex + 6),
        out_shape=jax.ShapeDtypeStruct(local.shape, BF16),
        out_specs=VMEM,
        scratch_shapes=[pltpu.VMEM((ex,) + messages[0].shape, F32)],
        compiler_params=pltpu.CompilerParams(**PARAMS),
        name="weights",
    )(*messages, first, rest, local, risk, cumulative, squares)


def encode(values, message):
    columns = len(values)
    powers = []
    for i, value in enumerate(values):
        power = power_of(jnp.max(jnp.abs(value), axis=0, keepdims=True))
        scaled = to_short(value * jnp.exp2(-power))
        for j in range(value.shape[0] // 16):
            message[j * columns + i] = scaled[j * 16 : (j + 1) * 16]
        powers.append(power)
    powers.append(jnp.zeros((16 - columns, 128), F32))
    message[message.shape[0] - 1] = to_short(jnp.concatenate(powers, axis=0))


def decode(message, columns):
    last = message.shape[0] - 1
    scales = jnp.exp2(from_short(message[last]))
    values = []
    for i in range(columns):
        value = jnp.concatenate([from_short(message[j]) for j in range(i, last, columns)], axis=0)
        values.append(value * scales[i : i + 1])
    return values


def decode_sum(mine, other, columns):
    return [one + two for one, two in zip(decode(mine, columns), decode(other, columns))]


def gradient_kernel(parts, kf, *refs):
    pieces, dosages, out, weighted = refs[:parts], refs[parts], refs[parts + 1], refs[parts + 2]
    for i in range(parts):
        weighted[i * kf : (i + 1) * kf, :] = pieces[i][...]
    total = jnp.dot(weighted[...], dosages[...], preferred_element_type=F32)
    encode([total[:, at : at + 128] for at in range(0, total.shape[1], 128)], out)


def gradients(pieces, dosages):
    parts = len(pieces)
    kf, persons = pieces[0].shape
    k, variants = kf * parts, dosages.shape[1]
    return pl.pallas_call(
        functools.partial(gradient_kernel, parts, kf),
        in_specs=[VMEM] * (parts + 1),
        out_shape=jax.ShapeDtypeStruct((k * variants // 2048 + 1, 16, 128), jnp.int16),
        out_specs=VMEM,
        scratch_shapes=[pltpu.VMEM((k, persons), BF16)],
        compiler_params=pltpu.CompilerParams(**PARAMS),
        cost_estimate=pl.CostEstimate(
            flops=2 * persons * variants * k, bytes_accessed=persons * (variants * 2 + k * 2), transcendentals=0
        ),
        name="gradients",
    )(*pieces, dosages)


def merge_kernel(columns, mine, other, out):
    encode(decode_sum(mine, other, columns), out)


def merge(mine, other, variants):
    return pl.pallas_call(
        functools.partial(merge_kernel, variants // 128),
        in_specs=[VMEM] * 2,
        out_shape=jax.ShapeDtypeStruct(mine.shape, jnp.int16),
        out_specs=VMEM,
        compiler_params=pltpu.CompilerParams(**PARAMS),
        name="merge",
    )(mine, other)


def add_kernel(mine, other, out):
    for i, value in enumerate(decode_sum(mine, other, out.shape[1] // 128)):
        out[:, i * 128 : (i + 1) * 128] = value


def add(mine, other, variants):
    return pl.pallas_call(
        add_kernel,
        in_specs=[VMEM] * 2,
        out_shape=jax.ShapeDtypeStruct(((mine.shape[0] - 1) * 2048 // variants, variants), F32),
        out_specs=VMEM,
        compiler_params=pltpu.CompilerParams(**PARAMS),
        name="add",
    )(mine, other)


def finish_kernel(feat, kf, first, mine, other, count, out, placed, total, sems):
    me = lax.axis_index("feat")
    variants = out.shape[0]
    scale = count[1:2, 0:1]
    copies = []
    for i, value in enumerate(decode_sum(mine, other, variants // 128)):
        at = slice(i * 128, (i + 1) * 128)
        for q in range(feat // 2):
            rows = slice(q * kf, (q + 1) * kf)
            placed[i, me ^ (2 * q)] = first[rows, at]
            placed[i, me ^ (2 * q + 1)] = value[rows]
        total[at] = placed[i].reshape(feat * kf, 128).T / scale
        copies.append(
            pltpu.make_async_copy(
                total.at[pl.ds(i * 128, 128)], out.at[pl.ds(i * 128, 128)], sems.at[i]
            )
        )
        copies[i].start()
    for copy in copies:
        copy.wait()


def finish(first, mine, other, count, feat):
    k, variants = 2 * first.shape[0], first.shape[1]
    kf = k // feat
    return pl.pallas_call(
        functools.partial(finish_kernel, feat, kf),
        in_specs=[VMEM] * 4,
        out_shape=jax.ShapeDtypeStruct((variants, k), F32),
        out_specs=HBM,
        scratch_shapes=[
            pltpu.VMEM((variants // 128, feat, kf, 128), F32),
            pltpu.VMEM((variants, k), F32),
            pltpu.SemaphoreType.DMA((variants // 128,)),
        ],
        compiler_params=pltpu.CompilerParams(**PARAMS),
        name="finish",
    )(first, mine, other, count)


def local(dosages, coefficients, directions, event_rank, events):
    feat, ex = lax.axis_size("feat"), lax.axis_size("ex")
    rows = dosages.shape[0]
    variants, k = directions.shape
    each = k // feat
    padded = -(-each // 16) * 16
    if padded != each:
        directions = jnp.pad(directions.reshape(variants, feat, each), ((0, 0), (0, 0), (0, padded - each)))
        directions = directions.reshape(variants, feat * padded)
    rank, event_row = event_rank[None], events[None]

    linear, keep, send = products(dosages, coefficients, directions, feat)
    order = list(reversed(range(1, feat // 2)))
    received = {q: swap(send[q], "feat", 1) for q in order + [0]}
    table = tables(rank, linear, rows)
    paired = pair(linear, received[order[0]], table)
    middle = min(3 * SPAN, rows // 2)
    firsts = [
        swap(join(keep[q], received[q], 0, middle, paired, []), "feat", 2 * q) for q in order
    ]
    rests = [
        swap(join(keep[q], received[q], middle, rows - middle, paired, [received[0]]), "feat", 2 * q)
        for q in order
    ]

    risk, total = risks(paired, firsts, event_row, rows)
    sums, ordered_events = risk_sums(risk, rank, event_row, table, rows)
    later = jnp.zeros_like(total)
    bit = 1
    while bit < ex:
        total, later = ranges(bit, total, swap(total, "ex", bit), later, rests + [sums] if bit == 1 else [])
        bit *= 2
    tangent, one, plain = ordered_values(keep[0], received[0], firsts, risk, rank, table, 0, middle)
    more_tangent, two, more = ordered_values(
        keep[0], received[0], rests, risk, rank, table, middle, rows - middle
    )
    later_sums = suffix_sums(one, two, padded)
    hazard, ordered_squares, message = shares(later, sums, ordered_events, plain, more, later_sums)
    places = list(range(ex))
    places[-2:] = places[:-3:-1]
    messages = [swap(message, "ex", i) if i else message for i in places]
    cumulative, squares = hazards(hazard, ordered_squares, rank, rows)
    summed = prefix_sums(later_sums, ordered_squares, rank, padded)
    own = weights(places, messages, tangent, more_tangent, summed, risk, cumulative, squares)

    chips = {0: own}
    for q in range(1, feat // 2):
        chips[q] = swap(own, "feat", 2 * q)
    near = [chips[q] for q in range(feat // 2)]
    far = [swap(chips[q], "feat", 1) for q in range(feat // 2)]
    partial_sums = [gradients(pieces, dosages) for pieces in (near, far)]
    bit = 1
    while 2 * bit < ex:
        received = [swap(message, "ex", bit) for message in partial_sums]
        partial_sums = [merge(mine, other, variants) for mine, other in zip(partial_sums, received)]
        bit *= 2
    received = [swap(message, "ex", bit) for message in partial_sums]
    first = add(partial_sums[0], received[0], variants)
    result = finish(first, partial_sums[1], received[1], total, feat)
    if padded != each:
        result = result.reshape(variants, feat, padded)[:, :, :each].reshape(variants, k)
    return result


def solution(mesh):
    placed = (P("ex", "feat"), P("feat"), P("feat", None), P("ex"), P("ex"))
    return jax.shard_map(
        local, mesh=mesh, in_specs=placed, out_specs=P("feat", None), check_vma=False
    )
```
